32 devices in a mesh: section: 4 (over y, x), tm: 2 (over core), space: 4 (over z).
Axes of the slice: x: 2, y: 2, z: 4, core: 2. Of those that a mesh axis runs over, the one named last changes fastest.
Arguments:
- video: bfloat16 [4, 32, 128, 128], P('tm', ('section', 'space')), may hold values from -6 to 6
- cotangent: bfloat16 [4, 32, 128, 128], P('tm', ('section', 'space')), may hold values from -6 to 6
- spatial_weights: bfloat16 [4, 9, 128, 128], P('section'), may hold values from -0.1875 to 0.1875
- temporal_weights: bfloat16 [4, 3, 128, 128], P('section'), may hold values from -0.3125 to 0.3125
Outputs:
- grad_spatial: float32 [4, 9, 128, 128], P('section')
- grad_temporal: float32 [4, 3, 128, 128], P('section')
- grad_video: bfloat16 [4, 32, 128, 128], P('tm', ('section', 'space'))
The draws below stay inside these ranges and needn't reach their ends.
All inputs are finite; a program needn't handle non-finite values.
Results may differ from the reference program's by a relative error of at most 0.019.
Values may be sent and summed in bfloat16 or wider, within the bound.
No kernel may reach another device: no remote copies, remote signals or barrier semaphores. Data moves between devices by JAX's collectives and lax.ppermute only.
A program may use at most 64 MiB of HBM per device.

```python
import jax
import jax.numpy as jnp

C = 128
W = 128
FRAMES = 4
H = 32
SECTIONS = 4


def block_scale(key, dims, shards, smallest, top_value):
    factor_of = 1.0
    for dim, blocks in shards:
        steps = jax.random.uniform(jax.random.fold_in(jax.random.fold_in(key, 6), dim), (blocks,), jnp.float32, smallest / len(shards), top_value / len(shards))
        factor_of = factor_of * jnp.repeat(jnp.exp(steps), dims[dim] // blocks).reshape((-1,) + (1,) * (len(dims) - 1 - dim))
    return factor_of


def normal_values(key, extent, deviation, most, pieces=(), dtype=jnp.bfloat16):
    loudness = block_scale(key, extent, pieces, -0.22, 0.18) if pieces else 1.0
    array = jax.random.normal(key, extent, jnp.float32) * deviation * loudness
    return jnp.minimum(jnp.maximum(array, -most), most).astype(dtype)


def setup_inputs(seed: int = 0) -> dict:
    splits = jax.random.split(jax.random.key(seed), 5)
    return {
        "video": normal_values(splits[0], (FRAMES, H, W, C), 1.0, 6.0, ((0, 2), (1, 16))),
        "cotangent": normal_values(splits[1], (FRAMES, H, W, C), 1.0, 6.0, ((0, 2), (1, 16))),
        "spatial_weights": normal_values(splits[2], (SECTIONS, 9, C, C), (9 * C) ** -0.5, 0.1875, ((0, 4),)),
        "temporal_weights": normal_values(splits[3], (SECTIONS, 3, C, C), (3 * C) ** -0.5, 0.3125, ((0, 4),)),
    }


def conv_forward(inputs, spatial_weight, temporal_weight):
    frames, height, columns, chans = inputs.shape
    padded = jnp.pad(inputs.astype(jnp.float32), ((0, 0), (1, 1), (1, 1), (0, 0)))
    before = jnp.zeros((frames, height, columns, chans), jnp.float32)
    for offset in range(9):
        row_off = offset // 3
        col_off = offset % 3
        before = before + jnp.einsum('frwc,cd->frwd', padded[:, row_off:row_off + height, col_off:col_off + columns], spatial_weight[offset].astype(jnp.float32))
    hidden = jax.nn.silu(before).astype(jnp.bfloat16)
    timeline = jnp.pad(hidden.astype(jnp.float32), ((2, 0), (0, 0), (0, 0), (0, 0)))
    mixed = jnp.zeros((frames, height, columns, chans), jnp.float32)
    for offset in range(3):
        mixed = mixed + jnp.einsum('frwc,cd->frwd', timeline[offset:offset + frames], temporal_weight[offset].astype(jnp.float32))
    outputs = (inputs.astype(jnp.float32) + mixed).astype(jnp.bfloat16)
    return (padded, before, timeline, outputs)

def conv_backward(grad, padded, before, timeline, spatial_weight, temporal_weight):
    frames, height, columns, chans = grad.shape
    grad_f = grad.astype(jnp.float32)
    ahead = jnp.pad(grad_f, ((0, 2), (0, 0), (0, 0), (0, 0)))
    temporal_list = []
    hidden_grad = jnp.zeros((frames, height, columns, chans), jnp.float32)
    for offset in range(3):
        temporal_list.append(jnp.einsum('frwc,frwd->cd', timeline[offset:offset + frames], grad_f))
        hidden_grad = hidden_grad + jnp.einsum('frwd,cd->frwc', ahead[2 - offset:2 - offset + frames], temporal_weight[offset].astype(jnp.float32))
    sigma = jax.nn.sigmoid(before)
    pre_grad = (hidden_grad * sigma * (1.0 + before * (1.0 - sigma))).astype(jnp.bfloat16)
    pre_f = pre_grad.astype(jnp.float32)
    rimmed = jnp.pad(pre_f, ((0, 0), (1, 1), (1, 1), (0, 0)))
    spatial_list = []
    back = jnp.zeros((frames, height, columns, chans), jnp.float32)
    for offset in range(9):
        row_off = offset // 3
        col_off = offset % 3
        spatial_list.append(jnp.einsum('frwc,frwd->cd', padded[:, row_off:row_off + height, col_off:col_off + columns], pre_f))
        back = back + jnp.einsum('frwd,cd->frwc', rimmed[:, 2 - row_off:2 - row_off + height, 2 - col_off:2 - col_off + columns], spatial_weight[offset].astype(jnp.float32))
    new_grad = (grad_f + back).astype(jnp.bfloat16)
    return (jnp.stack(spatial_list), jnp.stack(temporal_list), new_grad)

def reference(video, cotangent, spatial_weights, temporal_weights):
    blocks = spatial_weights.shape[0]
    records = []
    inputs = video
    for step in range(blocks):
        padded, before, timeline, outputs = conv_forward(inputs, spatial_weights[step], temporal_weights[step])
        records.append((padded, before, timeline))
        inputs = outputs
    grad = cotangent
    spatial_out = [None] * blocks
    temporal_out = [None] * blocks
    for step in reversed(range(blocks)):
        padded, before, timeline = records[step]
        spatial_grad, temporal_grad, grad = conv_backward(grad, padded, before, timeline, spatial_weights[step], temporal_weights[step])
        spatial_out[step] = spatial_grad
        temporal_out[step] = temporal_grad
    factor = 1.0 / math_sqrt(cotangent.shape[0] * cotangent.shape[1] * cotangent.shape[2])
    return (jnp.stack(spatial_out) * factor, jnp.stack(temporal_out) * factor, grad)

def math_sqrt(count):
    return float(count) ** 0.5
```

```python
import jax
import jax.numpy as jnp
from jax import lax
from jax.sharding import PartitionSpec as P


def with_halo(cells, sides, width):
    for axis, dim in sides:
        count = lax.axis_size(axis)
        ends = count - 1
        head = lax.slice_in_dim(cells, 0, width, axis=dim)
        tail = lax.slice_in_dim(cells, cells.shape[dim] - width, cells.shape[dim], axis=dim)
        cells = jnp.concatenate(
            [
                lax.ppermute(tail, axis, [(i, (i + 1) % count) for i in range(ends)]),
                cells,
                lax.ppermute(head, axis, [((i + 1) % count, i) for i in range(ends)]),
            ],
            axis=dim,
        )
    return cells


def shifted(value, axis, steps):
    count = lax.axis_size(axis)
    leading, last = (max(0, -steps), min(count, count - steps))
    return lax.ppermute(value, axis, [(source, source + steps) for source in range(leading, last)])


def forward_layer(inputs, spatial_weight, temporal_weight):
    frames = inputs.shape[0]
    height = inputs.shape[1]
    columns = inputs.shape[2]
    padded = with_halo(inputs, ((("section", "space"), 1),), 1)
    padded = jnp.pad(padded, ((0, 0), (0, 0), (1, 1), (0, 0)))
    before = jnp.einsum(
        "frwc,cd->frwd",
        padded[:, 0:height, 0:columns],
        spatial_weight[0],
        preferred_element_type=jnp.float32,
    )
    for offset in range(1, 9):
        row_off = offset // 3
        col_off = offset % 3
        before = before + jnp.einsum(
            "frwc,cd->frwd",
            padded[:, row_off : row_off + height, col_off : col_off + columns],
            spatial_weight[offset],
            preferred_element_type=jnp.float32,
        )
    hidden = jax.nn.silu(before).astype(jnp.bfloat16)
    earlier = shifted(hidden, "tm", 1)
    timeline = jnp.concatenate([earlier, hidden], 0)
    mixed = jnp.einsum(
        "frwc,cd->frwd", timeline[0:frames], temporal_weight[0], preferred_element_type=jnp.float32
    )
    for offset in range(1, 3):
        mixed = mixed + jnp.einsum(
            "frwc,cd->frwd",
            timeline[offset : offset + frames],
            temporal_weight[offset],
            preferred_element_type=jnp.float32,
        )
    outputs = (inputs.astype(jnp.float32) + mixed).astype(jnp.bfloat16)
    return (padded, before, timeline, outputs)


def backward_layer(grad, padded, before, timeline, spatial_weight, temporal_weight):
    frames = grad.shape[0]
    height = grad.shape[1]
    columns = grad.shape[2]
    later = shifted(grad, "tm", -1)
    ahead = jnp.concatenate([grad, later], 0)
    temporal_list = []
    hidden_grad = jnp.zeros(grad.shape, jnp.float32)
    for offset in range(3):
        temporal_list.append(
            jnp.einsum(
                "frwc,frwd->cd",
                timeline[offset : offset + frames],
                grad,
                preferred_element_type=jnp.float32,
            )
        )
        hidden_grad = hidden_grad + jnp.einsum(
            "frwd,cd->frwc",
            ahead[2 - offset : 2 - offset + frames],
            temporal_weight[offset],
            preferred_element_type=jnp.float32,
        )
    sigma = jax.nn.sigmoid(before)
    pre_grad = (hidden_grad * sigma * (1.0 + before * (1.0 - sigma))).astype(jnp.bfloat16)
    rimmed = with_halo(pre_grad, ((("section", "space"), 1),), 1)
    rimmed = jnp.pad(rimmed, ((0, 0), (0, 0), (1, 1), (0, 0)))
    spatial_list = []
    back = jnp.zeros(grad.shape, jnp.float32)
    for offset in range(9):
        row_off = offset // 3
        col_off = offset % 3
        spatial_list.append(
            jnp.einsum(
                "frwc,frwd->cd",
                padded[:, row_off : row_off + height, col_off : col_off + columns],
                pre_grad,
                preferred_element_type=jnp.float32,
            )
        )
        back = back + jnp.einsum(
            "frwd,cd->frwc",
            rimmed[:, 2 - row_off : 2 - row_off + height, 2 - col_off : 2 - col_off + columns],
            spatial_weight[offset],
            preferred_element_type=jnp.float32,
        )
    new_grad = (grad.astype(jnp.float32) + back).astype(jnp.bfloat16)
    return (jnp.stack(spatial_list), jnp.stack(temporal_list), new_grad)


def gathered_kernels(spatial_weights, temporal_weights):
    cores = lax.axis_size("tm")
    blocks = lax.axis_size("section")
    own = jnp.concatenate([spatial_weights[0], temporal_weights[0]], 0)
    taps = own.shape[0] // cores
    half = lax.dynamic_slice_in_dim(own, lax.axis_index("tm") * taps, taps, 0)
    halves = lax.all_to_all(
        jnp.broadcast_to(half[None], (blocks,) + half.shape), "section", 0, 0, tiled=True
    )
    both = lax.all_to_all(
        jnp.broadcast_to(halves[None], (cores,) + halves.shape), "tm", 0, 0, tiled=True
    )
    whole = jnp.concatenate([both[core] for core in range(cores)], 1)
    split = spatial_weights.shape[1]
    return whole[:, :split], whole[:, split:]


def summed_kernels(partial):
    blocks, taps, chans, outs = partial.shape
    cores, tiles = lax.axis_size("tm"), lax.axis_size("space")
    part = partial.astype(jnp.bfloat16).reshape(blocks, cores, taps // cores, chans, outs)
    part = lax.all_to_all(part.swapaxes(0, 1), "tm", 0, 0, tiled=True)
    part = part.astype(jnp.float32).sum(0).astype(jnp.bfloat16)
    part = lax.all_to_all(part, "section", 0, 0, tiled=True)
    part = part.astype(jnp.float32).sum(0).astype(jnp.bfloat16)
    part = lax.all_to_all(part.reshape(tiles, -1, outs), "space", 0, 0, tiled=True)
    part = part.astype(jnp.float32).sum(0).astype(jnp.bfloat16)
    whole = lax.all_to_all(
        jnp.broadcast_to(part[None], (cores * tiles,) + part.shape),
        ("tm", "space"), 0, 0, tiled=True,
    )
    return whole.reshape(taps, chans, outs).astype(jnp.float32)


def on_device(video, cotangent, spatial_weights, temporal_weights):
    spatial_all, temporal_all = gathered_kernels(spatial_weights, temporal_weights)
    blocks = spatial_all.shape[0]
    records = []
    inputs = video
    for step in range(blocks):
        padded, before, timeline, outputs = forward_layer(
            inputs, spatial_all[step], temporal_all[step]
        )
        records.append((padded, before, timeline))
        inputs = outputs
    grad = cotangent
    spatial_out = [None] * blocks
    temporal_out = [None] * blocks
    for step in reversed(range(blocks)):
        padded, before, timeline = records[step]
        spatial_grad, temporal_grad, grad = backward_layer(
            grad, padded, before, timeline, spatial_all[step], temporal_all[step]
        )
        spatial_out[step] = spatial_grad
        temporal_out[step] = temporal_grad
    pixel_count = (
        video.shape[0]
        * lax.axis_size("tm")
        * video.shape[1]
        * lax.axis_size("section")
        * lax.axis_size("space")
        * video.shape[2]
    )
    factor = 1.0 / float(pixel_count) ** 0.5
    stacked = jnp.concatenate([jnp.stack(spatial_out), jnp.stack(temporal_out)], 1) * factor
    own = summed_kernels(stacked)[None]
    split = spatial_weights.shape[1]
    return (own[:, :split], own[:, split:], grad)


def solution(mesh):
    return jax.shard_map(
        on_device,
        mesh=mesh,
        in_specs=(
            P("tm", ("section", "space"), None, None),
            P("tm", ("section", "space"), None, None),
            P("section", None, None, None),
            P("section", None, None, None),
        ),
        out_specs=(
            P("section", None, None, None),
            P("section", None, None, None),
            P("tm", ("section", "space"), None, None),
        ),
        check_vma=False,
    )
```

```python
import functools

import jax
import jax.numpy as jnp
from jax import lax
from jax.experimental import pallas as pl
from jax.experimental.pallas import tpu as pltpu
from jax.sharding import PartitionSpec as P

F32 = jnp.float32
BF16 = jnp.bfloat16


def rolled(value, steps):
    return pltpu.roll(value, steps % value.shape[0], 0)


def dot_t(left, right):
    return lax.dot_general(left, right, (((1,), (1,)), ((), ())), preferred_element_type=F32)


def dot_first(left, right):
    return lax.dot_general(left, right, (((0,), (0,)), ((), ())), preferred_element_type=F32)


def kernel_of(w_ref, block, tap):
    taps = w_ref.shape[2]
    return w_ref[tap // taps, block, tap % taps]


def rows_of(w_ref, block, first, last):
    return jnp.concatenate([kernel_of(w_ref, block, tap) for tap in range(first, last)], 0)


def lanes_of(w_ref, block, order):
    return jnp.concatenate([kernel_of(w_ref, block, tap) for tap in order], 1)


def forward_kernel(
    geometry, place_ref, w_ref, own_ref, above_ref, below_ref, xo_ref, ho_ref, *rest
):
    blocks, cores, group, frames_in, rows_in, halo, tile, width = geometry
    d_refs = rest[:blocks]
    x_ref, h_ref, mask_ref = rest[blocks:]
    frames = cores * frames_in
    high = tile + 2 * halo
    chans = w_ref.shape[-1]
    own_rows, own_cols = (halo, halo + tile), (halo, width - halo)
    height, columns = place_ref[2], place_ref[3]
    row = place_ref[0] + lax.broadcasted_iota(jnp.int32, (high, width, chans), 0)
    col = place_ref[1] + lax.broadcasted_iota(jnp.int32, (high, width, chans), 1)
    inside = (row >= 0) & (row < height) & (col >= 0) & (col < columns)
    mask_ref[...] = jnp.where(inside, 1.0, 0.0).astype(F32)

    def keep(block, frame, value, first):
        triple = [rolled(value, 1), value, rolled(value, -1)]
        count = value.shape[0] // width
        both = jnp.concatenate([part.astype(BF16) for part in triple], 1)
        x_ref[frame, first : first + count] = both.reshape(count, width, 3 * chans)
        start = own_rows[0] - 1 - first
        cut = [
            part.reshape(count, width, chans)[
                start : start + tile + 2, own_cols[0] : own_cols[1]
            ].astype(BF16)
            for part in triple
        ]
        xo_ref[block, frame] = jnp.concatenate(cut, 2)

    for frame in range(frames):
        core, inner = divmod(frame, frames_in)
        pieces = [
            ref[core * group + unit, inner]
            for ref in (above_ref, own_ref, below_ref)
            for unit in range(group)
        ]
        whole = jnp.concatenate(pieces, 0).reshape(high * width, chans)
        keep(0, frame, whole.astype(F32), 0)

    for block in range(blocks):
        first, last = block + 1, high - block - 1
        count = last - first
        spatial = rows_of(w_ref, block, 0, 9)
        mask = mask_ref[first:last].reshape(count * width, chans)
        for frame in range(frames):
            taps = jnp.concatenate(
                [
                    x_ref[frame, first - 1 + ky : last - 1 + ky].reshape(count * width, 3 * chans)
                    for ky in range(3)
                ],
                1,
            )
            before = jnp.dot(taps, spatial, preferred_element_type=F32)
            sigma = 1.0 / (1.0 + jnp.exp(-before))
            hidden = before * sigma * mask
            slope = (sigma * (1.0 + before * (1.0 - sigma))) * mask
            h_ref[frame, first:last] = hidden.astype(BF16).reshape(count, width, chans)
            ho_ref[block, frame] = hidden.reshape(count, width, chans)[
                own_rows[0] - first : own_rows[1] - first, own_cols[0] : own_cols[1]
            ].astype(BF16)
            rim = block + 1
            d_refs[block][frame] = slope.reshape(count, width, chans)[
                own_rows[0] - rim - first : own_rows[1] + rim - first
            ]
        if block + 1 == blocks:
            break
        for frame in range(frames):
            offsets = [kt for kt in range(3) if frame + kt - 2 >= 0]
            timeline = jnp.concatenate(
                [
                    h_ref[frame + kt - 2, first:last].reshape(count * width, chans)
                    for kt in offsets
                ],
                1,
            )
            mixed = jnp.dot(
                timeline, rows_of(w_ref, block, 9 + offsets[0], 12), preferred_element_type=F32
            )
            old = x_ref[frame, first:last, :, chans : 2 * chans].astype(F32)
            new = old.reshape(count * width, chans) + mixed
            keep(block + 1, frame, new.astype(BF16).astype(F32), first)


def backward_kernel(geometry, factor, w_ref, own_ref, above_ref, below_ref, xo_ref, ho_ref, *rest):
    blocks, cores, group, frames_in, rows_in, halo, tile, width = geometry
    d_refs = rest[:blocks]
    grad_ref, out_ref, g_ref, da_ref, dao_ref, go_ref = rest[blocks:]
    frames = cores * frames_in
    chans = w_ref.shape[-1]
    rim = blocks
    own_cols = (halo, width - halo)
    per_core = w_ref.shape[2]
    pixels = tile * (own_cols[1] - own_cols[0])

    for frame in range(frames):
        core, inner = divmod(frame, frames_in)
        half = group // 2
        pieces = [above_ref[core * half + unit, inner] for unit in range(half)]
        pieces += [own_ref[core * group + unit, inner] for unit in range(group)]
        pieces += [below_ref[core * half + unit, inner] for unit in range(half)]
        g_ref[frame] = jnp.concatenate(pieces, 0)

    def put(block, tap, value):
        grad_ref[tap // per_core, block, tap % per_core] = (value * factor).astype(BF16)

    for block in reversed(range(blocks)):
        edge = block + 1
        first, last = rim - edge, rim + tile + edge
        count = last - first
        for frame in range(frames):
            go_ref[frame] = g_ref[frame, rim : rim + tile].astype(F32)[
                :, own_cols[0] : own_cols[1]
            ].astype(BF16)
            offsets = [kt for kt in (2, 1, 0) if frame + 2 - kt < frames]
            ahead = jnp.concatenate(
                [
                    g_ref[frame + 2 - kt, first:last].reshape(count * width, chans)
                    for kt in offsets
                ],
                1,
            )
            hidden = dot_t(ahead, lanes_of(w_ref, block, [9 + kt for kt in offsets]))
            slope = d_refs[block][frame].reshape(count * width, chans)
            value = (hidden * slope).astype(BF16).astype(F32)
            triple = [rolled(value, -1), value, rolled(value, 1)]
            both = jnp.concatenate([part.astype(BF16) for part in triple], 1)
            da_ref[frame, first:last] = both.reshape(count, width, 3 * chans)
            dao_ref[frame] = value.reshape(count, width, chans)[
                edge : edge + tile, own_cols[0] : own_cols[1]
            ].astype(BF16)
        for frame in range(frames):
            inner = count - 2
            taps = jnp.concatenate(
                [
                    da_ref[frame, first + 2 - ky : first + 2 - ky + inner].reshape(
                        inner * width, 3 * chans
                    )
                    for ky in range(3)
                ],
                1,
            )
            back = dot_t(taps, lanes_of(w_ref, block, range(9)))
            old = g_ref[frame, first + 1 : last - 1].astype(F32).reshape(inner * width, chans)
            new = (old + back).astype(BF16)
            if block:
                g_ref[frame, first + 1 : last - 1] = new.reshape(inner, width, chans)
            else:
                out_ref[frame] = new.astype(F32).reshape(inner, width, chans)[
                    :, own_cols[0] : own_cols[1]
                ].astype(BF16)
        slopes = dao_ref[...].reshape(frames * pixels, chans)
        for ky in range(3):
            taps = xo_ref[block, :, ky : ky + tile].reshape(frames * pixels, 3 * chans)
            sums = dot_first(slopes, taps)
            for kx in range(3):
                put(block, 3 * ky + kx, sums[:, kx * chans : (kx + 1) * chans])
        for kt in range(3):
            skip = 2 - kt
            later = go_ref[skip:].reshape((frames - skip) * pixels, chans)
            earlier = ho_ref[block, : frames - skip].reshape((frames - skip) * pixels, chans)
            put(block, 9 + kt, dot_first(later, earlier))


def gathered_kernels(spatial_weights, temporal_weights):
    cores = lax.axis_size("tm")
    blocks = lax.axis_size("section")
    own = jnp.concatenate([spatial_weights[0], temporal_weights[0]], 0)
    taps = own.shape[0] // cores
    half = lax.dynamic_slice_in_dim(own, lax.axis_index("tm") * taps, taps, 0)
    halves = lax.all_to_all(
        jnp.broadcast_to(half[None], (blocks,) + half.shape), "section", 0, 0, tiled=True
    )
    return lax.all_to_all(
        jnp.broadcast_to(halves[None], (cores,) + halves.shape), "tm", 0, 0, tiled=True
    )


def summed_kernels(part):
    cores, blocks, taps, outs, chans = part.shape
    tiles = lax.axis_size("space")
    part = lax.all_to_all(part, "tm", 0, 0, tiled=True)
    part = part.astype(F32).sum(0).astype(BF16)
    part = lax.all_to_all(part, "section", 0, 0, tiled=True)
    part = part.astype(F32).sum(0).astype(BF16)
    part = lax.all_to_all(part.reshape(tiles, -1, chans), "space", 0, 0, tiled=True)
    part = part.astype(F32).sum(0).astype(BF16)
    whole = lax.all_to_all(
        jnp.broadcast_to(part[None], (cores * tiles,) + part.shape),
        ("tm", "space"), 0, 0, tiled=True,
    )
    return whole.reshape(cores * taps, outs, chans)


def on_device(video, cotangent, spatial_weights, temporal_weights):
    blocks, cores, tiles = (lax.axis_size(name) for name in ("section", "tm", "space"))
    frames_in, rows_in, columns, chans = video.shape
    halo = 2 * blocks
    tile = halo
    group = tile // rows_in
    parties = cores * group
    own_width = columns // parties
    width = own_width + 2 * halo
    sets = None
    if tiles != group:
        sets = [
            [core * tiles + base + unit for core in range(cores) for unit in range(group)]
            for base in range(0, tiles, group)
        ]

    kernels = gathered_kernels(spatial_weights, temporal_weights)

    both = jnp.stack([video, cotangent])
    padded = jnp.pad(both, ((0, 0), (0, 0), (0, 0), (halo, halo), (0, 0)))
    windows = jnp.stack(
        [padded[:, :, :, unit * own_width : unit * own_width + width] for unit in range(parties)]
    )
    mine = lax.all_to_all(
        windows, ("tm", "space"), 0, 0, axis_index_groups=sets, tiled=True
    )
    own_video, own_cot = mine[:, 0], mine[:, 1]
    half = group // 2
    split = own_cot.reshape((cores, group) + own_cot.shape[1:])
    upper, lower = split[:, :half], split[:, half:]
    rows = blocks * tiles

    def sent(cot, step):
        flat = jnp.concatenate([own_video, cot.reshape((cores * half,) + own_cot.shape[1:])], 0)
        pairs = [(i, i + step) for i in range(rows) if 0 <= i + step < rows]
        got = lax.ppermute(flat, ("section", "space"), pairs)
        return got[:parties], got[parties:]

    video_above, cot_above = sent(lower, group)
    video_below, cot_below = sent(upper, -group)

    place = lax.axis_index("space")
    band = (lax.axis_index("section") * tiles + place) // group
    unit = lax.axis_index("tm") * group + place % group
    total_rows = blocks * tiles * rows_in
    corner = jnp.stack(
        [band * tile - halo, unit * own_width - halo, total_rows, columns]
    ).astype(jnp.int32)
    geometry = (blocks, cores, group, frames_in, rows_in, halo, tile, width)
    frames = cores * frames_in
    high = tile + 2 * halo
    vmem = pl.BlockSpec(memory_space=pltpu.VMEM)
    params = pltpu.CompilerParams(vmem_limit_bytes=56 * 2**20)
    saved = [
        jax.ShapeDtypeStruct((frames, tile + 2 * block + 2, width, chans), F32)
        for block in range(blocks)
    ]
    features, hidden, *slopes = pl.pallas_call(
        functools.partial(forward_kernel, geometry),
        name="forward",
        in_specs=[pl.BlockSpec(memory_space=pltpu.SMEM)] + [vmem] * 4,
        out_specs=[vmem] * (2 + blocks),
        out_shape=[
            jax.ShapeDtypeStruct((blocks, frames, tile + 2, own_width, 3 * chans), BF16),
            jax.ShapeDtypeStruct((blocks, frames, tile, own_width, chans), BF16),
        ]
        + saved,
        scratch_shapes=[
            pltpu.VMEM((frames, high, width, 3 * chans), BF16),
            pltpu.VMEM((frames, high, width, chans), BF16),
            pltpu.VMEM((high, width, chans), F32),
        ],
        compiler_params=params,
    )(corner, kernels, own_video, video_above, video_below)

    pixel_count = frames * total_rows * columns
    factor = 1.0 / float(pixel_count) ** 0.5
    partial, tile_grad = pl.pallas_call(
        functools.partial(backward_kernel, geometry, factor),
        name="backward",
        in_specs=[vmem] * (6 + blocks),
        out_specs=[vmem] * 2,
        out_shape=[
            jax.ShapeDtypeStruct(kernels.shape, BF16),
            jax.ShapeDtypeStruct((frames, tile, own_width, chans), BF16),
        ],
        scratch_shapes=[
            pltpu.VMEM((frames, tile + 2 * blocks, width, chans), BF16),
            pltpu.VMEM((frames, tile + 2 * blocks, width, 3 * chans), BF16),
            pltpu.VMEM((frames, tile, own_width, chans), BF16),
            pltpu.VMEM((frames, tile, own_width, chans), BF16),
        ],
        compiler_params=params,
    )(kernels, own_cot, cot_above, cot_below, features, hidden, *slopes)

    back = tile_grad.reshape(cores, frames_in, group, rows_in, own_width, chans)
    back = back.swapaxes(1, 2).reshape(parties, frames_in, rows_in, own_width, chans)
    back = lax.all_to_all(back, ("tm", "space"), 0, 0, axis_index_groups=sets, tiled=True)
    grad_video = back.transpose(1, 2, 0, 3, 4).reshape(video.shape)

    own = summed_kernels(partial).swapaxes(1, 2).astype(F32)[None]
    count = spatial_weights.shape[1]
    return own[:, :count], own[:, count:], grad_video


def solution(mesh):
    return jax.shard_map(
        on_device,
        mesh=mesh,
        in_specs=(
            P("tm", ("section", "space"), None, None),
            P("tm", ("section", "space"), None, None),
            P("section", None, None, None),
            P("section", None, None, None),
        ),
        out_specs=(
            P("section", None, None, None),
            P("section", None, None, None),
            P("tm", ("section", "space"), None, None),
        ),
        check_vma=False,
    )
```

```python
import functools

import jax
import jax.numpy as jnp
from jax import lax
from jax.experimental import pallas as pl
from jax.experimental.pallas import tpu as pltpu
from jax.sharding import PartitionSpec as P

F32 = jnp.float32
BF16 = jnp.bfloat16


def rolled(value, steps):
    return pltpu.roll(value, steps % value.shape[0], 0)


def dot_t(left, right):
    return lax.dot_general(left, right, (((1,), (1,)), ((), ())), preferred_element_type=F32)


def dot_first(left, right):
    return lax.dot_general(left, right, (((0,), (0,)), ((), ())), preferred_element_type=F32)


def kernel_of(w_ref, block, tap):
    taps = w_ref.shape[2]
    return w_ref[tap // taps, block, tap % taps]


def rows_of(w_ref, block, first, last):
    return jnp.concatenate([kernel_of(w_ref, block, tap) for tap in range(first, last)], 0)


def lanes_of(w_ref, block, order):
    return jnp.concatenate([kernel_of(w_ref, block, tap) for tap in order], 1)


def window_kernel(halo, width, video_ref, cot_ref, video_out, cot_out):
    parties = video_out.shape[0]
    frames, rows, columns, chans = video_ref.shape
    own = width - 2 * halo
    for source, target in ((video_ref, video_out), (cot_ref, cot_out)):
        whole = source[...].astype(F32)
        for unit in range(parties):
            first, last = unit * own - halo, unit * own - halo + width
            parts = []
            if first < 0:
                parts.append(jnp.zeros((frames, rows, -first, chans), F32))
            parts.append(whole[:, :, max(first, 0) : min(last, columns)])
            if last > columns:
                parts.append(jnp.zeros((frames, rows, last - columns, chans), F32))
            piece = jnp.concatenate(parts, 2) if len(parts) > 1 else parts[0]
            target[unit] = piece.astype(BF16)


def place_kernels(place_ref, w_ref, mine_ref, other_ref):
    core = place_ref[4]
    w_ref[core] = mine_ref[...]
    w_ref[1 - core] = other_ref[...]


def forward_kernel(
    geometry, place_ref, mine_ref, other_ref, own_ref, above_ref, below_ref, xo_ref, ho_ref, *rest
):
    blocks, cores, group, frames_in, rows_in, halo, tile, width = geometry
    d_refs = rest[:blocks]
    x_ref, h_ref, mask_ref, w_ref = rest[blocks:]
    place_kernels(place_ref, w_ref, mine_ref, other_ref)
    frames = cores * frames_in
    high = tile + 2 * halo
    chans = w_ref.shape[-1]
    own_rows, own_cols = (halo, halo + tile), (halo, width - halo)
    height, columns = place_ref[2], place_ref[3]
    row = place_ref[0] + lax.broadcasted_iota(jnp.int32, (high, width, chans), 0)
    col = place_ref[1] + lax.broadcasted_iota(jnp.int32, (high, width, chans), 1)
    inside = (row >= 0) & (row < height) & (col >= 0) & (col < columns)
    mask_ref[...] = jnp.where(inside, 1.0, 0.0).astype(F32)

    def keep(block, frame, value, first):
        triple = [rolled(value, 1), value, rolled(value, -1)]
        count = value.shape[0] // width
        both = jnp.concatenate([part.astype(BF16) for part in triple], 1)
        x_ref[frame, first : first + count] = both.reshape(count, width, 3 * chans)
        start = own_rows[0] - 1 - first
        cut = [
            part.reshape(count, width, chans)[
                start : start + tile + 2, own_cols[0] : own_cols[1]
            ].astype(BF16)
            for part in triple
        ]
        xo_ref[block, frame] = jnp.concatenate(cut, 2)

    for frame in range(frames):
        core, inner = divmod(frame, frames_in)
        pieces = [
            ref[core * group + unit, inner]
            for ref in (above_ref, own_ref, below_ref)
            for unit in range(group)
        ]
        whole = jnp.concatenate(pieces, 0).reshape(high * width, chans)
        keep(0, frame, whole.astype(F32), 0)

    for block in range(blocks):
        first, last = block + 1, high - block - 1
        count = last - first
        spatial = rows_of(w_ref, block, 0, 9)
        mask = mask_ref[first:last].reshape(count * width, chans)
        for frame in range(frames):
            taps = jnp.concatenate(
                [
                    x_ref[frame, first - 1 + ky : last - 1 + ky].reshape(count * width, 3 * chans)
                    for ky in range(3)
                ],
                1,
            )
            before = jnp.dot(taps, spatial, preferred_element_type=F32)
            sigma = 1.0 / (1.0 + jnp.exp(-before))
            hidden = before * sigma * mask
            slope = (sigma * (1.0 + before * (1.0 - sigma))) * mask
            h_ref[frame, first:last] = hidden.astype(BF16).reshape(count, width, chans)
            ho_ref[block, frame] = hidden.reshape(count, width, chans)[
                own_rows[0] - first : own_rows[1] - first, own_cols[0] : own_cols[1]
            ].astype(BF16)
            rim = block + 1
            d_refs[block][frame] = slope.reshape(count, width, chans)[
                own_rows[0] - rim - first : own_rows[1] + rim - first
            ]
        if block + 1 == blocks:
            break
        for frame in range(frames):
            offsets = [kt for kt in range(3) if frame + kt - 2 >= 0]
            timeline = jnp.concatenate(
                [
                    h_ref[frame + kt - 2, first:last].reshape(count * width, chans)
                    for kt in offsets
                ],
                1,
            )
            mixed = jnp.dot(
                timeline, rows_of(w_ref, block, 9 + offsets[0], 12), preferred_element_type=F32
            )
            old = x_ref[frame, first:last, :, chans : 2 * chans].astype(F32)
            new = old.reshape(count * width, chans) + mixed
            keep(block + 1, frame, new.astype(BF16).astype(F32), first)


def backward_kernel(
    geometry, factor, place_ref, mine_ref, other_ref, own_ref, above_ref, below_ref, xo_ref, ho_ref, *rest
):
    blocks, cores, group, frames_in, rows_in, halo, tile, width = geometry
    d_refs = rest[:blocks]
    keep_ref, give_ref, out_ref, g_ref, da_ref, dao_ref, go_ref, w_ref, grad_ref = rest[blocks:]
    place_kernels(place_ref, w_ref, mine_ref, other_ref)
    frames = cores * frames_in
    chans = w_ref.shape[-1]
    rim = blocks
    own_cols = (halo, width - halo)
    per_core = w_ref.shape[2]
    pixels = tile * (own_cols[1] - own_cols[0])

    for frame in range(frames):
        core, inner = divmod(frame, frames_in)
        half = group // 2
        pieces = [above_ref[core * half + unit, inner] for unit in range(half)]
        pieces += [own_ref[core * group + unit, inner] for unit in range(group)]
        pieces += [below_ref[core * half + unit, inner] for unit in range(half)]
        g_ref[frame] = jnp.concatenate(pieces, 0)

    def put(block, tap, value):
        slot = jnp.where(place_ref[4] == tap // per_core, 0, 1)
        grad_ref[slot, block, tap % per_core] = (value * factor).astype(BF16)

    for block in reversed(range(blocks)):
        edge = block + 1
        first, last = rim - edge, rim + tile + edge
        count = last - first
        for frame in range(frames):
            go_ref[frame] = g_ref[frame, rim : rim + tile].astype(F32)[
                :, own_cols[0] : own_cols[1]
            ].astype(BF16)
            offsets = [kt for kt in (2, 1, 0) if frame + 2 - kt < frames]
            ahead = jnp.concatenate(
                [
                    g_ref[frame + 2 - kt, first:last].reshape(count * width, chans)
                    for kt in offsets
                ],
                1,
            )
            hidden = dot_t(ahead, lanes_of(w_ref, block, [9 + kt for kt in offsets]))
            slope = d_refs[block][frame].reshape(count * width, chans)
            value = (hidden * slope).astype(BF16).astype(F32)
            triple = [rolled(value, -1), value, rolled(value, 1)]
            both = jnp.concatenate([part.astype(BF16) for part in triple], 1)
            da_ref[frame, first:last] = both.reshape(count, width, 3 * chans)
            dao_ref[frame] = value.reshape(count, width, chans)[
                edge : edge + tile, own_cols[0] : own_cols[1]
            ].astype(BF16)
        for frame in range(frames):
            inner = count - 2
            taps = jnp.concatenate(
                [
                    da_ref[frame, first + 2 - ky : first + 2 - ky + inner].reshape(
                        inner * width, 3 * chans
                    )
                    for ky in range(3)
                ],
                1,
            )
            back = dot_t(taps, lanes_of(w_ref, block, range(9)))
            old = g_ref[frame, first + 1 : last - 1].astype(F32).reshape(inner * width, chans)
            new = (old + back).astype(BF16)
            if block:
                g_ref[frame, first + 1 : last - 1] = new.reshape(inner, width, chans)
            else:
                core, within = divmod(frame, frames_in)
                cut = new.astype(F32).reshape(inner, width, chans)[:, own_cols[0] : own_cols[1]]
                for unit in range(group):
                    out_ref[core * group + unit, within] = cut[
                        unit * rows_in : (unit + 1) * rows_in
                    ].astype(BF16)
        slopes = dao_ref[...].reshape(frames * pixels, chans)
        for ky in range(3):
            taps = xo_ref[block, :, ky : ky + tile].reshape(frames * pixels, 3 * chans)
            sums = dot_first(slopes, taps)
            for kx in range(3):
                put(block, 3 * ky + kx, sums[:, kx * chans : (kx + 1) * chans])
        for kt in range(3):
            skip = 2 - kt
            later = go_ref[skip:].reshape((frames - skip) * pixels, chans)
            earlier = ho_ref[block, : frames - skip].reshape((frames - skip) * pixels, chans)
            put(block, 9 + kt, dot_first(later, earlier))
    keep_ref[...] = grad_ref[0]
    give_ref[...] = grad_ref[1]


def swapped(value):
    return lax.ppermute(value, "tm", [(0, 1), (1, 0)])


def own_half(spatial_weights, temporal_weights):
    own = jnp.concatenate([spatial_weights[0], temporal_weights[0]], 0)
    taps = own.shape[0] // lax.axis_size("tm")
    return lax.dynamic_slice_in_dim(own, lax.axis_index("tm") * taps, taps, 0)


def on_device(video, cotangent, spatial_weights, temporal_weights):
    blocks, cores, tiles = (lax.axis_size(name) for name in ("section", "tm", "space"))
    frames_in, rows_in, columns, chans = video.shape
    halo = 2 * blocks
    tile = halo
    group = tile // rows_in
    parties = cores * group
    own_width = columns // parties
    width = own_width + 2 * halo
    sets = None
    if tiles != group:
        sets = [
            [core * tiles + base + unit for core in range(cores) for unit in range(group)]
            for base in range(0, tiles, group)
        ]
    vmem = pl.BlockSpec(memory_space=pltpu.VMEM)
    smem = pl.BlockSpec(memory_space=pltpu.SMEM)
    params = pltpu.CompilerParams(vmem_limit_bytes=56 * 2**20)

    windows = jax.ShapeDtypeStruct((parties, frames_in, rows_in, width, chans), BF16)
    video_windows, cot_windows = pl.pallas_call(
        functools.partial(window_kernel, halo, width),
        name="windows",
        in_specs=[vmem] * 2,
        out_specs=[vmem] * 2,
        out_shape=[windows] * 2,
        compiler_params=params,
    )(video, cotangent)

    def spread(value):
        return lax.all_to_all(value, ("tm", "space"), 0, 0, axis_index_groups=sets, tiled=True)

    def moved(value, step):
        rows = blocks * tiles
        pairs = [(i, i + step) for i in range(rows) if 0 <= i + step < rows]
        return lax.ppermute(value, ("section", "space"), pairs)

    own_video = spread(video_windows)
    half_kernels = own_half(spatial_weights, temporal_weights)
    mine = lax.all_to_all(
        jnp.broadcast_to(half_kernels[None], (blocks,) + half_kernels.shape),
        "section", 0, 0, tiled=True,
    )
    video_above, video_below = moved(own_video, group), moved(own_video, -group)
    other = swapped(mine)

    own_cot = spread(cot_windows)
    half = group // 2
    split = own_cot.reshape((cores, group) + own_cot.shape[1:])
    edge = (cores * half,) + own_cot.shape[1:]
    cot_above = moved(split[:, half:].reshape(edge), group)
    cot_below = moved(split[:, :half].reshape(edge), -group)

    place = lax.axis_index("space")
    band = (lax.axis_index("section") * tiles + place) // group
    unit = lax.axis_index("tm") * group + place % group
    total_rows = blocks * tiles * rows_in
    corner = jnp.stack(
        [band * tile - halo, unit * own_width - halo, total_rows, columns, lax.axis_index("tm")]
    ).astype(jnp.int32)
    geometry = (blocks, cores, group, frames_in, rows_in, halo, tile, width)
    frames = cores * frames_in
    high = tile + 2 * halo
    all_kernels = (cores,) + mine.shape
    saved = [
        jax.ShapeDtypeStruct((frames, tile + 2 * block + 2, width, chans), F32)
        for block in range(blocks)
    ]
    cost = pl.CostEstimate(flops=6 * 10**9, bytes_accessed=8 * 10**6, transcendentals=10**6)
    features, hidden, *slopes = pl.pallas_call(
        functools.partial(forward_kernel, geometry),
        name="forward",
        in_specs=[smem] + [vmem] * 5,
        out_specs=[vmem] * (2 + blocks),
        out_shape=[
            jax.ShapeDtypeStruct((blocks, frames, tile + 2, own_width, 3 * chans), BF16),
            jax.ShapeDtypeStruct((blocks, frames, tile, own_width, chans), BF16),
        ]
        + saved,
        scratch_shapes=[
            pltpu.VMEM((frames, high, width, 3 * chans), BF16),
            pltpu.VMEM((frames, high, width, chans), BF16),
            pltpu.VMEM((high, width, chans), F32),
            pltpu.VMEM(all_kernels, BF16),
        ],
        compiler_params=params,
        cost_estimate=cost,
    )(corner, mine, other, own_video, video_above, video_below)

    pixel_count = frames * total_rows * columns
    factor = 1.0 / float(pixel_count) ** 0.5
    keep, give, tile_grad = pl.pallas_call(
        functools.partial(backward_kernel, geometry, factor),
        name="backward",
        in_specs=[smem] + [vmem] * (7 + blocks),
        out_specs=[vmem] * 3,
        out_shape=[
            jax.ShapeDtypeStruct(mine.shape, BF16),
            jax.ShapeDtypeStruct(mine.shape, BF16),
            jax.ShapeDtypeStruct((parties, frames_in, rows_in, own_width, chans), BF16),
        ],
        scratch_shapes=[
            pltpu.VMEM((frames, tile + 2 * blocks, width, chans), BF16),
            pltpu.VMEM((frames, tile + 2 * blocks, width, 3 * chans), BF16),
            pltpu.VMEM((frames, tile, own_width, chans), BF16),
            pltpu.VMEM((frames, tile, own_width, chans), BF16),
            pltpu.VMEM(all_kernels, BF16),
            pltpu.VMEM(all_kernels, BF16),
        ],
        compiler_params=params,
        cost_estimate=cost,
    )(corner, mine, other, own_cot, cot_above, cot_below, features, hidden, *slopes)

    part = (keep.astype(F32) + swapped(give).astype(F32)).astype(BF16)
    part = lax.all_to_all(part, "section", 0, 0, tiled=True)
    part = part.astype(F32).sum(0).astype(BF16)
    part = lax.all_to_all(part.reshape(tiles, -1, chans), "space", 0, 0, tiled=True)
    part = part.astype(F32).sum(0).astype(BF16)
    shares = jnp.broadcast_to(part[None], (cores * tiles,) + part.shape)
    back = tile_grad.reshape(parties, -1, chans)
    everyone = ("tm", "space")
    if sets is None:
        got = lax.all_to_all(
            jnp.concatenate([shares, back], 1), everyone, 0, 0, tiled=True
        )
        whole, back = got[:, : part.shape[0]], got[:, part.shape[0] :]
    else:
        whole, back = lax.all_to_all(shares, everyone, 0, 0, tiled=True), spread(back)
    back = back.reshape(parties, frames_in, rows_in, own_width, chans)
    grad_video = back.transpose(1, 2, 0, 3, 4).reshape(video.shape)
    own = whole.reshape(-1, chans, chans).swapaxes(1, 2).astype(F32)[None]
    count = spatial_weights.shape[1]
    return own[:, :count], own[:, count:], grad_video


def solution(mesh):
    return jax.shard_map(
        on_device,
        mesh=mesh,
        in_specs=(
            P("tm", ("section", "space"), None, None),
            P("tm", ("section", "space"), None, None),
            P("section", None, None, None),
            P("section", None, None, None),
        ),
        out_specs=(
            P("section", None, None, None),
            P("section", None, None, None),
            P("tm", ("section", "space"), None, None),
        ),
        check_vma=False,
    )
```

```python
import functools

import jax
import jax.numpy as jnp
from jax import lax
from jax.experimental import pallas as pl
from jax.experimental.pallas import tpu as pltpu
from jax.sharding import PartitionSpec as P

F32 = jnp.float32
BF16 = jnp.bfloat16


def rolled(value, steps):
    return pltpu.roll(value, steps % value.shape[0], 0)


def dot_t(left, right):
    return lax.dot_general(left, right, (((1,), (1,)), ((), ())), preferred_element_type=F32)


def dot_first(left, right):
    return lax.dot_general(left, right, (((0,), (0,)), ((), ())), preferred_element_type=F32)


def kernel_of(w_ref, block, tap):
    taps = w_ref.shape[2]
    return w_ref[tap // taps, block, tap % taps]


def rows_of(w_ref, block, first, last):
    return jnp.concatenate([kernel_of(w_ref, block, tap) for tap in range(first, last)], 0)


def lanes_of(w_ref, block, order):
    return jnp.concatenate([kernel_of(w_ref, block, tap) for tap in order], 1)


def window_kernel(halo, width, video_ref, cot_ref, video_out, cot_out):
    parties = video_out.shape[0]
    frames, rows, columns, chans = video_ref.shape
    own = width - 2 * halo
    for source, target in ((video_ref, video_out), (cot_ref, cot_out)):
        whole = source[...].astype(F32)
        for unit in range(parties):
            first, last = unit * own - halo, unit * own - halo + width
            parts = []
            if first < 0:
                parts.append(jnp.zeros((frames, rows, -first, chans), F32))
            parts.append(whole[:, :, max(first, 0) : min(last, columns)])
            if last > columns:
                parts.append(jnp.zeros((frames, rows, last - columns, chans), F32))
            piece = jnp.concatenate(parts, 2) if len(parts) > 1 else parts[0]
            target[unit] = piece.astype(BF16)


def place_kernels(place_ref, w_ref, spatial_ref, temporal_ref, mine_refs, other_refs):
    core, section = place_ref[4], place_ref[5]
    cores, _, taps = w_ref.shape[:3]
    count = spatial_ref.shape[1]
    for tap in range(cores * taps):
        one = spatial_ref[0, tap] if tap < count else temporal_ref[0, tap - count]
        w_ref[tap // taps, section, tap % taps] = one
    for step, (mine_ref, other_ref) in enumerate(zip(mine_refs, other_refs)):
        block = jnp.bitwise_xor(section, step + 1)
        w_ref[core, block] = mine_ref[...]
        w_ref[1 - core, block] = other_ref[...]


def forward_kernel(geometry, place_ref, *rest):
    blocks, cores, group, frames_in, rows_in, halo, tile, width = geometry
    shared, rest = rest[: 2 * blocks], rest[2 * blocks :]
    own_ref, inner_ref, outer_ref, xo_ref, ho_ref = rest[:5]
    d_refs = rest[5 : 5 + blocks]
    x_ref, h_ref, mask_ref, w_ref = rest[5 + blocks :]
    place_kernels(place_ref, w_ref, shared[0], shared[1], shared[2 : 1 + blocks], shared[1 + blocks :])
    odd = place_ref[6] == 1
    frames = cores * frames_in
    high = tile + 2 * halo
    chans = w_ref.shape[-1]
    own_rows, own_cols = (halo, halo + tile), (halo, width - halo)
    height, columns = place_ref[2], place_ref[3]
    row = place_ref[0] + lax.broadcasted_iota(jnp.int32, (high, width, chans), 0)
    col = place_ref[1] + lax.broadcasted_iota(jnp.int32, (high, width, chans), 1)
    inside = (row >= 0) & (row < height) & (col >= 0) & (col < columns)
    mask_ref[...] = jnp.where(inside, 1.0, 0.0).astype(F32)

    def keep(block, frame, value, first):
        triple = [rolled(value, 1), value, rolled(value, -1)]
        count = value.shape[0] // width
        both = jnp.concatenate([part.astype(BF16) for part in triple], 1)
        x_ref[frame, first : first + count] = both.reshape(count, width, 3 * chans)
        start = own_rows[0] - 1 - first
        cut = [
            part.reshape(count, width, chans)[
                start : start + tile + 2, own_cols[0] : own_cols[1]
            ].astype(BF16)
            for part in triple
        ]
        xo_ref[block, frame] = jnp.concatenate(cut, 2)

    for frame in range(frames):
        core, inner = divmod(frame, frames_in)
        units = [core * group + unit for unit in range(group)]
        near = [inner_ref[unit, inner] for unit in units]
        far = [outer_ref[unit, inner] for unit in units]
        pieces = [jnp.where(odd, a, b) for a, b in zip(near, far)]
        pieces += [own_ref[unit, inner] for unit in units]
        pieces += [jnp.where(odd, b, a) for a, b in zip(near, far)]
        whole = jnp.concatenate(pieces, 0).reshape(high * width, chans)
        keep(0, frame, whole.astype(F32), 0)

    for block in range(blocks):
        first, last = block + 1, high - block - 1
        count = last - first
        spatial = rows_of(w_ref, block, 0, 9)
        mask = mask_ref[first:last].reshape(count * width, chans)
        for frame in range(frames):
            taps = jnp.concatenate(
                [
                    x_ref[frame, first - 1 + ky : last - 1 + ky].reshape(count * width, 3 * chans)
                    for ky in range(3)
                ],
                1,
            )
            before = jnp.dot(taps, spatial, preferred_element_type=F32)
            sigma = 1.0 / (1.0 + jnp.exp(-before))
            hidden = before * sigma * mask
            slope = (sigma * (1.0 + before * (1.0 - sigma))) * mask
            h_ref[frame, first:last] = hidden.astype(BF16).reshape(count, width, chans)
            ho_ref[block, frame] = hidden.reshape(count, width, chans)[
                own_rows[0] - first : own_rows[1] - first, own_cols[0] : own_cols[1]
            ].astype(BF16)
            rim = block + 1
            d_refs[block][frame] = slope.reshape(count, width, chans)[
                own_rows[0] - rim - first : own_rows[1] + rim - first
            ]
        if block + 1 == blocks:
            break
        for frame in range(frames):
            offsets = [kt for kt in range(3) if frame + kt - 2 >= 0]
            timeline = jnp.concatenate(
                [
                    h_ref[frame + kt - 2, first:last].reshape(count * width, chans)
                    for kt in offsets
                ],
                1,
            )
            mixed = jnp.dot(
                timeline, rows_of(w_ref, block, 9 + offsets[0], 12), preferred_element_type=F32
            )
            old = x_ref[frame, first:last, :, chans : 2 * chans].astype(F32)
            new = old.reshape(count * width, chans) + mixed
            keep(block + 1, frame, new.astype(BF16).astype(F32), first)


def backward_kernel(geometry, factor, place_ref, *rest):
    blocks, cores, group, frames_in, rows_in, halo, tile, width = geometry
    shared, rest = rest[: 2 * blocks], rest[2 * blocks :]
    own_ref, inner_ref, outer_ref, xo_ref, ho_ref = rest[:5]
    d_refs = rest[5 : 5 + blocks]
    keep_ref, give_ref, out_ref, g_ref, da_ref, dao_ref, go_ref, w_ref, grad_ref = rest[5 + blocks :]
    place_kernels(place_ref, w_ref, shared[0], shared[1], shared[2 : 1 + blocks], shared[1 + blocks :])
    odd = place_ref[6] == 1
    frames = cores * frames_in
    chans = w_ref.shape[-1]
    rim = blocks
    own_cols = (halo, width - halo)
    per_core = w_ref.shape[2]
    pixels = tile * (own_cols[1] - own_cols[0])

    for frame in range(frames):
        core, inner = divmod(frame, frames_in)
        half = group // 2
        near = [inner_ref[core * half + unit, inner] for unit in range(half)]
        far = [outer_ref[core * half + unit, inner] for unit in range(half)]
        pieces = [jnp.where(odd, a, b) for a, b in zip(near, far)]
        pieces += [own_ref[core * group + unit, inner] for unit in range(group)]
        pieces += [jnp.where(odd, b, a) for a, b in zip(near, far)]
        g_ref[frame] = jnp.concatenate(pieces, 0)

    def put(block, tap, value):
        slot = jnp.where(place_ref[4] == tap // per_core, 0, 1)
        where = jnp.bitwise_xor(place_ref[5], block)
        grad_ref[slot, where, tap % per_core] = (value * factor).astype(BF16)

    for block in reversed(range(blocks)):
        edge = block + 1
        first, last = rim - edge, rim + tile + edge
        count = last - first
        for frame in range(frames):
            go_ref[frame] = g_ref[frame, rim : rim + tile].astype(F32)[
                :, own_cols[0] : own_cols[1]
            ].astype(BF16)
            offsets = [kt for kt in (2, 1, 0) if frame + 2 - kt < frames]
            ahead = jnp.concatenate(
                [
                    g_ref[frame + 2 - kt, first:last].reshape(count * width, chans)
                    for kt in offsets
                ],
                1,
            )
            hidden = dot_t(ahead, lanes_of(w_ref, block, [9 + kt for kt in offsets]))
            slope = d_refs[block][frame].reshape(count * width, chans)
            value = (hidden * slope).astype(BF16).astype(F32)
            triple = [rolled(value, -1), value, rolled(value, 1)]
            both = jnp.concatenate([part.astype(BF16) for part in triple], 1)
            da_ref[frame, first:last] = both.reshape(count, width, 3 * chans)
            dao_ref[frame] = value.reshape(count, width, chans)[
                edge : edge + tile, own_cols[0] : own_cols[1]
            ].astype(BF16)
        for frame in range(frames):
            inner = count - 2
            taps = jnp.concatenate(
                [
                    da_ref[frame, first + 2 - ky : first + 2 - ky + inner].reshape(
                        inner * width, 3 * chans
                    )
                    for ky in range(3)
                ],
                1,
            )
            back = dot_t(taps, lanes_of(w_ref, block, range(9)))
            old = g_ref[frame, first + 1 : last - 1].astype(F32).reshape(inner * width, chans)
            new = (old + back).astype(BF16)
            if block:
                g_ref[frame, first + 1 : last - 1] = new.reshape(inner, width, chans)
            else:
                core, within = divmod(frame, frames_in)
                cut = new.astype(F32).reshape(inner, width, chans)[:, own_cols[0] : own_cols[1]]
                for unit in range(group):
                    out_ref[core * group + unit, within] = cut[
                        unit * rows_in : (unit + 1) * rows_in
                    ].astype(BF16)
        slopes = dao_ref[...].reshape(frames * pixels, chans)
        for ky in range(3):
            taps = xo_ref[block, :, ky : ky + tile].reshape(frames * pixels, 3 * chans)
            sums = dot_first(slopes, taps)
            for kx in range(3):
                put(block, 3 * ky + kx, sums[:, kx * chans : (kx + 1) * chans])
        for kt in range(3):
            skip = 2 - kt
            later = go_ref[skip:].reshape((frames - skip) * pixels, chans)
            earlier = ho_ref[block, : frames - skip].reshape((frames - skip) * pixels, chans)
            put(block, 9 + kt, dot_first(later, earlier))
    keep_ref[...] = grad_ref[0]
    give_ref[...] = grad_ref[1]


def swapped(value, axis="tm", step=1):
    count = lax.axis_size(axis)
    return lax.ppermute(value, axis, [(i, i ^ step) for i in range(count)])


def own_half(spatial_weights, temporal_weights):
    own = jnp.concatenate([spatial_weights[0], temporal_weights[0]], 0)
    taps = own.shape[0] // lax.axis_size("tm")
    return lax.dynamic_slice_in_dim(own, lax.axis_index("tm") * taps, taps, 0)


def on_device(video, cotangent, spatial_weights, temporal_weights):
    blocks, cores, tiles = (lax.axis_size(name) for name in ("section", "tm", "space"))
    frames_in, rows_in, columns, chans = video.shape
    halo = 2 * blocks
    tile = halo
    group = tile // rows_in
    parties = cores * group
    own_width = columns // parties
    width = own_width + 2 * halo
    sets = None
    if tiles != group:
        sets = [
            [core * tiles + base + unit for core in range(cores) for unit in range(group)]
            for base in range(0, tiles, group)
        ]
    vmem = pl.BlockSpec(memory_space=pltpu.VMEM)
    smem = pl.BlockSpec(memory_space=pltpu.SMEM)
    params = pltpu.CompilerParams(vmem_limit_bytes=56 * 2**20)

    windows = jax.ShapeDtypeStruct((parties, frames_in, rows_in, width, chans), BF16)
    video_windows, cot_windows = pl.pallas_call(
        functools.partial(window_kernel, halo, width),
        name="windows",
        in_specs=[vmem] * 2,
        out_specs=[vmem] * 2,
        out_shape=[windows] * 2,
        compiler_params=params,
    )(video, cotangent)

    def spread(value):
        return lax.all_to_all(value, ("tm", "space"), 0, 0, axis_index_groups=sets, tiled=True)

    bands = blocks * tiles // group
    place = lax.axis_index("space")
    band = (lax.axis_index("section") * tiles + place) // group
    odd = band % 2

    def traded(value, shift):
        pairs = []
        for one in range(bands):
            other = ((one + shift) ^ 1) - shift
            if 0 <= other < bands:
                pairs += [(one * group + i, other * group + i) for i in range(group)]
        return lax.ppermute(value, ("section", "space"), pairs)

    half_kernels = own_half(spatial_weights, temporal_weights)
    mine = [swapped(half_kernels, "section", step) for step in range(1, blocks)]
    own_video = spread(video_windows)
    video_near, video_far = traded(own_video, 0), traded(own_video, 1)
    shared = [spatial_weights, temporal_weights] + mine + [swapped(each) for each in mine]

    own_cot = spread(cot_windows)
    half = group // 2
    split = own_cot.reshape((cores, group) + own_cot.shape[1:])
    edge = (cores * half,) + own_cot.shape[1:]
    cot_near = traded(lax.dynamic_slice_in_dim(split, (1 - odd) * half, half, 1).reshape(edge), 0)
    cot_far = traded(lax.dynamic_slice_in_dim(split, odd * half, half, 1).reshape(edge), 1)

    unit = lax.axis_index("tm") * group + place % group
    total_rows = blocks * tiles * rows_in
    corner = jnp.stack(
        [
            band * tile - halo, unit * own_width - halo, total_rows, columns,
            lax.axis_index("tm"), lax.axis_index("section"), odd,
        ]
    ).astype(jnp.int32)
    geometry = (blocks, cores, group, frames_in, rows_in, halo, tile, width)
    frames = cores * frames_in
    high = tile + 2 * halo
    per_section = (blocks,) + half_kernels.shape
    all_kernels = (cores,) + per_section
    saved = [
        jax.ShapeDtypeStruct((frames, tile + 2 * block + 2, width, chans), F32)
        for block in range(blocks)
    ]
    cost = pl.CostEstimate(flops=6 * 10**9, bytes_accessed=8 * 10**6, transcendentals=10**6)
    features, hidden, *slopes = pl.pallas_call(
        functools.partial(forward_kernel, geometry),
        name="forward",
        in_specs=[smem] + [vmem] * (2 * blocks + 3),
        out_specs=[vmem] * (2 + blocks),
        out_shape=[
            jax.ShapeDtypeStruct((blocks, frames, tile + 2, own_width, 3 * chans), BF16),
            jax.ShapeDtypeStruct((blocks, frames, tile, own_width, chans), BF16),
        ]
        + saved,
        scratch_shapes=[
            pltpu.VMEM((frames, high, width, 3 * chans), BF16),
            pltpu.VMEM((frames, high, width, chans), BF16),
            pltpu.VMEM((high, width, chans), F32),
            pltpu.VMEM(all_kernels, BF16),
        ],
        compiler_params=params,
        cost_estimate=cost,
    )(corner, *shared, own_video, video_near, video_far)

    pixel_count = frames * total_rows * columns
    factor = 1.0 / float(pixel_count) ** 0.5
    keep, give, tile_grad = pl.pallas_call(
        functools.partial(backward_kernel, geometry, factor),
        name="backward",
        in_specs=[smem] + [vmem] * (3 * blocks + 5),
        out_specs=[vmem] * 3,
        out_shape=[
            jax.ShapeDtypeStruct(per_section, BF16),
            jax.ShapeDtypeStruct(per_section, BF16),
            jax.ShapeDtypeStruct((parties, frames_in, rows_in, own_width, chans), BF16),
        ],
        scratch_shapes=[
            pltpu.VMEM((frames, tile + 2 * blocks, width, chans), BF16),
            pltpu.VMEM((frames, tile + 2 * blocks, width, 3 * chans), BF16),
            pltpu.VMEM((frames, tile, own_width, chans), BF16),
            pltpu.VMEM((frames, tile, own_width, chans), BF16),
            pltpu.VMEM(all_kernels, BF16),
            pltpu.VMEM(all_kernels, BF16),
        ],
        compiler_params=params,
        cost_estimate=cost,
    )(corner, *shared, own_cot, cot_near, cot_far, features, hidden, *slopes)

    got = swapped(give)
    parts = [(keep[i].astype(F32) + got[i].astype(F32)).astype(BF16) for i in range(blocks)]
    back = spread(tile_grad)
    parts = parts[:1] + [swapped(parts[i], "section", i) for i in range(1, blocks)]
    part = sum(each.astype(F32) for each in parts).astype(BF16)
    units = part.reshape(group, -1, chans)
    unit = place % group

    def chunk(step):
        return lax.dynamic_index_in_dim(units, unit ^ step, 0, keepdims=False)

    parts = [chunk(0)] + [swapped(chunk(i), "space", i) for i in range(1, group)]
    part = sum(each.astype(F32) for each in parts)
    if sets is not None:
        part = lax.psum(
            part, "space", axis_index_groups=[list(range(i, tiles, group)) for i in range(group)]
        )
    part = part.astype(BF16)
    mine = [part] + [swapped(part, "space", i) for i in range(1, group)]
    other = [swapped(each) for each in mine]
    core = lax.axis_index("tm")
    whole = jnp.zeros((cores, group) + part.shape, BF16)
    for which, chunks in ((core, mine), (1 - core, other)):
        for step, each in enumerate(chunks):
            whole = lax.dynamic_update_slice(
                whole, each[None, None], (which, unit ^ step, 0, 0)
            )
    grad_video = back.transpose(1, 2, 0, 3, 4).reshape(video.shape)
    own = whole.reshape(-1, chans, chans).swapaxes(1, 2).astype(F32)[None]
    count = spatial_weights.shape[1]
    return own[:, :count], own[:, count:], grad_video


def solution(mesh):
    return jax.shard_map(
        on_device,
        mesh=mesh,
        in_specs=(
            P("tm", ("section", "space"), None, None),
            P("tm", ("section", "space"), None, None),
            P("section", None, None, None),
            P("section", None, None, None),
        ),
        out_specs=(
            P("section", None, None, None),
            P("section", None, None, None),
            P("tm", ("section", "space"), None, None),
        ),
        check_vma=False,
    )
```

```python
import functools

import jax
import jax.numpy as jnp
from jax import lax
from jax.experimental import pallas as pl
from jax.experimental.pallas import tpu as pltpu
from jax.sharding import PartitionSpec as P

F32 = jnp.float32
BF16 = jnp.bfloat16


def rolled(value, steps):
    return pltpu.roll(value, steps % value.shape[0], 0)


def dot_t(left, right):
    return lax.dot_general(left, right, (((1,), (1,)), ((), ())), preferred_element_type=F32)


def dot_first(left, right):
    return lax.dot_general(left, right, (((0,), (0,)), ((), ())), preferred_element_type=F32)


def kernel_of(w_ref, block, tap):
    taps = w_ref.shape[2]
    return w_ref[tap // taps, block, tap % taps]


def rows_of(w_ref, block, first, last):
    return jnp.concatenate([kernel_of(w_ref, block, tap) for tap in range(first, last)], 0)


def lanes_of(w_ref, block, order):
    return jnp.concatenate([kernel_of(w_ref, block, tap) for tap in order], 1)


def window_kernel(halo, span, place_ref, video_ref, cot_ref, *rest):
    video_outs, cot_outs, cut_ref = rest[: len(rest) // 2], rest[len(rest) // 2 : -1], rest[-1]
    frames, rows, columns, chans = video_ref.shape
    own = span - 2 * halo
    for source, targets in ((video_ref, video_outs), (cot_ref, cot_outs)):
        whole = source[...].astype(F32)
        for unit in range(len(targets)):
            first, last = unit * own - halo, unit * own - halo + span
            parts = []
            if first < 0:
                parts.append(jnp.zeros((frames, rows, -first, chans), F32))
            parts.append(whole[:, :, max(first, 0) : min(last, columns)])
            if last > columns:
                parts.append(jnp.zeros((frames, rows, last - columns, chans), F32))
            piece = jnp.concatenate(parts, 2) if len(parts) > 1 else parts[0]
            cut_ref[unit] = piece.astype(BF16)
        for step, target in enumerate(targets):
            target[...] = cut_ref[jnp.bitwise_xor(place_ref[7], step)]


def place_kernels(place_ref, w_ref, spatial_ref, temporal_ref, mine_refs, other_refs):
    core, section = place_ref[4], place_ref[5]
    cores, _, taps = w_ref.shape[:3]
    count = spatial_ref.shape[1]
    for tap in range(cores * taps):
        one = spatial_ref[0, tap] if tap < count else temporal_ref[0, tap - count]
        w_ref[tap // taps, section, tap % taps] = one
    for step, (mine_ref, other_ref) in enumerate(zip(mine_refs, other_refs)):
        block = jnp.bitwise_xor(section, step + 1)
        w_ref[core, block] = mine_ref[...]
        w_ref[1 - core, block] = other_ref[...]


def forward_kernel(geometry, place_ref, *rest):
    blocks, cores, group, frames_in, rows_in, halo, tile, width = geometry
    shared, rest = rest[: 2 * blocks], rest[2 * blocks :]
    arrived, rest = rest[:6], rest[6:]
    xo_ref, ho_ref = rest[:2]
    d_refs = rest[2 : 2 + blocks]
    x_ref, h_ref, mask_ref, w_ref, start_ref = rest[2 + blocks :]
    place_kernels(place_ref, w_ref, shared[0], shared[1], shared[2 : 1 + blocks], shared[1 + blocks :])
    frames = cores * frames_in
    high = tile + 2 * halo
    chans = w_ref.shape[-1]
    own_rows, own_cols = (halo, halo + tile), (halo, width - halo)
    height, columns = place_ref[2], place_ref[3]
    row = place_ref[0] + lax.broadcasted_iota(jnp.int32, (high, width, chans), 0)
    col = place_ref[1] + lax.broadcasted_iota(jnp.int32, (high, width, chans), 1)
    inside = (row >= 0) & (row < height) & (col >= 0) & (col < columns)
    mask_ref[...] = jnp.where(inside, 1.0, 0.0).astype(F32)

    def keep(block, frame, value, first):
        triple = [rolled(value, 1), value, rolled(value, -1)]
        count = value.shape[0] // width
        both = jnp.concatenate([part.astype(BF16) for part in triple], 1)
        x_ref[frame, first : first + count] = both.reshape(count, width, 3 * chans)
        start = own_rows[0] - 1 - first
        cut = [
            part.reshape(count, width, chans)[
                start : start + tile + 2, own_cols[0] : own_cols[1]
            ].astype(BF16)
            for part in triple
        ]
        xo_ref[block, frame] = jnp.concatenate(cut, 2)

    core, odd, unit = place_ref[4], place_ref[6], place_ref[7]
    near = tile + halo - odd * (tile + halo)
    columns_at = pl.ds(pl.multiple_of(core * (width - 2 * halo), 16), width)
    for index, ref in enumerate(arrived):
        base = (halo, near, tile + halo - near)[index % 3]
        whose = core if index < 3 else 1 - core
        for step in range(group):
            row = base + jnp.bitwise_xor(unit, step) * rows_in
            start_ref[pl.ds(whose * frames_in, frames_in), pl.ds(row, rows_in)] = ref[
                step, :, :, columns_at, :
            ]
    for frame in range(frames):
        keep(0, frame, start_ref[frame].reshape(high * width, chans).astype(F32), 0)

    for block in range(blocks):
        first, last = block + 1, high - block - 1
        count = last - first
        spatial = rows_of(w_ref, block, 0, 9)
        mask = mask_ref[first:last].reshape(count * width, chans)
        for frame in range(frames):
            taps = jnp.concatenate(
                [
                    x_ref[frame, first - 1 + ky : last - 1 + ky].reshape(count * width, 3 * chans)
                    for ky in range(3)
                ],
                1,
            )
            before = jnp.dot(taps, spatial, preferred_element_type=F32)
            sigma = 1.0 / (1.0 + jnp.exp(-before))
            hidden = before * sigma * mask
            slope = (sigma * (1.0 + before * (1.0 - sigma))) * mask
            h_ref[frame, first:last] = hidden.astype(BF16).reshape(count, width, chans)
            ho_ref[block, frame] = hidden.reshape(count, width, chans)[
                own_rows[0] - first : own_rows[1] - first, own_cols[0] : own_cols[1]
            ].astype(BF16)
            rim = block + 1
            d_refs[block][frame] = slope.reshape(count, width, chans)[
                own_rows[0] - rim - first : own_rows[1] + rim - first
            ]
        if block + 1 == blocks:
            break
        for frame in range(frames):
            offsets = [kt for kt in range(3) if frame + kt - 2 >= 0]
            timeline = jnp.concatenate(
                [
                    h_ref[frame + kt - 2, first:last].reshape(count * width, chans)
                    for kt in offsets
                ],
                1,
            )
            mixed = jnp.dot(
                timeline, rows_of(w_ref, block, 9 + offsets[0], 12), preferred_element_type=F32
            )
            old = x_ref[frame, first:last, :, chans : 2 * chans].astype(F32)
            new = old.reshape(count * width, chans) + mixed
            keep(block + 1, frame, new.astype(BF16).astype(F32), first)


def backward_kernel(geometry, factor, place_ref, *rest):
    blocks, cores, group, frames_in, rows_in, halo, tile, width = geometry
    shared, rest = rest[: 2 * blocks], rest[2 * blocks :]
    arrived, rest = rest[:6], rest[6:]
    xo_ref, ho_ref = rest[:2]
    d_refs = rest[2 : 2 + blocks]
    keep_ref, give_ref, mine_out, other_out = rest[2 + blocks : 6 + blocks]
    g_ref, da_ref, dao_ref, go_ref, w_ref, grad_ref, out_ref = rest[6 + blocks :]
    place_kernels(place_ref, w_ref, shared[0], shared[1], shared[2 : 1 + blocks], shared[1 + blocks :])
    frames = cores * frames_in
    chans = w_ref.shape[-1]
    rim = blocks
    own_cols = (halo, width - halo)
    per_core = w_ref.shape[2]
    pixels = tile * (own_cols[1] - own_cols[0])

    core, odd, unit = place_ref[4], place_ref[6], place_ref[7]
    half = group // 2
    near = tile + rim - odd * (tile + rim)
    columns_at = pl.ds(pl.multiple_of(core * (width - 2 * halo), 16), width)
    for index, ref in enumerate(arrived):
        base = (rim, near, tile + rim - near)[index % 3]
        whose = core if index < 3 else 1 - core
        mask = group - 1 if index % 3 == 0 else half - 1
        for step in range(ref.shape[0]):
            row = base + jnp.bitwise_and(jnp.bitwise_xor(unit, step), mask) * rows_in
            g_ref[pl.ds(whose * frames_in, frames_in), pl.ds(row, rows_in)] = ref[
                step, :, :, columns_at, :
            ]

    def put(block, tap, value):
        slot = jnp.where(place_ref[4] == tap // per_core, 0, 1)
        where = jnp.bitwise_xor(place_ref[5], block)
        grad_ref[slot, where, tap % per_core] = (value * factor).astype(BF16)

    for block in reversed(range(blocks)):
        edge = block + 1
        first, last = rim - edge, rim + tile + edge
        count = last - first
        for frame in range(frames):
            go_ref[frame] = g_ref[frame, rim : rim + tile].astype(F32)[
                :, own_cols[0] : own_cols[1]
            ].astype(BF16)
            offsets = [kt for kt in (2, 1, 0) if frame + 2 - kt < frames]
            ahead = jnp.concatenate(
                [
                    g_ref[frame + 2 - kt, first:last].reshape(count * width, chans)
                    for kt in offsets
                ],
                1,
            )
            hidden = dot_t(ahead, lanes_of(w_ref, block, [9 + kt for kt in offsets]))
            slope = d_refs[block][frame].reshape(count * width, chans)
            value = (hidden * slope).astype(BF16).astype(F32)
            triple = [rolled(value, -1), value, rolled(value, 1)]
            both = jnp.concatenate([part.astype(BF16) for part in triple], 1)
            da_ref[frame, first:last] = both.reshape(count, width, 3 * chans)
            dao_ref[frame] = value.reshape(count, width, chans)[
                edge : edge + tile, own_cols[0] : own_cols[1]
            ].astype(BF16)
        for frame in range(frames):
            inner = count - 2
            taps = jnp.concatenate(
                [
                    da_ref[frame, first + 2 - ky : first + 2 - ky + inner].reshape(
                        inner * width, 3 * chans
                    )
                    for ky in range(3)
                ],
                1,
            )
            back = dot_t(taps, lanes_of(w_ref, block, range(9)))
            old = g_ref[frame, first + 1 : last - 1].astype(F32).reshape(inner * width, chans)
            new = (old + back).astype(BF16)
            if block:
                g_ref[frame, first + 1 : last - 1] = new.reshape(inner, width, chans)
            else:
                cut = new.astype(F32).reshape(inner, width, chans)[:, own_cols[0] : own_cols[1]]
                out_ref[frame] = cut.astype(BF16)
        slopes = dao_ref[...].reshape(frames * pixels, chans)
        for ky in range(3):
            taps = xo_ref[block, :, ky : ky + tile].reshape(frames * pixels, 3 * chans)
            sums = dot_first(slopes, taps)
            for kx in range(3):
                put(block, 3 * ky + kx, sums[:, kx * chans : (kx + 1) * chans])
        for kt in range(3):
            skip = 2 - kt
            later = go_ref[skip:].reshape((frames - skip) * pixels, chans)
            earlier = ho_ref[block, : frames - skip].reshape((frames - skip) * pixels, chans)
            put(block, 9 + kt, dot_first(later, earlier))
    keep_ref[...] = grad_ref[0]
    give_ref[...] = grad_ref[1]
    for whose, target in ((core, mine_out), (1 - core, other_out)):
        for step in range(group):
            row = jnp.bitwise_xor(unit, step) * rows_in
            target[step] = out_ref[pl.ds(whose * frames_in, frames_in), pl.ds(row, rows_in)]


def swapped(value, axis="tm", step=1):
    count = lax.axis_size(axis)
    return lax.ppermute(value, axis, [(i, i ^ step) for i in range(count)])


def own_half(spatial_weights, temporal_weights):
    own = jnp.concatenate([spatial_weights[0], temporal_weights[0]], 0)
    taps = own.shape[0] // lax.axis_size("tm")
    return lax.dynamic_slice_in_dim(own, lax.axis_index("tm") * taps, taps, 0)


def on_device(video, cotangent, spatial_weights, temporal_weights):
    blocks, cores, tiles = (lax.axis_size(name) for name in ("section", "tm", "space"))
    frames_in, rows_in, columns, chans = video.shape
    halo = 2 * blocks
    tile = halo
    group = tile // rows_in
    parties = cores * group
    own_width = columns // parties
    width = own_width + 2 * halo
    span = cores * own_width + 2 * halo
    vmem = pl.BlockSpec(memory_space=pltpu.VMEM)
    smem = pl.BlockSpec(memory_space=pltpu.SMEM)
    params = pltpu.CompilerParams(vmem_limit_bytes=32 * 2**20)

    bands = blocks * tiles // group
    place = lax.axis_index("space")
    band = (lax.axis_index("section") * tiles + place) // group
    odd = band % 2

    def traded(value, shift):
        pairs = []
        for one in range(bands):
            other = ((one + shift) ^ 1) - shift
            if 0 <= other < bands:
                pairs += [(one * group + i, other * group + i) for i in range(group)]
        return lax.ppermute(value, ("section", "space"), pairs)

    core, section = lax.axis_index("tm"), lax.axis_index("section")
    unit = place % group
    total_rows = blocks * tiles * rows_in
    corner = jnp.stack(
        [
            band * tile - halo, (unit * cores + core) * own_width - halo, total_rows, columns,
            core, section, odd, unit,
        ]
    ).astype(jnp.int32)

    half_kernels = own_half(spatial_weights, temporal_weights)
    mine = [swapped(half_kernels, "section", step) for step in range(1, blocks)]

    windows = jax.ShapeDtypeStruct((frames_in, rows_in, span, chans), BF16)
    cuts = pl.pallas_call(
        functools.partial(window_kernel, halo, span),
        name="windows",
        in_specs=[smem] + [vmem] * 2,
        out_specs=[vmem] * (2 * group),
        out_shape=[windows] * (2 * group),
        scratch_shapes=[pltpu.VMEM((group,) + windows.shape, BF16)],
        compiler_params=params,
    )(corner, video, cotangent)

    def gathered(pieces):
        return jnp.stack([pieces[0]] + [swapped(pieces[i], "space", i) for i in range(1, group)])

    own_video = gathered(cuts[:group])
    videos = [own_video, traded(own_video, 0), traded(own_video, 1)]
    videos += [swapped(each) for each in videos]
    shared = [spatial_weights, temporal_weights] + mine + [swapped(each) for each in mine]

    own_cot = gathered(cuts[group:])
    half = group // 2
    upper = unit // half
    cots = [own_cot] + [
        traded(lax.dynamic_slice_in_dim(own_cot, (upper ^ side) * half, half, 0), shift)
        for shift, side in ((0, 1 - odd), (1, odd))
    ]
    cots += [swapped(each) for each in cots]

    geometry = (blocks, cores, group, frames_in, rows_in, halo, tile, width)
    frames = cores * frames_in
    high = tile + 2 * halo
    per_section = (blocks,) + half_kernels.shape
    all_kernels = (cores,) + per_section
    saved = [
        jax.ShapeDtypeStruct((frames, tile + 2 * block + 2, width, chans), F32)
        for block in range(blocks)
    ]
    cost = pl.CostEstimate(flops=6 * 10**9, bytes_accessed=8 * 10**6, transcendentals=10**6)
    features, hidden, *slopes = pl.pallas_call(
        functools.partial(forward_kernel, geometry),
        name="forward",
        in_specs=[smem] + [vmem] * (2 * blocks + 6),
        out_specs=[vmem] * (2 + blocks),
        out_shape=[
            jax.ShapeDtypeStruct((blocks, frames, tile + 2, own_width, 3 * chans), BF16),
            jax.ShapeDtypeStruct((blocks, frames, tile, own_width, chans), BF16),
        ]
        + saved,
        scratch_shapes=[
            pltpu.VMEM((frames, high, width, 3 * chans), BF16),
            pltpu.VMEM((frames, high, width, chans), BF16),
            pltpu.VMEM((high, width, chans), F32),
            pltpu.VMEM(all_kernels, BF16),
            pltpu.VMEM((frames, high, width, chans), BF16),
        ],
        compiler_params=params,
        cost_estimate=cost,
    )(corner, *shared, *videos)

    back = jax.ShapeDtypeStruct((group, frames_in, rows_in, own_width, chans), BF16)
    pixel_count = frames * total_rows * columns
    factor = 1.0 / float(pixel_count) ** 0.5
    keep, give, mine_grad, other_grad = pl.pallas_call(
        functools.partial(backward_kernel, geometry, factor),
        name="backward",
        in_specs=[smem] + [vmem] * (3 * blocks + 8),
        out_specs=[vmem] * 4,
        out_shape=[
            jax.ShapeDtypeStruct(per_section, BF16),
            jax.ShapeDtypeStruct(per_section, BF16),
            back,
            back,
        ],
        scratch_shapes=[
            pltpu.VMEM((frames, tile + 2 * blocks, width, chans), BF16),
            pltpu.VMEM((frames, tile + 2 * blocks, width, 3 * chans), BF16),
            pltpu.VMEM((frames, tile, own_width, chans), BF16),
            pltpu.VMEM((frames, tile, own_width, chans), BF16),
            pltpu.VMEM(all_kernels, BF16),
            pltpu.VMEM(all_kernels, BF16),
            pltpu.VMEM((frames, tile, own_width, chans), BF16),
        ],
        compiler_params=params,
        cost_estimate=cost,
    )(corner, *shared, *cots, features, hidden, *slopes)

    got = swapped(give)
    parts = [(keep[i].astype(F32) + got[i].astype(F32)).astype(BF16) for i in range(blocks)]
    other_grad = swapped(other_grad)
    first = core == 0
    wide = jnp.concatenate(
        [jnp.where(first, mine_grad, other_grad), jnp.where(first, other_grad, mine_grad)], 3
    )
    strips = [wide[0]] + [swapped(wide[i], "space", i) for i in range(1, group)]
    parts = parts[:1] + [swapped(parts[i], "section", i) for i in range(1, blocks)]
    part = sum(each.astype(F32) for each in parts).astype(BF16)
    units = part.reshape(group, -1, chans)

    def chunk(step):
        return lax.dynamic_index_in_dim(units, unit ^ step, 0, keepdims=False)

    parts = [chunk(0)] + [swapped(chunk(i), "space", i) for i in range(1, group)]
    part = sum(each.astype(F32) for each in parts)
    if tiles != group:
        part = lax.psum(
            part, "space", axis_index_groups=[list(range(i, tiles, group)) for i in range(group)]
        )
    part = part.astype(BF16)
    chunks = jnp.stack([part] + [swapped(part, "space", i) for i in range(1, group)])
    whole = jnp.zeros((cores,) + chunks.shape, BF16)
    for which, each in ((core, chunks), (1 - core, swapped(chunks))):
        for step in range(group):
            whole = lax.dynamic_update_slice(
                whole, each[step][None, None], (which, unit ^ step, 0, 0)
            )
    grad_video = jnp.zeros(video.shape, BF16)
    for step, strip in enumerate(strips):
        grad_video = lax.dynamic_update_slice(
            grad_video, strip, (0, 0, (unit ^ step) * cores * own_width, 0)
        )
    own = whole.reshape(-1, chans, chans).swapaxes(1, 2).astype(F32)[None]
    count = spatial_weights.shape[1]
    return own[:, :count], own[:, count:], grad_video


def solution(mesh):
    return jax.shard_map(
        on_device,
        mesh=mesh,
        in_specs=(
            P("tm", ("section", "space"), None, None),
            P("tm", ("section", "space"), None, None),
            P("section", None, None, None),
            P("section", None, None, None),
        ),
        out_specs=(
            P("section", None, None, None),
            P("section", None, None, None),
            P("tm", ("section", "space"), None, None),
        ),
        check_vma=False,
    )
```

```python
import functools

import jax
import jax.numpy as jnp
from jax import lax
from jax.experimental import pallas as pl
from jax.experimental.pallas import tpu as pltpu
from jax.sharding import PartitionSpec as P

F32 = jnp.float32
BF16 = jnp.bfloat16


def rolled(value, steps):
    return pltpu.roll(value, steps % value.shape[0], 0)


def dot_t(left, right):
    return lax.dot_general(left, right, (((1,), (1,)), ((), ())), preferred_element_type=F32)


def dot_first(left, right):
    return lax.dot_general(left, right, (((0,), (0,)), ((), ())), preferred_element_type=F32)


def kernel_of(w_ref, block, tap):
    taps = w_ref.shape[2]
    return w_ref[tap // taps, block, tap % taps]


def rows_of(w_ref, block, first, last):
    return jnp.concatenate([kernel_of(w_ref, block, tap) for tap in range(first, last)], 0)


def lanes_of(w_ref, block, order):
    return jnp.concatenate([kernel_of(w_ref, block, tap) for tap in order], 1)


def opening_kernel(
    halo, span, place_ref, video_hbm, spatial_hbm, temporal_hbm, mine_ref, other_ref, *rest
):
    targets, (video_ref, wide_ref, sems) = rest[:-3], rest[-3:]
    taps, count = mine_ref.shape[0], spatial_hbm.shape[1]
    copy_video = pltpu.make_async_copy(video_hbm, video_ref, sems.at[0])
    copy_video.start()

    def kernel_copies(core):
        copies = []
        for half, ref in ((core, mine_ref), (1 - core, other_ref)):
            first, last = half * taps, (half + 1) * taps
            split = min(max(count, first), last)
            if split > first:
                source, target = spatial_hbm.at[0, first:split], ref.at[: split - first]
                copies.append(pltpu.make_async_copy(source, target, sems.at[1 + len(copies)]))
            if last > split:
                source, target = temporal_hbm.at[0, split - count : last - count], ref.at[split - first :]
                copies.append(pltpu.make_async_copy(source, target, sems.at[1 + len(copies)]))
        return copies

    for core in range(2):
        @pl.when(place_ref[4] == core)
        def _(core=core):
            for copy in kernel_copies(core):
                copy.start()

    frames, rows, columns, chans = video_ref.shape
    edge = jnp.zeros((frames, rows, halo, chans), F32)
    wide_ref[:, :, :halo] = edge
    wide_ref[:, :, halo + columns :] = edge
    copy_video.wait()
    wide_ref[:, :, halo : halo + columns] = video_ref[...].astype(F32)
    for step, target in enumerate(targets):
        at = jnp.bitwise_xor(place_ref[7], step) * (span - 2 * halo)
        target[...] = wide_ref[:, :, pl.ds(pl.multiple_of(at, 16), span)].astype(BF16)
    for core in range(2):
        @pl.when(place_ref[4] == core)
        def _(core=core):
            for copy in kernel_copies(core):
                copy.wait()


def cotangent_kernel(halo, width, place_ref, mine_ref, other_ref, *rest):
    targets, wide_ref = rest[:-1], rest[-1]
    frames_in, rows, columns, chans = mine_ref.shape
    core = place_ref[4]
    edge = jnp.zeros((2 * frames_in, rows, halo, chans), F32)
    wide_ref[:, :, :halo] = edge
    wide_ref[:, :, halo + columns :] = edge
    for whose, ref in ((core, mine_ref), (1 - core, other_ref)):
        wide_ref[pl.ds(whose * frames_in, frames_in), :, halo : halo + columns] = ref[...].astype(F32)
    own = width - 2 * halo
    for step, target in enumerate(targets):
        at = (jnp.bitwise_xor(place_ref[7], step) * 2 + core) * own
        target[...] = wide_ref[:, :, pl.ds(pl.multiple_of(at, 16), width)].astype(BF16)


def closing_kernel(place_ref, mine_ref, other_ref, spatial_ref, temporal_ref, flat_ref):
    pieces, rows, chans = mine_ref.shape
    core, unit = place_ref[4], place_ref[7]
    for whose, ref in ((core, mine_ref), (1 - core, other_ref)):
        for step in range(pieces):
            index = whose * pieces + jnp.bitwise_xor(jnp.bitwise_and(unit, pieces - 1), step)
            flat_ref[pl.ds(pl.multiple_of(index * rows, 16), rows)] = ref[step]
    count = spatial_ref.shape[1]
    for tap in range(count + temporal_ref.shape[1]):
        turned = flat_ref[tap * chans : (tap + 1) * chans].astype(F32).T
        if tap < count:
            spatial_ref[0, tap] = turned
        else:
            temporal_ref[0, tap - count] = turned


def place_kernels(place_ref, w_ref, own_ref, mine_refs, other_refs):
    core, section = place_ref[4], place_ref[5]
    w_ref[core, section] = own_ref[0]
    w_ref[1 - core, section] = own_ref[1]
    for step, (mine_ref, other_ref) in enumerate(zip(mine_refs, other_refs)):
        block = jnp.bitwise_xor(section, step + 1)
        w_ref[core, block] = mine_ref[...]
        w_ref[1 - core, block] = other_ref[...]


def forward_kernel(geometry, place_ref, *rest):
    blocks, cores, group, frames_in, rows_in, halo, tile, width = geometry
    shared, rest = rest[: 2 * blocks - 1], rest[2 * blocks - 1 :]
    arrived, rest = rest[:6], rest[6:]
    xo_ref, ho_ref = rest[:2]
    d_refs = rest[2 : 2 + blocks]
    x_ref, h_ref, mask_ref, w_ref, start_ref = rest[2 + blocks :]
    place_kernels(place_ref, w_ref, shared[0], shared[1:blocks], shared[blocks:])
    frames = cores * frames_in
    high = tile + 2 * halo
    chans = w_ref.shape[-1]
    own_rows, own_cols = (halo, halo + tile), (halo, width - halo)
    height, columns = place_ref[2], place_ref[3]
    row = place_ref[0] + lax.broadcasted_iota(jnp.int32, (high, width, chans), 0)
    col = place_ref[1] + lax.broadcasted_iota(jnp.int32, (high, width, chans), 1)
    inside = (row >= 0) & (row < height) & (col >= 0) & (col < columns)
    mask_ref[...] = jnp.where(inside, 1.0, 0.0).astype(F32)

    def keep(block, frame, value, first):
        triple = [rolled(value, 1), value, rolled(value, -1)]
        count = value.shape[0] // width
        both = jnp.concatenate([part.astype(BF16) for part in triple], 1)
        x_ref[frame, first : first + count] = both.reshape(count, width, 3 * chans)
        start = own_rows[0] - 1 - first
        cut = [
            part.reshape(count, width, chans)[
                start : start + tile + 2, own_cols[0] : own_cols[1]
            ].astype(BF16)
            for part in triple
        ]
        xo_ref[block, frame] = jnp.concatenate(cut, 2)

    core, odd, unit = place_ref[4], place_ref[6], place_ref[7]
    near = tile + halo - odd * (tile + halo)
    columns_at = pl.ds(pl.multiple_of(core * (width - 2 * halo), 16), width)
    for index, ref in enumerate(arrived):
        base = (halo, near, tile + halo - near)[index % 3]
        whose = core if index < 3 else 1 - core
        for step in range(group):
            row = base + jnp.bitwise_xor(unit, step) * rows_in
            start_ref[pl.ds(whose * frames_in, frames_in), pl.ds(row, rows_in)] = ref[
                step, :, :, columns_at, :
            ]
    for frame in range(frames):
        keep(0, frame, start_ref[frame].reshape(high * width, chans).astype(F32), 0)

    for block in range(blocks):
        first, last = block + 1, high - block - 1
        count = last - first
        spatial = rows_of(w_ref, block, 0, 9)
        mask = mask_ref[first:last].reshape(count * width, chans)
        for frame in range(frames):
            taps = jnp.concatenate(
                [
                    x_ref[frame, first - 1 + ky : last - 1 + ky].reshape(count * width, 3 * chans)
                    for ky in range(3)
                ],
                1,
            )
            before = jnp.dot(taps, spatial, preferred_element_type=F32)
            sigma = 1.0 / (1.0 + jnp.exp(-before))
            hidden = before * sigma * mask
            slope = (sigma * (1.0 + before * (1.0 - sigma))) * mask
            h_ref[frame, first:last] = hidden.astype(BF16).reshape(count, width, chans)
            ho_ref[block, frame] = hidden.reshape(count, width, chans)[
                own_rows[0] - first : own_rows[1] - first, own_cols[0] : own_cols[1]
            ].astype(BF16)
            rim = block + 1
            d_refs[block][frame] = slope.reshape(count, width, chans)[
                own_rows[0] - rim - first : own_rows[1] + rim - first
            ]
        if block + 1 == blocks:
            break
        for frame in range(frames):
            offsets = [kt for kt in range(3) if frame + kt - 2 >= 0]
            timeline = jnp.concatenate(
                [
                    h_ref[frame + kt - 2, first:last].reshape(count * width, chans)
                    for kt in offsets
                ],
                1,
            )
            mixed = jnp.dot(
                timeline, rows_of(w_ref, block, 9 + offsets[0], 12), preferred_element_type=F32
            )
            old = x_ref[frame, first:last, :, chans : 2 * chans].astype(F32)
            new = old.reshape(count * width, chans) + mixed
            keep(block + 1, frame, new.astype(BF16).astype(F32), first)


def backward_kernel(geometry, factor, place_ref, *rest):
    blocks, cores, group, frames_in, rows_in, halo, tile, width = geometry
    shared, rest = rest[: 2 * blocks - 1], rest[2 * blocks - 1 :]
    arrived, rest = rest[:3], rest[3:]
    xo_ref, ho_ref = rest[:2]
    d_refs = rest[2 : 2 + blocks]
    keep_ref, give_ref, mine_out, other_out = rest[2 + blocks : 6 + blocks]
    g_ref, da_ref, dao_ref, go_ref, w_ref, grad_ref, out_ref = rest[6 + blocks :]
    place_kernels(place_ref, w_ref, shared[0], shared[1:blocks], shared[blocks:])
    frames = cores * frames_in
    chans = w_ref.shape[-1]
    rim = blocks
    own_cols = (halo, width - halo)
    per_core = w_ref.shape[2]
    pixels = tile * (own_cols[1] - own_cols[0])

    core, odd, unit = place_ref[4], place_ref[6], place_ref[7]
    near = tile + rim - odd * (tile + rim)
    for base, ref in zip((rim, near, tile + rim - near), arrived):
        count = ref.shape[0]
        for step in range(count):
            row = base + jnp.bitwise_and(jnp.bitwise_xor(unit, step), count - 1) * rows_in
            g_ref[:, pl.ds(row, rows_in)] = ref[step]

    def put(block, tap, value):
        slot = jnp.where(place_ref[4] == tap // per_core, 0, 1)
        where = jnp.bitwise_xor(place_ref[5], block)
        grad_ref[slot, where, tap % per_core] = (value * factor).astype(BF16)

    for block in reversed(range(blocks)):
        edge = block + 1
        first, last = rim - edge, rim + tile + edge
        count = last - first
        for frame in range(frames):
            go_ref[frame] = g_ref[frame, rim : rim + tile].astype(F32)[
                :, own_cols[0] : own_cols[1]
            ].astype(BF16)
            offsets = [kt for kt in (2, 1, 0) if frame + 2 - kt < frames]
            ahead = jnp.concatenate(
                [
                    g_ref[frame + 2 - kt, first:last].reshape(count * width, chans)
                    for kt in offsets
                ],
                1,
            )
            hidden = dot_t(ahead, lanes_of(w_ref, block, [9 + kt for kt in offsets]))
            slope = d_refs[block][frame].reshape(count * width, chans)
            value = (hidden * slope).astype(BF16).astype(F32)
            triple = [rolled(value, -1), value, rolled(value, 1)]
            both = jnp.concatenate([part.astype(BF16) for part in triple], 1)
            da_ref[frame, first:last] = both.reshape(count, width, 3 * chans)
            dao_ref[frame] = value.reshape(count, width, chans)[
                edge : edge + tile, own_cols[0] : own_cols[1]
            ].astype(BF16)
        for frame in range(frames):
            inner = count - 2
            taps = jnp.concatenate(
                [
                    da_ref[frame, first + 2 - ky : first + 2 - ky + inner].reshape(
                        inner * width, 3 * chans
                    )
                    for ky in range(3)
                ],
                1,
            )
            back = dot_t(taps, lanes_of(w_ref, block, range(9)))
            old = g_ref[frame, first + 1 : last - 1].astype(F32).reshape(inner * width, chans)
            new = (old + back).astype(BF16)
            if block:
                g_ref[frame, first + 1 : last - 1] = new.reshape(inner, width, chans)
            else:
                cut = new.astype(F32).reshape(inner, width, chans)[:, own_cols[0] : own_cols[1]]
                out_ref[frame] = cut.astype(BF16)
        slopes = dao_ref[...].reshape(frames * pixels, chans)
        for ky in range(3):
            taps = xo_ref[block, :, ky : ky + tile].reshape(frames * pixels, 3 * chans)
            sums = dot_first(slopes, taps)
            for kx in range(3):
                put(block, 3 * ky + kx, sums[:, kx * chans : (kx + 1) * chans])
        for kt in range(3):
            skip = 2 - kt
            later = go_ref[skip:].reshape((frames - skip) * pixels, chans)
            earlier = ho_ref[block, : frames - skip].reshape((frames - skip) * pixels, chans)
            put(block, 9 + kt, dot_first(later, earlier))
    keep_ref[...] = grad_ref[0]
    give_ref[...] = grad_ref[1]
    for whose, target in ((core, mine_out), (1 - core, other_out)):
        for step in range(group):
            row = jnp.bitwise_xor(unit, step) * rows_in
            target[step] = out_ref[pl.ds(whose * frames_in, frames_in), pl.ds(row, rows_in)]


def swapped(value, axis="tm", step=1):
    count = lax.axis_size(axis)
    return lax.ppermute(value, axis, [(i, i ^ step) for i in range(count)])


def on_device(video, cotangent, spatial_weights, temporal_weights):
    blocks, cores, tiles = (lax.axis_size(name) for name in ("section", "tm", "space"))
    frames_in, rows_in, columns, chans = video.shape
    halo = 2 * blocks
    tile = halo
    group = tile // rows_in
    parties = cores * group
    own_width = columns // parties
    width = own_width + 2 * halo
    span = cores * own_width + 2 * halo
    vmem = pl.BlockSpec(memory_space=pltpu.VMEM)
    smem = pl.BlockSpec(memory_space=pltpu.SMEM)
    params = pltpu.CompilerParams(vmem_limit_bytes=32 * 2**20)

    bands = blocks * tiles // group
    place = lax.axis_index("space")
    band = (lax.axis_index("section") * tiles + place) // group
    odd = band % 2

    def traded(value, shift):
        pairs = []
        for one in range(bands):
            other = ((one + shift) ^ 1) - shift
            if 0 <= other < bands:
                pairs += [(one * group + i, other * group + i) for i in range(group)]
        return lax.ppermute(value, ("section", "space"), pairs)

    core, section = lax.axis_index("tm"), lax.axis_index("section")
    unit = place % group
    total_rows = blocks * tiles * rows_in
    corner = jnp.stack(
        [
            band * tile - halo, (unit * cores + core) * own_width - halo, total_rows, columns,
            core, section, odd, unit,
        ]
    ).astype(jnp.int32)

    hbm = pl.BlockSpec(memory_space=pltpu.HBM)
    taps = (spatial_weights.shape[1] + temporal_weights.shape[1]) // cores
    one_half = jax.ShapeDtypeStruct((taps, chans, chans), BF16)
    padded = columns + 2 * halo
    cot_other = swapped(cotangent)
    half_kernels, rest_kernels, *cuts = pl.pallas_call(
        functools.partial(opening_kernel, halo, span),
        name="opening",
        in_specs=[smem] + [hbm] * 3,
        out_specs=[vmem] * (2 + group),
        out_shape=[one_half] * 2
        + [jax.ShapeDtypeStruct((frames_in, rows_in, span, chans), BF16)] * group,
        scratch_shapes=[
            pltpu.VMEM(video.shape, BF16),
            pltpu.VMEM((frames_in, rows_in, padded, chans), F32),
            pltpu.SemaphoreType.DMA((4,)),
        ],
        compiler_params=pltpu.CompilerParams(vmem_limit_bytes=60 * 2**20),
    )(corner, video, spatial_weights, temporal_weights)

    def gathered(pieces):
        return jnp.stack([pieces[0]] + [swapped(pieces[i], "space", i) for i in range(1, group)])

    along_x = swapped(half_kernels, "section", 1)
    along_y = swapped(half_kernels, "section", 2)
    own_video, along_x, along_y = lax.optimization_barrier([gathered(cuts), along_x, along_y])
    near, far = traded(own_video, 0), traded(own_video, 1)
    mine = [along_x, along_y, swapped(along_x, "section", 2)]
    shared = mine + [swapped(each) for each in mine]
    own_kernels = jnp.stack([half_kernels, rest_kernels])

    cuts = pl.pallas_call(
        functools.partial(cotangent_kernel, halo, width),
        name="cotangent",
        in_specs=[smem] + [vmem] * 2,
        out_specs=[vmem] * group,
        out_shape=[jax.ShapeDtypeStruct((cores * frames_in, rows_in, width, chans), BF16)] * group,
        scratch_shapes=[pltpu.VMEM((cores * frames_in, rows_in, padded, chans), F32)],
        compiler_params=params,
    )(corner, cotangent, cot_other)
    near, own_kernels, *cuts = lax.optimization_barrier([near, own_kernels] + list(cuts))
    shared = [own_kernels] + shared
    videos = [own_video, near, far]
    videos += [swapped(each) for each in videos]
    own_cot = gathered(cuts)
    half = group // 2
    upper = unit // half
    cots = [own_cot] + [
        traded(lax.dynamic_slice_in_dim(own_cot, (upper ^ side) * half, half, 0), shift)
        for shift, side in ((0, 1 - odd), (1, odd))
    ]

    geometry = (blocks, cores, group, frames_in, rows_in, halo, tile, width)
    frames = cores * frames_in
    high = tile + 2 * halo
    per_section = (blocks,) + one_half.shape
    all_kernels = (cores,) + per_section
    saved = [
        jax.ShapeDtypeStruct((frames, tile + 2 * block + 2, width, chans), F32)
        for block in range(blocks)
    ]
    cost = pl.CostEstimate(flops=6 * 10**9, bytes_accessed=8 * 10**6, transcendentals=10**6)
    features, hidden, *slopes = pl.pallas_call(
        functools.partial(forward_kernel, geometry),
        name="forward",
        in_specs=[smem] + [vmem] * (2 * blocks + 5),
        out_specs=[vmem] * (2 + blocks),
        out_shape=[
            jax.ShapeDtypeStruct((blocks, frames, tile + 2, own_width, 3 * chans), BF16),
            jax.ShapeDtypeStruct((blocks, frames, tile, own_width, chans), BF16),
        ]
        + saved,
        scratch_shapes=[
            pltpu.VMEM((frames, high, width, 3 * chans), BF16),
            pltpu.VMEM((frames, high, width, chans), BF16),
            pltpu.VMEM((high, width, chans), F32),
            pltpu.VMEM(all_kernels, BF16),
            pltpu.VMEM((frames, high, width, chans), BF16),
        ],
        compiler_params=params,
        cost_estimate=cost,
    )(corner, *shared, *videos)

    back = jax.ShapeDtypeStruct((group, frames_in, rows_in, own_width, chans), BF16)
    pixel_count = frames * total_rows * columns
    factor = 1.0 / float(pixel_count) ** 0.5
    keep, give, mine_grad, other_grad = pl.pallas_call(
        functools.partial(backward_kernel, geometry, factor),
        name="backward",
        in_specs=[smem] + [vmem] * (3 * blocks + 4),
        out_specs=[vmem] * 4,
        out_shape=[
            jax.ShapeDtypeStruct(per_section, BF16),
            jax.ShapeDtypeStruct(per_section, BF16),
            back,
            back,
        ],
        scratch_shapes=[
            pltpu.VMEM((frames, tile + 2 * blocks, width, chans), BF16),
            pltpu.VMEM((frames, tile + 2 * blocks, width, 3 * chans), BF16),
            pltpu.VMEM((frames, tile, own_width, chans), BF16),
            pltpu.VMEM((frames, tile, own_width, chans), BF16),
            pltpu.VMEM(all_kernels, BF16),
            pltpu.VMEM(all_kernels, BF16),
            pltpu.VMEM((frames, tile, own_width, chans), BF16),
        ],
        compiler_params=params,
        cost_estimate=cost,
    )(corner, *shared, *cots, features, hidden, *slopes)

    got = swapped(give)
    parts = [(keep[i].astype(F32) + got[i].astype(F32)).astype(BF16) for i in range(blocks)]
    other_grad, *parts = lax.optimization_barrier([other_grad] + parts)
    parts = parts[:1] + [swapped(parts[i], "section", i) for i in range(1, blocks)]
    part = sum(each.astype(F32) for each in parts).astype(BF16)

    halves = part.reshape(2, -1, chans)
    low = unit % 2

    def picked(which):
        return lax.dynamic_index_in_dim(halves, which, 0, keepdims=False)

    part = (picked(low).astype(F32) + swapped(picked(1 - low), "space", 1).astype(F32)).astype(BF16)
    part = part.astype(F32) + swapped(part, "space", 2).astype(F32)
    if tiles != group:
        part = lax.psum(
            part, "space", axis_index_groups=[list(range(i, tiles, group)) for i in range(group)]
        )
    part = part.astype(BF16)
    pair = jnp.stack([part, swapped(part, "space", 1)])
    spatial_out, temporal_out = pl.pallas_call(
        closing_kernel,
        name="closing",
        in_specs=[smem] + [vmem] * 2,
        out_specs=[vmem] * 2,
        out_shape=[
            jax.ShapeDtypeStruct(spatial_weights.shape, F32),
            jax.ShapeDtypeStruct(temporal_weights.shape, F32),
        ],
        scratch_shapes=[pltpu.VMEM((cores * taps * chans, chans), BF16)],
        compiler_params=params,
    )(corner, pair, swapped(pair))

    other_grad = swapped(other_grad)
    first = core == 0
    wide = jnp.concatenate(
        [jnp.where(first, mine_grad, other_grad), jnp.where(first, other_grad, mine_grad)], 3
    )
    strips = [wide[0]] + [swapped(wide[i], "space", i) for i in range(1, group)]
    grad_video = jnp.zeros(video.shape, BF16)
    for step, strip in enumerate(strips):
        grad_video = lax.dynamic_update_slice(
            grad_video, strip, (0, 0, (unit ^ step) * cores * own_width, 0)
        )
    return spatial_out, temporal_out, grad_video


def solution(mesh):
    return jax.shard_map(
        on_device,
        mesh=mesh,
        in_specs=(
            P("tm", ("section", "space"), None, None),
            P("tm", ("section", "space"), None, None),
            P("section", None, None, None),
            P("section", None, None, None),
        ),
        out_specs=(
            P("section", None, None, None),
            P("section", None, None, None),
            P("tm", ("section", "space"), None, None),
        ),
        check_vma=False,
    )
```

```python
import functools

import jax
import jax.numpy as jnp
from jax import lax
from jax.experimental import pallas as pl
from jax.experimental.pallas import tpu as pltpu
from jax.sharding import PartitionSpec as P

F32 = jnp.float32
BF16 = jnp.bfloat16


def rolled(value, steps):
    return pltpu.roll(value, steps % value.shape[0], 0)


def dot_t(left, right):
    return lax.dot_general(left, right, (((1,), (1,)), ((), ())), preferred_element_type=F32)


def dot_first(left, right):
    return lax.dot_general(left, right, (((0,), (0,)), ((), ())), preferred_element_type=F32)


def kernel_of(w_ref, block, tap):
    taps = w_ref.shape[2]
    return w_ref[tap // taps, block, tap % taps]


def rows_of(w_ref, block, first, last):
    return jnp.concatenate([kernel_of(w_ref, block, tap) for tap in range(first, last)], 0)


def lanes_of(w_ref, block, order):
    return jnp.concatenate([kernel_of(w_ref, block, tap) for tap in order], 1)


def placed(group):
    place, section = lax.axis_index("space"), lax.axis_index("section")
    band = (section * lax.axis_size("space") + place) // group
    return lax.axis_index("tm"), section, band, place % group


def window_kernel(halo, span, video_ref, *rest):
    targets, wide_ref = rest[:-1], rest[-1]
    unit = placed(len(targets))[3]
    frames, rows, columns, chans = video_ref.shape
    edge = jnp.zeros((frames, rows, halo, chans), F32)
    wide_ref[:, :, :halo] = edge
    wide_ref[:, :, halo + columns :] = edge
    wide_ref[:, :, halo : halo + columns] = video_ref[...].astype(F32)
    for step, target in enumerate(targets):
        at = jnp.bitwise_xor(unit, step) * (span - 2 * halo)
        target[...] = wide_ref[:, :, pl.ds(pl.multiple_of(at, 16), span)].astype(BF16)


def halves_kernel(spatial_ref, temporal_ref, half_ref, both_ref, all_ref):
    core = lax.axis_index("tm")
    count = spatial_ref.shape[1]
    taps = half_ref.shape[0]
    all_ref[:count] = spatial_ref[0]
    all_ref[count:] = temporal_ref[0]
    half_ref[...] = all_ref[pl.ds(core * taps, taps)]
    both_ref[0] = all_ref[pl.ds(core * taps, taps)]
    both_ref[1] = all_ref[pl.ds((1 - core) * taps, taps)]


def cotangent_kernel(halo, width, *rest):
    sources, targets, wide_ref = rest[:4], rest[4:-1], rest[-1]
    core, _, _, unit = placed(len(targets))
    frames_in, rows, columns, chans = sources[0].shape
    edge = jnp.zeros((2, 2 * frames_in, rows, halo, chans), F32)
    wide_ref[:, :, :, :halo] = edge
    wide_ref[:, :, :, halo + columns :] = edge
    for index, ref in enumerate(sources):
        whose = core if index % 2 == 0 else 1 - core
        wide_ref[index // 2, pl.ds(whose * frames_in, frames_in), :, halo : halo + columns] = ref[
            ...
        ].astype(F32)
    own = width - 2 * halo
    for step, target in enumerate(targets):
        at = (jnp.bitwise_xor(unit, step) * 2 + core) * own
        target[...] = wide_ref[:, :, :, pl.ds(pl.multiple_of(at, 16), width)].astype(BF16)


def closing_kernel(group, mine_ref, other_ref, spatial_ref, temporal_ref, flat_ref):
    pieces, rows, chans = mine_ref.shape
    core, _, _, unit = placed(group)
    for whose, ref in ((core, mine_ref), (1 - core, other_ref)):
        for step in range(pieces):
            index = whose * pieces + jnp.bitwise_xor(jnp.bitwise_and(unit, pieces - 1), step)
            flat_ref[pl.ds(pl.multiple_of(index * rows, 16), rows)] = ref[step]
    count = spatial_ref.shape[1]
    for tap in range(count + temporal_ref.shape[1]):
        turned = flat_ref[tap * chans : (tap + 1) * chans].astype(F32).T
        if tap < count:
            spatial_ref[0, tap] = turned
        else:
            temporal_ref[0, tap - count] = turned


def place_kernels(core, section, w_ref, own_ref, mine_refs, other_refs):
    w_ref[core, section] = own_ref[0]
    w_ref[1 - core, section] = own_ref[1]
    for step, (mine_ref, other_ref) in enumerate(zip(mine_refs, other_refs)):
        block = jnp.bitwise_xor(section, step + 1)
        w_ref[core, block] = mine_ref[...]
        w_ref[1 - core, block] = other_ref[...]


def forward_kernel(geometry, *rest):
    blocks, cores, group, frames_in, rows_in, halo, tile, width, height, columns = geometry
    core, section, band, unit = placed(group)
    odd = band % 2
    shared, rest = rest[: 2 * blocks - 1], rest[2 * blocks - 1 :]
    arrived, rest = rest[:6], rest[6:]
    xo_ref, ho_ref = rest[:2]
    d_refs = rest[2 : 2 + blocks]
    x_ref, h_ref, mask_ref, w_ref, start_ref = rest[2 + blocks :]
    place_kernels(core, section, w_ref, shared[0], shared[1:blocks], shared[blocks:])
    frames = cores * frames_in
    high = tile + 2 * halo
    chans = w_ref.shape[-1]
    own_rows, own_cols = (halo, halo + tile), (halo, width - halo)
    row = band * tile - halo + lax.broadcasted_iota(jnp.int32, (high, width, chans), 0)
    left = (unit * cores + core) * (width - 2 * halo) - halo
    col = left + lax.broadcasted_iota(jnp.int32, (high, width, chans), 1)
    inside = (row >= 0) & (row < height) & (col >= 0) & (col < columns)
    mask_ref[...] = jnp.where(inside, 1.0, 0.0).astype(F32)

    def keep(block, frame, value, first):
        triple = [rolled(value, 1), value, rolled(value, -1)]
        count = value.shape[0] // width
        both = jnp.concatenate([part.astype(BF16) for part in triple], 1)
        x_ref[frame, first : first + count] = both.reshape(count, width, 3 * chans)
        start = own_rows[0] - 1 - first
        cut = [
            part.reshape(count, width, chans)[
                start : start + tile + 2, own_cols[0] : own_cols[1]
            ].astype(BF16)
            for part in triple
        ]
        xo_ref[block, frame] = jnp.concatenate(cut, 2)

    near = tile + halo - odd * (tile + halo)
    columns_at = pl.ds(pl.multiple_of(core * (width - 2 * halo), 16), width)
    for index, ref in enumerate(arrived):
        base = (halo, near, tile + halo - near)[index % 3]
        whose = core if index < 3 else 1 - core
        for step in range(group):
            row = base + jnp.bitwise_xor(unit, step) * rows_in
            start_ref[pl.ds(whose * frames_in, frames_in), pl.ds(row, rows_in)] = ref[
                step, :, :, columns_at, :
            ]
    for frame in range(frames):
        keep(0, frame, start_ref[frame].reshape(high * width, chans).astype(F32), 0)

    for block in range(blocks):
        first, last = block + 1, high - block - 1
        count = last - first
        spatial = rows_of(w_ref, block, 0, 9)
        mask = mask_ref[first:last].reshape(count * width, chans)
        for frame in range(frames):
            taps = jnp.concatenate(
                [
                    x_ref[frame, first - 1 + ky : last - 1 + ky].reshape(count * width, 3 * chans)
                    for ky in range(3)
                ],
                1,
            )
            before = jnp.dot(taps, spatial, preferred_element_type=F32)
            sigma = 1.0 / (1.0 + jnp.exp(-before))
            hidden = before * sigma * mask
            slope = (sigma * (1.0 + before * (1.0 - sigma))) * mask
            h_ref[frame, first:last] = hidden.astype(BF16).reshape(count, width, chans)
            ho_ref[block, frame] = hidden.reshape(count, width, chans)[
                own_rows[0] - first : own_rows[1] - first, own_cols[0] : own_cols[1]
            ].astype(BF16)
            rim = block + 1
            d_refs[block][frame] = slope.reshape(count, width, chans)[
                own_rows[0] - rim - first : own_rows[1] + rim - first
            ]
        if block + 1 == blocks:
            break
        for frame in range(frames):
            offsets = [kt for kt in range(3) if frame + kt - 2 >= 0]
            timeline = jnp.concatenate(
                [
                    h_ref[frame + kt - 2, first:last].reshape(count * width, chans)
                    for kt in offsets
                ],
                1,
            )
            mixed = jnp.dot(
                timeline, rows_of(w_ref, block, 9 + offsets[0], 12), preferred_element_type=F32
            )
            old = x_ref[frame, first:last, :, chans : 2 * chans].astype(F32)
            new = old.reshape(count * width, chans) + mixed
            keep(block + 1, frame, new.astype(BF16).astype(F32), first)


def backward_kernel(geometry, factor, *rest):
    blocks, cores, group, frames_in, rows_in, halo, tile, width, height, columns = geometry
    core, section, band, unit = placed(group)
    shared, rest = rest[: 2 * blocks - 1], rest[2 * blocks - 1 :]
    arrived, rest = rest[:group], rest[group:]
    xo_ref, ho_ref = rest[:2]
    d_refs = rest[2 : 2 + blocks]
    keep_ref, give_ref, mine_out, other_out = rest[2 + blocks : 6 + blocks]
    g_ref, da_ref, dao_ref, go_ref, w_ref, grad_ref, out_ref = rest[6 + blocks :]
    place_kernels(core, section, w_ref, shared[0], shared[1:blocks], shared[blocks:])
    frames = cores * frames_in
    chans = w_ref.shape[-1]
    rim = blocks
    own_cols = (halo, width - halo)
    per_core = w_ref.shape[2]
    pixels = tile * (own_cols[1] - own_cols[0])

    half = group // 2
    for step, ref in enumerate(arrived):
        at = jnp.bitwise_xor(unit, step)
        g_ref[:, pl.ds(rim + at * rows_in, rows_in)] = ref[0]
        beyond = jnp.where(at < half, rim + tile + at * rows_in, (at - half) * rows_in)
        g_ref[:, pl.ds(beyond, rows_in)] = ref[1]

    def put(block, tap, value):
        slot = jnp.where(core == tap // per_core, 0, 1)
        where = jnp.bitwise_xor(section, block)
        grad_ref[slot, where, tap % per_core] = (value * factor).astype(BF16)

    for block in reversed(range(blocks)):
        edge = block + 1
        first, last = rim - edge, rim + tile + edge
        count = last - first
        for frame in range(frames):
            go_ref[frame] = g_ref[frame, rim : rim + tile].astype(F32)[
                :, own_cols[0] : own_cols[1]
            ].astype(BF16)
            offsets = [kt for kt in (2, 1, 0) if frame + 2 - kt < frames]
            ahead = jnp.concatenate(
                [
                    g_ref[frame + 2 - kt, first:last].reshape(count * width, chans)
                    for kt in offsets
                ],
                1,
            )
            hidden = dot_t(ahead, lanes_of(w_ref, block, [9 + kt for kt in offsets]))
            slope = d_refs[block][frame].reshape(count * width, chans)
            value = (hidden * slope).astype(BF16).astype(F32)
            triple = [rolled(value, -1), value, rolled(value, 1)]
            both = jnp.concatenate([part.astype(BF16) for part in triple], 1)
            da_ref[frame, first:last] = both.reshape(count, width, 3 * chans)
            dao_ref[frame] = value.reshape(count, width, chans)[
                edge : edge + tile, own_cols[0] : own_cols[1]
            ].astype(BF16)
        for frame in range(frames):
            inner = count - 2
            taps = jnp.concatenate(
                [
                    da_ref[frame, first + 2 - ky : first + 2 - ky + inner].reshape(
                        inner * width, 3 * chans
                    )
                    for ky in range(3)
                ],
                1,
            )
            back = dot_t(taps, lanes_of(w_ref, block, range(9)))
            old = g_ref[frame, first + 1 : last - 1].astype(F32).reshape(inner * width, chans)
            new = (old + back).astype(BF16)
            if block:
                g_ref[frame, first + 1 : last - 1] = new.reshape(inner, width, chans)
            else:
                cut = new.astype(F32).reshape(inner, width, chans)[:, own_cols[0] : own_cols[1]]
                out_ref[frame] = cut.astype(BF16)
        slopes = dao_ref[...].reshape(frames * pixels, chans)
        for ky in range(3):
            taps = xo_ref[block, :, ky : ky + tile].reshape(frames * pixels, 3 * chans)
            sums = dot_first(slopes, taps)
            for kx in range(3):
                put(block, 3 * ky + kx, sums[:, kx * chans : (kx + 1) * chans])
        for kt in range(3):
            skip = 2 - kt
            later = go_ref[skip:].reshape((frames - skip) * pixels, chans)
            earlier = ho_ref[block, : frames - skip].reshape((frames - skip) * pixels, chans)
            put(block, 9 + kt, dot_first(later, earlier))
    keep_ref[...] = grad_ref[0]
    give_ref[...] = grad_ref[1]
    for whose, target in ((core, mine_out), (1 - core, other_out)):
        for step in range(group):
            row = jnp.bitwise_xor(unit, step) * rows_in
            target[step] = out_ref[pl.ds(whose * frames_in, frames_in), pl.ds(row, rows_in)]


def swapped(value, axis="tm", step=1):
    count = lax.axis_size(axis)
    return lax.ppermute(value, axis, [(i, i ^ step) for i in range(count)])


def on_device(video, cotangent, spatial_weights, temporal_weights):
    blocks, cores, tiles = (lax.axis_size(name) for name in ("section", "tm", "space"))
    frames_in, rows_in, columns, chans = video.shape
    halo = 2 * blocks
    tile = halo
    group = tile // rows_in
    parties = cores * group
    own_width = columns // parties
    width = own_width + 2 * halo
    span = cores * own_width + 2 * halo
    vmem = pl.BlockSpec(memory_space=pltpu.VMEM)
    params = pltpu.CompilerParams(vmem_limit_bytes=32 * 2**20)

    bands = blocks * tiles // group
    core, section, band, unit = placed(group)

    def traded(value, shift):
        pairs = []
        for one in range(bands):
            other = ((one + shift) ^ 1) - shift
            if 0 <= other < bands:
                pairs += [(one * group + i, other * group + i) for i in range(group)]
        return lax.ppermute(value, ("section", "space"), pairs)

    total_rows = blocks * tiles * rows_in
    half = group // 2
    passed = []
    for one in range(bands - 1):
        for i in range(group):
            low, high = one * group + i, (one + 1) * group + i
            passed.append((high, low) if i < half else (low, high))
    cot_halo = lax.ppermute(cotangent, ("section", "space"), passed)

    padded = columns + 2 * halo
    cuts = pl.pallas_call(
        functools.partial(window_kernel, halo, span),
        name="windows",
        in_specs=[vmem],
        out_specs=[vmem] * group,
        out_shape=[jax.ShapeDtypeStruct((frames_in, rows_in, span, chans), BF16)] * group,
        scratch_shapes=[pltpu.VMEM((frames_in, rows_in, padded, chans), F32)],
        compiler_params=params,
    )(video)
    *cuts, spatial, temporal = lax.optimization_barrier(
        list(cuts) + [spatial_weights, temporal_weights]
    )
    count = spatial_weights.shape[1]
    taps = (count + temporal_weights.shape[1]) // cores
    one_half = jax.ShapeDtypeStruct((taps, chans, chans), BF16)
    half_kernels, own_kernels = pl.pallas_call(
        halves_kernel,
        name="halves",
        in_specs=[vmem] * 2,
        out_specs=[vmem] * 2,
        out_shape=[one_half, jax.ShapeDtypeStruct((cores,) + one_half.shape, BF16)],
        scratch_shapes=[pltpu.VMEM((cores * taps, chans, chans), BF16)],
        compiler_params=params,
    )(spatial, temporal)

    def gathered(pieces):
        return jnp.stack([pieces[0]] + [swapped(pieces[i], "space", i) for i in range(1, group)])

    along_x = swapped(half_kernels, "section", 1)
    along_y = swapped(half_kernels, "section", 2)
    own_video, along_x, along_y = lax.optimization_barrier([gathered(cuts), along_x, along_y])
    near, far = traded(own_video, 0), traded(own_video, 1)
    mine = [along_x, along_y, swapped(along_x, "section", 2)]
    shared = mine + [swapped(each) for each in mine]
    shared = [own_kernels] + shared

    cuts = pl.pallas_call(
        functools.partial(cotangent_kernel, halo, width),
        name="cotangent",
        in_specs=[vmem] * 4,
        out_specs=[vmem] * group,
        out_shape=[jax.ShapeDtypeStruct((2, cores * frames_in, rows_in, width, chans), BF16)] * group,
        scratch_shapes=[pltpu.VMEM((2, cores * frames_in, rows_in, padded, chans), F32)],
        compiler_params=params,
    )(cotangent, swapped(cotangent), cot_halo, swapped(cot_halo))
    near, *cuts = lax.optimization_barrier([near] + list(cuts))
    videos = [own_video, near, far]
    videos += [swapped(each) for each in videos]
    cots = [cuts[0]] + [swapped(cuts[i], "space", i) for i in range(1, group)]

    geometry = (blocks, cores, group, frames_in, rows_in, halo, tile, width, total_rows, columns)
    frames = cores * frames_in
    high = tile + 2 * halo
    per_section = (blocks,) + one_half.shape
    all_kernels = (cores,) + per_section
    saved = [
        jax.ShapeDtypeStruct((frames, tile + 2 * block + 2, width, chans), F32)
        for block in range(blocks)
    ]
    cost = pl.CostEstimate(flops=6 * 10**9, bytes_accessed=8 * 10**6, transcendentals=10**6)
    features, hidden, *slopes = pl.pallas_call(
        functools.partial(forward_kernel, geometry),
        name="forward",
        in_specs=[vmem] * (2 * blocks + 5),
        out_specs=[vmem] * (2 + blocks),
        out_shape=[
            jax.ShapeDtypeStruct((blocks, frames, tile + 2, own_width, 3 * chans), BF16),
            jax.ShapeDtypeStruct((blocks, frames, tile, own_width, chans), BF16),
        ]
        + saved,
        scratch_shapes=[
            pltpu.VMEM((frames, high, width, 3 * chans), BF16),
            pltpu.VMEM((frames, high, width, chans), BF16),
            pltpu.VMEM((high, width, chans), F32),
            pltpu.VMEM(all_kernels, BF16),
            pltpu.VMEM((frames, high, width, chans), BF16),
        ],
        compiler_params=params,
        cost_estimate=cost,
    )(*shared, *videos)

    back = jax.ShapeDtypeStruct((group, frames_in, rows_in, own_width, chans), BF16)
    pixel_count = frames * total_rows * columns
    factor = 1.0 / float(pixel_count) ** 0.5
    keep, give, mine_grad, other_grad = pl.pallas_call(
        functools.partial(backward_kernel, geometry, factor),
        name="backward",
        in_specs=[vmem] * (3 * blocks + group + 1),
        out_specs=[vmem] * 4,
        out_shape=[
            jax.ShapeDtypeStruct(per_section, BF16),
            jax.ShapeDtypeStruct(per_section, BF16),
            back,
            back,
        ],
        scratch_shapes=[
            pltpu.VMEM((frames, tile + 2 * blocks, width, chans), BF16),
            pltpu.VMEM((frames, tile + 2 * blocks, width, 3 * chans), BF16),
            pltpu.VMEM((frames, tile, own_width, chans), BF16),
            pltpu.VMEM((frames, tile, own_width, chans), BF16),
            pltpu.VMEM(all_kernels, BF16),
            pltpu.VMEM(all_kernels, BF16),
            pltpu.VMEM((frames, tile, own_width, chans), BF16),
        ],
        compiler_params=params,
        cost_estimate=cost,
    )(*shared, *cots, features, hidden, *slopes)

    got = swapped(give)
    parts = [(keep[i].astype(F32) + got[i].astype(F32)).astype(BF16) for i in range(blocks)]
    other_grad, *parts = lax.optimization_barrier([other_grad] + parts)
    parts = parts[:1] + [swapped(parts[i], "section", i) for i in range(1, blocks)]
    other_grad = swapped(other_grad)
    first = core == 0
    wide = jnp.concatenate(
        [jnp.where(first, mine_grad, other_grad), jnp.where(first, other_grad, mine_grad)], 3
    )
    strips = [wide[0]] + [swapped(wide[i], "space", i) for i in range(1, group)]
    received = lax.optimization_barrier(parts + strips)
    parts, strips = received[:blocks], received[blocks:]
    part = sum(each.astype(F32) for each in parts).astype(BF16)

    halves = part.reshape(2, -1, chans)
    low = unit % 2

    def picked(which):
        return lax.dynamic_index_in_dim(halves, which, 0, keepdims=False)

    part = (picked(low).astype(F32) + swapped(picked(1 - low), "space", 1).astype(F32)).astype(BF16)
    part = part.astype(F32) + swapped(part, "space", 2).astype(F32)
    if tiles != group:
        part = lax.psum(
            part, "space", axis_index_groups=[list(range(i, tiles, group)) for i in range(group)]
        )
    part = part.astype(BF16)
    pair = jnp.stack([part, swapped(part, "space", 1)])
    spatial_out, temporal_out = pl.pallas_call(
        functools.partial(closing_kernel, group),
        name="closing",
        in_specs=[vmem] * 2,
        out_specs=[vmem] * 2,
        out_shape=[
            jax.ShapeDtypeStruct(spatial_weights.shape, F32),
            jax.ShapeDtypeStruct(temporal_weights.shape, F32),
        ],
        scratch_shapes=[pltpu.VMEM((cores * taps * chans, chans), BF16)],
        compiler_params=params,
    )(pair, swapped(pair))

    grad_video = jnp.zeros(video.shape, BF16)
    for step, strip in enumerate(strips):
        grad_video = lax.dynamic_update_slice(
            grad_video, strip, (0, 0, (unit ^ step) * cores * own_width, 0)
        )
    return spatial_out, temporal_out, grad_video


def solution(mesh):
    return jax.shard_map(
        on_device,
        mesh=mesh,
        in_specs=(
            P("tm", ("section", "space"), None, None),
            P("tm", ("section", "space"), None, None),
            P("section", None, None, None),
            P("section", None, None, None),
        ),
        out_specs=(
            P("section", None, None, None),
            P("section", None, None, None),
            P("tm", ("section", "space"), None, None),
        ),
        check_vma=False,
    )
```

```python
import functools

import jax
import jax.numpy as jnp
from jax import lax
from jax.experimental import pallas as pl
from jax.experimental.pallas import tpu as pltpu
from jax.sharding import PartitionSpec as P

F32 = jnp.float32
BF16 = jnp.bfloat16


def rolled(value, steps):
    return pltpu.roll(value, steps % value.shape[0], 0)


def dot_t(left, right):
    return lax.dot_general(left, right, (((1,), (1,)), ((), ())), preferred_element_type=F32)


def dot_first(left, right):
    return lax.dot_general(left, right, (((0,), (0,)), ((), ())), preferred_element_type=F32)


def kernel_of(w_ref, block, tap):
    taps = w_ref.shape[2]
    return w_ref[tap // taps, block, tap % taps]


def rows_of(w_ref, block, first, last):
    return jnp.concatenate([kernel_of(w_ref, block, tap) for tap in range(first, last)], 0)


def lanes_of(w_ref, block, order):
    return jnp.concatenate([kernel_of(w_ref, block, tap) for tap in order], 1)


def placed(group):
    place, section = lax.axis_index("space"), lax.axis_index("section")
    band = (section * lax.axis_size("space") + place) // group
    return lax.axis_index("tm"), section, band, place % group


def window_kernel(halo, width, *rest):
    (mine_ref, other_ref), targets, wide_ref = rest[:2], rest[2:-1], rest[-1]
    core, _, _, unit = placed(len(targets))
    lead, frames_in, rows, columns, chans = mine_ref.shape
    edge = jnp.zeros((lead, 2 * frames_in, rows, halo, chans), F32)
    wide_ref[:, :, :, :halo] = edge
    wide_ref[:, :, :, halo + columns :] = edge
    for whose, ref in ((core, mine_ref), (1 - core, other_ref)):
        wide_ref[:, pl.ds(whose * frames_in, frames_in), :, halo : halo + columns] = ref[
            ...
        ].astype(F32)
    own = width - 2 * halo
    for step, target in enumerate(targets):
        at = (jnp.bitwise_xor(unit, step) * 2 + core) * own
        target[...] = wide_ref[:, :, :, pl.ds(pl.multiple_of(at, 16), width)].astype(BF16)


def halves_kernel(spatial_ref, temporal_ref, half_ref, both_ref, all_ref):
    core = lax.axis_index("tm")
    count = spatial_ref.shape[1]
    taps = half_ref.shape[0]
    all_ref[:count] = spatial_ref[0]
    all_ref[count:] = temporal_ref[0]
    half_ref[...] = all_ref[pl.ds(core * taps, taps)]
    both_ref[0] = all_ref[pl.ds(core * taps, taps)]
    both_ref[1] = all_ref[pl.ds((1 - core) * taps, taps)]


def closing_kernel(group, mine_ref, other_ref, spatial_ref, temporal_ref, flat_ref):
    pieces, rows, chans = mine_ref.shape
    core, _, _, unit = placed(group)
    for whose, ref in ((core, mine_ref), (1 - core, other_ref)):
        for step in range(pieces):
            index = whose * pieces + jnp.bitwise_xor(jnp.bitwise_and(unit, pieces - 1), step)
            flat_ref[pl.ds(pl.multiple_of(index * rows, 16), rows)] = ref[step]
    count = spatial_ref.shape[1]
    for tap in range(count + temporal_ref.shape[1]):
        turned = flat_ref[tap * chans : (tap + 1) * chans].astype(F32).T
        if tap < count:
            spatial_ref[0, tap] = turned
        else:
            temporal_ref[0, tap - count] = turned


def place_kernels(core, section, w_ref, own_ref, x_mine, x_other, y_mine, y_other):
    w_ref[core, section] = own_ref[0]
    w_ref[1 - core, section] = own_ref[1]
    for half, x_ref, y_ref in ((core, x_mine, y_mine), (1 - core, x_other, y_other)):
        w_ref[half, jnp.bitwise_xor(section, 1)] = x_ref[...]
        for step in range(2):
            w_ref[half, jnp.bitwise_xor(section, 2 + step)] = y_ref[step]


def forward_kernel(geometry, *rest):
    blocks, cores, group, frames_in, rows_in, halo, tile, width, height, columns = geometry
    core, section, band, unit = placed(group)
    odd = band % 2
    shared, rest = rest[:5], rest[5:]
    arrived, rest = rest[:3], rest[3:]
    xo_ref, ho_ref = rest[:2]
    d_refs = rest[2 : 2 + blocks]
    x_ref, h_ref, mask_ref, w_ref, start_ref = rest[2 + blocks :]
    place_kernels(core, section, w_ref, *shared)
    frames = cores * frames_in
    high = tile + 2 * halo
    chans = w_ref.shape[-1]
    own_rows, own_cols = (halo, halo + tile), (halo, width - halo)
    row = band * tile - halo + lax.broadcasted_iota(jnp.int32, (high, width, chans), 0)
    left = (unit * cores + core) * (width - 2 * halo) - halo
    col = left + lax.broadcasted_iota(jnp.int32, (high, width, chans), 1)
    inside = (row >= 0) & (row < height) & (col >= 0) & (col < columns)
    mask_ref[...] = jnp.where(inside, 1.0, 0.0).astype(F32)

    def keep(block, frame, value, first):
        triple = [rolled(value, 1), value, rolled(value, -1)]
        count = value.shape[0] // width
        both = jnp.concatenate([part.astype(BF16) for part in triple], 1)
        x_ref[frame, first : first + count] = both.reshape(count, width, 3 * chans)
        start = own_rows[0] - 1 - first
        cut = [
            part.reshape(count, width, chans)[
                start : start + tile + 2, own_cols[0] : own_cols[1]
            ].astype(BF16)
            for part in triple
        ]
        xo_ref[block, frame] = jnp.concatenate(cut, 2)

    near = tile + halo - odd * (tile + halo)
    for base, ref in zip((halo, near, tile + halo - near), arrived):
        for step in range(group):
            row = base + jnp.bitwise_xor(unit, step) * rows_in
            start_ref[:, pl.ds(row, rows_in)] = ref[step]
    for frame in range(frames):
        keep(0, frame, start_ref[frame].reshape(high * width, chans).astype(F32), 0)

    for block in range(blocks):
        first, last = block + 1, high - block - 1
        count = last - first
        spatial = rows_of(w_ref, block, 0, 9)
        mask = mask_ref[first:last].reshape(count * width, chans)
        for frame in range(frames):
            taps = jnp.concatenate(
                [
                    x_ref[frame, first - 1 + ky : last - 1 + ky].reshape(count * width, 3 * chans)
                    for ky in range(3)
                ],
                1,
            )
            before = jnp.dot(taps, spatial, preferred_element_type=F32)
            sigma = 1.0 / (1.0 + jnp.exp(-before))
            hidden = before * sigma * mask
            slope = (sigma * (1.0 + before * (1.0 - sigma))) * mask
            h_ref[frame, first:last] = hidden.astype(BF16).reshape(count, width, chans)
            ho_ref[block, frame] = hidden.reshape(count, width, chans)[
                own_rows[0] - first : own_rows[1] - first, own_cols[0] : own_cols[1]
            ].astype(BF16)
            rim = block + 1
            d_refs[block][frame] = slope.reshape(count, width, chans)[
                own_rows[0] - rim - first : own_rows[1] + rim - first
            ]
        if block + 1 == blocks:
            break
        for frame in range(frames):
            offsets = [kt for kt in range(3) if frame + kt - 2 >= 0]
            timeline = jnp.concatenate(
                [
                    h_ref[frame + kt - 2, first:last].reshape(count * width, chans)
                    for kt in offsets
                ],
                1,
            )
            mixed = jnp.dot(
                timeline, rows_of(w_ref, block, 9 + offsets[0], 12), preferred_element_type=F32
            )
            old = x_ref[frame, first:last, :, chans : 2 * chans].astype(F32)
            new = old.reshape(count * width, chans) + mixed
            keep(block + 1, frame, new.astype(BF16).astype(F32), first)


def backward_kernel(geometry, factor, *rest):
    blocks, cores, group, frames_in, rows_in, halo, tile, width, height, columns = geometry
    core, section, band, unit = placed(group)
    shared, rest = rest[:5], rest[5:]
    arrived, rest = rest[:group], rest[group:]
    xo_ref, ho_ref = rest[:2]
    d_refs = rest[2 : 2 + blocks]
    keep_ref, give_ref, mine_out, other_out = rest[2 + blocks : 6 + blocks]
    g_ref, da_ref, dao_ref, go_ref, w_ref, grad_ref, out_ref = rest[6 + blocks :]
    place_kernels(core, section, w_ref, *shared)
    frames = cores * frames_in
    chans = w_ref.shape[-1]
    rim = blocks
    own_cols = (halo, width - halo)
    per_core = w_ref.shape[2]
    pixels = tile * (own_cols[1] - own_cols[0])

    half = group // 2
    for step, ref in enumerate(arrived):
        at = jnp.bitwise_xor(unit, step)
        g_ref[:, pl.ds(rim + at * rows_in, rows_in)] = ref[0]
        beyond = jnp.where(at < half, rim + tile + at * rows_in, (at - half) * rows_in)
        g_ref[:, pl.ds(beyond, rows_in)] = ref[1]

    def put(block, tap, value):
        slot = jnp.where(core == tap // per_core, 0, 1)
        where = jnp.bitwise_xor(section, block)
        grad_ref[slot, where, tap % per_core] = (value * factor).astype(BF16)

    for block in reversed(range(blocks)):
        edge = block + 1
        first, last = rim - edge, rim + tile + edge
        count = last - first
        for frame in range(frames):
            go_ref[frame] = g_ref[frame, rim : rim + tile].astype(F32)[
                :, own_cols[0] : own_cols[1]
            ].astype(BF16)
            offsets = [kt for kt in (2, 1, 0) if frame + 2 - kt < frames]
            ahead = jnp.concatenate(
                [
                    g_ref[frame + 2 - kt, first:last].reshape(count * width, chans)
                    for kt in offsets
                ],
                1,
            )
            hidden = dot_t(ahead, lanes_of(w_ref, block, [9 + kt for kt in offsets]))
            slope = d_refs[block][frame].reshape(count * width, chans)
            value = (hidden * slope).astype(BF16).astype(F32)
            triple = [rolled(value, -1), value, rolled(value, 1)]
            both = jnp.concatenate([part.astype(BF16) for part in triple], 1)
            da_ref[frame, first:last] = both.reshape(count, width, 3 * chans)
            dao_ref[frame] = value.reshape(count, width, chans)[
                edge : edge + tile, own_cols[0] : own_cols[1]
            ].astype(BF16)
        for frame in range(frames):
            inner = count - 2
            taps = jnp.concatenate(
                [
                    da_ref[frame, first + 2 - ky : first + 2 - ky + inner].reshape(
                        inner * width, 3 * chans
                    )
                    for ky in range(3)
                ],
                1,
            )
            back = dot_t(taps, lanes_of(w_ref, block, range(9)))
            old = g_ref[frame, first + 1 : last - 1].astype(F32).reshape(inner * width, chans)
            new = (old + back).astype(BF16)
            if block:
                g_ref[frame, first + 1 : last - 1] = new.reshape(inner, width, chans)
            else:
                cut = new.astype(F32).reshape(inner, width, chans)[:, own_cols[0] : own_cols[1]]
                out_ref[frame] = cut.astype(BF16)
        slopes = dao_ref[...].reshape(frames * pixels, chans)
        for ky in range(3):
            taps = xo_ref[block, :, ky : ky + tile].reshape(frames * pixels, 3 * chans)
            sums = dot_first(slopes, taps)
            for kx in range(3):
                put(block, 3 * ky + kx, sums[:, kx * chans : (kx + 1) * chans])
        for kt in range(3):
            skip = 2 - kt
            later = go_ref[skip:].reshape((frames - skip) * pixels, chans)
            earlier = ho_ref[block, : frames - skip].reshape((frames - skip) * pixels, chans)
            put(block, 9 + kt, dot_first(later, earlier))
    keep_ref[...] = grad_ref[0]
    give_ref[...] = grad_ref[1]
    for whose, target in ((core, mine_out), (1 - core, other_out)):
        for step in range(group):
            row = jnp.bitwise_xor(unit, step) * rows_in
            target[step] = out_ref[pl.ds(whose * frames_in, frames_in), pl.ds(row, rows_in)]


def swapped(value, axis="tm", step=1):
    count = lax.axis_size(axis)
    return lax.ppermute(value, axis, [(i, i ^ step) for i in range(count)])


def on_device(video, cotangent, spatial_weights, temporal_weights):
    blocks, cores, tiles = (lax.axis_size(name) for name in ("section", "tm", "space"))
    frames_in, rows_in, columns, chans = video.shape
    halo = 2 * blocks
    tile = halo
    group = tile // rows_in
    parties = cores * group
    own_width = columns // parties
    width = own_width + 2 * halo
    vmem = pl.BlockSpec(memory_space=pltpu.VMEM)
    params = pltpu.CompilerParams(vmem_limit_bytes=32 * 2**20)

    bands = blocks * tiles // group
    core, section, band, unit = placed(group)

    def traded(value, shift):
        pairs = []
        for one in range(bands):
            other = ((one + shift) ^ 1) - shift
            if 0 <= other < bands:
                pairs += [(one * group + i, other * group + i) for i in range(group)]
        return lax.ppermute(value, ("section", "space"), pairs)

    total_rows = blocks * tiles * rows_in
    half = group // 2
    passed = []
    for one in range(bands - 1):
        for i in range(group):
            low, high = one * group + i, (one + 1) * group + i
            passed.append((high, low) if i < half else (low, high))
    cot_halo = lax.ppermute(cotangent, ("section", "space"), passed)

    frames = cores * frames_in

    def windows(name, mine, other):
        lead = mine.shape[0]
        one = (lead, frames, rows_in, width, chans)
        return pl.pallas_call(
            functools.partial(window_kernel, halo, width),
            name=name,
            in_specs=[vmem] * 2,
            out_specs=[vmem] * group,
            out_shape=[jax.ShapeDtypeStruct(one, BF16)] * group,
            scratch_shapes=[
                pltpu.VMEM((lead, frames, rows_in, columns + 2 * halo, chans), F32)
            ],
            compiler_params=params,
        )(mine, other)

    cuts = windows("video_windows", video[None], swapped(video)[None])
    count = spatial_weights.shape[1]
    taps = (count + temporal_weights.shape[1]) // cores
    one_half = jax.ShapeDtypeStruct((taps, chans, chans), BF16)
    half_kernels, own_kernels = pl.pallas_call(
        halves_kernel,
        name="halves",
        in_specs=[vmem] * 2,
        out_specs=[vmem] * 2,
        out_shape=[one_half, jax.ShapeDtypeStruct((cores,) + one_half.shape, BF16)],
        scratch_shapes=[pltpu.VMEM((cores * taps, chans, chans), BF16)],
        compiler_params=params,
    )(spatial_weights, temporal_weights)

    def gathered(pieces):
        return jnp.stack([pieces[0]] + [swapped(pieces[i], "space", i) for i in range(1, group)])

    along_x = swapped(half_kernels, "section", 1)
    own_video, along_x, cot_halo = lax.optimization_barrier(
        [gathered([cut[0] for cut in cuts]), along_x, cot_halo]
    )
    near, far = traded(own_video, 0), traded(own_video, 1)
    along_y = swapped(jnp.stack([half_kernels, along_x]), "section", 2)

    both = jnp.stack([cotangent, cot_halo])
    cuts = windows("cotangent_windows", both, swapped(both))
    near, along_y, *cuts = lax.optimization_barrier([near, along_y] + list(cuts))
    shared = [own_kernels, along_x, swapped(along_x), along_y, swapped(along_y)]
    videos = [own_video, near, far]
    cots = [cuts[0]] + [swapped(cuts[i], "space", i) for i in range(1, group)]

    geometry = (blocks, cores, group, frames_in, rows_in, halo, tile, width, total_rows, columns)
    high = tile + 2 * halo
    per_section = (blocks,) + one_half.shape
    all_kernels = (cores,) + per_section
    saved = [
        jax.ShapeDtypeStruct((frames, tile + 2 * block + 2, width, chans), F32)
        for block in range(blocks)
    ]
    cost = pl.CostEstimate(flops=6 * 10**9, bytes_accessed=8 * 10**6, transcendentals=10**6)
    features, hidden, *slopes = pl.pallas_call(
        functools.partial(forward_kernel, geometry),
        name="forward",
        in_specs=[vmem] * 8,
        out_specs=[vmem] * (2 + blocks),
        out_shape=[
            jax.ShapeDtypeStruct((blocks, frames, tile + 2, own_width, 3 * chans), BF16),
            jax.ShapeDtypeStruct((blocks, frames, tile, own_width, chans), BF16),
        ]
        + saved,
        scratch_shapes=[
            pltpu.VMEM((frames, high, width, 3 * chans), BF16),
            pltpu.VMEM((frames, high, width, chans), BF16),
            pltpu.VMEM((high, width, chans), F32),
            pltpu.VMEM(all_kernels, BF16),
            pltpu.VMEM((frames, high, width, chans), BF16),
        ],
        compiler_params=params,
        cost_estimate=cost,
    )(*shared, *videos)

    back = jax.ShapeDtypeStruct((group, frames_in, rows_in, own_width, chans), BF16)
    pixel_count = frames * total_rows * columns
    factor = 1.0 / float(pixel_count) ** 0.5
    keep, give, mine_grad, other_grad = pl.pallas_call(
        functools.partial(backward_kernel, geometry, factor),
        name="backward",
        in_specs=[vmem] * (blocks + group + 7),
        out_specs=[vmem] * 4,
        out_shape=[
            jax.ShapeDtypeStruct(per_section, BF16),
            jax.ShapeDtypeStruct(per_section, BF16),
            back,
            back,
        ],
        scratch_shapes=[
            pltpu.VMEM((frames, tile + 2 * blocks, width, chans), BF16),
            pltpu.VMEM((frames, tile + 2 * blocks, width, 3 * chans), BF16),
            pltpu.VMEM((frames, tile, own_width, chans), BF16),
            pltpu.VMEM((frames, tile, own_width, chans), BF16),
            pltpu.VMEM(all_kernels, BF16),
            pltpu.VMEM(all_kernels, BF16),
            pltpu.VMEM((frames, tile, own_width, chans), BF16),
        ],
        compiler_params=params,
        cost_estimate=cost,
    )(*shared, *cots, features, hidden, *slopes)

    got = swapped(give)
    parts = [(keep[i].astype(F32) + got[i].astype(F32)).astype(BF16) for i in range(blocks)]
    other_grad, *parts = lax.optimization_barrier([other_grad] + parts)
    parts = parts[:1] + [swapped(parts[i], "section", i) for i in range(1, blocks)]
    other_grad = swapped(other_grad)
    first = core == 0
    wide = jnp.concatenate(
        [jnp.where(first, mine_grad, other_grad), jnp.where(first, other_grad, mine_grad)], 3
    )
    strips = [wide[0]] + [swapped(wide[i], "space", i) for i in range(1, group)]
    received = lax.optimization_barrier(parts + strips)
    parts, strips = received[:blocks], received[blocks:]
    part = sum(each.astype(F32) for each in parts).astype(BF16)

    halves = part.reshape(2, -1, chans)
    low = unit % 2

    def picked(which):
        return lax.dynamic_index_in_dim(halves, which, 0, keepdims=False)

    part = (picked(low).astype(F32) + swapped(picked(1 - low), "space", 1).astype(F32)).astype(BF16)
    part = part.astype(F32) + swapped(part, "space", 2).astype(F32)
    if tiles != group:
        part = lax.psum(
            part, "space", axis_index_groups=[list(range(i, tiles, group)) for i in range(group)]
        )
    part = part.astype(BF16)
    pair = jnp.stack([part, swapped(part, "space", 1)])
    spatial_out, temporal_out = pl.pallas_call(
        functools.partial(closing_kernel, group),
        name="closing",
        in_specs=[vmem] * 2,
        out_specs=[vmem] * 2,
        out_shape=[
            jax.ShapeDtypeStruct(spatial_weights.shape, F32),
            jax.ShapeDtypeStruct(temporal_weights.shape, F32),
        ],
        scratch_shapes=[pltpu.VMEM((cores * taps * chans, chans), BF16)],
        compiler_params=params,
    )(pair, swapped(pair))

    grad_video = jnp.zeros(video.shape, BF16)
    for step, strip in enumerate(strips):
        grad_video = lax.dynamic_update_slice(
            grad_video, strip, (0, 0, (unit ^ step) * cores * own_width, 0)
        )
    return spatial_out, temporal_out, grad_video


def solution(mesh):
    return jax.shard_map(
        on_device,
        mesh=mesh,
        in_specs=(
            P("tm", ("section", "space"), None, None),
            P("tm", ("section", "space"), None, None),
            P("section", None, None, None),
            P("section", None, None, None),
        ),
        out_specs=(
            P("section", None, None, None),
            P("section", None, None, None),
            P("tm", ("section", "space"), None, None),
        ),
        check_vma=False,
    )
```

```python
import functools

import jax
import jax.numpy as jnp
from jax import lax
from jax.experimental import pallas as pl
from jax.experimental.pallas import tpu as pltpu
from jax.sharding import PartitionSpec as P

F32 = jnp.float32
BF16 = jnp.bfloat16


def rolled(value, steps):
    return pltpu.roll(value, steps % value.shape[0], 0)


def dot_t(left, right):
    return lax.dot_general(left, right, (((1,), (1,)), ((), ())), preferred_element_type=F32)


def dot_first(left, right):
    return lax.dot_general(left, right, (((0,), (0,)), ((), ())), preferred_element_type=F32)


def kernel_of(w_ref, block, tap):
    taps = w_ref.shape[2]
    return w_ref[tap // taps, block, tap % taps]


def rows_of(w_ref, block, first, last):
    return jnp.concatenate([kernel_of(w_ref, block, tap) for tap in range(first, last)], 0)


def lanes_of(w_ref, block, order):
    return jnp.concatenate([kernel_of(w_ref, block, tap) for tap in order], 1)


def placed(group):
    place, section = lax.axis_index("space"), lax.axis_index("section")
    band = (section * lax.axis_size("space") + place) // group
    return lax.axis_index("tm"), section, band, place % group


def window_kernel(halo, span, video_ref, *rest):
    targets, wide_ref = rest[:-1], rest[-1]
    unit = placed(len(targets))[3]
    frames, rows, columns, chans = video_ref.shape
    edge = jnp.zeros((frames, rows, halo, chans), F32)
    wide_ref[:, :, :halo] = edge
    wide_ref[:, :, halo + columns :] = edge
    wide_ref[:, :, halo : halo + columns] = video_ref[...].astype(F32)
    for step, target in enumerate(targets):
        at = jnp.bitwise_xor(unit, step) * (span - 2 * halo)
        target[...] = wide_ref[:, :, pl.ds(pl.multiple_of(at, 16), span)].astype(BF16)


def halves_kernel(spatial_ref, temporal_ref, half_ref, both_ref, all_ref):
    core = lax.axis_index("tm")
    count = spatial_ref.shape[1]
    taps = half_ref.shape[0]
    all_ref[:count] = spatial_ref[0]
    all_ref[count:] = temporal_ref[0]
    half_ref[...] = all_ref[pl.ds(core * taps, taps)]
    both_ref[0] = all_ref[pl.ds(core * taps, taps)]
    both_ref[1] = all_ref[pl.ds((1 - core) * taps, taps)]


def cotangent_kernel(halo, width, *rest):
    sources, targets, wide_ref = rest[:4], rest[4:-1], rest[-1]
    core, _, _, unit = placed(len(targets))
    frames_in, rows, columns, chans = sources[0].shape
    edge = jnp.zeros((2, 2 * frames_in, rows, halo, chans), F32)
    wide_ref[:, :, :, :halo] = edge
    wide_ref[:, :, :, halo + columns :] = edge
    for index, ref in enumerate(sources):
        whose = core if index % 2 == 0 else 1 - core
        wide_ref[index // 2, pl.ds(whose * frames_in, frames_in), :, halo : halo + columns] = ref[
            ...
        ].astype(F32)
    own = width - 2 * halo
    for step, target in enumerate(targets):
        at = (jnp.bitwise_xor(unit, step) * 2 + core) * own
        target[...] = wide_ref[:, :, :, pl.ds(pl.multiple_of(at, 16), width)].astype(BF16)


def closing_kernel(group, *rest):
    pairs, (spatial_ref, temporal_ref, flat_ref) = rest[:-3], rest[-3:]
    core, _, _, unit = placed(group)
    shares = len(pairs) // 2
    pieces, rows, chans = pairs[0].shape
    for index, ref in enumerate(pairs):
        whose = core if index % 2 == 0 else 1 - core
        for step in range(pieces):
            piece = jnp.bitwise_xor(jnp.bitwise_and(unit, pieces - 1), step)
            first = ((whose * shares + index // 2) * pieces + piece) * rows
            flat_ref[pl.ds(pl.multiple_of(first, 16), rows)] = ref[step]
    count = spatial_ref.shape[1]
    for tap in range(count + temporal_ref.shape[1]):
        turned = flat_ref[tap * chans : (tap + 1) * chans].astype(F32).T
        if tap < count:
            spatial_ref[0, tap] = turned
        else:
            temporal_ref[0, tap - count] = turned


def place_kernels(core, section, w_ref, own_ref, mine_refs, other_refs):
    w_ref[core, section] = own_ref[0]
    w_ref[1 - core, section] = own_ref[1]
    for step, (mine_ref, other_ref) in enumerate(zip(mine_refs, other_refs)):
        block = jnp.bitwise_xor(section, step + 1)
        w_ref[core, block] = mine_ref[...]
        w_ref[1 - core, block] = other_ref[...]


def forward_kernel(geometry, *rest):
    blocks, cores, group, frames_in, rows_in, halo, tile, width, height, columns = geometry
    core, section, band, unit = placed(group)
    odd = band % 2
    shared, rest = rest[: 2 * blocks - 1], rest[2 * blocks - 1 :]
    arrived, rest = rest[:6], rest[6:]
    xo_ref, ho_ref = rest[:2]
    d_refs = rest[2 : 2 + blocks]
    x_ref, h_ref, mask_ref, w_ref, start_ref = rest[2 + blocks :]
    place_kernels(core, section, w_ref, shared[0], shared[1:blocks], shared[blocks:])
    frames = cores * frames_in
    high = tile + 2 * halo
    chans = w_ref.shape[-1]
    own_rows, own_cols = (halo, halo + tile), (halo, width - halo)
    row = band * tile - halo + lax.broadcasted_iota(jnp.int32, (high, width, chans), 0)
    left = (unit * cores + core) * (width - 2 * halo) - halo
    col = left + lax.broadcasted_iota(jnp.int32, (high, width, chans), 1)
    inside = (row >= 0) & (row < height) & (col >= 0) & (col < columns)
    mask_ref[...] = jnp.where(inside, 1.0, 0.0).astype(F32)

    def keep(block, frame, value, first):
        triple = [rolled(value, 1), value, rolled(value, -1)]
        count = value.shape[0] // width
        both = jnp.concatenate([part.astype(BF16) for part in triple], 1)
        x_ref[frame, first : first + count] = both.reshape(count, width, 3 * chans)
        start = own_rows[0] - 1 - first
        cut = [
            part.reshape(count, width, chans)[
                start : start + tile + 2, own_cols[0] : own_cols[1]
            ].astype(BF16)
            for part in triple
        ]
        xo_ref[block, frame] = jnp.concatenate(cut, 2)

    near = tile + halo - odd * (tile + halo)
    columns_at = pl.ds(pl.multiple_of(core * (width - 2 * halo), 16), width)
    for index, ref in enumerate(arrived):
        base = (halo, near, tile + halo - near)[index % 3]
        whose = core if index < 3 else 1 - core
        for step in range(group):
            row = base + jnp.bitwise_xor(unit, step) * rows_in
            start_ref[pl.ds(whose * frames_in, frames_in), pl.ds(row, rows_in)] = ref[
                step, :, :, columns_at, :
            ]
    for frame in range(frames):
        keep(0, frame, start_ref[frame].reshape(high * width, chans).astype(F32), 0)

    for block in range(blocks):
        first, last = block + 1, high - block - 1
        count = last - first
        spatial = rows_of(w_ref, block, 0, 9)
        mask = mask_ref[first:last].reshape(count * width, chans)
        for frame in range(frames):
            taps = jnp.concatenate(
                [
                    x_ref[frame, first - 1 + ky : last - 1 + ky].reshape(count * width, 3 * chans)
                    for ky in range(3)
                ],
                1,
            )
            before = jnp.dot(taps, spatial, preferred_element_type=F32)
            sigma = 1.0 / (1.0 + jnp.exp(-before))
            hidden = before * sigma * mask
            slope = (sigma * (1.0 + before * (1.0 - sigma))) * mask
            h_ref[frame, first:last] = hidden.astype(BF16).reshape(count, width, chans)
            ho_ref[block, frame] = hidden.reshape(count, width, chans)[
                own_rows[0] - first : own_rows[1] - first, own_cols[0] : own_cols[1]
            ].astype(BF16)
            rim = block + 1
            d_refs[block][frame] = slope.reshape(count, width, chans)[
                own_rows[0] - rim - first : own_rows[1] + rim - first
            ]
        if block + 1 == blocks:
            break
        for frame in range(frames):
            offsets = [kt for kt in range(3) if frame + kt - 2 >= 0]
            timeline = jnp.concatenate(
                [
                    h_ref[frame + kt - 2, first:last].reshape(count * width, chans)
                    for kt in offsets
                ],
                1,
            )
            mixed = jnp.dot(
                timeline, rows_of(w_ref, block, 9 + offsets[0], 12), preferred_element_type=F32
            )
            old = x_ref[frame, first:last, :, chans : 2 * chans].astype(F32)
            new = old.reshape(count * width, chans) + mixed
            keep(block + 1, frame, new.astype(BF16).astype(F32), first)


def backward_kernel(geometry, factor, *rest):
    blocks, cores, group, frames_in, rows_in, halo, tile, width, height, columns = geometry
    core, section, band, unit = placed(group)
    shared, rest = rest[: 2 * blocks - 1], rest[2 * blocks - 1 :]
    arrived, rest = rest[:group], rest[group:]
    xo_ref, ho_ref = rest[:2]
    d_refs = rest[2 : 2 + blocks]
    keep_ref, give_ref, mine_out, other_out = rest[2 + blocks : 6 + blocks]
    g_ref, da_ref, dao_ref, go_ref, w_ref, grad_ref, out_ref = rest[6 + blocks :]
    place_kernels(core, section, w_ref, shared[0], shared[1:blocks], shared[blocks:])
    frames = cores * frames_in
    chans = w_ref.shape[-1]
    rim = blocks
    own_cols = (halo, width - halo)
    per_core = w_ref.shape[2]
    pixels = tile * (own_cols[1] - own_cols[0])

    half = group // 2
    for step, ref in enumerate(arrived):
        at = jnp.bitwise_xor(unit, step)
        g_ref[:, pl.ds(rim + at * rows_in, rows_in)] = ref[0]
        beyond = jnp.where(at < half, rim + tile + at * rows_in, (at - half) * rows_in)
        g_ref[:, pl.ds(beyond, rows_in)] = ref[1]

    def put(block, tap, value):
        slot = jnp.where(core == tap // per_core, 0, 1)
        where = jnp.bitwise_xor(section, block)
        grad_ref[slot, where, tap % per_core] = (value * factor).astype(BF16)

    for block in reversed(range(blocks)):
        edge = block + 1
        first, last = rim - edge, rim + tile + edge
        count = last - first
        for frame in range(frames):
            go_ref[frame] = g_ref[frame, rim : rim + tile].astype(F32)[
                :, own_cols[0] : own_cols[1]
            ].astype(BF16)
            offsets = [kt for kt in (2, 1, 0) if frame + 2 - kt < frames]
            ahead = jnp.concatenate(
                [
                    g_ref[frame + 2 - kt, first:last].reshape(count * width, chans)
                    for kt in offsets
                ],
                1,
            )
            hidden = dot_t(ahead, lanes_of(w_ref, block, [9 + kt for kt in offsets]))
            slope = d_refs[block][frame].reshape(count * width, chans)
            value = (hidden * slope).astype(BF16).astype(F32)
            triple = [rolled(value, -1), value, rolled(value, 1)]
            both = jnp.concatenate([part.astype(BF16) for part in triple], 1)
            da_ref[frame, first:last] = both.reshape(count, width, 3 * chans)
            dao_ref[frame] = value.reshape(count, width, chans)[
                edge : edge + tile, own_cols[0] : own_cols[1]
            ].astype(BF16)
        for frame in range(frames):
            inner = count - 2
            taps = jnp.concatenate(
                [
                    da_ref[frame, first + 2 - ky : first + 2 - ky + inner].reshape(
                        inner * width, 3 * chans
                    )
                    for ky in range(3)
                ],
                1,
            )
            back = dot_t(taps, lanes_of(w_ref, block, range(9)))
            old = g_ref[frame, first + 1 : last - 1].astype(F32).reshape(inner * width, chans)
            new = (old + back).astype(BF16)
            if block:
                g_ref[frame, first + 1 : last - 1] = new.reshape(inner, width, chans)
            else:
                cut = new.astype(F32).reshape(inner, width, chans)[:, own_cols[0] : own_cols[1]]
                out_ref[frame] = cut.astype(BF16)
        slopes = dao_ref[...].reshape(frames * pixels, chans)
        for ky in range(3):
            taps = xo_ref[block, :, ky : ky + tile].reshape(frames * pixels, 3 * chans)
            sums = dot_first(slopes, taps)
            for kx in range(3):
                put(block, 3 * ky + kx, sums[:, kx * chans : (kx + 1) * chans])
        for kt in range(3):
            skip = 2 - kt
            later = go_ref[skip:].reshape((frames - skip) * pixels, chans)
            earlier = ho_ref[block, : frames - skip].reshape((frames - skip) * pixels, chans)
            put(block, 9 + kt, dot_first(later, earlier))
    keep_ref[...] = grad_ref[0]
    give_ref[...] = grad_ref[1]
    for whose, target in ((core, mine_out), (1 - core, other_out)):
        for step in range(group):
            row = jnp.bitwise_xor(unit, step) * rows_in
            target[step] = out_ref[pl.ds(whose * frames_in, frames_in), pl.ds(row, rows_in)]


def swapped(value, axis="tm", step=1):
    count = lax.axis_size(axis)
    return lax.ppermute(value, axis, [(i, i ^ step) for i in range(count)])


def on_device(video, cotangent, spatial_weights, temporal_weights):
    blocks, cores, tiles = (lax.axis_size(name) for name in ("section", "tm", "space"))
    frames_in, rows_in, columns, chans = video.shape
    halo = 2 * blocks
    tile = halo
    group = tile // rows_in
    parties = cores * group
    own_width = columns // parties
    width = own_width + 2 * halo
    span = cores * own_width + 2 * halo
    vmem = pl.BlockSpec(memory_space=pltpu.VMEM)
    params = pltpu.CompilerParams(vmem_limit_bytes=32 * 2**20)

    bands = blocks * tiles // group
    core, section, band, unit = placed(group)

    def traded(value, shift):
        pairs = []
        for one in range(bands):
            other = ((one + shift) ^ 1) - shift
            if 0 <= other < bands:
                pairs += [(one * group + i, other * group + i) for i in range(group)]
        return lax.ppermute(value, ("section", "space"), pairs)

    total_rows = blocks * tiles * rows_in
    half = group // 2
    passed = []
    for one in range(bands - 1):
        for i in range(group):
            low, high = one * group + i, (one + 1) * group + i
            passed.append((high, low) if i < half else (low, high))
    cot_halo = lax.ppermute(cotangent, ("section", "space"), passed)

    padded = columns + 2 * halo
    cuts = pl.pallas_call(
        functools.partial(window_kernel, halo, span),
        name="windows",
        in_specs=[vmem],
        out_specs=[vmem] * group,
        out_shape=[jax.ShapeDtypeStruct((frames_in, rows_in, span, chans), BF16)] * group,
        scratch_shapes=[pltpu.VMEM((frames_in, rows_in, padded, chans), F32)],
        compiler_params=params,
    )(video)
    *cuts, spatial, temporal = lax.optimization_barrier(
        list(cuts) + [spatial_weights, temporal_weights]
    )
    count = spatial_weights.shape[1]
    taps = (count + temporal_weights.shape[1]) // cores
    one_half = jax.ShapeDtypeStruct((taps, chans, chans), BF16)
    half_kernels, own_kernels = pl.pallas_call(
        halves_kernel,
        name="halves",
        in_specs=[vmem] * 2,
        out_specs=[vmem] * 2,
        out_shape=[one_half, jax.ShapeDtypeStruct((cores,) + one_half.shape, BF16)],
        scratch_shapes=[pltpu.VMEM((cores * taps, chans, chans), BF16)],
        compiler_params=params,
    )(spatial, temporal)

    def gathered(pieces):
        return jnp.stack([pieces[0]] + [swapped(pieces[i], "space", i) for i in range(1, group)])

    along_x = swapped(half_kernels, "section", 1)
    along_y = swapped(half_kernels, "section", 2)
    own_video, along_x, along_y = lax.optimization_barrier([gathered(cuts), along_x, along_y])
    near, far = traded(own_video, 0), traded(own_video, 1)
    mine = [along_x, along_y, swapped(along_x, "section", 2)]
    shared = mine + [swapped(each) for each in mine]
    shared = [own_kernels] + shared

    cuts = pl.pallas_call(
        functools.partial(cotangent_kernel, halo, width),
        name="cotangent",
        in_specs=[vmem] * 4,
        out_specs=[vmem] * group,
        out_shape=[jax.ShapeDtypeStruct((2, cores * frames_in, rows_in, width, chans), BF16)] * group,
        scratch_shapes=[pltpu.VMEM((2, cores * frames_in, rows_in, padded, chans), F32)],
        compiler_params=params,
    )(cotangent, swapped(cotangent), cot_halo, swapped(cot_halo))
    near, *cuts = lax.optimization_barrier([near] + list(cuts))
    videos = [own_video, near, far]
    videos += [swapped(each) for each in videos]
    cots = [cuts[0]] + [swapped(cuts[i], "space", i) for i in range(1, group)]

    geometry = (blocks, cores, group, frames_in, rows_in, halo, tile, width, total_rows, columns)
    frames = cores * frames_in
    high = tile + 2 * halo
    per_section = (blocks,) + one_half.shape
    all_kernels = (cores,) + per_section
    saved = [
        jax.ShapeDtypeStruct((frames, tile + 2 * block + 2, width, chans), F32)
        for block in range(blocks)
    ]
    cost = pl.CostEstimate(flops=6 * 10**9, bytes_accessed=8 * 10**6, transcendentals=10**6)
    features, hidden, *slopes = pl.pallas_call(
        functools.partial(forward_kernel, geometry),
        name="forward",
        in_specs=[vmem] * (2 * blocks + 5),
        out_specs=[vmem] * (2 + blocks),
        out_shape=[
            jax.ShapeDtypeStruct((blocks, frames, tile + 2, own_width, 3 * chans), BF16),
            jax.ShapeDtypeStruct((blocks, frames, tile, own_width, chans), BF16),
        ]
        + saved,
        scratch_shapes=[
            pltpu.VMEM((frames, high, width, 3 * chans), BF16),
            pltpu.VMEM((frames, high, width, chans), BF16),
            pltpu.VMEM((high, width, chans), F32),
            pltpu.VMEM(all_kernels, BF16),
            pltpu.VMEM((frames, high, width, chans), BF16),
        ],
        compiler_params=params,
        cost_estimate=cost,
    )(*shared, *videos)

    back = jax.ShapeDtypeStruct((group, frames_in, rows_in, own_width, chans), BF16)
    pixel_count = frames * total_rows * columns
    factor = 1.0 / float(pixel_count) ** 0.5
    keep, give, mine_grad, other_grad = pl.pallas_call(
        functools.partial(backward_kernel, geometry, factor),
        name="backward",
        in_specs=[vmem] * (3 * blocks + group + 1),
        out_specs=[vmem] * 4,
        out_shape=[
            jax.ShapeDtypeStruct(per_section, BF16),
            jax.ShapeDtypeStruct(per_section, BF16),
            back,
            back,
        ],
        scratch_shapes=[
            pltpu.VMEM((frames, tile + 2 * blocks, width, chans), BF16),
            pltpu.VMEM((frames, tile + 2 * blocks, width, 3 * chans), BF16),
            pltpu.VMEM((frames, tile, own_width, chans), BF16),
            pltpu.VMEM((frames, tile, own_width, chans), BF16),
            pltpu.VMEM(all_kernels, BF16),
            pltpu.VMEM(all_kernels, BF16),
            pltpu.VMEM((frames, tile, own_width, chans), BF16),
        ],
        compiler_params=params,
        cost_estimate=cost,
    )(*shared, *cots, features, hidden, *slopes)

    got = swapped(give)
    shares = 2
    many = taps // shares
    parts = [
        [
            (keep[i, at : at + many].astype(F32) + got[i, at : at + many].astype(F32)).astype(BF16)
            for i in range(blocks)
        ]
        for at in range(0, taps, many)
    ]
    other_grad, *parts = lax.optimization_barrier([other_grad] + parts)
    parts = [
        part[:1] + [swapped(part[i], "section", i) for i in range(1, blocks)] for part in parts
    ]
    other_grad = swapped(other_grad)
    first = core == 0
    wide = jnp.concatenate(
        [jnp.where(first, mine_grad, other_grad), jnp.where(first, other_grad, mine_grad)], 3
    )

    def along_z(part):
        part = sum(each.astype(F32) for each in part).astype(BF16)
        halves = part.reshape(2, -1, chans)
        low = unit % 2

        def picked(which):
            return lax.dynamic_index_in_dim(halves, which, 0, keepdims=False)

        part = picked(low).astype(F32) + swapped(picked(1 - low), "space", 1).astype(F32)
        return part.astype(BF16)

    def whole_z(part):
        part = part.astype(F32) + swapped(part, "space", 2).astype(F32)
        if tiles != group:
            sets = [list(range(i, tiles, group)) for i in range(group)]
            part = lax.psum(part, "space", axis_index_groups=sets)
        return part.astype(BF16)

    def gathered_pair(part):
        pair = jnp.stack([part, swapped(part, "space", 1)])
        return [pair, swapped(pair)]

    early = along_z(parts[0])
    early, *parts[1] = lax.optimization_barrier([early] + parts[1])
    early = whole_z(early)
    early, wide = lax.optimization_barrier([early, wide])
    strips = [wide[0]] + [swapped(wide[i], "space", i) for i in range(1, group)]
    pairs = gathered_pair(early) + gathered_pair(whole_z(along_z(parts[1])))
    spatial_out, temporal_out = pl.pallas_call(
        functools.partial(closing_kernel, group),
        name="closing",
        in_specs=[vmem] * len(pairs),
        out_specs=[vmem] * 2,
        out_shape=[
            jax.ShapeDtypeStruct(spatial_weights.shape, F32),
            jax.ShapeDtypeStruct(temporal_weights.shape, F32),
        ],
        scratch_shapes=[pltpu.VMEM((cores * taps * chans, chans), BF16)],
        compiler_params=params,
    )(*pairs)

    grad_video = jnp.zeros(video.shape, BF16)
    for step, strip in enumerate(strips):
        grad_video = lax.dynamic_update_slice(
            grad_video, strip, (0, 0, (unit ^ step) * cores * own_width, 0)
        )
    return spatial_out, temporal_out, grad_video


def solution(mesh):
    return jax.shard_map(
        on_device,
        mesh=mesh,
        in_specs=(
            P("tm", ("section", "space"), None, None),
            P("tm", ("section", "space"), None, None),
            P("section", None, None, None),
            P("section", None, None, None),
        ),
        out_specs=(
            P("section", None, None, None),
            P("section", None, None, None),
            P("tm", ("section", "space"), None, None),
        ),
        check_vma=False,
    )
```

```python
import functools

import jax
import jax.numpy as jnp
from jax import lax
from jax.experimental import pallas as pl
from jax.experimental.pallas import tpu as pltpu
from jax.sharding import PartitionSpec as P

F32 = jnp.float32
BF16 = jnp.bfloat16


def rolled(value, steps):
    return pltpu.roll(value, steps % value.shape[0], 0)


def dot_t(left, right):
    return lax.dot_general(left, right, (((1,), (1,)), ((), ())), preferred_element_type=F32)


def dot_first(left, right):
    return lax.dot_general(left, right, (((0,), (0,)), ((), ())), preferred_element_type=F32)


def kernel_of(w_ref, block, tap):
    taps = w_ref.shape[2]
    return w_ref[tap // taps, block, tap % taps]


def rows_of(w_ref, block, first, last):
    return jnp.concatenate([kernel_of(w_ref, block, tap) for tap in range(first, last)], 0)


def lanes_of(w_ref, block, order):
    return jnp.concatenate([kernel_of(w_ref, block, tap) for tap in order], 1)


def placed(group):
    place, section = lax.axis_index("space"), lax.axis_index("section")
    band = (section * lax.axis_size("space") + place) // group
    return lax.axis_index("tm"), section, band, place % group


def window_kernel(halo, span, video_ref, *rest):
    targets, wide_ref = rest[:-1], rest[-1]
    unit = placed(len(targets))[3]
    frames, rows, columns, chans = video_ref.shape
    edge = jnp.zeros((frames, rows, halo, chans), F32)
    wide_ref[:, :, :halo] = edge
    wide_ref[:, :, halo + columns :] = edge
    wide_ref[:, :, halo : halo + columns] = video_ref[...].astype(F32)
    for step, target in enumerate(targets):
        at = jnp.bitwise_xor(unit, step) * (span - 2 * halo)
        target[...] = wide_ref[:, :, pl.ds(pl.multiple_of(at, 16), span)].astype(BF16)


def cotangent_kernel(halo, width, mine_ref, other_ref, *rest):
    targets, wide_ref = rest[:-1], rest[-1]
    count = targets[0].shape[0]
    core, _, _, unit = placed(count * len(targets))
    frames_in, rows, columns, chans = mine_ref.shape
    edge = jnp.zeros((2 * frames_in, rows, halo, chans), F32)
    wide_ref[:, :, :halo] = edge
    wide_ref[:, :, halo + columns :] = edge
    for whose, ref in ((core, mine_ref), (1 - core, other_ref)):
        wide_ref[pl.ds(whose * frames_in, frames_in), :, halo : halo + columns] = ref[...].astype(F32)
    own = width - 2 * halo
    for index, target in enumerate(targets):
        for step in range(count):
            at = (jnp.bitwise_xor(unit, index * count + step) * 2 + core) * own
            at = pl.ds(pl.multiple_of(at, 16), width)
            target[step] = wide_ref[:, :, at].astype(BF16)


def closing_kernel(group, mine_ref, other_ref, spatial_ref, temporal_ref, flat_ref):
    pieces, rows, chans = mine_ref.shape
    core, _, _, unit = placed(group)
    for whose, ref in ((core, mine_ref), (1 - core, other_ref)):
        for step in range(pieces):
            index = whose * pieces + jnp.bitwise_xor(jnp.bitwise_and(unit, pieces - 1), step)
            flat_ref[pl.ds(pl.multiple_of(index * rows, 16), rows)] = ref[step]
    count = spatial_ref.shape[1]
    for tap in range(count + temporal_ref.shape[1]):
        turned = flat_ref[tap * chans : (tap + 1) * chans].astype(F32).T
        if tap < count:
            spatial_ref[0, tap] = turned
        else:
            temporal_ref[0, tap - count] = turned


def place_kernels(core, section, w_ref, own_mine, own_other, mine_refs, other_refs):
    w_ref[core, section] = own_mine[...]
    w_ref[1 - core, section] = own_other[...]
    for step, (mine_ref, other_ref) in enumerate(zip(mine_refs, other_refs)):
        block = jnp.bitwise_xor(section, step + 1)
        w_ref[core, block] = mine_ref[...]
        w_ref[1 - core, block] = other_ref[...]


def forward_kernel(geometry, *rest):
    blocks, cores, group, frames_in, rows_in, halo, tile, width, height, columns = geometry
    core, section, band, unit = placed(group)
    odd = band % 2
    shared, rest = rest[: 2 * blocks], rest[2 * blocks :]
    arrived, rest = rest[:6], rest[6:]
    xo_ref, ho_ref = rest[:2]
    d_refs = rest[2 : 2 + blocks]
    x_ref, h_ref, mask_ref, w_ref, start_ref = rest[2 + blocks :]
    place_kernels(core, section, w_ref, *shared[:2], shared[2 : 1 + blocks], shared[1 + blocks :])
    frames = cores * frames_in
    high = tile + 2 * halo
    chans = w_ref.shape[-1]
    own_rows, own_cols = (halo, halo + tile), (halo, width - halo)
    row = band * tile - halo + lax.broadcasted_iota(jnp.int32, (high, width, chans), 0)
    left = (unit * cores + core) * (width - 2 * halo) - halo
    col = left + lax.broadcasted_iota(jnp.int32, (high, width, chans), 1)
    inside = (row >= 0) & (row < height) & (col >= 0) & (col < columns)
    mask_ref[...] = jnp.where(inside, 1.0, 0.0).astype(F32)

    def keep(block, frame, value, first):
        triple = [rolled(value, 1), value, rolled(value, -1)]
        count = value.shape[0] // width
        both = jnp.concatenate([part.astype(BF16) for part in triple], 1)
        x_ref[frame, first : first + count] = both.reshape(count, width, 3 * chans)
        start = own_rows[0] - 1 - first
        cut = [
            part.reshape(count, width, chans)[
                start : start + tile + 2, own_cols[0] : own_cols[1]
            ].astype(BF16)
            for part in triple
        ]
        xo_ref[block, frame] = jnp.concatenate(cut, 2)

    near = tile + halo - odd * (tile + halo)
    columns_at = pl.ds(pl.multiple_of(core * (width - 2 * halo), 16), width)
    for index, ref in enumerate(arrived):
        base = (halo, near, tile + halo - near)[index % 3]
        whose = core if index < 3 else 1 - core
        for step in range(group):
            row = base + jnp.bitwise_xor(unit, step) * rows_in
            start_ref[pl.ds(whose * frames_in, frames_in), pl.ds(row, rows_in)] = ref[
                step, :, :, columns_at, :
            ]
    for frame in range(frames):
        keep(0, frame, start_ref[frame].reshape(high * width, chans).astype(F32), 0)

    for block in range(blocks):
        first, last = block + 1, high - block - 1
        count = last - first
        spatial = rows_of(w_ref, block, 0, 9)
        mask = mask_ref[first:last].reshape(count * width, chans)
        for frame in range(frames):
            taps = jnp.concatenate(
                [
                    x_ref[frame, first - 1 + ky : last - 1 + ky].reshape(count * width, 3 * chans)
                    for ky in range(3)
                ],
                1,
            )
            before = jnp.dot(taps, spatial, preferred_element_type=F32)
            sigma = 1.0 / (1.0 + jnp.exp(-before))
            hidden = before * sigma * mask
            slope = (sigma * (1.0 + before * (1.0 - sigma))) * mask
            h_ref[frame, first:last] = hidden.astype(BF16).reshape(count, width, chans)
            ho_ref[block, frame] = hidden.reshape(count, width, chans)[
                own_rows[0] - first : own_rows[1] - first, own_cols[0] : own_cols[1]
            ].astype(BF16)
            rim = block + 1
            d_refs[block][frame] = slope.reshape(count, width, chans)[
                own_rows[0] - rim - first : own_rows[1] + rim - first
            ]
        if block + 1 == blocks:
            break
        for frame in range(frames):
            offsets = [kt for kt in range(3) if frame + kt - 2 >= 0]
            timeline = jnp.concatenate(
                [
                    h_ref[frame + kt - 2, first:last].reshape(count * width, chans)
                    for kt in offsets
                ],
                1,
            )
            mixed = jnp.dot(
                timeline, rows_of(w_ref, block, 9 + offsets[0], 12), preferred_element_type=F32
            )
            old = x_ref[frame, first:last, :, chans : 2 * chans].astype(F32)
            new = old.reshape(count * width, chans) + mixed
            keep(block + 1, frame, new.astype(BF16).astype(F32), first)


def backward_kernel(geometry, factor, *rest):
    blocks, cores, group, frames_in, rows_in, halo, tile, width, height, columns = geometry
    core, section, band, unit = placed(group)
    shared, rest = rest[: 2 * blocks], rest[2 * blocks :]
    arrived, rest = rest[:4], rest[4:]
    xo_ref, ho_ref = rest[:2]
    d_refs = rest[2 : 2 + blocks]
    keep_ref, give_ref, mine_out, other_out = rest[2 + blocks : 6 + blocks]
    g_ref, da_ref, dao_ref, go_ref, w_ref, grad_ref, out_ref = rest[6 + blocks :]
    place_kernels(core, section, w_ref, *shared[:2], shared[2 : 1 + blocks], shared[1 + blocks :])
    frames = cores * frames_in
    chans = w_ref.shape[-1]
    rim = blocks
    own_cols = (halo, width - halo)
    per_core = w_ref.shape[2]
    pixels = tile * (own_cols[1] - own_cols[0])

    odd = band % 2
    near = tile + rim - odd * (tile + rim)
    half = group // 2
    for index, (base, ref) in enumerate(zip((rim, rim, near, tile + rim - near), arrived)):
        for step in range(half):
            at = jnp.bitwise_xor(unit, (half if index == 1 else 0) + step)
            at = at if index < 2 else jnp.bitwise_and(at, half - 1)
            g_ref[:, pl.ds(base + at * rows_in, rows_in)] = ref[step]

    def put(block, tap, value):
        slot = jnp.where(core == tap // per_core, 0, 1)
        where = jnp.bitwise_xor(section, block)
        grad_ref[slot, where, tap % per_core] = (value * factor).astype(BF16)

    for block in reversed(range(blocks)):
        edge = block + 1
        first, last = rim - edge, rim + tile + edge
        count = last - first
        for frame in range(frames):
            go_ref[frame] = g_ref[frame, rim : rim + tile].astype(F32)[
                :, own_cols[0] : own_cols[1]
            ].astype(BF16)
            offsets = [kt for kt in (2, 1, 0) if frame + 2 - kt < frames]
            ahead = jnp.concatenate(
                [
                    g_ref[frame + 2 - kt, first:last].reshape(count * width, chans)
                    for kt in offsets
                ],
                1,
            )
            hidden = dot_t(ahead, lanes_of(w_ref, block, [9 + kt for kt in offsets]))
            slope = d_refs[block][frame].reshape(count * width, chans)
            value = (hidden * slope).astype(BF16).astype(F32)
            triple = [rolled(value, -1), value, rolled(value, 1)]
            both = jnp.concatenate([part.astype(BF16) for part in triple], 1)
            da_ref[frame, first:last] = both.reshape(count, width, 3 * chans)
            dao_ref[frame] = value.reshape(count, width, chans)[
                edge : edge + tile, own_cols[0] : own_cols[1]
            ].astype(BF16)
        for frame in range(frames):
            inner = count - 2
            taps = jnp.concatenate(
                [
                    da_ref[frame, first + 2 - ky : first + 2 - ky + inner].reshape(
                        inner * width, 3 * chans
                    )
                    for ky in range(3)
                ],
                1,
            )
            back = dot_t(taps, lanes_of(w_ref, block, range(9)))
            old = g_ref[frame, first + 1 : last - 1].astype(F32).reshape(inner * width, chans)
            new = (old + back).astype(BF16)
            if block:
                g_ref[frame, first + 1 : last - 1] = new.reshape(inner, width, chans)
            else:
                cut = new.astype(F32).reshape(inner, width, chans)[:, own_cols[0] : own_cols[1]]
                out_ref[frame] = cut.astype(BF16)
        slopes = dao_ref[...].reshape(frames * pixels, chans)
        for ky in range(3):
            taps = xo_ref[block, :, ky : ky + tile].reshape(frames * pixels, 3 * chans)
            sums = dot_first(slopes, taps)
            for kx in range(3):
                put(block, 3 * ky + kx, sums[:, kx * chans : (kx + 1) * chans])
        for kt in range(3):
            skip = 2 - kt
            later = go_ref[skip:].reshape((frames - skip) * pixels, chans)
            earlier = ho_ref[block, : frames - skip].reshape((frames - skip) * pixels, chans)
            put(block, 9 + kt, dot_first(later, earlier))
    keep_ref[...] = grad_ref[0]
    give_ref[...] = grad_ref[1]
    for whose, target in ((core, mine_out), (1 - core, other_out)):
        for step in range(group):
            row = jnp.bitwise_xor(unit, step) * rows_in
            target[step] = out_ref[pl.ds(whose * frames_in, frames_in), pl.ds(row, rows_in)]


def swapped(value, axis="tm", step=1):
    count = lax.axis_size(axis)
    return lax.ppermute(value, axis, [(i, i ^ step) for i in range(count)])


def on_device(video, cotangent, spatial_weights, temporal_weights):
    blocks, cores, tiles = (lax.axis_size(name) for name in ("section", "tm", "space"))
    frames_in, rows_in, columns, chans = video.shape
    halo = 2 * blocks
    tile = halo
    group = tile // rows_in
    parties = cores * group
    own_width = columns // parties
    width = own_width + 2 * halo
    span = cores * own_width + 2 * halo
    vmem = pl.BlockSpec(memory_space=pltpu.VMEM)
    params = pltpu.CompilerParams(vmem_limit_bytes=32 * 2**20)

    bands = blocks * tiles // group
    core, section, band, unit = placed(group)
    odd = band % 2

    def traded(value, shift):
        pairs = []
        for one in range(bands):
            other = ((one + shift) ^ 1) - shift
            if 0 <= other < bands:
                pairs += [(one * group + i, other * group + i) for i in range(group)]
        return lax.ppermute(value, ("section", "space"), pairs)

    total_rows = blocks * tiles * rows_in
    half = group // 2
    padded = columns + 2 * halo
    cuts = pl.pallas_call(
        functools.partial(window_kernel, halo, span),
        name="windows",
        in_specs=[vmem],
        out_specs=[vmem] * group,
        out_shape=[jax.ShapeDtypeStruct((frames_in, rows_in, span, chans), BF16)] * group,
        scratch_shapes=[pltpu.VMEM((frames_in, rows_in, padded, chans), F32)],
        compiler_params=params,
    )(video)
    pair = jax.ShapeDtypeStruct((half, cores * frames_in, rows_in, width, chans), BF16)
    low, high_pair = pl.pallas_call(
        functools.partial(cotangent_kernel, halo, width),
        name="cotangent",
        in_specs=[vmem] * 2,
        out_specs=[vmem] * 2,
        out_shape=[pair] * 2,
        scratch_shapes=[pltpu.VMEM((cores * frames_in, rows_in, padded, chans), F32)],
        compiler_params=params,
    )(cotangent, swapped(cotangent))

    def core_half(which, spatial, temporal):
        whole = jnp.concatenate([spatial[0], temporal[0]], 0)
        taps = whole.shape[0] // cores
        return lax.dynamic_slice_in_dim(whole, which * taps, taps, 0)

    half_kernels = core_half(core, spatial_weights, temporal_weights)

    def gathered(pieces):
        return jnp.stack([pieces[0]] + [swapped(pieces[i], "space", i) for i in range(1, group)])

    along_x = swapped(half_kernels, "section", 1)
    along_y = swapped(half_kernels, "section", 2)
    own_video, along_x, along_y, spatial, temporal = lax.optimization_barrier(
        [gathered(cuts), along_x, along_y, spatial_weights, temporal_weights]
    )
    near, far = traded(own_video, 0), traded(own_video, 1)
    mine = [along_x, along_y, swapped(along_x, "section", 2)]
    rest_kernels = core_half(1 - core, spatial, temporal)
    shared = [half_kernels, rest_kernels] + mine + [swapped(each) for each in mine]
    videos = [own_video, near, far]
    videos += [swapped(each) for each in videos]

    from_far = swapped(high_pair, "space", 2)
    from_near = swapped(jnp.stack([low[1], from_far[1]]), "space", 1)
    low = jnp.stack([low[0], from_near[0]])
    high_pair = jnp.stack([from_far[0], from_near[1]])
    upper = unit < half
    cots = [
        low,
        high_pair,
        traded(jnp.where(upper == (odd == 1), low, high_pair), 0),
        traded(jnp.where(upper == (odd == 0), low, high_pair), 1),
    ]

    geometry = (blocks, cores, group, frames_in, rows_in, halo, tile, width, total_rows, columns)
    frames = cores * frames_in
    high = tile + 2 * halo
    per_section = (blocks,) + half_kernels.shape
    taps = half_kernels.shape[0]
    all_kernels = (cores,) + per_section
    saved = [
        jax.ShapeDtypeStruct((frames, tile + 2 * block + 2, width, chans), F32)
        for block in range(blocks)
    ]
    cost = pl.CostEstimate(flops=6 * 10**9, bytes_accessed=8 * 10**6, transcendentals=10**6)
    features, hidden, *slopes = pl.pallas_call(
        functools.partial(forward_kernel, geometry),
        name="forward",
        in_specs=[vmem] * (2 * blocks + 6),
        out_specs=[vmem] * (2 + blocks),
        out_shape=[
            jax.ShapeDtypeStruct((blocks, frames, tile + 2, own_width, 3 * chans), BF16),
            jax.ShapeDtypeStruct((blocks, frames, tile, own_width, chans), BF16),
        ]
        + saved,
        scratch_shapes=[
            pltpu.VMEM((frames, high, width, 3 * chans), BF16),
            pltpu.VMEM((frames, high, width, chans), BF16),
            pltpu.VMEM((high, width, chans), F32),
            pltpu.VMEM(all_kernels, BF16),
            pltpu.VMEM((frames, high, width, chans), BF16),
        ],
        compiler_params=params,
        cost_estimate=cost,
    )(*shared, *videos)

    back = jax.ShapeDtypeStruct((group, frames_in, rows_in, own_width, chans), BF16)
    pixel_count = frames * total_rows * columns
    factor = 1.0 / float(pixel_count) ** 0.5
    keep, give, mine_grad, other_grad = pl.pallas_call(
        functools.partial(backward_kernel, geometry, factor),
        name="backward",
        in_specs=[vmem] * (3 * blocks + 6),
        out_specs=[vmem] * 4,
        out_shape=[
            jax.ShapeDtypeStruct(per_section, BF16),
            jax.ShapeDtypeStruct(per_section, BF16),
            back,
            back,
        ],
        scratch_shapes=[
            pltpu.VMEM((frames, tile + 2 * blocks, width, chans), BF16),
            pltpu.VMEM((frames, tile + 2 * blocks, width, 3 * chans), BF16),
            pltpu.VMEM((frames, tile, own_width, chans), BF16),
            pltpu.VMEM((frames, tile, own_width, chans), BF16),
            pltpu.VMEM(all_kernels, BF16),
            pltpu.VMEM(all_kernels, BF16),
            pltpu.VMEM((frames, tile, own_width, chans), BF16),
        ],
        compiler_params=params,
        cost_estimate=cost,
    )(*shared, *cots, features, hidden, *slopes)

    got = swapped(give)
    parts = [(keep[i].astype(F32) + got[i].astype(F32)).astype(BF16) for i in range(blocks)]
    other_grad, *parts = lax.optimization_barrier([other_grad] + parts)
    parts = parts[:1] + [swapped(parts[i], "section", i) for i in range(1, blocks)]
    other_grad = swapped(other_grad)
    first = core == 0
    wide = jnp.concatenate(
        [jnp.where(first, mine_grad, other_grad), jnp.where(first, other_grad, mine_grad)], 3
    )
    strips = [wide[0]] + [swapped(wide[i], "space", i) for i in range(1, group)]
    received = lax.optimization_barrier(parts + strips)
    parts, strips = received[:blocks], received[blocks:]
    part = sum(each.astype(F32) for each in parts).astype(BF16)

    halves = part.reshape(2, -1, chans)
    low = unit % 2

    def picked(which):
        return lax.dynamic_index_in_dim(halves, which, 0, keepdims=False)

    part = (picked(low).astype(F32) + swapped(picked(1 - low), "space", 1).astype(F32)).astype(BF16)
    part = part.astype(F32) + swapped(part, "space", 2).astype(F32)
    if tiles != group:
        part = lax.psum(
            part, "space", axis_index_groups=[list(range(i, tiles, group)) for i in range(group)]
        )
    part = part.astype(BF16)
    pair = jnp.stack([part, swapped(part, "space", 1)])
    spatial_out, temporal_out = pl.pallas_call(
        functools.partial(closing_kernel, group),
        name="closing",
        in_specs=[vmem] * 2,
        out_specs=[vmem] * 2,
        out_shape=[
            jax.ShapeDtypeStruct(spatial_weights.shape, F32),
            jax.ShapeDtypeStruct(temporal_weights.shape, F32),
        ],
        scratch_shapes=[pltpu.VMEM((cores * taps * chans, chans), BF16)],
        compiler_params=params,
    )(pair, swapped(pair))

    grad_video = jnp.zeros(video.shape, BF16)
    for step, strip in enumerate(strips):
        grad_video = lax.dynamic_update_slice(
            grad_video, strip, (0, 0, (unit ^ step) * cores * own_width, 0)
        )
    return spatial_out, temporal_out, grad_video


def solution(mesh):
    return jax.shard_map(
        on_device,
        mesh=mesh,
        in_specs=(
            P("tm", ("section", "space"), None, None),
            P("tm", ("section", "space"), None, None),
            P("section", None, None, None),
            P("section", None, None, None),
        ),
        out_specs=(
            P("section", None, None, None),
            P("section", None, None, None),
            P("tm", ("section", "space"), None, None),
        ),
        check_vma=False,
    )
```

```python
import functools

import jax
import jax.numpy as jnp
from jax import lax
from jax.experimental import pallas as pl
from jax.experimental.pallas import tpu as pltpu
from jax.sharding import PartitionSpec as P

F32 = jnp.float32
BF16 = jnp.bfloat16


def rolled(value, steps):
    return pltpu.roll(value, steps % value.shape[0], 0)


def dot_t(left, right):
    return lax.dot_general(left, right, (((1,), (1,)), ((), ())), preferred_element_type=F32)


def dot_first(left, right):
    return lax.dot_general(left, right, (((0,), (0,)), ((), ())), preferred_element_type=F32)


def kernel_of(w_ref, block, tap):
    taps = w_ref.shape[2]
    return w_ref[tap // taps, block, tap % taps]


def pair_rows(w_ref, block, pair_ref):
    chans = w_ref.shape[-1]
    for source in range(4):
        for target in range(2):
            ky = source - target
            for kx in range(3):
                at = (3 * source + kx) * chans
                tile = kernel_of(w_ref, block, 3 * ky + kx) if 0 <= ky < 3 else jnp.zeros((chans, chans), BF16)
                pair_ref[at : at + chans, target * chans : (target + 1) * chans] = tile


def pair_rows_back(w_ref, block, pair_ref):
    chans = w_ref.shape[-1]
    for source in range(4):
        for target in range(2):
            ky = 2 + target - source
            for kx in range(3):
                at = (3 * source + kx) * chans
                tile = kernel_of(w_ref, block, 3 * ky + kx) if 0 <= ky < 3 else jnp.zeros((chans, chans), BF16)
                pair_ref[target * chans : (target + 1) * chans, at : at + chans] = tile


def pair_frames(w_ref, block, first, count):
    chans = w_ref.shape[-1]
    columns = []
    for target in (count - 2, count - 1):
        tiles = []
        for source in range(count):
            kt = source - target + 2
            tiles.append(kernel_of(w_ref, block, 9 + kt) if 0 <= kt < 3 else jnp.zeros((chans, chans), BF16))
        columns.append(jnp.concatenate(tiles, 0))
    return jnp.concatenate(columns, 1)


def pair_frames_back(w_ref, block, count):
    chans = w_ref.shape[-1]
    rows = []
    for target in range(2):
        tiles = []
        for source in range(count):
            kt = 2 - (source - target)
            tiles.append(kernel_of(w_ref, block, 9 + kt) if 0 <= kt < 3 else jnp.zeros((chans, chans), BF16))
        rows.append(jnp.concatenate(tiles, 1))
    return jnp.concatenate(rows, 0)


def row_pairs(ref, frame, first, pairs):
    width, lanes = ref.shape[2:]
    rows = []
    for start in (first, first + 2):
        value = ref[frame, start : start + 2 * pairs].reshape(pairs, 2, width, lanes)
        rows += [value[:, 0], value[:, 1]]
    return jnp.concatenate(rows, 2).reshape(pairs * width, 4 * lanes)


def woven(value, width):
    chans = value.shape[1] // 2
    split = [value[:, i * chans : (i + 1) * chans].reshape(-1, 1, width, chans) for i in range(2)]
    return jnp.concatenate(split, 1).reshape(-1, chans)


def placed(group):
    place, section = lax.axis_index("space"), lax.axis_index("section")
    band = (section * lax.axis_size("space") + place) // group
    return lax.axis_index("tm"), section, band, place % group


def window_kernel(halo, span, video_ref, *rest):
    targets, wide_ref = rest[:-1], rest[-1]
    unit = placed(len(targets))[3]
    frames, rows, columns, chans = video_ref.shape
    edge = jnp.zeros((frames, rows, halo, chans), F32)
    wide_ref[:, :, :halo] = edge
    wide_ref[:, :, halo + columns :] = edge
    wide_ref[:, :, halo : halo + columns] = video_ref[...].astype(F32)
    for step, target in enumerate(targets):
        at = jnp.bitwise_xor(unit, step) * (span - 2 * halo)
        target[...] = wide_ref[:, :, pl.ds(pl.multiple_of(at, 16), span)].astype(BF16)


def cotangent_kernel(halo, width, mine_ref, other_ref, *rest):
    targets, wide_ref = rest[:-1], rest[-1]
    count = targets[0].shape[0]
    core, _, _, unit = placed(count * len(targets))
    frames_in, rows, columns, chans = mine_ref.shape
    edge = jnp.zeros((2 * frames_in, rows, halo, chans), F32)
    wide_ref[:, :, :halo] = edge
    wide_ref[:, :, halo + columns :] = edge
    for whose, ref in ((core, mine_ref), (1 - core, other_ref)):
        wide_ref[pl.ds(whose * frames_in, frames_in), :, halo : halo + columns] = ref[...].astype(F32)
    own = width - 2 * halo
    for index, target in enumerate(targets):
        for step in range(count):
            at = (jnp.bitwise_xor(unit, index * count + step) * 2 + core) * own
            at = pl.ds(pl.multiple_of(at, 16), width)
            target[step] = wide_ref[:, :, at].astype(BF16)


def closing_kernel(group, mine_ref, other_ref, spatial_ref, temporal_ref, flat_ref):
    pieces, rows, chans = mine_ref.shape
    core, _, _, unit = placed(group)
    for whose, ref in ((core, mine_ref), (1 - core, other_ref)):
        for step in range(pieces):
            index = whose * pieces + jnp.bitwise_xor(jnp.bitwise_and(unit, pieces - 1), step)
            flat_ref[pl.ds(pl.multiple_of(index * rows, 16), rows)] = ref[step]
    count = spatial_ref.shape[1]
    for tap in range(count + temporal_ref.shape[1]):
        turned = flat_ref[tap * chans : (tap + 1) * chans].astype(F32).T
        if tap < count:
            spatial_ref[0, tap] = turned
        else:
            temporal_ref[0, tap - count] = turned


def place_kernels(core, section, w_ref, own_mine, own_other, mine_refs, other_refs):
    w_ref[core, section] = own_mine[...]
    w_ref[1 - core, section] = own_other[...]
    for step, (mine_ref, other_ref) in enumerate(zip(mine_refs, other_refs)):
        block = jnp.bitwise_xor(section, step + 1)
        w_ref[core, block] = mine_ref[...]
        w_ref[1 - core, block] = other_ref[...]


def forward_kernel(geometry, *rest):
    blocks, cores, group, frames_in, rows_in, halo, tile, width, height, columns = geometry
    core, section, band, unit = placed(group)
    odd = band % 2
    shared, rest = rest[: 2 * blocks], rest[2 * blocks :]
    arrived, rest = rest[:6], rest[6:]
    xo_ref, ho_ref = rest[:2]
    d_refs = rest[2 : 2 + blocks]
    x_ref, h_ref, mask_ref, w_ref, start_ref, pair_ref = rest[2 + blocks :]
    place_kernels(core, section, w_ref, *shared[:2], shared[2 : 1 + blocks], shared[1 + blocks :])
    frames = cores * frames_in
    high = tile + 2 * halo
    chans = w_ref.shape[-1]
    own_rows, own_cols = (halo, halo + tile), (halo, width - halo)
    row = band * tile - halo + lax.broadcasted_iota(jnp.int32, (high, width, chans), 0)
    left = (unit * cores + core) * (width - 2 * halo) - halo
    col = left + lax.broadcasted_iota(jnp.int32, (high, width, chans), 1)
    inside = (row >= 0) & (row < height) & (col >= 0) & (col < columns)
    mask_ref[...] = jnp.where(inside, 1.0, 0.0).astype(F32)

    def keep(block, frame, value, first):
        triple = [rolled(value, 1), value, rolled(value, -1)]
        count = value.shape[0] // width
        both = jnp.concatenate([part.astype(BF16) for part in triple], 1)
        x_ref[frame, first : first + count] = both.reshape(count, width, 3 * chans)
        start = own_rows[0] - 1 - first
        cut = [
            part.reshape(count, width, chans)[
                start : start + tile + 2, own_cols[0] : own_cols[1]
            ].astype(BF16)
            for part in triple
        ]
        xo_ref[block, frame] = jnp.concatenate(cut, 2)

    near = tile + halo - odd * (tile + halo)
    columns_at = pl.ds(pl.multiple_of(core * (width - 2 * halo), 16), width)
    for index, ref in enumerate(arrived):
        base = (halo, near, tile + halo - near)[index % 3]
        whose = core if index < 3 else 1 - core
        for step in range(group):
            row = base + jnp.bitwise_xor(unit, step) * rows_in
            start_ref[pl.ds(whose * frames_in, frames_in), pl.ds(row, rows_in)] = ref[
                step, :, :, columns_at, :
            ]
    for frame in range(frames):
        keep(0, frame, start_ref[frame].reshape(high * width, chans).astype(F32), 0)

    for block in range(blocks):
        first, last = block + 1, high - block - 1
        count = last - first
        pair_rows(w_ref, block, pair_ref)
        mask = mask_ref[first:last].reshape(count * width, chans)
        for frame in range(frames):
            taps = row_pairs(x_ref, frame, first - 1, count // 2)
            before = jnp.dot(taps, pair_ref[...], preferred_element_type=F32)
            before = woven(before, width)
            sigma = 1.0 / (1.0 + jnp.exp(-before))
            hidden = before * sigma * mask
            slope = (sigma * (1.0 + before * (1.0 - sigma))) * mask
            h_ref[frame, first:last] = hidden.astype(BF16).reshape(count, width, chans)
            ho_ref[block, frame] = hidden.reshape(count, width, chans)[
                own_rows[0] - first : own_rows[1] - first, own_cols[0] : own_cols[1]
            ].astype(BF16)
            rim = block + 1
            d_refs[block][frame] = slope.reshape(count, width, chans)[
                own_rows[0] - rim - first : own_rows[1] + rim - first
            ]
        if block + 1 == blocks:
            break
        for frame in range(0, frames, 2):
            start = max(frame - 2, 0)
            timeline = jnp.concatenate(
                [
                    h_ref[each, first:last].reshape(count * width, chans)
                    for each in range(start, frame + 2)
                ],
                1,
            )
            weights = pair_frames(w_ref, block, start, frame + 2 - start)
            both = jnp.dot(timeline, weights, preferred_element_type=F32)
            for inner in range(2):
                mixed = both[:, inner * chans : (inner + 1) * chans]
                old = x_ref[frame + inner, first:last, :, chans : 2 * chans].astype(F32)
                new = old.reshape(count * width, chans) + mixed
                keep(block + 1, frame + inner, new.astype(BF16).astype(F32), first)


def backward_kernel(geometry, factor, *rest):
    blocks, cores, group, frames_in, rows_in, halo, tile, width, height, columns = geometry
    core, section, band, unit = placed(group)
    shared, rest = rest[: 2 * blocks], rest[2 * blocks :]
    arrived, rest = rest[:4], rest[4:]
    xo_ref, ho_ref = rest[:2]
    d_refs = rest[2 : 2 + blocks]
    keep_ref, give_ref, mine_out, other_out = rest[2 + blocks : 6 + blocks]
    g_ref, da_ref, dao_ref, go_ref, w_ref, grad_ref, out_ref, pair_ref = rest[6 + blocks :]
    place_kernels(core, section, w_ref, *shared[:2], shared[2 : 1 + blocks], shared[1 + blocks :])
    frames = cores * frames_in
    chans = w_ref.shape[-1]
    rim = blocks
    own_cols = (halo, width - halo)
    per_core = w_ref.shape[2]
    pixels = tile * (own_cols[1] - own_cols[0])

    odd = band % 2
    near = tile + rim - odd * (tile + rim)
    half = group // 2
    for index, (base, ref) in enumerate(zip((rim, rim, near, tile + rim - near), arrived)):
        for step in range(half):
            at = jnp.bitwise_xor(unit, (half if index == 1 else 0) + step)
            at = at if index < 2 else jnp.bitwise_and(at, half - 1)
            g_ref[:, pl.ds(base + at * rows_in, rows_in)] = ref[step]

    def put(block, tap, value):
        slot = jnp.where(core == tap // per_core, 0, 1)
        where = jnp.bitwise_xor(section, block)
        grad_ref[slot, where, tap % per_core] = (value * factor).astype(BF16)

    for block in reversed(range(blocks)):
        edge = block + 1
        first, last = rim - edge, rim + tile + edge
        count = last - first
        for frame in range(frames):
            go_ref[frame] = g_ref[frame, rim : rim + tile].astype(F32)[
                :, own_cols[0] : own_cols[1]
            ].astype(BF16)
        pair_rows_back(w_ref, block, pair_ref)
        hiddens = []
        for frame in range(0, frames, 2):
            stop = min(frame + 4, frames)
            ahead = jnp.concatenate(
                [
                    g_ref[each, first:last].reshape(count * width, chans)
                    for each in range(frame, stop)
                ],
                1,
            )
            both = dot_t(ahead, pair_frames_back(w_ref, block, stop - frame))
            hiddens += [both[:, :chans], both[:, chans:]]
        for frame in range(frames):
            hidden = hiddens[frame]
            slope = d_refs[block][frame].reshape(count * width, chans)
            value = (hidden * slope).astype(BF16).astype(F32)
            triple = [rolled(value, -1), value, rolled(value, 1)]
            both = jnp.concatenate([part.astype(BF16) for part in triple], 1)
            da_ref[frame, first:last] = both.reshape(count, width, 3 * chans)
            dao_ref[frame] = value.reshape(count, width, chans)[
                edge : edge + tile, own_cols[0] : own_cols[1]
            ].astype(BF16)
        for frame in range(frames):
            inner = count - 2
            taps = row_pairs(da_ref, frame, first, inner // 2)
            back = woven(dot_t(taps, pair_ref[...]), width)
            old = g_ref[frame, first + 1 : last - 1].astype(F32).reshape(inner * width, chans)
            new = (old + back).astype(BF16)
            if block:
                g_ref[frame, first + 1 : last - 1] = new.reshape(inner, width, chans)
            else:
                cut = new.astype(F32).reshape(inner, width, chans)[:, own_cols[0] : own_cols[1]]
                out_ref[frame] = cut.astype(BF16)
        slopes = dao_ref[...].reshape(frames * pixels, chans)
        for ky in range(3):
            taps = xo_ref[block, :, ky : ky + tile].reshape(frames * pixels, 3 * chans)
            sums = dot_first(slopes, taps)
            for kx in range(3):
                put(block, 3 * ky + kx, sums[:, kx * chans : (kx + 1) * chans])
        for kt in range(3):
            skip = 2 - kt
            later = go_ref[skip:].reshape((frames - skip) * pixels, chans)
            earlier = ho_ref[block, : frames - skip].reshape((frames - skip) * pixels, chans)
            put(block, 9 + kt, dot_first(later, earlier))
    keep_ref[...] = grad_ref[0]
    give_ref[...] = grad_ref[1]
    for whose, target in ((core, mine_out), (1 - core, other_out)):
        for step in range(group):
            row = jnp.bitwise_xor(unit, step) * rows_in
            target[step] = out_ref[pl.ds(whose * frames_in, frames_in), pl.ds(row, rows_in)]


def swapped(value, axis="tm", step=1):
    count = lax.axis_size(axis)
    return lax.ppermute(value, axis, [(i, i ^ step) for i in range(count)])


def on_device(video, cotangent, spatial_weights, temporal_weights):
    blocks, cores, tiles = (lax.axis_size(name) for name in ("section", "tm", "space"))
    frames_in, rows_in, columns, chans = video.shape
    halo = 2 * blocks
    tile = halo
    group = tile // rows_in
    parties = cores * group
    own_width = columns // parties
    width = own_width + 2 * halo
    span = cores * own_width + 2 * halo
    vmem = pl.BlockSpec(memory_space=pltpu.VMEM)
    params = pltpu.CompilerParams(vmem_limit_bytes=32 * 2**20)

    bands = blocks * tiles // group
    core, section, band, unit = placed(group)
    odd = band % 2

    def traded(value, shift):
        pairs = []
        for one in range(bands):
            other = ((one + shift) ^ 1) - shift
            if 0 <= other < bands:
                pairs += [(one * group + i, other * group + i) for i in range(group)]
        return lax.ppermute(value, ("section", "space"), pairs)

    total_rows = blocks * tiles * rows_in
    half = group // 2
    padded = columns + 2 * halo
    cuts = pl.pallas_call(
        functools.partial(window_kernel, halo, span),
        name="windows",
        in_specs=[vmem],
        out_specs=[vmem] * group,
        out_shape=[jax.ShapeDtypeStruct((frames_in, rows_in, span, chans), BF16)] * group,
        scratch_shapes=[pltpu.VMEM((frames_in, rows_in, padded, chans), F32)],
        compiler_params=params,
    )(video)
    pair = jax.ShapeDtypeStruct((half, cores * frames_in, rows_in, width, chans), BF16)
    low, high_pair = pl.pallas_call(
        functools.partial(cotangent_kernel, halo, width),
        name="cotangent",
        in_specs=[vmem] * 2,
        out_specs=[vmem] * 2,
        out_shape=[pair] * 2,
        scratch_shapes=[pltpu.VMEM((cores * frames_in, rows_in, padded, chans), F32)],
        compiler_params=params,
    )(cotangent, swapped(cotangent))

    def core_half(which, spatial, temporal):
        whole = jnp.concatenate([spatial[0], temporal[0]], 0)
        taps = whole.shape[0] // cores
        return lax.dynamic_slice_in_dim(whole, which * taps, taps, 0)

    _, spatial, temporal = lax.optimization_barrier([cuts[0], spatial_weights, temporal_weights])
    half_kernels = core_half(core, spatial, temporal)

    def gathered(pieces):
        return jnp.stack([pieces[0]] + [swapped(pieces[i], "space", i) for i in range(1, group)])

    along_x = swapped(half_kernels, "section", 1)
    along_y = swapped(half_kernels, "section", 2)
    own_video = gathered(cuts)
    near, far = traded(own_video, 0), traded(own_video, 1)
    _, along_x, along_y, high_pair, spatial, temporal = lax.optimization_barrier(
        [own_video, along_x, along_y, high_pair, spatial_weights, temporal_weights]
    )
    mine = [along_x, along_y, swapped(along_x, "section", 2)]
    rest_kernels = core_half(1 - core, spatial, temporal)
    shared = [half_kernels, rest_kernels] + mine + [swapped(each) for each in mine]
    videos = [own_video, near, far]
    videos += [swapped(each) for each in videos]

    from_far = swapped(high_pair, "space", 2)
    from_near = swapped(jnp.stack([low[1], from_far[1]]), "space", 1)
    low = jnp.stack([low[0], from_near[0]])
    high_pair = jnp.stack([from_far[0], from_near[1]])
    upper = unit < half
    cots = [
        low,
        high_pair,
        traded(jnp.where(upper == (odd == 1), low, high_pair), 0),
        traded(jnp.where(upper == (odd == 0), low, high_pair), 1),
    ]

    geometry = (blocks, cores, group, frames_in, rows_in, halo, tile, width, total_rows, columns)
    frames = cores * frames_in
    high = tile + 2 * halo
    per_section = (blocks,) + half_kernels.shape
    taps = half_kernels.shape[0]
    all_kernels = (cores,) + per_section
    saved = [
        jax.ShapeDtypeStruct((frames, tile + 2 * block + 2, width, chans), F32)
        for block in range(blocks)
    ]
    cost = pl.CostEstimate(flops=6 * 10**9, bytes_accessed=8 * 10**6, transcendentals=10**6)
    features, hidden, *slopes = pl.pallas_call(
        functools.partial(forward_kernel, geometry),
        name="forward",
        in_specs=[vmem] * (2 * blocks + 6),
        out_specs=[vmem] * (2 + blocks),
        out_shape=[
            jax.ShapeDtypeStruct((blocks, frames, tile + 2, own_width, 3 * chans), BF16),
            jax.ShapeDtypeStruct((blocks, frames, tile, own_width, chans), BF16),
        ]
        + saved,
        scratch_shapes=[
            pltpu.VMEM((frames, high, width, 3 * chans), BF16),
            pltpu.VMEM((frames, high, width, chans), BF16),
            pltpu.VMEM((high, width, chans), F32),
            pltpu.VMEM(all_kernels, BF16),
            pltpu.VMEM((frames, high, width, chans), BF16),
            pltpu.VMEM((12 * chans, 2 * chans), BF16),
        ],
        compiler_params=params,
        cost_estimate=cost,
    )(*shared, *videos)

    back = jax.ShapeDtypeStruct((group, frames_in, rows_in, own_width, chans), BF16)
    pixel_count = frames * total_rows * columns
    factor = 1.0 / float(pixel_count) ** 0.5
    keep, give, mine_grad, other_grad = pl.pallas_call(
        functools.partial(backward_kernel, geometry, factor),
        name="backward",
        in_specs=[vmem] * (3 * blocks + 6),
        out_specs=[vmem] * 4,
        out_shape=[
            jax.ShapeDtypeStruct(per_section, BF16),
            jax.ShapeDtypeStruct(per_section, BF16),
            back,
            back,
        ],
        scratch_shapes=[
            pltpu.VMEM((frames, tile + 2 * blocks, width, chans), BF16),
            pltpu.VMEM((frames, tile + 2 * blocks, width, 3 * chans), BF16),
            pltpu.VMEM((frames, tile, own_width, chans), BF16),
            pltpu.VMEM((frames, tile, own_width, chans), BF16),
            pltpu.VMEM(all_kernels, BF16),
            pltpu.VMEM(all_kernels, BF16),
            pltpu.VMEM((frames, tile, own_width, chans), BF16),
            pltpu.VMEM((2 * chans, 12 * chans), BF16),
        ],
        compiler_params=params,
        cost_estimate=cost,
    )(*shared, *cots, features, hidden, *slopes)

    got = swapped(give)
    parts = [(keep[i].astype(F32) + got[i].astype(F32)).astype(BF16) for i in range(blocks)]
    other_grad, *parts = lax.optimization_barrier([other_grad] + parts)
    parts = parts[:1] + [swapped(parts[i], "section", i) for i in range(1, blocks)]
    other_grad = swapped(other_grad)
    first = core == 0
    wide = jnp.concatenate(
        [jnp.where(first, mine_grad, other_grad), jnp.where(first, other_grad, mine_grad)], 3
    )
    strips = [wide[0]] + [swapped(wide[i], "space", i) for i in range(1, group)]
    received = lax.optimization_barrier(parts + strips)
    parts, strips = received[:blocks], received[blocks:]
    part = sum(each.astype(F32) for each in parts).astype(BF16)

    halves = part.reshape(2, -1, chans)
    low = unit % 2

    def picked(which):
        return lax.dynamic_index_in_dim(halves, which, 0, keepdims=False)

    part = (picked(low).astype(F32) + swapped(picked(1 - low), "space", 1).astype(F32)).astype(BF16)
    part = part.astype(F32) + swapped(part, "space", 2).astype(F32)
    if tiles != group:
        part = lax.psum(
            part, "space", axis_index_groups=[list(range(i, tiles, group)) for i in range(group)]
        )
    part = part.astype(BF16)
    pair = jnp.stack([part, swapped(part, "space", 1)])
    spatial_out, temporal_out = pl.pallas_call(
        functools.partial(closing_kernel, group),
        name="closing",
        in_specs=[vmem] * 2,
        out_specs=[vmem] * 2,
        out_shape=[
            jax.ShapeDtypeStruct(spatial_weights.shape, F32),
            jax.ShapeDtypeStruct(temporal_weights.shape, F32),
        ],
        scratch_shapes=[pltpu.VMEM((cores * taps * chans, chans), BF16)],
        compiler_params=params,
    )(pair, swapped(pair))

    grad_video = jnp.zeros(video.shape, BF16)
    for step, strip in enumerate(strips):
        grad_video = lax.dynamic_update_slice(
            grad_video, strip, (0, 0, (unit ^ step) * cores * own_width, 0)
        )
    return spatial_out, temporal_out, grad_video


def solution(mesh):
    return jax.shard_map(
        on_device,
        mesh=mesh,
        in_specs=(
            P("tm", ("section", "space"), None, None),
            P("tm", ("section", "space"), None, None),
            P("section", None, None, None),
            P("section", None, None, None),
        ),
        out_specs=(
            P("section", None, None, None),
            P("section", None, None, None),
            P("tm", ("section", "space"), None, None),
        ),
        check_vma=False,
    )
```

```python
import functools

import jax
import jax.numpy as jnp
from jax import lax
from jax.experimental import pallas as pl
from jax.experimental.pallas import tpu as pltpu
from jax.sharding import PartitionSpec as P

F32 = jnp.float32
BF16 = jnp.bfloat16


def rolled(value, steps):
    return pltpu.roll(value, steps % value.shape[0], 0)


def dot_first(left, right):
    return lax.dot_general(left, right, (((0,), (0,)), ((), ())), preferred_element_type=F32)


def kernel_of(w_ref, block, tap):
    taps = w_ref.shape[2]
    return w_ref[tap // taps, block, tap % taps]


def pair_rows(w_ref, block, pair_ref):
    chans = w_ref.shape[-1]
    for source in range(4):
        for target in range(2):
            ky = source - target
            for kx in range(3):
                at = (3 * source + kx) * chans
                tile = kernel_of(w_ref, block, 3 * ky + kx) if 0 <= ky < 3 else jnp.zeros((chans, chans), BF16)
                pair_ref[at : at + chans, target * chans : (target + 1) * chans] = tile


def turned(w_ref, block, tap):
    return kernel_of(w_ref, block, tap).astype(F32).T.astype(BF16)


def pair_rows_back(w_ref, block, pair_ref):
    chans = w_ref.shape[-1]
    nothing = jnp.zeros((chans, chans), BF16)
    for kx in range(3):
        for ky in range(3):
            tile = turned(w_ref, block, 3 * ky + kx)
            for target in range(2):
                at = (3 * (2 + target - ky) + kx) * chans
                pair_ref[at : at + chans, target * chans : (target + 1) * chans] = tile
        for source, target in ((3, 0), (0, 1)):
            at = (3 * source + kx) * chans
            pair_ref[at : at + chans, target * chans : (target + 1) * chans] = nothing


def pair_frames(w_ref, block, first, count):
    chans = w_ref.shape[-1]
    columns = []
    for target in (count - 2, count - 1):
        tiles = []
        for source in range(count):
            kt = source - target + 2
            tiles.append(kernel_of(w_ref, block, 9 + kt) if 0 <= kt < 3 else jnp.zeros((chans, chans), BF16))
        columns.append(jnp.concatenate(tiles, 0))
    return jnp.concatenate(columns, 1)


def pair_frames_back(w_ref, block, count):
    chans = w_ref.shape[-1]
    tiles = [turned(w_ref, block, 9 + kt) for kt in range(3)]
    columns = []
    for target in range(2):
        column = []
        for source in range(count):
            kt = 2 - (source - target)
            column.append(tiles[kt] if 0 <= kt < 3 else jnp.zeros((chans, chans), BF16))
        columns.append(jnp.concatenate(column, 0))
    return jnp.concatenate(columns, 1)


def row_pairs(ref, frame, first, pairs):
    width, lanes = ref.shape[2:]
    rows = []
    for start in (first, first + 2):
        value = ref[frame, start : start + 2 * pairs].reshape(pairs, 2, width, lanes)
        rows += [value[:, 0], value[:, 1]]
    return jnp.concatenate(rows, 2).reshape(pairs * width, 4 * lanes)


def woven(value, width):
    chans = value.shape[1] // 2
    split = [value[:, i * chans : (i + 1) * chans].reshape(-1, 1, width, chans) for i in range(2)]
    return jnp.concatenate(split, 1).reshape(-1, chans)


def placed(group):
    place, section = lax.axis_index("space"), lax.axis_index("section")
    band = (section * lax.axis_size("space") + place) // group
    return lax.axis_index("tm"), section, band, place % group


def window_kernel(halo, span, video_ref, *rest):
    targets, wide_ref = rest[:-1], rest[-1]
    unit = placed(len(targets))[3]
    frames, rows, columns, chans = video_ref.shape
    edge = jnp.zeros((frames, rows, halo, chans), F32)
    wide_ref[:, :, :halo] = edge
    wide_ref[:, :, halo + columns :] = edge
    wide_ref[:, :, halo : halo + columns] = video_ref[...].astype(F32)
    for step, target in enumerate(targets):
        at = jnp.bitwise_xor(unit, step) * (span - 2 * halo)
        target[...] = wide_ref[:, :, pl.ds(pl.multiple_of(at, 16), span)].astype(BF16)


def cotangent_kernel(halo, width, mine_ref, other_ref, *rest):
    targets, wide_ref = rest[:-1], rest[-1]
    count = targets[0].shape[0]
    core, _, _, unit = placed(count * len(targets))
    frames_in, rows, columns, chans = mine_ref.shape
    edge = jnp.zeros((2 * frames_in, rows, halo, chans), F32)
    wide_ref[:, :, :halo] = edge
    wide_ref[:, :, halo + columns :] = edge
    for whose, ref in ((core, mine_ref), (1 - core, other_ref)):
        wide_ref[pl.ds(whose * frames_in, frames_in), :, halo : halo + columns] = ref[...].astype(F32)
    own = width - 2 * halo
    for index, target in enumerate(targets):
        for step in range(count):
            at = (jnp.bitwise_xor(unit, index * count + step) * 2 + core) * own
            at = pl.ds(pl.multiple_of(at, 16), width)
            target[step] = wide_ref[:, :, at].astype(BF16)


def closing_kernel(group, mine_ref, other_ref, spatial_ref, temporal_ref, flat_ref):
    pieces, rows, chans = mine_ref.shape
    core, _, _, unit = placed(group)
    for whose, ref in ((core, mine_ref), (1 - core, other_ref)):
        for step in range(pieces):
            index = whose * pieces + jnp.bitwise_xor(jnp.bitwise_and(unit, pieces - 1), step)
            flat_ref[pl.ds(pl.multiple_of(index * rows, 16), rows)] = ref[step]
    count = spatial_ref.shape[1]
    for tap in range(count + temporal_ref.shape[1]):
        turned = flat_ref[tap * chans : (tap + 1) * chans].astype(F32).T
        if tap < count:
            spatial_ref[0, tap] = turned
        else:
            temporal_ref[0, tap - count] = turned


def forward_kernel(geometry, *rest):
    blocks, cores, group, frames_in, rows_in, halo, tile, width, height, columns = geometry
    core, section, band, unit = placed(group)
    odd = band % 2
    shared, rest = rest[:2], rest[2:]
    arrived, rest = rest[:6], rest[6:]
    xo_ref, ho_ref = rest[:2]
    d_refs = rest[2 : 2 + blocks]
    x_ref, h_ref, mask_ref, w_ref, start_ref, pair_ref = rest[2 + blocks :]
    w_ref[core] = shared[0][...]
    w_ref[1 - core] = shared[1][...]
    frames = cores * frames_in
    high = tile + 2 * halo
    chans = w_ref.shape[-1]
    own_rows, own_cols = (halo, halo + tile), (halo, width - halo)
    row = band * tile - halo + lax.broadcasted_iota(jnp.int32, (high, width, chans), 0)
    left = (unit * cores + core) * (width - 2 * halo) - halo
    col = left + lax.broadcasted_iota(jnp.int32, (high, width, chans), 1)
    inside = (row >= 0) & (row < height) & (col >= 0) & (col < columns)
    mask_ref[...] = jnp.where(inside, 1.0, 0.0).astype(F32)

    def keep(block, frame, value, first):
        triple = [rolled(value, 1), value, rolled(value, -1)]
        count = value.shape[0] // width
        both = jnp.concatenate([part.astype(BF16) for part in triple], 1)
        x_ref[frame, first : first + count] = both.reshape(count, width, 3 * chans)
        start = own_rows[0] - 1 - first
        cut = [
            part.reshape(count, width, chans)[
                start : start + tile + 2, own_cols[0] : own_cols[1]
            ].astype(BF16)
            for part in triple
        ]
        xo_ref[block, frame] = jnp.concatenate(cut, 2)

    near = tile + halo - odd * (tile + halo)
    columns_at = pl.ds(pl.multiple_of(core * (width - 2 * halo), 16), width)
    for index, ref in enumerate(arrived):
        base = (halo, near, tile + halo - near)[index % 3]
        whose = core if index < 3 else 1 - core
        for step in range(group):
            row = base + jnp.bitwise_xor(unit, step) * rows_in
            start_ref[pl.ds(whose * frames_in, frames_in), pl.ds(row, rows_in)] = ref[
                step, :, :, columns_at, :
            ]
    for frame in range(frames):
        keep(0, frame, start_ref[frame].reshape(high * width, chans).astype(F32), 0)

    for block in range(blocks):
        first, last = block + 1, high - block - 1
        count = last - first
        pair_rows(w_ref, block, pair_ref)
        mask = mask_ref[first:last].reshape(count * width, chans)
        for frame in range(frames):
            taps = row_pairs(x_ref, frame, first - 1, count // 2)
            before = jnp.dot(taps, pair_ref[...], preferred_element_type=F32)
            before = woven(before, width)
            sigma = 1.0 / (1.0 + jnp.exp(-before))
            hidden = before * sigma * mask
            slope = (sigma * (1.0 + before * (1.0 - sigma))) * mask
            h_ref[frame, first:last] = hidden.astype(BF16).reshape(count, width, chans)
            ho_ref[block, frame] = hidden.reshape(count, width, chans)[
                own_rows[0] - first : own_rows[1] - first, own_cols[0] : own_cols[1]
            ].astype(BF16)
            rim = block + 1
            d_refs[block][frame] = slope.reshape(count, width, chans)[
                own_rows[0] - rim - first : own_rows[1] + rim - first
            ]
        if block + 1 == blocks:
            break
        for frame in range(0, frames, 2):
            start = max(frame - 2, 0)
            timeline = jnp.concatenate(
                [
                    h_ref[each, first:last].reshape(count * width, chans)
                    for each in range(start, frame + 2)
                ],
                1,
            )
            weights = pair_frames(w_ref, block, start, frame + 2 - start)
            both = jnp.dot(timeline, weights, preferred_element_type=F32)
            for inner in range(2):
                mixed = both[:, inner * chans : (inner + 1) * chans]
                old = x_ref[frame + inner, first:last, :, chans : 2 * chans].astype(F32)
                new = old.reshape(count * width, chans) + mixed
                keep(block + 1, frame + inner, new.astype(BF16).astype(F32), first)


def backward_kernel(geometry, factor, *rest):
    blocks, cores, group, frames_in, rows_in, halo, tile, width, height, columns = geometry
    core, section, band, unit = placed(group)
    shared, rest = rest[:2], rest[2:]
    arrived, rest = rest[:4], rest[4:]
    xo_ref, ho_ref = rest[:2]
    d_refs = rest[2 : 2 + blocks]
    keep_ref, give_ref, mine_out, other_out = rest[2 + blocks : 6 + blocks]
    g_ref, da_ref, dao_ref, go_ref, w_ref, grad_ref, out_ref, pair_ref = rest[6 + blocks :]
    w_ref[core] = shared[0][...]
    w_ref[1 - core] = shared[1][...]
    frames = cores * frames_in
    chans = w_ref.shape[-1]
    rim = blocks
    own_cols = (halo, width - halo)
    per_core = w_ref.shape[2]
    pixels = tile * (own_cols[1] - own_cols[0])

    odd = band % 2
    near = tile + rim - odd * (tile + rim)
    half = group // 2
    for index, (base, ref) in enumerate(zip((rim, rim, near, tile + rim - near), arrived)):
        for step in range(half):
            at = jnp.bitwise_xor(unit, (half if index == 1 else 0) + step)
            at = at if index < 2 else jnp.bitwise_and(at, half - 1)
            g_ref[:, pl.ds(base + at * rows_in, rows_in)] = ref[step]

    def put(block, tap, value):
        slot = jnp.where(core == tap // per_core, 0, 1)
        where = jnp.bitwise_xor(section, block)
        grad_ref[slot, where, tap % per_core] = (value * factor).astype(BF16)

    for block in reversed(range(blocks)):
        edge = block + 1
        first, last = rim - edge, rim + tile + edge
        count = last - first
        for frame in range(frames):
            go_ref[frame] = g_ref[frame, rim : rim + tile].astype(F32)[
                :, own_cols[0] : own_cols[1]
            ].astype(BF16)
        pair_rows_back(w_ref, block, pair_ref)
        hiddens = []
        for frame in range(0, frames, 2):
            stop = min(frame + 4, frames)
            ahead = jnp.concatenate(
                [
                    g_ref[each, first:last].reshape(count * width, chans)
                    for each in range(frame, stop)
                ],
                1,
            )
            weights = pair_frames_back(w_ref, block, stop - frame)
            both = jnp.dot(ahead, weights, preferred_element_type=F32)
            hiddens += [both[:, :chans], both[:, chans:]]
        for frame in range(frames):
            hidden = hiddens[frame]
            slope = d_refs[block][frame].reshape(count * width, chans)
            value = (hidden * slope).astype(BF16).astype(F32)
            triple = [rolled(value, -1), value, rolled(value, 1)]
            both = jnp.concatenate([part.astype(BF16) for part in triple], 1)
            da_ref[frame, first:last] = both.reshape(count, width, 3 * chans)
            dao_ref[frame] = value.reshape(count, width, chans)[
                edge : edge + tile, own_cols[0] : own_cols[1]
            ].astype(BF16)
        for frame in range(frames):
            inner = count - 2
            taps = row_pairs(da_ref, frame, first, inner // 2)
            back = woven(jnp.dot(taps, pair_ref[...], preferred_element_type=F32), width)
            old = g_ref[frame, first + 1 : last - 1].astype(F32).reshape(inner * width, chans)
            new = (old + back).astype(BF16)
            if block:
                g_ref[frame, first + 1 : last - 1] = new.reshape(inner, width, chans)
            else:
                cut = new.astype(F32).reshape(inner, width, chans)[:, own_cols[0] : own_cols[1]]
                out_ref[frame] = cut.astype(BF16)
        slopes = dao_ref[...].reshape(frames * pixels, chans)
        for ky in range(3):
            taps = xo_ref[block, :, ky : ky + tile].reshape(frames * pixels, 3 * chans)
            sums = dot_first(slopes, taps)
            for kx in range(3):
                put(block, 3 * ky + kx, sums[:, kx * chans : (kx + 1) * chans])
        for kt in range(3):
            skip = 2 - kt
            later = go_ref[skip:].reshape((frames - skip) * pixels, chans)
            earlier = ho_ref[block, : frames - skip].reshape((frames - skip) * pixels, chans)
            put(block, 9 + kt, dot_first(later, earlier))
    keep_ref[...] = grad_ref[0]
    give_ref[...] = grad_ref[1]
    for whose, target in ((core, mine_out), (1 - core, other_out)):
        for step in range(group):
            row = jnp.bitwise_xor(unit, step) * rows_in
            target[step] = out_ref[pl.ds(whose * frames_in, frames_in), pl.ds(row, rows_in)]


def swapped(value, axis="tm", step=1):
    count = lax.axis_size(axis)
    return lax.ppermute(value, axis, [(i, i ^ step) for i in range(count)])


def on_device(video, cotangent, spatial_weights, temporal_weights):
    blocks, cores, tiles = (lax.axis_size(name) for name in ("section", "tm", "space"))
    frames_in, rows_in, columns, chans = video.shape
    halo = 2 * blocks
    tile = halo
    group = tile // rows_in
    parties = cores * group
    own_width = columns // parties
    width = own_width + 2 * halo
    span = cores * own_width + 2 * halo
    vmem = pl.BlockSpec(memory_space=pltpu.VMEM)
    params = pltpu.CompilerParams(vmem_limit_bytes=32 * 2**20)

    bands = blocks * tiles // group
    core, section, band, unit = placed(group)
    odd = band % 2

    def traded(value, shift):
        pairs = []
        for one in range(bands):
            other = ((one + shift) ^ 1) - shift
            if 0 <= other < bands:
                pairs += [(one * group + i, other * group + i) for i in range(group)]
        return lax.ppermute(value, ("section", "space"), pairs)

    total_rows = blocks * tiles * rows_in
    half = group // 2
    padded = columns + 2 * halo
    cuts = pl.pallas_call(
        functools.partial(window_kernel, halo, span),
        name="windows",
        in_specs=[vmem],
        out_specs=[vmem] * group,
        out_shape=[jax.ShapeDtypeStruct((frames_in, rows_in, span, chans), BF16)] * group,
        scratch_shapes=[pltpu.VMEM((frames_in, rows_in, padded, chans), F32)],
        compiler_params=params,
    )(video)
    pair = jax.ShapeDtypeStruct((half, cores * frames_in, rows_in, width, chans), BF16)
    low, high_pair = pl.pallas_call(
        functools.partial(cotangent_kernel, halo, width),
        name="cotangent",
        in_specs=[vmem] * 2,
        out_specs=[vmem] * 2,
        out_shape=[pair] * 2,
        scratch_shapes=[pltpu.VMEM((cores * frames_in, rows_in, padded, chans), F32)],
        compiler_params=params,
    )(cotangent, swapped(cotangent))

    def core_half(which, spatial, temporal):
        whole = jnp.concatenate([spatial[0], temporal[0]], 0)
        taps = whole.shape[0] // cores
        return lax.dynamic_slice_in_dim(whole, which * taps, taps, 0)

    _, spatial, temporal = lax.optimization_barrier([cuts[0], spatial_weights, temporal_weights])
    half_kernels = core_half(core, spatial, temporal)

    def gathered(pieces):
        return jnp.stack([pieces[0]] + [swapped(pieces[i], "space", i) for i in range(1, group)])

    mine = lax.all_gather(half_kernels, "section")
    own_video = gathered(cuts)
    near, far = traded(own_video, 0), traded(own_video, 1)
    near, mine = lax.optimization_barrier([near, mine])
    shared = [mine, swapped(mine)]
    videos = [own_video, near, far]
    videos += [swapped(each) for each in videos]

    from_far = swapped(high_pair, "space", 2)
    from_near = swapped(jnp.stack([low[1], from_far[1]]), "space", 1)
    low = jnp.stack([low[0], from_near[0]])
    high_pair = jnp.stack([from_far[0], from_near[1]])
    upper = unit < half
    cots = [
        low,
        high_pair,
        traded(jnp.where(upper == (odd == 1), low, high_pair), 0),
        traded(jnp.where(upper == (odd == 0), low, high_pair), 1),
    ]

    geometry = (blocks, cores, group, frames_in, rows_in, halo, tile, width, total_rows, columns)
    frames = cores * frames_in
    high = tile + 2 * halo
    per_section = (blocks,) + half_kernels.shape
    taps = half_kernels.shape[0]
    all_kernels = (cores,) + per_section
    saved = [
        jax.ShapeDtypeStruct((frames, tile + 2 * block + 2, width, chans), F32)
        for block in range(blocks)
    ]
    cost = pl.CostEstimate(flops=6 * 10**9, bytes_accessed=8 * 10**6, transcendentals=10**6)
    features, hidden, *slopes = pl.pallas_call(
        functools.partial(forward_kernel, geometry),
        name="forward",
        in_specs=[vmem] * 8,
        out_specs=[vmem] * (2 + blocks),
        out_shape=[
            jax.ShapeDtypeStruct((blocks, frames, tile + 2, own_width, 3 * chans), BF16),
            jax.ShapeDtypeStruct((blocks, frames, tile, own_width, chans), BF16),
        ]
        + saved,
        scratch_shapes=[
            pltpu.VMEM((frames, high, width, 3 * chans), BF16),
            pltpu.VMEM((frames, high, width, chans), BF16),
            pltpu.VMEM((high, width, chans), F32),
            pltpu.VMEM(all_kernels, BF16),
            pltpu.VMEM((frames, high, width, chans), BF16),
            pltpu.VMEM((12 * chans, 2 * chans), BF16),
        ],
        compiler_params=params,
        cost_estimate=cost,
    )(*shared, *videos)

    back = jax.ShapeDtypeStruct((group, frames_in, rows_in, own_width, chans), BF16)
    pixel_count = frames * total_rows * columns
    factor = 1.0 / float(pixel_count) ** 0.5
    keep, give, mine_grad, other_grad = pl.pallas_call(
        functools.partial(backward_kernel, geometry, factor),
        name="backward",
        in_specs=[vmem] * (blocks + 8),
        out_specs=[vmem] * 4,
        out_shape=[
            jax.ShapeDtypeStruct(per_section, BF16),
            jax.ShapeDtypeStruct(per_section, BF16),
            back,
            back,
        ],
        scratch_shapes=[
            pltpu.VMEM((frames, tile + 2 * blocks, width, chans), BF16),
            pltpu.VMEM((frames, tile + 2 * blocks, width, 3 * chans), BF16),
            pltpu.VMEM((frames, tile, own_width, chans), BF16),
            pltpu.VMEM((frames, tile, own_width, chans), BF16),
            pltpu.VMEM(all_kernels, BF16),
            pltpu.VMEM(all_kernels, BF16),
            pltpu.VMEM((frames, tile, own_width, chans), BF16),
            pltpu.VMEM((12 * chans, 2 * chans), BF16),
        ],
        compiler_params=params,
        cost_estimate=cost,
    )(*shared, *cots, features, hidden, *slopes)

    got = swapped(give)
    parts = [(keep[i].astype(F32) + got[i].astype(F32)).astype(BF16) for i in range(blocks)]
    other_grad, *parts = lax.optimization_barrier([other_grad] + parts)
    parts = parts[:1] + [swapped(parts[i], "section", i) for i in range(1, blocks)]
    other_grad = swapped(other_grad)
    first = core == 0
    wide = jnp.concatenate(
        [jnp.where(first, mine_grad, other_grad), jnp.where(first, other_grad, mine_grad)], 3
    )
    strips = [wide[0]] + [swapped(wide[i], "space", i) for i in range(1, group)]
    received = lax.optimization_barrier(parts + strips)
    parts, strips = received[:blocks], received[blocks:]
    part = sum(each.astype(F32) for each in parts).astype(BF16)

    halves = part.reshape(2, -1, chans)
    low = unit % 2

    def picked(which):
        return lax.dynamic_index_in_dim(halves, which, 0, keepdims=False)

    part = (picked(low).astype(F32) + swapped(picked(1 - low), "space", 1).astype(F32)).astype(BF16)
    part = part.astype(F32) + swapped(part, "space", 2).astype(F32)
    if tiles != group:
        part = lax.psum(
            part, "space", axis_index_groups=[list(range(i, tiles, group)) for i in range(group)]
        )
    part = part.astype(BF16)
    pair = jnp.stack([part, swapped(part, "space", 1)])
    spatial_out, temporal_out = pl.pallas_call(
        functools.partial(closing_kernel, group),
        name="closing",
        in_specs=[vmem] * 2,
        out_specs=[vmem] * 2,
        out_shape=[
            jax.ShapeDtypeStruct(spatial_weights.shape, F32),
            jax.ShapeDtypeStruct(temporal_weights.shape, F32),
        ],
        scratch_shapes=[pltpu.VMEM((cores * taps * chans, chans), BF16)],
        compiler_params=params,
    )(pair, swapped(pair))

    grad_video = jnp.zeros(video.shape, BF16)
    for step, strip in enumerate(strips):
        grad_video = lax.dynamic_update_slice(
            grad_video, strip, (0, 0, (unit ^ step) * cores * own_width, 0)
        )
    return spatial_out, temporal_out, grad_video


def solution(mesh):
    return jax.shard_map(
        on_device,
        mesh=mesh,
        in_specs=(
            P("tm", ("section", "space"), None, None),
            P("tm", ("section", "space"), None, None),
            P("section", None, None, None),
            P("section", None, None, None),
        ),
        out_specs=(
            P("section", None, None, None),
            P("section", None, None, None),
            P("tm", ("section", "space"), None, None),
        ),
        check_vma=False,
    )
```

```python
import functools

import jax
import jax.numpy as jnp
from jax import lax
from jax.experimental import pallas as pl
from jax.experimental.pallas import tpu as pltpu
from jax.sharding import PartitionSpec as P

F32 = jnp.float32
BF16 = jnp.bfloat16


def rolled(value, steps):
    return pltpu.roll(value, steps % value.shape[0], 0)


def dot_first(left, right):
    return lax.dot_general(left, right, (((0,), (0,)), ((), ())), preferred_element_type=F32)


def kernel_of(w_ref, block, tap):
    taps = w_ref.shape[2]
    return w_ref[tap // taps, block, tap % taps]


def pair_rows(w_ref, block, pair_ref):
    chans = w_ref.shape[-1]
    for source in range(4):
        for target in range(2):
            ky = source - target
            for kx in range(3):
                at = (3 * source + kx) * chans
                tile = kernel_of(w_ref, block, 3 * ky + kx) if 0 <= ky < 3 else jnp.zeros((chans, chans), BF16)
                pair_ref[at : at + chans, target * chans : (target + 1) * chans] = tile


def turned(w_ref, block, tap):
    return kernel_of(w_ref, block, tap).astype(F32).T.astype(BF16)


def pair_rows_back(w_ref, block, pair_ref):
    chans = w_ref.shape[-1]
    nothing = jnp.zeros((chans, chans), BF16)
    for kx in range(3):
        for ky in range(3):
            tile = turned(w_ref, block, 3 * ky + kx)
            for target in range(2):
                at = (3 * (2 + target - ky) + kx) * chans
                pair_ref[at : at + chans, target * chans : (target + 1) * chans] = tile
        for source, target in ((3, 0), (0, 1)):
            at = (3 * source + kx) * chans
            pair_ref[at : at + chans, target * chans : (target + 1) * chans] = nothing


def pair_frames(w_ref, block, first, count):
    chans = w_ref.shape[-1]
    columns = []
    for target in (count - 2, count - 1):
        tiles = []
        for source in range(count):
            kt = source - target + 2
            tiles.append(kernel_of(w_ref, block, 9 + kt) if 0 <= kt < 3 else jnp.zeros((chans, chans), BF16))
        columns.append(jnp.concatenate(tiles, 0))
    return jnp.concatenate(columns, 1)


def pair_frames_back(w_ref, block, count):
    chans = w_ref.shape[-1]
    tiles = [turned(w_ref, block, 9 + kt) for kt in range(3)]
    columns = []
    for target in range(2):
        column = []
        for source in range(count):
            kt = 2 - (source - target)
            column.append(tiles[kt] if 0 <= kt < 3 else jnp.zeros((chans, chans), BF16))
        columns.append(jnp.concatenate(column, 0))
    return jnp.concatenate(columns, 1)


def row_pairs(ref, frame, first, pairs):
    width, lanes = ref.shape[2:]
    rows = []
    for start in (first, first + 2):
        value = ref[frame, start : start + 2 * pairs].reshape(pairs, 2, width, lanes)
        rows += [value[:, 0], value[:, 1]]
    return jnp.concatenate(rows, 2).reshape(pairs * width, 4 * lanes)


def woven(value, width):
    chans = value.shape[1] // 2
    split = [value[:, i * chans : (i + 1) * chans].reshape(-1, 1, width, chans) for i in range(2)]
    return jnp.concatenate(split, 1).reshape(-1, chans)


def placed(group):
    place, section = lax.axis_index("space"), lax.axis_index("section")
    band = (section * lax.axis_size("space") + place) // group
    return lax.axis_index("tm"), section, band, place % group


def window_kernel(halo, span, video_ref, *rest):
    targets, wide_ref = rest[:-1], rest[-1]
    unit = placed(len(targets))[3]
    frames, rows, columns, chans = video_ref.shape
    edge = jnp.zeros((frames, rows, halo, chans), F32)
    wide_ref[:, :, :halo] = edge
    wide_ref[:, :, halo + columns :] = edge
    wide_ref[:, :, halo : halo + columns] = video_ref[...].astype(F32)
    for step, target in enumerate(targets):
        at = jnp.bitwise_xor(unit, step) * (span - 2 * halo)
        target[...] = wide_ref[:, :, pl.ds(pl.multiple_of(at, 16), span)].astype(BF16)


def cotangent_kernel(halo, width, *rest):
    sources, targets, wide_ref = rest[:4], rest[4:-1], rest[-1]
    core, _, _, unit = placed(len(targets))
    frames_in, rows, columns, chans = sources[0].shape
    edge = jnp.zeros((2, 2 * frames_in, rows, halo, chans), F32)
    wide_ref[:, :, :, :halo] = edge
    wide_ref[:, :, :, halo + columns :] = edge
    for index, ref in enumerate(sources):
        whose = core if index % 2 == 0 else 1 - core
        wide_ref[index // 2, pl.ds(whose * frames_in, frames_in), :, halo : halo + columns] = ref[
            ...
        ].astype(F32)
    own = width - 2 * halo
    for step, target in enumerate(targets):
        at = (jnp.bitwise_xor(unit, step) * 2 + core) * own
        target[...] = wide_ref[:, :, :, pl.ds(pl.multiple_of(at, 16), width)].astype(BF16)


def closing_kernel(group, mine_ref, other_ref, spatial_ref, temporal_ref, flat_ref):
    pieces, rows, chans = mine_ref.shape
    core, _, _, unit = placed(group)
    for whose, ref in ((core, mine_ref), (1 - core, other_ref)):
        for step in range(pieces):
            index = whose * pieces + jnp.bitwise_xor(jnp.bitwise_and(unit, pieces - 1), step)
            flat_ref[pl.ds(pl.multiple_of(index * rows, 16), rows)] = ref[step]
    count = spatial_ref.shape[1]
    for tap in range(count + temporal_ref.shape[1]):
        turned = flat_ref[tap * chans : (tap + 1) * chans].astype(F32).T
        if tap < count:
            spatial_ref[0, tap] = turned
        else:
            temporal_ref[0, tap - count] = turned


def place_kernels(core, section, w_ref, own_mine, own_other, mine_refs, other_refs):
    w_ref[core, section] = own_mine[...]
    w_ref[1 - core, section] = own_other[...]
    for step, (mine_ref, other_ref) in enumerate(zip(mine_refs, other_refs)):
        block = jnp.bitwise_xor(section, step + 1)
        w_ref[core, block] = mine_ref[...]
        w_ref[1 - core, block] = other_ref[...]


def forward_kernel(geometry, *rest):
    blocks, cores, group, frames_in, rows_in, halo, tile, width, height, columns = geometry
    core, section, band, unit = placed(group)
    odd = band % 2
    shared, rest = rest[: 2 * blocks], rest[2 * blocks :]
    arrived, rest = rest[:6], rest[6:]
    xo_ref, ho_ref = rest[:2]
    d_refs = rest[2 : 2 + blocks]
    x_ref, h_ref, mask_ref, w_ref, start_ref, pair_ref = rest[2 + blocks :]
    place_kernels(core, section, w_ref, *shared[:2], shared[2 : 1 + blocks], shared[1 + blocks :])
    frames = cores * frames_in
    high = tile + 2 * halo
    chans = w_ref.shape[-1]
    own_rows, own_cols = (halo, halo + tile), (halo, width - halo)
    row = band * tile - halo + lax.broadcasted_iota(jnp.int32, (high, width, chans), 0)
    left = (unit * cores + core) * (width - 2 * halo) - halo
    col = left + lax.broadcasted_iota(jnp.int32, (high, width, chans), 1)
    inside = (row >= 0) & (row < height) & (col >= 0) & (col < columns)
    mask_ref[...] = jnp.where(inside, 1.0, 0.0).astype(F32)

    def keep(block, frame, value, first):
        triple = [rolled(value, 1), value, rolled(value, -1)]
        count = value.shape[0] // width
        both = jnp.concatenate([part.astype(BF16) for part in triple], 1)
        x_ref[frame, first : first + count] = both.reshape(count, width, 3 * chans)
        start = own_rows[0] - 1 - first
        cut = [
            part.reshape(count, width, chans)[
                start : start + tile + 2, own_cols[0] : own_cols[1]
            ].astype(BF16)
            for part in triple
        ]
        xo_ref[block, frame] = jnp.concatenate(cut, 2)

    near = tile + halo - odd * (tile + halo)
    columns_at = pl.ds(pl.multiple_of(core * (width - 2 * halo), 16), width)
    for index, ref in enumerate(arrived):
        base = (halo, near, tile + halo - near)[index % 3]
        whose = core if index < 3 else 1 - core
        for step in range(group):
            row = base + jnp.bitwise_xor(unit, step) * rows_in
            start_ref[pl.ds(whose * frames_in, frames_in), pl.ds(row, rows_in)] = ref[
                step, :, :, columns_at, :
            ]
    for frame in range(frames):
        keep(0, frame, start_ref[frame].reshape(high * width, chans).astype(F32), 0)

    for block in range(blocks):
        first, last = block + 1, high - block - 1
        count = last - first
        pair_rows(w_ref, block, pair_ref)
        mask = mask_ref[first:last].reshape(count * width, chans)
        for frame in range(frames):
            taps = row_pairs(x_ref, frame, first - 1, count // 2)
            before = jnp.dot(taps, pair_ref[...], preferred_element_type=F32)
            before = woven(before, width)
            sigma = 1.0 / (1.0 + jnp.exp(-before))
            hidden = before * sigma * mask
            slope = (sigma * (1.0 + before * (1.0 - sigma))) * mask
            h_ref[frame, first:last] = hidden.astype(BF16).reshape(count, width, chans)
            ho_ref[block, frame] = hidden.reshape(count, width, chans)[
                own_rows[0] - first : own_rows[1] - first, own_cols[0] : own_cols[1]
            ].astype(BF16)
            rim = block + 1
            d_refs[block][frame] = slope.reshape(count, width, chans)[
                own_rows[0] - rim - first : own_rows[1] + rim - first
            ]
        if block + 1 == blocks:
            break
        for frame in range(0, frames, 2):
            start = max(frame - 2, 0)
            timeline = jnp.concatenate(
                [
                    h_ref[each, first:last].reshape(count * width, chans)
                    for each in range(start, frame + 2)
                ],
                1,
            )
            weights = pair_frames(w_ref, block, start, frame + 2 - start)
            both = jnp.dot(timeline, weights, preferred_element_type=F32)
            for inner in range(2):
                mixed = both[:, inner * chans : (inner + 1) * chans]
                old = x_ref[frame + inner, first:last, :, chans : 2 * chans].astype(F32)
                new = old.reshape(count * width, chans) + mixed
                keep(block + 1, frame + inner, new.astype(BF16).astype(F32), first)


def backward_kernel(geometry, factor, *rest):
    blocks, cores, group, frames_in, rows_in, halo, tile, width, height, columns = geometry
    core, section, band, unit = placed(group)
    shared, rest = rest[: 2 * blocks], rest[2 * blocks :]
    arrived, rest = rest[:group], rest[group:]
    xo_ref, ho_ref = rest[:2]
    d_refs = rest[2 : 2 + blocks]
    keep_ref, give_ref, mine_out, other_out = rest[2 + blocks : 6 + blocks]
    g_ref, da_ref, dao_ref, go_ref, w_ref, grad_ref, out_ref, pair_ref = rest[6 + blocks :]
    place_kernels(core, section, w_ref, *shared[:2], shared[2 : 1 + blocks], shared[1 + blocks :])
    frames = cores * frames_in
    chans = w_ref.shape[-1]
    rim = blocks
    own_cols = (halo, width - halo)
    per_core = w_ref.shape[2]
    pixels = tile * (own_cols[1] - own_cols[0])

    half = group // 2
    for step, ref in enumerate(arrived):
        at = jnp.bitwise_xor(unit, step)
        g_ref[:, pl.ds(rim + at * rows_in, rows_in)] = ref[0]
        beyond = jnp.where(at < half, rim + tile + at * rows_in, (at - half) * rows_in)
        g_ref[:, pl.ds(beyond, rows_in)] = ref[1]

    def put(block, tap, value):
        slot = jnp.where(core == tap // per_core, 0, 1)
        where = jnp.bitwise_xor(section, block)
        grad_ref[slot, where, tap % per_core] = (value * factor).astype(BF16)

    for block in reversed(range(blocks)):
        edge = block + 1
        first, last = rim - edge, rim + tile + edge
        count = last - first
        for frame in range(frames):
            go_ref[frame] = g_ref[frame, rim : rim + tile].astype(F32)[
                :, own_cols[0] : own_cols[1]
            ].astype(BF16)
        pair_rows_back(w_ref, block, pair_ref)
        hiddens = []
        for frame in range(0, frames, 2):
            stop = min(frame + 4, frames)
            ahead = jnp.concatenate(
                [
                    g_ref[each, first:last].reshape(count * width, chans)
                    for each in range(frame, stop)
                ],
                1,
            )
            weights = pair_frames_back(w_ref, block, stop - frame)
            both = jnp.dot(ahead, weights, preferred_element_type=F32)
            hiddens += [both[:, :chans], both[:, chans:]]
        for frame in range(frames):
            hidden = hiddens[frame]
            slope = d_refs[block][frame].reshape(count * width, chans)
            value = (hidden * slope).astype(BF16).astype(F32)
            triple = [rolled(value, -1), value, rolled(value, 1)]
            both = jnp.concatenate([part.astype(BF16) for part in triple], 1)
            da_ref[frame, first:last] = both.reshape(count, width, 3 * chans)
            dao_ref[frame] = value.reshape(count, width, chans)[
                edge : edge + tile, own_cols[0] : own_cols[1]
            ].astype(BF16)
        for frame in range(frames):
            inner = count - 2
            taps = row_pairs(da_ref, frame, first, inner // 2)
            back = woven(jnp.dot(taps, pair_ref[...], preferred_element_type=F32), width)
            old = g_ref[frame, first + 1 : last - 1].astype(F32).reshape(inner * width, chans)
            new = (old + back).astype(BF16)
            if block:
                g_ref[frame, first + 1 : last - 1] = new.reshape(inner, width, chans)
            else:
                cut = new.astype(F32).reshape(inner, width, chans)[:, own_cols[0] : own_cols[1]]
                out_ref[frame] = cut.astype(BF16)
        slopes = dao_ref[...].reshape(frames * pixels, chans)
        for ky in range(3):
            taps = xo_ref[block, :, ky : ky + tile].reshape(frames * pixels, 3 * chans)
            sums = dot_first(slopes, taps)
            for kx in range(3):
                put(block, 3 * ky + kx, sums[:, kx * chans : (kx + 1) * chans])
        for kt in range(3):
            skip = 2 - kt
            later = go_ref[skip:].reshape((frames - skip) * pixels, chans)
            earlier = ho_ref[block, : frames - skip].reshape((frames - skip) * pixels, chans)
            put(block, 9 + kt, dot_first(later, earlier))
    keep_ref[...] = grad_ref[0]
    give_ref[...] = grad_ref[1]
    for whose, target in ((core, mine_out), (1 - core, other_out)):
        for step in range(group):
            row = jnp.bitwise_xor(unit, step) * rows_in
            target[step] = out_ref[pl.ds(whose * frames_in, frames_in), pl.ds(row, rows_in)]


def swapped(value, axis="tm", step=1):
    count = lax.axis_size(axis)
    return lax.ppermute(value, axis, [(i, i ^ step) for i in range(count)])


def on_device(video, cotangent, spatial_weights, temporal_weights):
    blocks, cores, tiles = (lax.axis_size(name) for name in ("section", "tm", "space"))
    frames_in, rows_in, columns, chans = video.shape
    halo = 2 * blocks
    tile = halo
    group = tile // rows_in
    parties = cores * group
    own_width = columns // parties
    width = own_width + 2 * halo
    span = cores * own_width + 2 * halo
    vmem = pl.BlockSpec(memory_space=pltpu.VMEM)
    params = pltpu.CompilerParams(vmem_limit_bytes=32 * 2**20)

    bands = blocks * tiles // group
    core, section, band, unit = placed(group)
    odd = band % 2

    def traded(value, shift):
        pairs = []
        for one in range(bands):
            other = ((one + shift) ^ 1) - shift
            if 0 <= other < bands:
                pairs += [(one * group + i, other * group + i) for i in range(group)]
        return lax.ppermute(value, ("section", "space"), pairs)

    total_rows = blocks * tiles * rows_in
    half = group // 2
    passed = []
    for one in range(bands - 1):
        for i in range(group):
            low, high = one * group + i, (one + 1) * group + i
            passed.append((high, low) if i < half else (low, high))
    cot_halo = lax.ppermute(cotangent, ("section", "space"), passed)

    padded = columns + 2 * halo
    cuts = pl.pallas_call(
        functools.partial(window_kernel, halo, span),
        name="windows",
        in_specs=[vmem],
        out_specs=[vmem] * group,
        out_shape=[jax.ShapeDtypeStruct((frames_in, rows_in, span, chans), BF16)] * group,
        scratch_shapes=[pltpu.VMEM((frames_in, rows_in, padded, chans), F32)],
        compiler_params=params,
    )(video)
    def core_half(which, spatial, temporal):
        whole = jnp.concatenate([spatial[0], temporal[0]], 0)
        taps = whole.shape[0] // cores
        return lax.dynamic_slice_in_dim(whole, which * taps, taps, 0)

    _, spatial, temporal = lax.optimization_barrier([cuts[0], spatial_weights, temporal_weights])
    half_kernels = core_half(core, spatial, temporal)

    def gathered(pieces):
        return jnp.stack([pieces[0]] + [swapped(pieces[i], "space", i) for i in range(1, group)])

    along_x = swapped(half_kernels, "section", 1)
    along_y = swapped(half_kernels, "section", 2)
    own_video = gathered(cuts)
    near, far = traded(own_video, 0), traded(own_video, 1)
    _, along_x, along_y, cot_halo, spatial, temporal = lax.optimization_barrier(
        [own_video, along_x, along_y, cot_halo, spatial_weights, temporal_weights]
    )
    mine = [along_x, along_y, swapped(along_x, "section", 2)]
    rest_kernels = core_half(1 - core, spatial, temporal)
    shared = [half_kernels, rest_kernels] + mine + [swapped(each) for each in mine]

    cots = pl.pallas_call(
        functools.partial(cotangent_kernel, halo, width),
        name="cotangent",
        in_specs=[vmem] * 4,
        out_specs=[vmem] * group,
        out_shape=[jax.ShapeDtypeStruct((2, cores * frames_in, rows_in, width, chans), BF16)] * group,
        scratch_shapes=[pltpu.VMEM((2, cores * frames_in, rows_in, padded, chans), F32)],
        compiler_params=params,
    )(cotangent, swapped(cotangent), cot_halo, swapped(cot_halo))
    cots = [cots[0]] + [swapped(cots[i], "space", i) for i in range(1, group)]
    near, cots[1] = lax.optimization_barrier([near, cots[1]])
    videos = [own_video, near, far]
    videos += [swapped(each) for each in videos]

    geometry = (blocks, cores, group, frames_in, rows_in, halo, tile, width, total_rows, columns)
    frames = cores * frames_in
    high = tile + 2 * halo
    per_section = (blocks,) + half_kernels.shape
    taps = half_kernels.shape[0]
    all_kernels = (cores,) + per_section
    saved = [
        jax.ShapeDtypeStruct((frames, tile + 2 * block + 2, width, chans), F32)
        for block in range(blocks)
    ]
    cost = pl.CostEstimate(flops=6 * 10**9, bytes_accessed=8 * 10**6, transcendentals=10**6)
    features, hidden, *slopes = pl.pallas_call(
        functools.partial(forward_kernel, geometry),
        name="forward",
        in_specs=[vmem] * (2 * blocks + 6),
        out_specs=[vmem] * (2 + blocks),
        out_shape=[
            jax.ShapeDtypeStruct((blocks, frames, tile + 2, own_width, 3 * chans), BF16),
            jax.ShapeDtypeStruct((blocks, frames, tile, own_width, chans), BF16),
        ]
        + saved,
        scratch_shapes=[
            pltpu.VMEM((frames, high, width, 3 * chans), BF16),
            pltpu.VMEM((frames, high, width, chans), BF16),
            pltpu.VMEM((high, width, chans), F32),
            pltpu.VMEM(all_kernels, BF16),
            pltpu.VMEM((frames, high, width, chans), BF16),
            pltpu.VMEM((12 * chans, 2 * chans), BF16),
        ],
        compiler_params=params,
        cost_estimate=cost,
    )(*shared, *videos)

    back = jax.ShapeDtypeStruct((group, frames_in, rows_in, own_width, chans), BF16)
    pixel_count = frames * total_rows * columns
    factor = 1.0 / float(pixel_count) ** 0.5
    keep, give, mine_grad, other_grad = pl.pallas_call(
        functools.partial(backward_kernel, geometry, factor),
        name="backward",
        in_specs=[vmem] * (3 * blocks + group + 2),
        out_specs=[vmem] * 4,
        out_shape=[
            jax.ShapeDtypeStruct(per_section, BF16),
            jax.ShapeDtypeStruct(per_section, BF16),
            back,
            back,
        ],
        scratch_shapes=[
            pltpu.VMEM((frames, tile + 2 * blocks, width, chans), BF16),
            pltpu.VMEM((frames, tile + 2 * blocks, width, 3 * chans), BF16),
            pltpu.VMEM((frames, tile, own_width, chans), BF16),
            pltpu.VMEM((frames, tile, own_width, chans), BF16),
            pltpu.VMEM(all_kernels, BF16),
            pltpu.VMEM(all_kernels, BF16),
            pltpu.VMEM((frames, tile, own_width, chans), BF16),
            pltpu.VMEM((12 * chans, 2 * chans), BF16),
        ],
        compiler_params=params,
        cost_estimate=cost,
    )(*shared, *cots, features, hidden, *slopes)

    got = swapped(give)
    parts = [(keep[i].astype(F32) + got[i].astype(F32)).astype(BF16) for i in range(blocks)]
    other_grad, *parts = lax.optimization_barrier([other_grad] + parts)
    parts = parts[:1] + [swapped(parts[i], "section", i) for i in range(1, blocks)]
    other_grad = swapped(other_grad)
    first = core == 0
    wide = jnp.concatenate(
        [jnp.where(first, mine_grad, other_grad), jnp.where(first, other_grad, mine_grad)], 3
    )
    strips = [wide[0]] + [swapped(wide[i], "space", i) for i in range(1, group)]
    received = lax.optimization_barrier(parts + strips)
    parts, strips = received[:blocks], received[blocks:]
    part = sum(each.astype(F32) for each in parts).astype(BF16)

    units = part.reshape(group, -1, chans)

    def chunk(step):
        return lax.dynamic_index_in_dim(units, unit ^ step, 0, keepdims=False)

    part = sum(
        each.astype(F32)
        for each in [chunk(0)] + [swapped(chunk(i), "space", i) for i in range(1, group)]
    )
    if tiles != group:
        part = lax.psum(
            part, "space", axis_index_groups=[list(range(i, tiles, group)) for i in range(group)]
        )
    part = part.astype(BF16)
    pair = jnp.stack([part] + [swapped(part, "space", i) for i in range(1, group)])
    spatial_out, temporal_out = pl.pallas_call(
        functools.partial(closing_kernel, group),
        name="closing",
        in_specs=[vmem] * 2,
        out_specs=[vmem] * 2,
        out_shape=[
            jax.ShapeDtypeStruct(spatial_weights.shape, F32),
            jax.ShapeDtypeStruct(temporal_weights.shape, F32),
        ],
        scratch_shapes=[pltpu.VMEM((cores * taps * chans, chans), BF16)],
        compiler_params=params,
    )(pair, swapped(pair))

    grad_video = jnp.zeros(video.shape, BF16)
    for step, strip in enumerate(strips):
        grad_video = lax.dynamic_update_slice(
            grad_video, strip, (0, 0, (unit ^ step) * cores * own_width, 0)
        )
    return spatial_out, temporal_out, grad_video


def solution(mesh):
    return jax.shard_map(
        on_device,
        mesh=mesh,
        in_specs=(
            P("tm", ("section", "space"), None, None),
            P("tm", ("section", "space"), None, None),
            P("section", None, None, None),
            P("section", None, None, None),
        ),
        out_specs=(
            P("section", None, None, None),
            P("section", None, None, None),
            P("tm", ("section", "space"), None, None),
        ),
        check_vma=False,
    )
```

```python
import functools

import jax
import jax.numpy as jnp
from jax import lax
from jax.experimental import pallas as pl
from jax.experimental.pallas import tpu as pltpu
from jax.sharding import PartitionSpec as P

F32 = jnp.float32
BF16 = jnp.bfloat16


def rolled(value, steps):
    return pltpu.roll(value, steps % value.shape[0], 0)


def dot_first(left, right):
    return lax.dot_general(left, right, (((0,), (0,)), ((), ())), preferred_element_type=F32)


def kernel_of(w_ref, block, tap):
    taps = w_ref.shape[2]
    return w_ref[tap // taps, block, tap % taps]


def pair_rows(w_ref, block, pair_ref):
    chans = w_ref.shape[-1]
    for source in range(4):
        for target in range(2):
            ky = source - target
            for kx in range(3):
                at = (3 * source + kx) * chans
                tile = kernel_of(w_ref, block, 3 * ky + kx) if 0 <= ky < 3 else jnp.zeros((chans, chans), BF16)
                pair_ref[at : at + chans, target * chans : (target + 1) * chans] = tile


def turned(w_ref, block, tap):
    return kernel_of(w_ref, block, tap).astype(F32).T.astype(BF16)


def pair_rows_back(w_ref, block, pair_ref):
    chans = w_ref.shape[-1]
    nothing = jnp.zeros((chans, chans), BF16)
    for kx in range(3):
        for ky in range(3):
            tile = turned(w_ref, block, 3 * ky + kx)
            for target in range(2):
                at = (3 * (2 + target - ky) + kx) * chans
                pair_ref[at : at + chans, target * chans : (target + 1) * chans] = tile
        for source, target in ((3, 0), (0, 1)):
            at = (3 * source + kx) * chans
            pair_ref[at : at + chans, target * chans : (target + 1) * chans] = nothing


def pair_frames(w_ref, block, first, count):
    chans = w_ref.shape[-1]
    columns = []
    for target in (count - 2, count - 1):
        tiles = []
        for source in range(count):
            kt = source - target + 2
            tiles.append(kernel_of(w_ref, block, 9 + kt) if 0 <= kt < 3 else jnp.zeros((chans, chans), BF16))
        columns.append(jnp.concatenate(tiles, 0))
    return jnp.concatenate(columns, 1)


def pair_frames_back(w_ref, block, count):
    chans = w_ref.shape[-1]
    tiles = [turned(w_ref, block, 9 + kt) for kt in range(3)]
    columns = []
    for target in range(2):
        column = []
        for source in range(count):
            kt = 2 - (source - target)
            column.append(tiles[kt] if 0 <= kt < 3 else jnp.zeros((chans, chans), BF16))
        columns.append(jnp.concatenate(column, 0))
    return jnp.concatenate(columns, 1)


def row_pairs(ref, frame, first, pairs):
    width, lanes = ref.shape[2:]
    rows = []
    for start in (first, first + 2):
        value = ref[frame, start : start + 2 * pairs].reshape(pairs, 2, width, lanes)
        rows += [value[:, 0], value[:, 1]]
    return jnp.concatenate(rows, 2).reshape(pairs * width, 4 * lanes)


def woven(value, width):
    chans = value.shape[1] // 2
    split = [value[:, i * chans : (i + 1) * chans].reshape(-1, 1, width, chans) for i in range(2)]
    return jnp.concatenate(split, 1).reshape(-1, chans)


def placed(group):
    place, section = lax.axis_index("space"), lax.axis_index("section")
    band = (section * lax.axis_size("space") + place) // group
    return lax.axis_index("tm"), section, band, place % group


def window_kernel(halo, span, video_ref, *rest):
    targets, wide_ref = rest[:-1], rest[-1]
    unit = placed(len(targets))[3]
    frames, rows, columns, chans = video_ref.shape
    edge = jnp.zeros((frames, rows, halo, chans), F32)
    wide_ref[:, :, :halo] = edge
    wide_ref[:, :, halo + columns :] = edge
    wide_ref[:, :, halo : halo + columns] = video_ref[...].astype(F32)
    for step, target in enumerate(targets):
        at = jnp.bitwise_xor(unit, step) * (span - 2 * halo)
        target[...] = wide_ref[:, :, pl.ds(pl.multiple_of(at, 16), span)].astype(BF16)


def cotangent_kernel(reach, width, *rest):
    sources, targets, wide_ref = rest[:4], rest[4:-1], rest[-1]
    core, _, _, unit = placed(len(targets))
    frames_in, rows, columns, chans = sources[0].shape
    edge = jnp.zeros((2, 2 * frames_in, rows, reach, chans), F32)
    wide_ref[:, :, :, :reach] = edge
    wide_ref[:, :, :, reach + columns :] = edge
    for index, ref in enumerate(sources):
        whose = core if index % 2 == 0 else 1 - core
        wide_ref[index // 2, pl.ds(whose * frames_in, frames_in), :, reach : reach + columns] = ref[
            ...
        ].astype(F32)
    own = width - 2 * reach
    for step, target in enumerate(targets):
        at = (jnp.bitwise_xor(unit, step) * 2 + core) * own
        window = wide_ref[:, :, :, pl.ds(pl.multiple_of(at, 16), width)]
        target[...] = window.reshape(target.shape).astype(BF16)


def closing_kernel(group, mine_ref, other_ref, spatial_ref, temporal_ref, flat_ref):
    pieces, rows, chans = mine_ref.shape
    core, _, _, unit = placed(group)
    for whose, ref in ((core, mine_ref), (1 - core, other_ref)):
        for step in range(pieces):
            index = whose * pieces + jnp.bitwise_xor(jnp.bitwise_and(unit, pieces - 1), step)
            flat_ref[pl.ds(pl.multiple_of(index * rows, 16), rows)] = ref[step]
    count = spatial_ref.shape[1]
    for tap in range(count + temporal_ref.shape[1]):
        turned = flat_ref[tap * chans : (tap + 1) * chans].astype(F32).T
        if tap < count:
            spatial_ref[0, tap] = turned
        else:
            temporal_ref[0, tap - count] = turned


def place_kernels(core, section, w_ref, own_mine, own_other, mine_refs, other_refs):
    w_ref[core, section] = own_mine[...]
    w_ref[1 - core, section] = own_other[...]
    for step, (mine_ref, other_ref) in enumerate(zip(mine_refs, other_refs)):
        block = jnp.bitwise_xor(section, step + 1)
        w_ref[core, block] = mine_ref[...]
        w_ref[1 - core, block] = other_ref[...]


def forward_kernel(geometry, *rest):
    blocks, cores, group, frames_in, rows_in, halo, tile, width, height, columns = geometry
    core, section, band, unit = placed(group)
    odd = band % 2
    shared, rest = rest[: 2 * blocks], rest[2 * blocks :]
    arrived, rest = rest[:6], rest[6:]
    xo_ref, ho_ref = rest[:2]
    d_refs = rest[2 : 2 + blocks]
    x_ref, h_ref, mask_ref, w_ref, start_ref, pair_ref = rest[2 + blocks :]
    place_kernels(core, section, w_ref, *shared[:2], shared[2 : 1 + blocks], shared[1 + blocks :])
    frames = cores * frames_in
    high = tile + 2 * halo
    chans = w_ref.shape[-1]
    own_rows, own_cols = (halo, halo + tile), (halo, width - halo)
    row = band * tile - halo + lax.broadcasted_iota(jnp.int32, (high, width, chans), 0)
    left = (unit * cores + core) * (width - 2 * halo) - halo
    col = left + lax.broadcasted_iota(jnp.int32, (high, width, chans), 1)
    inside = (row >= 0) & (row < height) & (col >= 0) & (col < columns)
    mask_ref[...] = jnp.where(inside, 1.0, 0.0).astype(F32)

    def keep(block, frame, value, first):
        triple = [rolled(value, 1), value, rolled(value, -1)]
        count = value.shape[0] // width
        both = jnp.concatenate([part.astype(BF16) for part in triple], 1)
        x_ref[frame, first : first + count] = both.reshape(count, width, 3 * chans)
        start = own_rows[0] - 1 - first
        cut = [
            part.reshape(count, width, chans)[
                start : start + tile + 2, own_cols[0] : own_cols[1]
            ].astype(BF16)
            for part in triple
        ]
        xo_ref[block, frame] = jnp.concatenate(cut, 2)

    near = tile + halo - odd * (tile + halo)
    columns_at = pl.ds(pl.multiple_of(core * (width - 2 * halo), 16), width)
    for index, ref in enumerate(arrived):
        base = (halo, near, tile + halo - near)[index % 3]
        whose = core if index < 3 else 1 - core
        for step in range(group):
            row = base + jnp.bitwise_xor(unit, step) * rows_in
            start_ref[pl.ds(whose * frames_in, frames_in), pl.ds(row, rows_in)] = ref[
                step, :, :, columns_at, :
            ]
    for frame in range(frames):
        keep(0, frame, start_ref[frame].reshape(high * width, chans).astype(F32), 0)

    for block in range(blocks):
        first, last = block + 1, high - block - 1
        count = last - first
        pair_rows(w_ref, block, pair_ref)
        mask = mask_ref[first:last].reshape(count * width, chans)
        for frame in range(frames):
            taps = row_pairs(x_ref, frame, first - 1, count // 2)
            before = jnp.dot(taps, pair_ref[...], preferred_element_type=F32)
            before = woven(before, width)
            sigma = 1.0 / (1.0 + jnp.exp(-before))
            hidden = before * sigma * mask
            slope = (sigma * (1.0 + before * (1.0 - sigma))) * mask
            h_ref[frame, first:last] = hidden.astype(BF16).reshape(count, width, chans)
            ho_ref[block, frame] = hidden.reshape(count, width, chans)[
                own_rows[0] - first : own_rows[1] - first, own_cols[0] : own_cols[1]
            ].astype(BF16)
            rim = block + 1
            d_refs[block][frame] = slope.reshape(count, width, chans)[
                own_rows[0] - rim - first : own_rows[1] + rim - first
            ]
        if block + 1 == blocks:
            break
        for frame in range(0, frames, 2):
            start = max(frame - 2, 0)
            timeline = jnp.concatenate(
                [
                    h_ref[each, first:last].reshape(count * width, chans)
                    for each in range(start, frame + 2)
                ],
                1,
            )
            weights = pair_frames(w_ref, block, start, frame + 2 - start)
            both = jnp.dot(timeline, weights, preferred_element_type=F32)
            for inner in range(2):
                mixed = both[:, inner * chans : (inner + 1) * chans]
                old = x_ref[frame + inner, first:last, :, chans : 2 * chans].astype(F32)
                new = old.reshape(count * width, chans) + mixed
                keep(block + 1, frame + inner, new.astype(BF16).astype(F32), first)


def backward_kernel(geometry, factor, *rest):
    blocks, cores, group, frames_in, rows_in, halo, tile, width, height, columns = geometry
    core, section, band, unit = placed(group)
    shared, rest = rest[: 2 * blocks], rest[2 * blocks :]
    arrived, rest = rest[:group], rest[group:]
    xo_ref, ho_ref = rest[:2]
    d_refs = rest[2 : 2 + blocks]
    keep_ref, give_ref, mine_out, other_out = rest[2 + blocks : 6 + blocks]
    g_ref, da_ref, dao_ref, go_ref, w_ref, grad_ref, out_ref, pair_ref = rest[6 + blocks :]
    place_kernels(core, section, w_ref, *shared[:2], shared[2 : 1 + blocks], shared[1 + blocks :])
    frames = cores * frames_in
    chans = w_ref.shape[-1]
    rim = blocks
    own_cols = (halo, width - halo)
    per_core = w_ref.shape[2]
    pixels = tile * (own_cols[1] - own_cols[0])

    half = group // 2
    side = halo - rim
    edge = jnp.zeros((frames, rows_in, side, chans), F32)

    def widened(value):
        value = value.astype(F32).reshape(frames, rows_in, width - 2 * side, chans)
        return jnp.concatenate([edge, value, edge], 2).astype(BF16)

    for step, ref in enumerate(arrived):
        at = jnp.bitwise_xor(unit, step)
        g_ref[:, pl.ds(rim + at * rows_in, rows_in)] = widened(ref[0])
        beyond = jnp.where(at < half, rim + tile + at * rows_in, (at - half) * rows_in)
        g_ref[:, pl.ds(beyond, rows_in)] = widened(ref[1])

    def put(block, tap, value):
        slot = jnp.where(core == tap // per_core, 0, 1)
        where = jnp.bitwise_xor(section, block)
        grad_ref[slot, where, tap % per_core] = (value * factor).astype(BF16)

    for block in reversed(range(blocks)):
        edge = block + 1
        first, last = rim - edge, rim + tile + edge
        count = last - first
        for frame in range(frames):
            go_ref[frame] = g_ref[frame, rim : rim + tile].astype(F32)[
                :, own_cols[0] : own_cols[1]
            ].astype(BF16)
        pair_rows_back(w_ref, block, pair_ref)
        hiddens = []
        for frame in range(0, frames, 2):
            stop = min(frame + 4, frames)
            ahead = jnp.concatenate(
                [
                    g_ref[each, first:last].reshape(count * width, chans)
                    for each in range(frame, stop)
                ],
                1,
            )
            weights = pair_frames_back(w_ref, block, stop - frame)
            both = jnp.dot(ahead, weights, preferred_element_type=F32)
            hiddens += [both[:, :chans], both[:, chans:]]
        for frame in range(frames):
            hidden = hiddens[frame]
            slope = d_refs[block][frame].reshape(count * width, chans)
            value = (hidden * slope).astype(BF16).astype(F32)
            triple = [rolled(value, -1), value, rolled(value, 1)]
            both = jnp.concatenate([part.astype(BF16) for part in triple], 1)
            da_ref[frame, first:last] = both.reshape(count, width, 3 * chans)
            dao_ref[frame] = value.reshape(count, width, chans)[
                edge : edge + tile, own_cols[0] : own_cols[1]
            ].astype(BF16)
        for frame in range(frames):
            inner = count - 2
            taps = row_pairs(da_ref, frame, first, inner // 2)
            back = woven(jnp.dot(taps, pair_ref[...], preferred_element_type=F32), width)
            old = g_ref[frame, first + 1 : last - 1].astype(F32).reshape(inner * width, chans)
            new = (old + back).astype(BF16)
            if block:
                g_ref[frame, first + 1 : last - 1] = new.reshape(inner, width, chans)
            else:
                cut = new.astype(F32).reshape(inner, width, chans)[:, own_cols[0] : own_cols[1]]
                out_ref[frame] = cut.astype(BF16)
        slopes = dao_ref[...].reshape(frames * pixels, chans)
        for ky in range(3):
            taps = xo_ref[block, :, ky : ky + tile].reshape(frames * pixels, 3 * chans)
            sums = dot_first(slopes, taps)
            for kx in range(3):
                put(block, 3 * ky + kx, sums[:, kx * chans : (kx + 1) * chans])
        for kt in range(3):
            skip = 2 - kt
            later = go_ref[skip:].reshape((frames - skip) * pixels, chans)
            earlier = ho_ref[block, : frames - skip].reshape((frames - skip) * pixels, chans)
            put(block, 9 + kt, dot_first(later, earlier))
    keep_ref[...] = grad_ref[0]
    give_ref[...] = grad_ref[1]
    for whose, target in ((core, mine_out), (1 - core, other_out)):
        for step in range(group):
            row = jnp.bitwise_xor(unit, step) * rows_in
            target[step] = out_ref[pl.ds(whose * frames_in, frames_in), pl.ds(row, rows_in)]


def swapped(value, axis="tm", step=1):
    count = lax.axis_size(axis)
    return lax.ppermute(value, axis, [(i, i ^ step) for i in range(count)])


def on_device(video, cotangent, spatial_weights, temporal_weights):
    blocks, cores, tiles = (lax.axis_size(name) for name in ("section", "tm", "space"))
    frames_in, rows_in, columns, chans = video.shape
    halo = 2 * blocks
    tile = halo
    group = tile // rows_in
    parties = cores * group
    own_width = columns // parties
    width = own_width + 2 * halo
    span = cores * own_width + 2 * halo
    vmem = pl.BlockSpec(memory_space=pltpu.VMEM)
    params = pltpu.CompilerParams(vmem_limit_bytes=32 * 2**20)

    bands = blocks * tiles // group
    core, section, band, unit = placed(group)

    def traded(value, shift):
        pairs = []
        for one in range(bands):
            other = ((one + shift) ^ 1) - shift
            if 0 <= other < bands:
                pairs += [(one * group + i, other * group + i) for i in range(group)]
        return lax.ppermute(value, ("section", "space"), pairs)

    total_rows = blocks * tiles * rows_in
    half = group // 2
    passed = []
    for one in range(bands - 1):
        for i in range(group):
            low, high = one * group + i, (one + 1) * group + i
            passed.append((high, low) if i < half else (low, high))
    cot_halo = lax.ppermute(cotangent, ("section", "space"), passed)

    padded = columns + 2 * halo
    cuts = pl.pallas_call(
        functools.partial(window_kernel, halo, span),
        name="windows",
        in_specs=[vmem],
        out_specs=[vmem] * group,
        out_shape=[jax.ShapeDtypeStruct((frames_in, rows_in, span, chans), BF16)] * group,
        scratch_shapes=[pltpu.VMEM((frames_in, rows_in, padded, chans), F32)],
        compiler_params=params,
    )(video)
    *cuts, spatial, temporal = lax.optimization_barrier(
        list(cuts) + [spatial_weights, temporal_weights]
    )
    def core_half(which):
        whole = jnp.concatenate([spatial[0], temporal[0]], 0)
        taps = whole.shape[0] // cores
        return lax.dynamic_slice_in_dim(whole, which * taps, taps, 0)

    half_kernels = core_half(core)

    def gathered(pieces):
        return jnp.stack([pieces[0]] + [swapped(pieces[i], "space", i) for i in range(1, group)])

    along_x = swapped(half_kernels, "section", 1)
    along_y = swapped(half_kernels, "section", 2)
    own_video, along_x, along_y, spatial, temporal = lax.optimization_barrier(
        [gathered(cuts), along_x, along_y, spatial, temporal]
    )
    near, far = traded(own_video, 0), traded(own_video, 1)
    mine = [along_x, along_y, swapped(along_x, "section", 2)]
    shared = mine + [swapped(each) for each in mine]
    rest_kernels = core_half(1 - core)

    narrow = own_width + 2 * blocks
    cuts = pl.pallas_call(
        functools.partial(cotangent_kernel, blocks, narrow),
        name="cotangent",
        in_specs=[vmem] * 4,
        out_specs=[vmem] * group,
        out_shape=[jax.ShapeDtypeStruct((2, cores * frames_in, rows_in * narrow, chans), BF16)] * group,
        scratch_shapes=[
            pltpu.VMEM((2, cores * frames_in, rows_in, columns + 2 * blocks, chans), F32)
        ],
        compiler_params=params,
    )(cotangent, swapped(cotangent), cot_halo, swapped(cot_halo))
    near, rest_kernels, *cuts = lax.optimization_barrier([near, rest_kernels] + list(cuts))
    shared = [half_kernels, rest_kernels] + shared
    videos = [own_video, near, far]
    videos += [swapped(each) for each in videos]
    cots = [cuts[0]] + [swapped(cuts[i], "space", i) for i in range(1, group)]

    geometry = (blocks, cores, group, frames_in, rows_in, halo, tile, width, total_rows, columns)
    frames = cores * frames_in
    high = tile + 2 * halo
    per_section = (blocks,) + half_kernels.shape
    taps = half_kernels.shape[0]
    all_kernels = (cores,) + per_section
    saved = [
        jax.ShapeDtypeStruct((frames, tile + 2 * block + 2, width, chans), F32)
        for block in range(blocks)
    ]
    cost = pl.CostEstimate(flops=6 * 10**9, bytes_accessed=8 * 10**6, transcendentals=10**6)
    features, hidden, *slopes = pl.pallas_call(
        functools.partial(forward_kernel, geometry),
        name="forward",
        in_specs=[vmem] * (2 * blocks + 6),
        out_specs=[vmem] * (2 + blocks),
        out_shape=[
            jax.ShapeDtypeStruct((blocks, frames, tile + 2, own_width, 3 * chans), BF16),
            jax.ShapeDtypeStruct((blocks, frames, tile, own_width, chans), BF16),
        ]
        + saved,
        scratch_shapes=[
            pltpu.VMEM((frames, high, width, 3 * chans), BF16),
            pltpu.VMEM((frames, high, width, chans), BF16),
            pltpu.VMEM((high, width, chans), F32),
            pltpu.VMEM(all_kernels, BF16),
            pltpu.VMEM((frames, high, width, chans), BF16),
            pltpu.VMEM((12 * chans, 2 * chans), BF16),
        ],
        compiler_params=params,
        cost_estimate=cost,
    )(*shared, *videos)

    back = jax.ShapeDtypeStruct((group, frames_in, rows_in, own_width, chans), BF16)
    pixel_count = frames * total_rows * columns
    factor = 1.0 / float(pixel_count) ** 0.5
    keep, give, mine_grad, other_grad = pl.pallas_call(
        functools.partial(backward_kernel, geometry, factor),
        name="backward",
        in_specs=[vmem] * (3 * blocks + group + 2),
        out_specs=[vmem] * 4,
        out_shape=[
            jax.ShapeDtypeStruct(per_section, BF16),
            jax.ShapeDtypeStruct(per_section, BF16),
            back,
            back,
        ],
        scratch_shapes=[
            pltpu.VMEM((frames, tile + 2 * blocks, width, chans), BF16),
            pltpu.VMEM((frames, tile + 2 * blocks, width, 3 * chans), BF16),
            pltpu.VMEM((frames, tile, own_width, chans), BF16),
            pltpu.VMEM((frames, tile, own_width, chans), BF16),
            pltpu.VMEM(all_kernels, BF16),
            pltpu.VMEM(all_kernels, BF16),
            pltpu.VMEM((frames, tile, own_width, chans), BF16),
            pltpu.VMEM((12 * chans, 2 * chans), BF16),
        ],
        compiler_params=params,
        cost_estimate=cost,
    )(*shared, *cots, features, hidden, *slopes)

    got = swapped(give)
    parts = [(keep[i].astype(F32) + got[i].astype(F32)).astype(BF16) for i in range(blocks)]
    other_grad, *parts = lax.optimization_barrier([other_grad] + parts)
    parts = parts[:1] + [swapped(parts[i], "section", i) for i in range(1, blocks)]
    other_grad = swapped(other_grad)
    first = core == 0
    wide = jnp.concatenate(
        [jnp.where(first, mine_grad, other_grad), jnp.where(first, other_grad, mine_grad)], 3
    )
    strips = [wide[0]] + [swapped(wide[i], "space", i) for i in range(1, group)]
    received = lax.optimization_barrier(parts + strips)
    parts, strips = received[:blocks], received[blocks:]
    part = sum(each.astype(F32) for each in parts).astype(BF16)

    halves = part.reshape(2, -1, chans)
    low = unit % 2

    def picked(which):
        return lax.dynamic_index_in_dim(halves, which, 0, keepdims=False)

    part = (picked(low).astype(F32) + swapped(picked(1 - low), "space", 1).astype(F32)).astype(BF16)
    part = part.astype(F32) + swapped(part, "space", 2).astype(F32)
    if tiles != group:
        part = lax.psum(
            part, "space", axis_index_groups=[list(range(i, tiles, group)) for i in range(group)]
        )
    part = part.astype(BF16)
    pair = jnp.stack([part, swapped(part, "space", 1)])
    spatial_out, temporal_out = pl.pallas_call(
        functools.partial(closing_kernel, group),
        name="closing",
        in_specs=[vmem] * 2,
        out_specs=[vmem] * 2,
        out_shape=[
            jax.ShapeDtypeStruct(spatial_weights.shape, F32),
            jax.ShapeDtypeStruct(temporal_weights.shape, F32),
        ],
        scratch_shapes=[pltpu.VMEM((cores * taps * chans, chans), BF16)],
        compiler_params=params,
    )(pair, swapped(pair))

    grad_video = jnp.zeros(video.shape, BF16)
    for step, strip in enumerate(strips):
        grad_video = lax.dynamic_update_slice(
            grad_video, strip, (0, 0, (unit ^ step) * cores * own_width, 0)
        )
    return spatial_out, temporal_out, grad_video


def solution(mesh):
    return jax.shard_map(
        on_device,
        mesh=mesh,
        in_specs=(
            P("tm", ("section", "space"), None, None),
            P("tm", ("section", "space"), None, None),
            P("section", None, None, None),
            P("section", None, None, None),
        ),
        out_specs=(
            P("section", None, None, None),
            P("section", None, None, None),
            P("tm", ("section", "space"), None, None),
        ),
        check_vma=False,
    )
```

```python
import functools

import jax
import jax.numpy as jnp
from jax import lax
from jax.experimental import pallas as pl
from jax.experimental.pallas import tpu as pltpu
from jax.sharding import PartitionSpec as P

F32 = jnp.float32
BF16 = jnp.bfloat16


def rolled(value, steps):
    return pltpu.roll(value, steps % value.shape[0], 0)


def dot_first(left, right):
    return lax.dot_general(left, right, (((0,), (0,)), ((), ())), preferred_element_type=F32)


def kernel_of(w_ref, block, tap):
    taps = w_ref.shape[2]
    return w_ref[tap // taps, block, tap % taps]


def pair_rows(w_ref, block, pair_ref):
    chans = w_ref.shape[-1]
    for source in range(4):
        for target in range(2):
            ky = source - target
            for kx in range(3):
                at = (3 * source + kx) * chans
                tile = kernel_of(w_ref, block, 3 * ky + kx) if 0 <= ky < 3 else jnp.zeros((chans, chans), BF16)
                pair_ref[at : at + chans, target * chans : (target + 1) * chans] = tile


def turned(w_ref, block, tap):
    return kernel_of(w_ref, block, tap).astype(F32).T.astype(BF16)


def pair_rows_back(w_ref, block, pair_ref):
    chans = w_ref.shape[-1]
    nothing = jnp.zeros((chans, chans), BF16)
    for kx in range(3):
        for ky in range(3):
            tile = turned(w_ref, block, 3 * ky + kx)
            for target in range(2):
                at = (3 * (2 + target - ky) + kx) * chans
                pair_ref[at : at + chans, target * chans : (target + 1) * chans] = tile
        for source, target in ((3, 0), (0, 1)):
            at = (3 * source + kx) * chans
            pair_ref[at : at + chans, target * chans : (target + 1) * chans] = nothing


def pair_frames(w_ref, block, first, count):
    chans = w_ref.shape[-1]
    columns = []
    for target in (count - 2, count - 1):
        tiles = []
        for source in range(count):
            kt = source - target + 2
            tiles.append(kernel_of(w_ref, block, 9 + kt) if 0 <= kt < 3 else jnp.zeros((chans, chans), BF16))
        columns.append(jnp.concatenate(tiles, 0))
    return jnp.concatenate(columns, 1)


def pair_frames_back(w_ref, block, count):
    chans = w_ref.shape[-1]
    tiles = [turned(w_ref, block, 9 + kt) for kt in range(3)]
    columns = []
    for target in range(2):
        column = []
        for source in range(count):
            kt = 2 - (source - target)
            column.append(tiles[kt] if 0 <= kt < 3 else jnp.zeros((chans, chans), BF16))
        columns.append(jnp.concatenate(column, 0))
    return jnp.concatenate(columns, 1)


def row_pairs(ref, frame, first, pairs):
    width, lanes = ref.shape[2:]
    rows = []
    for start in (first, first + 2):
        value = ref[frame, start : start + 2 * pairs].reshape(pairs, 2, width, lanes)
        rows += [value[:, 0], value[:, 1]]
    return jnp.concatenate(rows, 2).reshape(pairs * width, 4 * lanes)


def woven(value, width):
    chans = value.shape[1] // 2
    split = [value[:, i * chans : (i + 1) * chans].reshape(-1, 1, width, chans) for i in range(2)]
    return jnp.concatenate(split, 1).reshape(-1, chans)


def placed(group):
    place, section = lax.axis_index("space"), lax.axis_index("section")
    band = (section * lax.axis_size("space") + place) // group
    return lax.axis_index("tm"), section, band, place % group


def window_kernel(halo, span, video_ref, *rest):
    targets, wide_ref = rest[:-1], rest[-1]
    unit = placed(len(targets))[3]
    frames, rows, columns, chans = video_ref.shape
    edge = jnp.zeros((frames, rows, halo, chans), F32)
    wide_ref[:, :, :halo] = edge
    wide_ref[:, :, halo + columns :] = edge
    wide_ref[:, :, halo : halo + columns] = video_ref[...].astype(F32)
    for step, target in enumerate(targets):
        at = jnp.bitwise_xor(unit, step) * (span - 2 * halo)
        target[...] = wide_ref[:, :, pl.ds(pl.multiple_of(at, 16), span)].astype(BF16)


def cotangent_kernel(reach, width, *rest):
    sources, targets, wide_ref = rest[:4], rest[4:-1], rest[-1]
    core, _, _, unit = placed(len(targets))
    frames_in, rows, columns, chans = sources[0].shape
    edge = jnp.zeros((2, 2 * frames_in, rows, reach, chans), F32)
    wide_ref[:, :, :, :reach] = edge
    wide_ref[:, :, :, reach + columns :] = edge
    for index, ref in enumerate(sources):
        whose = core if index % 2 == 0 else 1 - core
        wide_ref[index // 2, pl.ds(whose * frames_in, frames_in), :, reach : reach + columns] = ref[
            ...
        ].astype(F32)
    own = width - 2 * reach
    for step, target in enumerate(targets):
        at = (jnp.bitwise_xor(unit, step) * 2 + core) * own
        window = wide_ref[:, :, :, pl.ds(pl.multiple_of(at, 16), width)]
        target[...] = window.reshape(target.shape).astype(BF16)


def closing_kernel(group, mine_ref, other_ref, spatial_ref, temporal_ref, flat_ref):
    pieces, rows, chans = mine_ref.shape
    core, _, _, unit = placed(group)
    for whose, ref in ((core, mine_ref), (1 - core, other_ref)):
        for step in range(pieces):
            index = whose * pieces + jnp.bitwise_xor(jnp.bitwise_and(unit, pieces - 1), step)
            flat_ref[pl.ds(pl.multiple_of(index * rows, 16), rows)] = ref[step]
    count = spatial_ref.shape[1]
    for tap in range(count + temporal_ref.shape[1]):
        turned = flat_ref[tap * chans : (tap + 1) * chans].astype(F32).T
        if tap < count:
            spatial_ref[0, tap] = turned
        else:
            temporal_ref[0, tap - count] = turned


def place_kernels(core, section, w_ref, own_mine, own_other, mine_refs, other_refs):
    w_ref[core, section] = own_mine[...]
    w_ref[1 - core, section] = own_other[...]
    for step, (mine_ref, other_ref) in enumerate(zip(mine_refs, other_refs)):
        block = jnp.bitwise_xor(section, step + 1)
        w_ref[core, block] = mine_ref[...]
        w_ref[1 - core, block] = other_ref[...]


def forward_kernel(geometry, *rest):
    blocks, cores, group, frames_in, rows_in, halo, tile, width, height, columns = geometry
    core, section, band, unit = placed(group)
    odd = band % 2
    shared, rest = rest[: 2 * blocks], rest[2 * blocks :]
    arrived, rest = rest[:6], rest[6:]
    xo_ref, ho_ref = rest[:2]
    d_refs = rest[2 : 2 + blocks]
    x_ref, h_ref, mask_ref, w_ref, start_ref, pair_ref = rest[2 + blocks :]
    place_kernels(core, section, w_ref, *shared[:2], shared[2 : 1 + blocks], shared[1 + blocks :])
    frames = cores * frames_in
    high = tile + 2 * halo
    chans = w_ref.shape[-1]
    own_rows, own_cols = (halo, halo + tile), (halo, width - halo)
    row = band * tile - halo + lax.broadcasted_iota(jnp.int32, (high, width, chans), 0)
    left = (unit * cores + core) * (width - 2 * halo) - halo
    col = left + lax.broadcasted_iota(jnp.int32, (high, width, chans), 1)
    inside = (row >= 0) & (row < height) & (col >= 0) & (col < columns)
    mask_ref[...] = jnp.where(inside, 1.0, 0.0).astype(F32)

    def keep(block, frame, value, first):
        triple = [rolled(value, 1), value, rolled(value, -1)]
        count = value.shape[0] // width
        both = jnp.concatenate([part.astype(BF16) for part in triple], 1)
        x_ref[frame, first : first + count] = both.reshape(count, width, 3 * chans)
        start = own_rows[0] - 1 - first
        cut = [
            part.reshape(count, width, chans)[
                start : start + tile + 2, own_cols[0] : own_cols[1]
            ].astype(BF16)
            for part in triple
        ]
        xo_ref[block, frame] = jnp.concatenate(cut, 2)

    near = tile + halo - odd * (tile + halo)
    columns_at = pl.ds(pl.multiple_of(core * (width - 2 * halo), 16), width)
    for index, ref in enumerate(arrived):
        base = (halo, near, tile + halo - near)[index % 3]
        whose = core if index < 3 else 1 - core
        for step in range(group):
            row = base + jnp.bitwise_xor(unit, step) * rows_in
            start_ref[pl.ds(whose * frames_in, frames_in), pl.ds(row, rows_in)] = ref[
                step, :, :, columns_at, :
            ]
    for frame in range(frames):
        keep(0, frame, start_ref[frame].reshape(high * width, chans).astype(F32), 0)

    for block in range(blocks):
        first, last = block + 1, high - block - 1
        count = last - first
        pair_rows(w_ref, block, pair_ref)
        mask = mask_ref[first:last].reshape(count * width, chans)
        for frame in range(frames):
            taps = row_pairs(x_ref, frame, first - 1, count // 2)
            before = jnp.dot(taps, pair_ref[...], preferred_element_type=F32)
            before = woven(before, width)
            sigma = 0.5 + 0.5 * jnp.tanh(0.5 * before)
            masked = sigma * mask
            hidden = before * masked
            h_ref[frame, first:last] = hidden.astype(BF16).reshape(count, width, chans)
            hidden = hidden.reshape(count, width, chans)
            ho_ref[block, frame] = hidden[
                own_rows[0] - first : own_rows[1] - first, own_cols[0] : own_cols[1]
            ].astype(BF16)
            rim = block + 1
            kept = slice(own_rows[0] - rim - first, own_rows[1] + rim - first)
            sigma = sigma.reshape(count, width, chans)[kept]
            masked = masked.reshape(count, width, chans)[kept]
            d_refs[block][frame] = masked + hidden[kept] * (1.0 - sigma)
        if block + 1 == blocks:
            break
        for frame in range(0, frames, 2):
            start = max(frame - 2, 0)
            timeline = jnp.concatenate(
                [
                    h_ref[each, first:last].reshape(count * width, chans)
                    for each in range(start, frame + 2)
                ],
                1,
            )
            weights = pair_frames(w_ref, block, start, frame + 2 - start)
            both = jnp.dot(timeline, weights, preferred_element_type=F32)
            for inner in range(2):
                mixed = both[:, inner * chans : (inner + 1) * chans]
                old = x_ref[frame + inner, first:last, :, chans : 2 * chans].astype(F32)
                new = old.reshape(count * width, chans) + mixed
                keep(block + 1, frame + inner, new.astype(BF16).astype(F32), first)


def backward_kernel(geometry, factor, *rest):
    blocks, cores, group, frames_in, rows_in, halo, tile, width, height, columns = geometry
    core, section, band, unit = placed(group)
    shared, rest = rest[: 2 * blocks], rest[2 * blocks :]
    arrived, rest = rest[:group], rest[group:]
    xo_ref, ho_ref = rest[:2]
    d_refs = rest[2 : 2 + blocks]
    keep_ref, give_ref, mine_out, other_out = rest[2 + blocks : 6 + blocks]
    g_ref, da_ref, dao_ref, go_ref, w_ref, grad_ref, out_ref, pair_ref = rest[6 + blocks :]
    place_kernels(core, section, w_ref, *shared[:2], shared[2 : 1 + blocks], shared[1 + blocks :])
    frames = cores * frames_in
    chans = w_ref.shape[-1]
    rim = blocks
    own_cols = (halo, width - halo)
    per_core = w_ref.shape[2]
    pixels = tile * (own_cols[1] - own_cols[0])

    half = group // 2
    side = halo - rim
    edge = jnp.zeros((frames, rows_in, side, chans), F32)

    def widened(value):
        value = value.astype(F32).reshape(frames, rows_in, width - 2 * side, chans)
        return jnp.concatenate([edge, value, edge], 2).astype(BF16)

    for step, ref in enumerate(arrived):
        at = jnp.bitwise_xor(unit, step)
        g_ref[:, pl.ds(rim + at * rows_in, rows_in)] = widened(ref[0])
        beyond = jnp.where(at < half, rim + tile + at * rows_in, (at - half) * rows_in)
        g_ref[:, pl.ds(beyond, rows_in)] = widened(ref[1])

    def put(block, tap, value):
        slot = jnp.where(core == tap // per_core, 0, 1)
        where = jnp.bitwise_xor(section, block)
        grad_ref[slot, where, tap % per_core] = (value * factor).astype(BF16)

    for block in reversed(range(blocks)):
        edge = block + 1
        first, last = rim - edge, rim + tile + edge
        count = last - first
        for frame in range(frames):
            go_ref[frame] = g_ref[frame, rim : rim + tile].astype(F32)[
                :, own_cols[0] : own_cols[1]
            ].astype(BF16)
        pair_rows_back(w_ref, block, pair_ref)
        hiddens = []
        for frame in range(0, frames, 2):
            stop = min(frame + 4, frames)
            ahead = jnp.concatenate(
                [
                    g_ref[each, first:last].reshape(count * width, chans)
                    for each in range(frame, stop)
                ],
                1,
            )
            weights = pair_frames_back(w_ref, block, stop - frame)
            both = jnp.dot(ahead, weights, preferred_element_type=F32)
            hiddens += [both[:, :chans], both[:, chans:]]
        for frame in range(frames):
            hidden = hiddens[frame]
            slope = d_refs[block][frame].reshape(count * width, chans)
            value = (hidden * slope).astype(BF16).astype(F32)
            triple = [rolled(value, -1), value, rolled(value, 1)]
            both = jnp.concatenate([part.astype(BF16) for part in triple], 1)
            da_ref[frame, first:last] = both.reshape(count, width, 3 * chans)
            dao_ref[frame] = value.reshape(count, width, chans)[
                edge : edge + tile, own_cols[0] : own_cols[1]
            ].astype(BF16)
        for frame in range(frames):
            inner = count - 2
            taps = row_pairs(da_ref, frame, first, inner // 2)
            back = woven(jnp.dot(taps, pair_ref[...], preferred_element_type=F32), width)
            old = g_ref[frame, first + 1 : last - 1].astype(F32).reshape(inner * width, chans)
            new = (old + back).astype(BF16)
            if block:
                g_ref[frame, first + 1 : last - 1] = new.reshape(inner, width, chans)
            else:
                cut = new.astype(F32).reshape(inner, width, chans)[:, own_cols[0] : own_cols[1]]
                out_ref[frame] = cut.astype(BF16)
        slopes = dao_ref[...].reshape(frames * pixels, chans)
        taps = [
            xo_ref[block, :, ky : ky + tile].reshape(frames * pixels, 3 * chans) for ky in range(3)
        ]
        sums = dot_first(slopes, jnp.concatenate(taps, 1))
        for tap in range(9):
            put(block, tap, sums[:, tap * chans : (tap + 1) * chans])
        before = jnp.zeros((2 * pixels, chans), BF16)
        earlier = ho_ref[block].reshape(frames * pixels, chans)
        earlier = jnp.concatenate([before, earlier], 0)
        timeline = [earlier[kt * pixels : (kt + frames) * pixels] for kt in range(3)]
        sums = dot_first(
            go_ref[...].reshape(frames * pixels, chans), jnp.concatenate(timeline, 1)
        )
        for kt in range(3):
            put(block, 9 + kt, sums[:, kt * chans : (kt + 1) * chans])
    keep_ref[...] = grad_ref[0]
    give_ref[...] = grad_ref[1]
    for whose, target in ((core, mine_out), (1 - core, other_out)):
        for step in range(group):
            row = jnp.bitwise_xor(unit, step) * rows_in
            target[step] = out_ref[pl.ds(whose * frames_in, frames_in), pl.ds(row, rows_in)]


def swapped(value, axis="tm", step=1):
    count = lax.axis_size(axis)
    return lax.ppermute(value, axis, [(i, i ^ step) for i in range(count)])


def on_device(video, cotangent, spatial_weights, temporal_weights):
    blocks, cores, tiles = (lax.axis_size(name) for name in ("section", "tm", "space"))
    frames_in, rows_in, columns, chans = video.shape
    halo = 2 * blocks
    tile = halo
    group = tile // rows_in
    parties = cores * group
    own_width = columns // parties
    width = own_width + 2 * halo
    span = cores * own_width + 2 * halo
    vmem = pl.BlockSpec(memory_space=pltpu.VMEM)
    params = pltpu.CompilerParams(vmem_limit_bytes=32 * 2**20)

    bands = blocks * tiles // group
    core, section, band, unit = placed(group)

    def traded(value, shift):
        pairs = []
        for one in range(bands):
            other = ((one + shift) ^ 1) - shift
            if 0 <= other < bands:
                pairs += [(one * group + i, other * group + i) for i in range(group)]
        return lax.ppermute(value, ("section", "space"), pairs)

    total_rows = blocks * tiles * rows_in
    half = group // 2
    passed = []
    for one in range(bands - 1):
        for i in range(group):
            low, high = one * group + i, (one + 1) * group + i
            passed.append((high, low) if i < half else (low, high))
    cot_halo = lax.ppermute(cotangent, ("section", "space"), passed)

    padded = columns + 2 * halo
    cuts = pl.pallas_call(
        functools.partial(window_kernel, halo, span),
        name="windows",
        in_specs=[vmem],
        out_specs=[vmem] * group,
        out_shape=[jax.ShapeDtypeStruct((frames_in, rows_in, span, chans), BF16)] * group,
        scratch_shapes=[pltpu.VMEM((frames_in, rows_in, padded, chans), F32)],
        compiler_params=params,
    )(video)
    *cuts, spatial, temporal = lax.optimization_barrier(
        list(cuts) + [spatial_weights, temporal_weights]
    )
    def core_half(which):
        whole = jnp.concatenate([spatial[0], temporal[0]], 0)
        taps = whole.shape[0] // cores
        return lax.dynamic_slice_in_dim(whole, which * taps, taps, 0)

    half_kernels = core_half(core)

    def gathered(pieces):
        return jnp.stack([pieces[0]] + [swapped(pieces[i], "space", i) for i in range(1, group)])

    along_x = swapped(half_kernels, "section", 1)
    along_y = swapped(half_kernels, "section", 2)
    own_video, along_x, along_y, spatial, temporal = lax.optimization_barrier(
        [gathered(cuts), along_x, along_y, spatial, temporal]
    )
    near, far = traded(own_video, 0), traded(own_video, 1)
    mine = [along_x, along_y, swapped(along_x, "section", 2)]
    shared = mine + [swapped(each) for each in mine]
    rest_kernels = core_half(1 - core)

    narrow = own_width + 2 * blocks
    cuts = pl.pallas_call(
        functools.partial(cotangent_kernel, blocks, narrow),
        name="cotangent",
        in_specs=[vmem] * 4,
        out_specs=[vmem] * group,
        out_shape=[jax.ShapeDtypeStruct((2, cores * frames_in, rows_in * narrow, chans), BF16)] * group,
        scratch_shapes=[
            pltpu.VMEM((2, cores * frames_in, rows_in, columns + 2 * blocks, chans), F32)
        ],
        compiler_params=params,
    )(cotangent, swapped(cotangent), cot_halo, swapped(cot_halo))
    near, rest_kernels, *cuts = lax.optimization_barrier([near, rest_kernels] + list(cuts))
    shared = [half_kernels, rest_kernels] + shared
    videos = [own_video, near, far]
    videos += [swapped(each) for each in videos]
    cots = [cuts[0]] + [swapped(cuts[i], "space", i) for i in range(1, group)]

    geometry = (blocks, cores, group, frames_in, rows_in, halo, tile, width, total_rows, columns)
    frames = cores * frames_in
    high = tile + 2 * halo
    per_section = (blocks,) + half_kernels.shape
    taps = half_kernels.shape[0]
    all_kernels = (cores,) + per_section
    saved = [
        jax.ShapeDtypeStruct((frames, tile + 2 * block + 2, width, chans), F32)
        for block in range(blocks)
    ]
    cost = pl.CostEstimate(flops=6 * 10**9, bytes_accessed=8 * 10**6, transcendentals=10**6)
    features, hidden, *slopes = pl.pallas_call(
        functools.partial(forward_kernel, geometry),
        name="forward",
        in_specs=[vmem] * (2 * blocks + 6),
        out_specs=[vmem] * (2 + blocks),
        out_shape=[
            jax.ShapeDtypeStruct((blocks, frames, tile + 2, own_width, 3 * chans), BF16),
            jax.ShapeDtypeStruct((blocks, frames, tile, own_width, chans), BF16),
        ]
        + saved,
        scratch_shapes=[
            pltpu.VMEM((frames, high, width, 3 * chans), BF16),
            pltpu.VMEM((frames, high, width, chans), BF16),
            pltpu.VMEM((high, width, chans), F32),
            pltpu.VMEM(all_kernels, BF16),
            pltpu.VMEM((frames, high, width, chans), BF16),
            pltpu.VMEM((12 * chans, 2 * chans), BF16),
        ],
        compiler_params=params,
        cost_estimate=cost,
    )(*shared, *videos)

    back = jax.ShapeDtypeStruct((group, frames_in, rows_in, own_width, chans), BF16)
    pixel_count = frames * total_rows * columns
    factor = 1.0 / float(pixel_count) ** 0.5
    keep, give, mine_grad, other_grad = pl.pallas_call(
        functools.partial(backward_kernel, geometry, factor),
        name="backward",
        in_specs=[vmem] * (3 * blocks + group + 2),
        out_specs=[vmem] * 4,
        out_shape=[
            jax.ShapeDtypeStruct(per_section, BF16),
            jax.ShapeDtypeStruct(per_section, BF16),
            back,
            back,
        ],
        scratch_shapes=[
            pltpu.VMEM((frames, tile + 2 * blocks, width, chans), BF16),
            pltpu.VMEM((frames, tile + 2 * blocks, width, 3 * chans), BF16),
            pltpu.VMEM((frames, tile, own_width, chans), BF16),
            pltpu.VMEM((frames, tile, own_width, chans), BF16),
            pltpu.VMEM(all_kernels, BF16),
            pltpu.VMEM(all_kernels, BF16),
            pltpu.VMEM((frames, tile, own_width, chans), BF16),
            pltpu.VMEM((12 * chans, 2 * chans), BF16),
        ],
        compiler_params=params,
        cost_estimate=cost,
    )(*shared, *cots, features, hidden, *slopes)

    got = swapped(give)
    parts = [(keep[i].astype(F32) + got[i].astype(F32)).astype(BF16) for i in range(blocks)]
    other_grad, *parts = lax.optimization_barrier([other_grad] + parts)
    parts = parts[:1] + [swapped(parts[i], "section", i) for i in range(1, blocks)]
    other_grad = swapped(other_grad)
    first = core == 0
    wide = jnp.concatenate(
        [jnp.where(first, mine_grad, other_grad), jnp.where(first, other_grad, mine_grad)], 3
    )
    strips = [wide[0]] + [swapped(wide[i], "space", i) for i in range(1, group)]
    received = lax.optimization_barrier(parts + strips)
    parts, strips = received[:blocks], received[blocks:]
    part = sum(each.astype(F32) for each in parts).astype(BF16)

    halves = part.reshape(2, -1, chans)
    low = unit % 2

    def picked(which):
        return lax.dynamic_index_in_dim(halves, which, 0, keepdims=False)

    part = (picked(low).astype(F32) + swapped(picked(1 - low), "space", 1).astype(F32)).astype(BF16)
    part = part.astype(F32) + swapped(part, "space", 2).astype(F32)
    if tiles != group:
        part = lax.psum(
            part, "space", axis_index_groups=[list(range(i, tiles, group)) for i in range(group)]
        )
    part = part.astype(BF16)
    pair = jnp.stack([part, swapped(part, "space", 1)])
    spatial_out, temporal_out = pl.pallas_call(
        functools.partial(closing_kernel, group),
        name="closing",
        in_specs=[vmem] * 2,
        out_specs=[vmem] * 2,
        out_shape=[
            jax.ShapeDtypeStruct(spatial_weights.shape, F32),
            jax.ShapeDtypeStruct(temporal_weights.shape, F32),
        ],
        scratch_shapes=[pltpu.VMEM((cores * taps * chans, chans), BF16)],
        compiler_params=params,
    )(pair, swapped(pair))

    grad_video = jnp.zeros(video.shape, BF16)
    for step, strip in enumerate(strips):
        grad_video = lax.dynamic_update_slice(
            grad_video, strip, (0, 0, (unit ^ step) * cores * own_width, 0)
        )
    return spatial_out, temporal_out, grad_video


def solution(mesh):
    return jax.shard_map(
        on_device,
        mesh=mesh,
        in_specs=(
            P("tm", ("section", "space"), None, None),
            P("tm", ("section", "space"), None, None),
            P("section", None, None, None),
            P("section", None, None, None),
        ),
        out_specs=(
            P("section", None, None, None),
            P("section", None, None, None),
            P("tm", ("section", "space"), None, None),
        ),
        check_vma=False,
    )
```

```python
import functools

import jax
import jax.numpy as jnp
from jax import lax
from jax.experimental import pallas as pl
from jax.experimental.pallas import tpu as pltpu
from jax.sharding import PartitionSpec as P

F32 = jnp.float32
BF16 = jnp.bfloat16


def rolled(value, steps):
    return pltpu.roll(value, steps % value.shape[0], 0)


def dot_first(left, right):
    return lax.dot_general(left, right, (((0,), (0,)), ((), ())), preferred_element_type=F32)


def kernel_of(w_ref, block, tap):
    taps = w_ref.shape[2]
    return w_ref[tap // taps, block, tap % taps]


def pair_rows(w_ref, block, pair_ref):
    chans = w_ref.shape[-1]
    for source in range(4):
        for target in range(2):
            ky = source - target
            for kx in range(3):
                at = (3 * source + kx) * chans
                tile = kernel_of(w_ref, block, 3 * ky + kx) if 0 <= ky < 3 else jnp.zeros((chans, chans), BF16)
                pair_ref[at : at + chans, target * chans : (target + 1) * chans] = tile


def turned(w_ref, block, tap):
    return kernel_of(w_ref, block, tap).astype(F32).T.astype(BF16)


def pair_rows_back(w_ref, block, pair_ref):
    chans = w_ref.shape[-1]
    nothing = jnp.zeros((chans, chans), BF16)
    for kx in range(3):
        for ky in range(3):
            tile = turned(w_ref, block, 3 * ky + kx)
            for target in range(2):
                at = (3 * (2 + target - ky) + kx) * chans
                pair_ref[at : at + chans, target * chans : (target + 1) * chans] = tile
        for source, target in ((3, 0), (0, 1)):
            at = (3 * source + kx) * chans
            pair_ref[at : at + chans, target * chans : (target + 1) * chans] = nothing


def pair_frames(w_ref, block, first, count):
    chans = w_ref.shape[-1]
    columns = []
    for target in (count - 2, count - 1):
        tiles = []
        for source in range(count):
            kt = source - target + 2
            tiles.append(kernel_of(w_ref, block, 9 + kt) if 0 <= kt < 3 else jnp.zeros((chans, chans), BF16))
        columns.append(jnp.concatenate(tiles, 0))
    return jnp.concatenate(columns, 1)


def pair_frames_back(w_ref, block, count):
    chans = w_ref.shape[-1]
    tiles = [turned(w_ref, block, 9 + kt) for kt in range(3)]
    columns = []
    for target in range(2):
        column = []
        for source in range(count):
            kt = 2 - (source - target)
            column.append(tiles[kt] if 0 <= kt < 3 else jnp.zeros((chans, chans), BF16))
        columns.append(jnp.concatenate(column, 0))
    return jnp.concatenate(columns, 1)


def row_pairs(ref, frame, first, pairs):
    width, lanes = ref.shape[2:]
    rows = []
    for start in (first, first + 2):
        value = ref[frame, start : start + 2 * pairs].reshape(pairs, 2, width, lanes)
        rows += [value[:, 0], value[:, 1]]
    return jnp.concatenate(rows, 2).reshape(pairs * width, 4 * lanes)


def woven(value, width):
    chans = value.shape[1] // 2
    split = [value[:, i * chans : (i + 1) * chans].reshape(-1, 1, width, chans) for i in range(2)]
    return jnp.concatenate(split, 1).reshape(-1, chans)


def ordered(count):
    return [0] + list(range(count - 1, 0, -1))


def placed(group):
    place, section = lax.axis_index("space"), lax.axis_index("section")
    band = (section * lax.axis_size("space") + place) // group
    return lax.axis_index("tm"), section, band, place % group


def window_kernel(halo, span, video_ref, *rest):
    targets, wide_ref = rest[:-1], rest[-1]
    unit = placed(len(targets))[3]
    frames, rows, columns, chans = video_ref.shape
    edge = jnp.zeros((frames, rows, halo, chans), F32)
    wide_ref[:, :, :halo] = edge
    wide_ref[:, :, halo + columns :] = edge
    wide_ref[:, :, halo : halo + columns] = video_ref[...].astype(F32)
    for step, target in enumerate(targets):
        at = jnp.bitwise_xor(unit, step) * (span - 2 * halo)
        target[...] = wide_ref[:, :, pl.ds(pl.multiple_of(at, 16), span)].astype(BF16)


def cotangent_kernel(reach, width, *rest):
    sources, targets, wide_ref = rest[:4], rest[4:-1], rest[-1]
    core, _, _, unit = placed(len(targets))
    frames_in, rows, columns, chans = sources[0].shape
    edge = jnp.zeros((2, 2 * frames_in, rows, reach, chans), F32)
    wide_ref[:, :, :, :reach] = edge
    wide_ref[:, :, :, reach + columns :] = edge
    for index, ref in enumerate(sources):
        whose = core if index % 2 == 0 else 1 - core
        wide_ref[index // 2, pl.ds(whose * frames_in, frames_in), :, reach : reach + columns] = ref[
            ...
        ].astype(F32)
    own = width - 2 * reach
    for step, target in enumerate(targets):
        at = (jnp.bitwise_xor(unit, step) * 2 + core) * own
        window = wide_ref[:, :, :, pl.ds(pl.multiple_of(at, 16), width)]
        target[...] = window.reshape(target.shape).astype(BF16)


def closing_kernel(group, mine_ref, other_ref, spatial_ref, temporal_ref, flat_ref):
    pieces, rows, chans = mine_ref.shape
    core, _, _, unit = placed(group)
    for whose, ref in ((core, mine_ref), (1 - core, other_ref)):
        for step in range(pieces):
            index = whose * pieces + jnp.bitwise_xor(jnp.bitwise_and(unit, pieces - 1), step)
            flat_ref[pl.ds(pl.multiple_of(index * rows, 16), rows)] = ref[step]
    count = spatial_ref.shape[1]
    for tap in range(count + temporal_ref.shape[1]):
        turned = flat_ref[tap * chans : (tap + 1) * chans].astype(F32).T
        if tap < count:
            spatial_ref[0, tap] = turned
        else:
            temporal_ref[0, tap - count] = turned


def place_kernels(core, section, w_ref, own_mine, own_other, mine_refs, other_refs):
    w_ref[core, section] = own_mine[...]
    w_ref[1 - core, section] = own_other[...]
    for step, (mine_ref, other_ref) in enumerate(zip(mine_refs, other_refs)):
        block = jnp.bitwise_xor(section, step + 1)
        w_ref[core, block] = mine_ref[...]
        w_ref[1 - core, block] = other_ref[...]


def forward_kernel(geometry, *rest):
    blocks, cores, group, frames_in, rows_in, halo, tile, width, height, columns = geometry
    core, section, band, unit = placed(group)
    odd = band % 2
    shared, rest = rest[: 2 * blocks], rest[2 * blocks :]
    arrived, rest = rest[:6], rest[6:]
    xo_ref, ho_ref = rest[:2]
    d_refs = rest[2 : 2 + blocks]
    x_ref, h_ref, mask_ref, w_ref, start_ref, pair_ref = rest[2 + blocks :]
    place_kernels(core, section, w_ref, *shared[:2], shared[2 : 1 + blocks], shared[1 + blocks :])
    frames = cores * frames_in
    high = tile + 2 * halo
    chans = w_ref.shape[-1]
    own_rows, own_cols = (halo, halo + tile), (halo, width - halo)
    row = band * tile - halo + lax.broadcasted_iota(jnp.int32, (high, width, chans), 0)
    left = (unit * cores + core) * (width - 2 * halo) - halo
    col = left + lax.broadcasted_iota(jnp.int32, (high, width, chans), 1)
    inside = (row >= 0) & (row < height) & (col >= 0) & (col < columns)
    mask_ref[...] = jnp.where(inside, 1.0, 0.0).astype(F32)

    def keep(block, frame, value, first):
        triple = [rolled(value, 1), value, rolled(value, -1)]
        count = value.shape[0] // width
        both = jnp.concatenate([part.astype(BF16) for part in triple], 1)
        x_ref[frame, first : first + count] = both.reshape(count, width, 3 * chans)
        start = own_rows[0] - 1 - first
        cut = [
            part.reshape(count, width, chans)[
                start : start + tile + 2, own_cols[0] : own_cols[1]
            ].astype(BF16)
            for part in triple
        ]
        xo_ref[block, frame] = jnp.concatenate(cut, 2)

    near = tile + halo - odd * (tile + halo)
    columns_at = pl.ds(pl.multiple_of(core * (width - 2 * halo), 16), width)
    for index, ref in enumerate(arrived):
        base = (halo, near, tile + halo - near)[index % 3]
        whose = core if index < 3 else 1 - core
        for piece, step in enumerate(ordered(group)):
            row = base + jnp.bitwise_xor(unit, step) * rows_in
            start_ref[pl.ds(whose * frames_in, frames_in), pl.ds(row, rows_in)] = ref[
                piece, :, :, columns_at, :
            ]
    for frame in range(frames):
        keep(0, frame, start_ref[frame].reshape(high * width, chans).astype(F32), 0)

    for block in range(blocks):
        first, last = block + 1, high - block - 1
        count = last - first
        pair_rows(w_ref, block, pair_ref)
        mask = mask_ref[first:last].reshape(count * width, chans)
        for frame in range(frames):
            taps = row_pairs(x_ref, frame, first - 1, count // 2)
            before = jnp.dot(taps, pair_ref[...], preferred_element_type=F32)
            before = woven(before, width)
            sigma = 0.5 + 0.5 * jnp.tanh(0.5 * before)
            masked = sigma * mask
            hidden = before * masked
            h_ref[frame, first:last] = hidden.astype(BF16).reshape(count, width, chans)
            hidden = hidden.reshape(count, width, chans)
            ho_ref[block, frame] = hidden[
                own_rows[0] - first : own_rows[1] - first, own_cols[0] : own_cols[1]
            ].astype(BF16)
            rim = block + 1
            kept = slice(own_rows[0] - rim - first, own_rows[1] + rim - first)
            sigma = sigma.reshape(count, width, chans)[kept]
            masked = masked.reshape(count, width, chans)[kept]
            d_refs[block][frame] = masked + hidden[kept] * (1.0 - sigma)
        if block + 1 == blocks:
            break
        for frame in range(0, frames, 2):
            start = max(frame - 2, 0)
            timeline = jnp.concatenate(
                [
                    h_ref[each, first:last].reshape(count * width, chans)
                    for each in range(start, frame + 2)
                ],
                1,
            )
            weights = pair_frames(w_ref, block, start, frame + 2 - start)
            both = jnp.dot(timeline, weights, preferred_element_type=F32)
            for inner in range(2):
                mixed = both[:, inner * chans : (inner + 1) * chans]
                old = x_ref[frame + inner, first:last, :, chans : 2 * chans].astype(F32)
                new = old.reshape(count * width, chans) + mixed
                keep(block + 1, frame + inner, new.astype(BF16).astype(F32), first)


def backward_kernel(geometry, factor, *rest):
    blocks, cores, group, frames_in, rows_in, halo, tile, width, height, columns = geometry
    core, section, band, unit = placed(group)
    shared, rest = rest[: 2 * blocks], rest[2 * blocks :]
    arrived, rest = rest[:group], rest[group:]
    xo_ref, ho_ref = rest[:2]
    d_refs = rest[2 : 2 + blocks]
    keep_ref, give_ref, mine_out, other_out = rest[2 + blocks : 6 + blocks]
    g_ref, da_ref, dao_ref, go_ref, w_ref, grad_ref, out_ref, pair_ref = rest[6 + blocks :]
    place_kernels(core, section, w_ref, *shared[:2], shared[2 : 1 + blocks], shared[1 + blocks :])
    frames = cores * frames_in
    chans = w_ref.shape[-1]
    rim = blocks
    own_cols = (halo, width - halo)
    per_core = w_ref.shape[2]
    pixels = tile * (own_cols[1] - own_cols[0])

    half = group // 2
    side = halo - rim
    edge = jnp.zeros((frames, rows_in, side, chans), F32)

    def widened(value):
        value = value.astype(F32).reshape(frames, rows_in, width - 2 * side, chans)
        return jnp.concatenate([edge, value, edge], 2).astype(BF16)

    for step, ref in zip(ordered(group), arrived):
        at = jnp.bitwise_xor(unit, step)
        g_ref[:, pl.ds(rim + at * rows_in, rows_in)] = widened(ref[0])
        beyond = jnp.where(at < half, rim + tile + at * rows_in, (at - half) * rows_in)
        g_ref[:, pl.ds(beyond, rows_in)] = widened(ref[1])

    def put(block, tap, value):
        slot = jnp.where(core == tap // per_core, 0, 1)
        where = jnp.bitwise_xor(section, block)
        grad_ref[slot, where, tap % per_core] = (value * factor).astype(BF16)

    for block in reversed(range(blocks)):
        edge = block + 1
        first, last = rim - edge, rim + tile + edge
        count = last - first
        for frame in range(frames):
            go_ref[frame] = g_ref[frame, rim : rim + tile].astype(F32)[
                :, own_cols[0] : own_cols[1]
            ].astype(BF16)
        pair_rows_back(w_ref, block, pair_ref)
        hiddens = []
        for frame in range(0, frames, 2):
            stop = min(frame + 4, frames)
            ahead = jnp.concatenate(
                [
                    g_ref[each, first:last].reshape(count * width, chans)
                    for each in range(frame, stop)
                ],
                1,
            )
            weights = pair_frames_back(w_ref, block, stop - frame)
            both = jnp.dot(ahead, weights, preferred_element_type=F32)
            hiddens += [both[:, :chans], both[:, chans:]]
        for frame in range(frames):
            hidden = hiddens[frame]
            slope = d_refs[block][frame].reshape(count * width, chans)
            value = (hidden * slope).astype(BF16).astype(F32)
            triple = [rolled(value, -1), value, rolled(value, 1)]
            both = jnp.concatenate([part.astype(BF16) for part in triple], 1)
            da_ref[frame, first:last] = both.reshape(count, width, 3 * chans)
            dao_ref[frame] = value.reshape(count, width, chans)[
                edge : edge + tile, own_cols[0] : own_cols[1]
            ].astype(BF16)
        for frame in range(frames):
            inner = count - 2
            taps = row_pairs(da_ref, frame, first, inner // 2)
            back = woven(jnp.dot(taps, pair_ref[...], preferred_element_type=F32), width)
            old = g_ref[frame, first + 1 : last - 1].astype(F32).reshape(inner * width, chans)
            new = (old + back).astype(BF16)
            if block:
                g_ref[frame, first + 1 : last - 1] = new.reshape(inner, width, chans)
            else:
                cut = new.astype(F32).reshape(inner, width, chans)[:, own_cols[0] : own_cols[1]]
                out_ref[frame] = cut.astype(BF16)
        slopes = dao_ref[...].reshape(frames * pixels, chans)
        taps = [
            xo_ref[block, :, ky : ky + tile].reshape(frames * pixels, 3 * chans) for ky in range(3)
        ]
        sums = dot_first(slopes, jnp.concatenate(taps, 1))
        for tap in range(9):
            put(block, tap, sums[:, tap * chans : (tap + 1) * chans])
        before = jnp.zeros((2 * pixels, chans), BF16)
        earlier = ho_ref[block].reshape(frames * pixels, chans)
        earlier = jnp.concatenate([before, earlier], 0)
        timeline = [earlier[kt * pixels : (kt + frames) * pixels] for kt in range(3)]
        sums = dot_first(
            go_ref[...].reshape(frames * pixels, chans), jnp.concatenate(timeline, 1)
        )
        for kt in range(3):
            put(block, 9 + kt, sums[:, kt * chans : (kt + 1) * chans])
    keep_ref[...] = grad_ref[0]
    give_ref[...] = grad_ref[1]
    for whose, target in ((core, mine_out), (1 - core, other_out)):
        for step in range(group):
            row = jnp.bitwise_xor(unit, step) * rows_in
            target[step] = out_ref[pl.ds(whose * frames_in, frames_in), pl.ds(row, rows_in)]


def swapped(value, axis="tm", step=1):
    count = lax.axis_size(axis)
    return lax.ppermute(value, axis, [(i, i ^ step) for i in range(count)])


def exchanged(pieces, axis):
    return [swapped(pieces[i], axis, i) if i else pieces[0] for i in ordered(len(pieces))]


def on_device(video, cotangent, spatial_weights, temporal_weights):
    blocks, cores, tiles = (lax.axis_size(name) for name in ("section", "tm", "space"))
    frames_in, rows_in, columns, chans = video.shape
    halo = 2 * blocks
    tile = halo
    group = tile // rows_in
    parties = cores * group
    own_width = columns // parties
    width = own_width + 2 * halo
    span = cores * own_width + 2 * halo
    vmem = pl.BlockSpec(memory_space=pltpu.VMEM)
    params = pltpu.CompilerParams(vmem_limit_bytes=32 * 2**20)

    bands = blocks * tiles // group
    core, section, band, unit = placed(group)

    def traded(value, shift):
        pairs = []
        for one in range(bands):
            other = ((one + shift) ^ 1) - shift
            if 0 <= other < bands:
                pairs += [(one * group + i, other * group + i) for i in range(group)]
        return lax.ppermute(value, ("section", "space"), pairs)

    total_rows = blocks * tiles * rows_in
    half = group // 2
    passed = []
    for one in range(bands - 1):
        for i in range(group):
            low, high = one * group + i, (one + 1) * group + i
            passed.append((high, low) if i < half else (low, high))
    cot_halo = lax.ppermute(cotangent, ("section", "space"), passed)

    padded = columns + 2 * halo
    cuts = pl.pallas_call(
        functools.partial(window_kernel, halo, span),
        name="windows",
        in_specs=[vmem],
        out_specs=[vmem] * group,
        out_shape=[jax.ShapeDtypeStruct((frames_in, rows_in, span, chans), BF16)] * group,
        scratch_shapes=[pltpu.VMEM((frames_in, rows_in, padded, chans), F32)],
        compiler_params=params,
    )(video)
    *cuts, spatial, temporal = lax.optimization_barrier(
        list(cuts) + [spatial_weights, temporal_weights]
    )
    def core_half(which):
        whole = jnp.concatenate([spatial[0], temporal[0]], 0)
        taps = whole.shape[0] // cores
        return lax.dynamic_slice_in_dim(whole, which * taps, taps, 0)

    half_kernels = core_half(core)

    def gathered(pieces):
        return jnp.stack(exchanged(pieces, "space"))

    along_x = swapped(half_kernels, "section", 1)
    along_y = swapped(half_kernels, "section", 2)
    own_video, along_x, along_y, spatial, temporal = lax.optimization_barrier(
        [gathered(cuts), along_x, along_y, spatial, temporal]
    )
    near, far = traded(own_video, 0), traded(own_video, 1)
    mine = [along_x, along_y, swapped(along_x, "section", 2)]
    shared = mine + [swapped(each) for each in mine]
    rest_kernels = core_half(1 - core)

    narrow = own_width + 2 * blocks
    cuts = pl.pallas_call(
        functools.partial(cotangent_kernel, blocks, narrow),
        name="cotangent",
        in_specs=[vmem] * 4,
        out_specs=[vmem] * group,
        out_shape=[jax.ShapeDtypeStruct((2, cores * frames_in, rows_in * narrow, chans), BF16)] * group,
        scratch_shapes=[
            pltpu.VMEM((2, cores * frames_in, rows_in, columns + 2 * blocks, chans), F32)
        ],
        compiler_params=params,
    )(cotangent, swapped(cotangent), cot_halo, swapped(cot_halo))
    near, rest_kernels, *cuts = lax.optimization_barrier([near, rest_kernels] + list(cuts))
    shared = [half_kernels, rest_kernels] + shared
    videos = [own_video, near, far]
    videos += [swapped(each) for each in videos]
    cots = exchanged(cuts, "space")

    geometry = (blocks, cores, group, frames_in, rows_in, halo, tile, width, total_rows, columns)
    frames = cores * frames_in
    high = tile + 2 * halo
    per_section = (blocks,) + half_kernels.shape
    taps = half_kernels.shape[0]
    all_kernels = (cores,) + per_section
    saved = [
        jax.ShapeDtypeStruct((frames, tile + 2 * block + 2, width, chans), F32)
        for block in range(blocks)
    ]
    cost = pl.CostEstimate(flops=6 * 10**9, bytes_accessed=8 * 10**6, transcendentals=10**6)
    features, hidden, *slopes = pl.pallas_call(
        functools.partial(forward_kernel, geometry),
        name="forward",
        in_specs=[vmem] * (2 * blocks + 6),
        out_specs=[vmem] * (2 + blocks),
        out_shape=[
            jax.ShapeDtypeStruct((blocks, frames, tile + 2, own_width, 3 * chans), BF16),
            jax.ShapeDtypeStruct((blocks, frames, tile, own_width, chans), BF16),
        ]
        + saved,
        scratch_shapes=[
            pltpu.VMEM((frames, high, width, 3 * chans), BF16),
            pltpu.VMEM((frames, high, width, chans), BF16),
            pltpu.VMEM((high, width, chans), F32),
            pltpu.VMEM(all_kernels, BF16),
            pltpu.VMEM((frames, high, width, chans), BF16),
            pltpu.VMEM((12 * chans, 2 * chans), BF16),
        ],
        compiler_params=params,
        cost_estimate=cost,
    )(*shared, *videos)

    back = jax.ShapeDtypeStruct((group, frames_in, rows_in, own_width, chans), BF16)
    pixel_count = frames * total_rows * columns
    factor = 1.0 / float(pixel_count) ** 0.5
    keep, give, mine_grad, other_grad = pl.pallas_call(
        functools.partial(backward_kernel, geometry, factor),
        name="backward",
        in_specs=[vmem] * (3 * blocks + group + 2),
        out_specs=[vmem] * 4,
        out_shape=[
            jax.ShapeDtypeStruct(per_section, BF16),
            jax.ShapeDtypeStruct(per_section, BF16),
            back,
            back,
        ],
        scratch_shapes=[
            pltpu.VMEM((frames, tile + 2 * blocks, width, chans), BF16),
            pltpu.VMEM((frames, tile + 2 * blocks, width, 3 * chans), BF16),
            pltpu.VMEM((frames, tile, own_width, chans), BF16),
            pltpu.VMEM((frames, tile, own_width, chans), BF16),
            pltpu.VMEM(all_kernels, BF16),
            pltpu.VMEM(all_kernels, BF16),
            pltpu.VMEM((frames, tile, own_width, chans), BF16),
            pltpu.VMEM((12 * chans, 2 * chans), BF16),
        ],
        compiler_params=params,
        cost_estimate=cost,
    )(*shared, *cots, features, hidden, *slopes)

    got = swapped(give)
    parts = [(keep[i].astype(F32) + got[i].astype(F32)).astype(BF16) for i in range(blocks)]
    other_grad, *parts = lax.optimization_barrier([other_grad] + parts)
    parts = exchanged(parts, "section")
    other_grad = swapped(other_grad)
    first = core == 0
    wide = jnp.concatenate(
        [jnp.where(first, mine_grad, other_grad), jnp.where(first, other_grad, mine_grad)], 3
    )
    strips = exchanged([wide[i] for i in range(group)], "space")
    received = lax.optimization_barrier(parts + strips)
    parts, strips = received[:blocks], received[blocks:]
    part = sum(each.astype(F32) for each in parts).astype(BF16)

    halves = part.reshape(2, -1, chans)
    low = unit % 2

    def picked(which):
        return lax.dynamic_index_in_dim(halves, which, 0, keepdims=False)

    part = (picked(low).astype(F32) + swapped(picked(1 - low), "space", 1).astype(F32)).astype(BF16)
    part = part.astype(F32) + swapped(part, "space", 2).astype(F32)
    if tiles != group:
        part = lax.psum(
            part, "space", axis_index_groups=[list(range(i, tiles, group)) for i in range(group)]
        )
    part = part.astype(BF16)
    pair = jnp.stack([part, swapped(part, "space", 1)])
    spatial_out, temporal_out = pl.pallas_call(
        functools.partial(closing_kernel, group),
        name="closing",
        in_specs=[vmem] * 2,
        out_specs=[vmem] * 2,
        out_shape=[
            jax.ShapeDtypeStruct(spatial_weights.shape, F32),
            jax.ShapeDtypeStruct(temporal_weights.shape, F32),
        ],
        scratch_shapes=[pltpu.VMEM((cores * taps * chans, chans), BF16)],
        compiler_params=params,
    )(pair, swapped(pair))

    grad_video = jnp.zeros(video.shape, BF16)
    for step, strip in zip(ordered(group), strips):
        grad_video = lax.dynamic_update_slice(
            grad_video, strip, (0, 0, (unit ^ step) * cores * own_width, 0)
        )
    return spatial_out, temporal_out, grad_video


def solution(mesh):
    return jax.shard_map(
        on_device,
        mesh=mesh,
        in_specs=(
            P("tm", ("section", "space"), None, None),
            P("tm", ("section", "space"), None, None),
            P("section", None, None, None),
            P("section", None, None, None),
        ),
        out_specs=(
            P("section", None, None, None),
            P("section", None, None, None),
            P("tm", ("section", "space"), None, None),
        ),
        check_vma=False,
    )
```

```python
import functools

import jax
import jax.numpy as jnp
from jax import lax
from jax.experimental import pallas as pl
from jax.experimental.pallas import tpu as pltpu
from jax.sharding import PartitionSpec as P

F32 = jnp.float32
BF16 = jnp.bfloat16


def rolled(value, steps):
    return pltpu.roll(value, steps % value.shape[0], 0)


def dot_first(left, right):
    return lax.dot_general(left, right, (((0,), (0,)), ((), ())), preferred_element_type=F32)


def kernel_of(w_ref, block, tap):
    taps = w_ref.shape[2]
    return w_ref[tap // taps, block, tap % taps]


def pair_rows(w_ref, block, pair_ref):
    chans = w_ref.shape[-1]
    for source in range(4):
        for target in range(2):
            ky = source - target
            for kx in range(3):
                at = (3 * source + kx) * chans
                tile = kernel_of(w_ref, block, 3 * ky + kx) if 0 <= ky < 3 else jnp.zeros((chans, chans), BF16)
                pair_ref[at : at + chans, target * chans : (target + 1) * chans] = tile


def turned(w_ref, block, tap):
    return kernel_of(w_ref, block, tap).astype(F32).T.astype(BF16)


def pair_rows_back(w_ref, block, pair_ref):
    chans = w_ref.shape[-1]
    nothing = jnp.zeros((chans, chans), BF16)
    for kx in range(3):
        for ky in range(3):
            tile = turned(w_ref, block, 3 * ky + kx)
            for target in range(2):
                at = (3 * (2 + target - ky) + kx) * chans
                pair_ref[at : at + chans, target * chans : (target + 1) * chans] = tile
        for source, target in ((3, 0), (0, 1)):
            at = (3 * source + kx) * chans
            pair_ref[at : at + chans, target * chans : (target + 1) * chans] = nothing


def pair_frames(w_ref, block, first, count):
    chans = w_ref.shape[-1]
    columns = []
    for target in (count - 2, count - 1):
        tiles = []
        for source in range(count):
            kt = source - target + 2
            tiles.append(kernel_of(w_ref, block, 9 + kt) if 0 <= kt < 3 else jnp.zeros((chans, chans), BF16))
        columns.append(jnp.concatenate(tiles, 0))
    return jnp.concatenate(columns, 1)


def pair_frames_back(w_ref, block, count):
    chans = w_ref.shape[-1]
    tiles = [turned(w_ref, block, 9 + kt) for kt in range(3)]
    columns = []
    for target in range(2):
        column = []
        for source in range(count):
            kt = 2 - (source - target)
            column.append(tiles[kt] if 0 <= kt < 3 else jnp.zeros((chans, chans), BF16))
        columns.append(jnp.concatenate(column, 0))
    return jnp.concatenate(columns, 1)


def row_pairs(ref, frame, first, pairs):
    width, lanes = ref.shape[2:]
    rows = []
    for start in (first, first + 2):
        value = ref[frame, start : start + 2 * pairs].reshape(pairs, 2, width, lanes)
        rows += [value[:, 0], value[:, 1]]
    return jnp.concatenate(rows, 2).reshape(pairs * width, 4 * lanes)


def woven(value, width):
    chans = value.shape[1] // 2
    split = [value[:, i * chans : (i + 1) * chans].reshape(-1, 1, width, chans) for i in range(2)]
    return jnp.concatenate(split, 1).reshape(-1, chans)


def placed(group):
    place, section = lax.axis_index("space"), lax.axis_index("section")
    band = (section * lax.axis_size("space") + place) // group
    return lax.axis_index("tm"), section, band, place % group


def window_kernel(halo, span, video_ref, *rest):
    targets, wide_ref = rest[:-1], rest[-1]
    unit = placed(len(targets))[3]
    frames, rows, columns, chans = video_ref.shape
    edge = jnp.zeros((frames, rows, halo, chans), F32)
    wide_ref[:, :, :halo] = edge
    wide_ref[:, :, halo + columns :] = edge
    wide_ref[:, :, halo : halo + columns] = video_ref[...].astype(F32)
    for step, target in enumerate(targets):
        at = jnp.bitwise_xor(unit, step) * (span - 2 * halo)
        target[...] = wide_ref[:, :, pl.ds(pl.multiple_of(at, 16), span)].astype(BF16)


def cotangent_kernel(reach, width, *rest):
    sources, targets, wide_ref = rest[:4], rest[4:-1], rest[-1]
    core, _, _, unit = placed(len(targets))
    frames_in, rows, columns, chans = sources[0].shape
    edge = jnp.zeros((2, 2 * frames_in, rows, reach, chans), F32)
    wide_ref[:, :, :, :reach] = edge
    wide_ref[:, :, :, reach + columns :] = edge
    for index, ref in enumerate(sources):
        whose = core if index % 2 == 0 else 1 - core
        wide_ref[index // 2, pl.ds(whose * frames_in, frames_in), :, reach : reach + columns] = ref[
            ...
        ].astype(F32)
    own = width - 2 * reach
    for step, target in enumerate(targets):
        at = (jnp.bitwise_xor(unit, step) * 2 + core) * own
        window = wide_ref[:, :, :, pl.ds(pl.multiple_of(at, 16), width)]
        target[...] = window.reshape(target.shape).astype(BF16)


def closing_kernel(group, mine_ref, other_ref, spatial_ref, temporal_ref, flat_ref):
    pieces, rows, chans = mine_ref.shape
    core, _, _, unit = placed(group)
    for whose, ref in ((core, mine_ref), (1 - core, other_ref)):
        for step in range(pieces):
            index = whose * pieces + jnp.bitwise_xor(jnp.bitwise_and(unit, pieces - 1), step)
            flat_ref[pl.ds(pl.multiple_of(index * rows, 16), rows)] = ref[step]
    count = spatial_ref.shape[1]
    for tap in range(count + temporal_ref.shape[1]):
        turned = flat_ref[tap * chans : (tap + 1) * chans].astype(F32).T
        if tap < count:
            spatial_ref[0, tap] = turned
        else:
            temporal_ref[0, tap - count] = turned


def place_kernels(core, section, w_ref, own_mine, own_other, mine_refs, other_refs):
    w_ref[core, section] = own_mine[...]
    w_ref[1 - core, section] = own_other[...]
    for step, (mine_ref, other_ref) in enumerate(zip(mine_refs, other_refs)):
        block = jnp.bitwise_xor(section, step + 1)
        w_ref[core, block] = mine_ref[...]
        w_ref[1 - core, block] = other_ref[...]


def forward_kernel(geometry, *rest):
    blocks, cores, group, frames_in, rows_in, halo, tile, width, height, columns = geometry
    core, section, band, unit = placed(group)
    odd = band % 2
    shared, rest = rest[: 2 * blocks], rest[2 * blocks :]
    arrived, rest = rest[:6], rest[6:]
    xo_ref, ho_ref = rest[:2]
    d_refs = rest[2 : 2 + blocks]
    x_ref, h_ref, mask_ref, w_ref, start_ref, pair_ref = rest[2 + blocks :]
    place_kernels(core, section, w_ref, *shared[:2], shared[2 : 1 + blocks], shared[1 + blocks :])
    frames = cores * frames_in
    high = tile + 2 * halo
    chans = w_ref.shape[-1]
    own_rows, own_cols = (halo, halo + tile), (halo, width - halo)
    row = band * tile - halo + lax.broadcasted_iota(jnp.int32, (high, width, chans), 0)
    left = (unit * cores + core) * (width - 2 * halo) - halo
    col = left + lax.broadcasted_iota(jnp.int32, (high, width, chans), 1)
    inside = (row >= 0) & (row < height) & (col >= 0) & (col < columns)
    mask_ref[...] = jnp.where(inside, 1.0, 0.0).astype(F32)

    def keep(block, frame, value, first):
        triple = [rolled(value, 1), value, rolled(value, -1)]
        count = value.shape[0] // width
        both = jnp.concatenate([part.astype(BF16) for part in triple], 1)
        x_ref[frame, first : first + count] = both.reshape(count, width, 3 * chans)
        start = own_rows[0] - 1 - first
        cut = [
            part.reshape(count, width, chans)[
                start : start + tile + 2, own_cols[0] : own_cols[1]
            ].astype(BF16)
            for part in triple
        ]
        xo_ref[block, frame] = jnp.concatenate(cut, 2)

    near = tile + halo - odd * (tile + halo)
    columns_at = pl.ds(pl.multiple_of(core * (width - 2 * halo), 16), width)
    for index, ref in enumerate(arrived):
        base = (halo, near, tile + halo - near)[index % 3]
        whose = core if index < 3 else 1 - core
        for step in range(group):
            row = base + jnp.bitwise_xor(unit, step) * rows_in
            start_ref[pl.ds(whose * frames_in, frames_in), pl.ds(row, rows_in)] = ref[
                step, :, :, columns_at, :
            ]
    for frame in range(frames):
        keep(0, frame, start_ref[frame].reshape(high * width, chans).astype(F32), 0)

    for block in range(blocks):
        first, last = block + 1, high - block - 1
        count = last - first
        pair_rows(w_ref, block, pair_ref)
        mask = mask_ref[first:last].reshape(count * width, chans)
        for frame in range(frames):
            taps = row_pairs(x_ref, frame, first - 1, count // 2)
            before = jnp.dot(taps, pair_ref[...], preferred_element_type=F32)
            before = woven(before, width)
            sigma = 0.5 + 0.5 * jnp.tanh(0.5 * before)
            masked = sigma * mask
            hidden = before * masked
            h_ref[frame, first:last] = hidden.astype(BF16).reshape(count, width, chans)
            hidden = hidden.reshape(count, width, chans)
            ho_ref[block, frame] = hidden[
                own_rows[0] - first : own_rows[1] - first, own_cols[0] : own_cols[1]
            ].astype(BF16)
            rim = block + 1
            kept = slice(own_rows[0] - rim - first, own_rows[1] + rim - first)
            sigma = sigma.reshape(count, width, chans)[kept]
            masked = masked.reshape(count, width, chans)[kept]
            d_refs[block][frame] = masked + hidden[kept] * (1.0 - sigma)
        if block + 1 == blocks:
            break
        for frame in range(0, frames, 2):
            start = max(frame - 2, 0)
            timeline = jnp.concatenate(
                [
                    h_ref[each, first:last].reshape(count * width, chans)
                    for each in range(start, frame + 2)
                ],
                1,
            )
            weights = pair_frames(w_ref, block, start, frame + 2 - start)
            both = jnp.dot(timeline, weights, preferred_element_type=F32)
            for inner in range(2):
                mixed = both[:, inner * chans : (inner + 1) * chans]
                old = x_ref[frame + inner, first:last, :, chans : 2 * chans].astype(F32)
                new = old.reshape(count * width, chans) + mixed
                keep(block + 1, frame + inner, new.astype(BF16).astype(F32), first)


def backward_kernel(geometry, factor, *rest):
    blocks, cores, group, frames_in, rows_in, halo, tile, width, height, columns = geometry
    core, section, band, unit = placed(group)
    shared, rest = rest[: 2 * blocks], rest[2 * blocks :]
    arrived, rest = rest[:group], rest[group:]
    xo_ref, ho_ref = rest[:2]
    d_refs = rest[2 : 2 + blocks]
    keep_ref, give_ref, mine_out, other_out = rest[2 + blocks : 6 + blocks]
    g_ref, da_ref, dao_ref, go_ref, w_ref, grad_ref, out_ref, pair_ref = rest[6 + blocks :]
    place_kernels(core, section, w_ref, *shared[:2], shared[2 : 1 + blocks], shared[1 + blocks :])
    frames = cores * frames_in
    chans = w_ref.shape[-1]
    rim = blocks
    own_cols = (halo, width - halo)
    per_core = w_ref.shape[2]
    pixels = tile * (own_cols[1] - own_cols[0])

    half = group // 2
    side = halo - rim
    edge = jnp.zeros((frames, rows_in, side, chans), F32)

    def widened(value):
        value = value.astype(F32).reshape(frames, rows_in, width - 2 * side, chans)
        return jnp.concatenate([edge, value, edge], 2).astype(BF16)

    for step, ref in enumerate(arrived):
        at = jnp.bitwise_xor(unit, step)
        g_ref[:, pl.ds(rim + at * rows_in, rows_in)] = widened(ref[0])
        beyond = jnp.where(at < half, rim + tile + at * rows_in, (at - half) * rows_in)
        g_ref[:, pl.ds(beyond, rows_in)] = widened(ref[1])

    def put(block, tap, value):
        slot = jnp.where(core == tap // per_core, 0, 1)
        where = jnp.bitwise_xor(section, block)
        grad_ref[slot, where, tap % per_core] = (value * factor).astype(BF16)

    for block in reversed(range(blocks)):
        edge = block + 1
        first, last = rim - edge, rim + tile + edge
        count = last - first
        for frame in range(frames):
            go_ref[frame] = g_ref[frame, rim : rim + tile].astype(F32)[
                :, own_cols[0] : own_cols[1]
            ].astype(BF16)
        pair_rows_back(w_ref, block, pair_ref)
        hiddens = []
        for frame in range(0, frames, 2):
            stop = min(frame + 4, frames)
            ahead = jnp.concatenate(
                [
                    g_ref[each, first:last].reshape(count * width, chans)
                    for each in range(frame, stop)
                ],
                1,
            )
            weights = pair_frames_back(w_ref, block, stop - frame)
            both = jnp.dot(ahead, weights, preferred_element_type=F32)
            hiddens += [both[:, :chans], both[:, chans:]]
        for frame in range(frames):
            hidden = hiddens[frame]
            slope = d_refs[block][frame].reshape(count * width, chans)
            value = (hidden * slope).astype(BF16).astype(F32)
            triple = [rolled(value, -1), value, rolled(value, 1)]
            both = jnp.concatenate([part.astype(BF16) for part in triple], 1)
            da_ref[frame, first:last] = both.reshape(count, width, 3 * chans)
            dao_ref[frame] = value.reshape(count, width, chans)[
                edge : edge + tile, own_cols[0] : own_cols[1]
            ].astype(BF16)
        for frame in range(frames):
            inner = count - 2
            taps = row_pairs(da_ref, frame, first, inner // 2)
            back = woven(jnp.dot(taps, pair_ref[...], preferred_element_type=F32), width)
            old = g_ref[frame, first + 1 : last - 1].astype(F32).reshape(inner * width, chans)
            new = (old + back).astype(BF16)
            if block:
                g_ref[frame, first + 1 : last - 1] = new.reshape(inner, width, chans)
            else:
                cut = new.astype(F32).reshape(inner, width, chans)[:, own_cols[0] : own_cols[1]]
                out_ref[frame] = cut.astype(BF16)
        slopes = dao_ref[...].reshape(frames * pixels, chans)
        taps = [
            xo_ref[block, :, ky : ky + tile].reshape(frames * pixels, 3 * chans) for ky in range(3)
        ]
        sums = dot_first(slopes, jnp.concatenate(taps, 1))
        for tap in range(9):
            put(block, tap, sums[:, tap * chans : (tap + 1) * chans])
        before = jnp.zeros((2 * pixels, chans), BF16)
        earlier = ho_ref[block].reshape(frames * pixels, chans)
        earlier = jnp.concatenate([before, earlier], 0)
        timeline = [earlier[kt * pixels : (kt + frames) * pixels] for kt in range(3)]
        sums = dot_first(
            go_ref[...].reshape(frames * pixels, chans), jnp.concatenate(timeline, 1)
        )
        for kt in range(3):
            put(block, 9 + kt, sums[:, kt * chans : (kt + 1) * chans])
    keep_ref[...] = grad_ref[0]
    give_ref[...] = grad_ref[1]
    for whose, target in ((core, mine_out), (1 - core, other_out)):
        for step in range(group):
            row = jnp.bitwise_xor(unit, step) * rows_in
            target[step] = out_ref[pl.ds(whose * frames_in, frames_in), pl.ds(row, rows_in)]


def swapped(value, axis="tm", step=1):
    count = lax.axis_size(axis)
    return lax.ppermute(value, axis, [(i, i ^ step) for i in range(count)])


def on_device(video, cotangent, spatial_weights, temporal_weights):
    blocks, cores, tiles = (lax.axis_size(name) for name in ("section", "tm", "space"))
    frames_in, rows_in, columns, chans = video.shape
    halo = 2 * blocks
    tile = halo
    group = tile // rows_in
    parties = cores * group
    own_width = columns // parties
    width = own_width + 2 * halo
    span = cores * own_width + 2 * halo
    vmem = pl.BlockSpec(memory_space=pltpu.VMEM)
    params = pltpu.CompilerParams(vmem_limit_bytes=32 * 2**20)

    bands = blocks * tiles // group
    core, section, band, unit = placed(group)

    def traded(value, shift):
        pairs = []
        for one in range(bands):
            other = ((one + shift) ^ 1) - shift
            if 0 <= other < bands:
                pairs += [(one * group + i, other * group + i) for i in range(group)]
        return lax.ppermute(value, ("section", "space"), pairs)

    total_rows = blocks * tiles * rows_in
    half = group // 2
    passed = []
    for one in range(bands - 1):
        for i in range(group):
            low, high = one * group + i, (one + 1) * group + i
            passed.append((high, low) if i < half else (low, high))
    cot_halo = lax.ppermute(cotangent, ("section", "space"), passed)

    padded = columns + 2 * halo
    cuts = pl.pallas_call(
        functools.partial(window_kernel, halo, span),
        name="windows",
        in_specs=[vmem],
        out_specs=[vmem] * group,
        out_shape=[jax.ShapeDtypeStruct((frames_in, rows_in, span, chans), BF16)] * group,
        scratch_shapes=[pltpu.VMEM((frames_in, rows_in, padded, chans), F32)],
        compiler_params=params,
    )(video)
    *cuts, spatial, temporal = lax.optimization_barrier(
        list(cuts) + [spatial_weights, temporal_weights]
    )
    def core_half(which):
        whole = jnp.concatenate([spatial[0], temporal[0]], 0)
        taps = whole.shape[0] // cores
        return lax.dynamic_slice_in_dim(whole, which * taps, taps, 0)

    half_kernels = core_half(core)

    def gathered(pieces):
        return jnp.stack([pieces[0]] + [swapped(pieces[i], "space", i) for i in range(1, group)])

    along_x = swapped(half_kernels, "section", 1)
    along_y = swapped(half_kernels, "section", 2)
    own_video, along_x, spatial, temporal = lax.optimization_barrier(
        [gathered(cuts), along_x, spatial, temporal]
    )
    near, far = traded(own_video, 0), traded(own_video, 1)
    mine = [along_x, along_y, swapped(along_x, "section", 2)]
    shared = mine + [swapped(each) for each in mine]
    rest_kernels = core_half(1 - core)

    narrow = own_width + 2 * blocks
    cuts = pl.pallas_call(
        functools.partial(cotangent_kernel, blocks, narrow),
        name="cotangent",
        in_specs=[vmem] * 4,
        out_specs=[vmem] * group,
        out_shape=[jax.ShapeDtypeStruct((2, cores * frames_in, rows_in * narrow, chans), BF16)] * group,
        scratch_shapes=[
            pltpu.VMEM((2, cores * frames_in, rows_in, columns + 2 * blocks, chans), F32)
        ],
        compiler_params=params,
    )(cotangent, swapped(cotangent), cot_halo, swapped(cot_halo))
    near, rest_kernels, *cuts = lax.optimization_barrier([near, rest_kernels] + list(cuts))
    shared = [half_kernels, rest_kernels] + shared
    videos = [own_video, near, far]
    videos += [swapped(each) for each in videos]
    cots = [cuts[0]] + [swapped(cuts[i], "space", i) for i in range(1, group)]

    geometry = (blocks, cores, group, frames_in, rows_in, halo, tile, width, total_rows, columns)
    frames = cores * frames_in
    high = tile + 2 * halo
    per_section = (blocks,) + half_kernels.shape
    taps = half_kernels.shape[0]
    all_kernels = (cores,) + per_section
    saved = [
        jax.ShapeDtypeStruct((frames, tile + 2 * block + 2, width, chans), F32)
        for block in range(blocks)
    ]
    cost = pl.CostEstimate(flops=6 * 10**9, bytes_accessed=8 * 10**6, transcendentals=10**6)
    features, hidden, *slopes = pl.pallas_call(
        functools.partial(forward_kernel, geometry),
        name="forward",
        in_specs=[vmem] * (2 * blocks + 6),
        out_specs=[vmem] * (2 + blocks),
        out_shape=[
            jax.ShapeDtypeStruct((blocks, frames, tile + 2, own_width, 3 * chans), BF16),
            jax.ShapeDtypeStruct((blocks, frames, tile, own_width, chans), BF16),
        ]
        + saved,
        scratch_shapes=[
            pltpu.VMEM((frames, high, width, 3 * chans), BF16),
            pltpu.VMEM((frames, high, width, chans), BF16),
            pltpu.VMEM((high, width, chans), F32),
            pltpu.VMEM(all_kernels, BF16),
            pltpu.VMEM((frames, high, width, chans), BF16),
            pltpu.VMEM((12 * chans, 2 * chans), BF16),
        ],
        compiler_params=params,
        cost_estimate=cost,
    )(*shared, *videos)

    back = jax.ShapeDtypeStruct((group, frames_in, rows_in, own_width, chans), BF16)
    pixel_count = frames * total_rows * columns
    factor = 1.0 / float(pixel_count) ** 0.5
    keep, give, mine_grad, other_grad = pl.pallas_call(
        functools.partial(backward_kernel, geometry, factor),
        name="backward",
        in_specs=[vmem] * (3 * blocks + group + 2),
        out_specs=[vmem] * 4,
        out_shape=[
            jax.ShapeDtypeStruct(per_section, BF16),
            jax.ShapeDtypeStruct(per_section, BF16),
            back,
            back,
        ],
        scratch_shapes=[
            pltpu.VMEM((frames, tile + 2 * blocks, width, chans), BF16),
            pltpu.VMEM((frames, tile + 2 * blocks, width, 3 * chans), BF16),
            pltpu.VMEM((frames, tile, own_width, chans), BF16),
            pltpu.VMEM((frames, tile, own_width, chans), BF16),
            pltpu.VMEM(all_kernels, BF16),
            pltpu.VMEM(all_kernels, BF16),
            pltpu.VMEM((frames, tile, own_width, chans), BF16),
            pltpu.VMEM((12 * chans, 2 * chans), BF16),
        ],
        compiler_params=params,
        cost_estimate=cost,
    )(*shared, *cots, features, hidden, *slopes)

    got = swapped(give)
    parts = [(keep[i].astype(F32) + got[i].astype(F32)).astype(BF16) for i in range(blocks)]
    other_grad, *parts = lax.optimization_barrier([other_grad] + parts)
    parts = parts[:1] + [swapped(parts[i], "section", i) for i in range(1, blocks)]
    other_grad = swapped(other_grad)
    first = core == 0
    wide = jnp.concatenate(
        [jnp.where(first, mine_grad, other_grad), jnp.where(first, other_grad, mine_grad)], 3
    )
    strips = [wide[0]] + [swapped(wide[i], "space", i) for i in range(1, group)]
    received = lax.optimization_barrier(parts + strips)
    parts, strips = received[:blocks], received[blocks:]
    part = sum(each.astype(F32) for each in parts).astype(BF16)

    halves = part.reshape(2, -1, chans)
    low = unit % 2

    def picked(which):
        return lax.dynamic_index_in_dim(halves, which, 0, keepdims=False)

    part = (picked(low).astype(F32) + swapped(picked(1 - low), "space", 1).astype(F32)).astype(BF16)
    part = part.astype(F32) + swapped(part, "space", 2).astype(F32)
    if tiles != group:
        part = lax.psum(
            part, "space", axis_index_groups=[list(range(i, tiles, group)) for i in range(group)]
        )
    part = part.astype(BF16)
    pair = jnp.stack([part, swapped(part, "space", 1)])
    spatial_out, temporal_out = pl.pallas_call(
        functools.partial(closing_kernel, group),
        name="closing",
        in_specs=[vmem] * 2,
        out_specs=[vmem] * 2,
        out_shape=[
            jax.ShapeDtypeStruct(spatial_weights.shape, F32),
            jax.ShapeDtypeStruct(temporal_weights.shape, F32),
        ],
        scratch_shapes=[pltpu.VMEM((cores * taps * chans, chans), BF16)],
        compiler_params=params,
    )(pair, swapped(pair))

    grad_video = jnp.zeros(video.shape, BF16)
    for step, strip in enumerate(strips):
        grad_video = lax.dynamic_update_slice(
            grad_video, strip, (0, 0, (unit ^ step) * cores * own_width, 0)
        )
    return spatial_out, temporal_out, grad_video


def solution(mesh):
    return jax.shard_map(
        on_device,
        mesh=mesh,
        in_specs=(
            P("tm", ("section", "space"), None, None),
            P("tm", ("section", "space"), None, None),
            P("section", None, None, None),
            P("section", None, None, None),
        ),
        out_specs=(
            P("section", None, None, None),
            P("section", None, None, None),
            P("tm", ("section", "space"), None, None),
        ),
        check_vma=False,
    )
```

```python
import functools

import jax
import jax.numpy as jnp
from jax import lax
from jax.experimental import pallas as pl
from jax.experimental.pallas import tpu as pltpu
from jax.sharding import PartitionSpec as P

F32 = jnp.float32
BF16 = jnp.bfloat16


def rolled(value, steps):
    return pltpu.roll(value, steps % value.shape[0], 0)


def dot_first(left, right):
    return lax.dot_general(left, right, (((0,), (0,)), ((), ())), preferred_element_type=F32)


def kernel_of(w_ref, block, tap):
    taps = w_ref.shape[2]
    return w_ref[tap // taps, block, tap % taps]


def pair_rows(w_ref, block, pair_ref):
    chans = w_ref.shape[-1]
    for source in range(4):
        for target in range(2):
            ky = source - target
            for kx in range(3):
                at = (3 * source + kx) * chans
                tile = kernel_of(w_ref, block, 3 * ky + kx) if 0 <= ky < 3 else jnp.zeros((chans, chans), BF16)
                pair_ref[at : at + chans, target * chans : (target + 1) * chans] = tile


def turned(w_ref, block, tap):
    return kernel_of(w_ref, block, tap).astype(F32).T.astype(BF16)


def arrangement_kernel(group, *rest):
    shared, (rows_ref, four_ref, two_ref, w_ref) = rest[:-4], rest[-4:]
    core, section, _, _ = placed(group)
    blocks = rows_ref.shape[0]
    place_kernels(core, section, w_ref, *shared[:2], shared[2 : 1 + blocks], shared[1 + blocks :])
    for block in range(blocks):
        pair_rows_back(w_ref, block, rows_ref.at[block])
        four_ref[block] = pair_frames_back(w_ref, block, 4)
        two_ref[block] = pair_frames_back(w_ref, block, 2)


def pair_rows_back(w_ref, block, pair_ref):
    chans = w_ref.shape[-1]
    nothing = jnp.zeros((chans, chans), BF16)
    for kx in range(3):
        for ky in range(3):
            tile = turned(w_ref, block, 3 * ky + kx)
            for target in range(2):
                at = (3 * (2 + target - ky) + kx) * chans
                pair_ref[at : at + chans, target * chans : (target + 1) * chans] = tile
        for source, target in ((3, 0), (0, 1)):
            at = (3 * source + kx) * chans
            pair_ref[at : at + chans, target * chans : (target + 1) * chans] = nothing


def pair_frames(w_ref, block, first, count):
    chans = w_ref.shape[-1]
    columns = []
    for target in (count - 2, count - 1):
        tiles = []
        for source in range(count):
            kt = source - target + 2
            tiles.append(kernel_of(w_ref, block, 9 + kt) if 0 <= kt < 3 else jnp.zeros((chans, chans), BF16))
        columns.append(jnp.concatenate(tiles, 0))
    return jnp.concatenate(columns, 1)


def pair_frames_back(w_ref, block, count):
    chans = w_ref.shape[-1]
    tiles = [turned(w_ref, block, 9 + kt) for kt in range(3)]
    columns = []
    for target in range(2):
        column = []
        for source in range(count):
            kt = 2 - (source - target)
            column.append(tiles[kt] if 0 <= kt < 3 else jnp.zeros((chans, chans), BF16))
        columns.append(jnp.concatenate(column, 0))
    return jnp.concatenate(columns, 1)


def row_pairs(ref, frame, first, pairs):
    width, lanes = ref.shape[2:]
    rows = []
    for start in (first, first + 2):
        value = ref[frame, start : start + 2 * pairs].reshape(pairs, 2, width, lanes)
        rows += [value[:, 0], value[:, 1]]
    return jnp.concatenate(rows, 2).reshape(pairs * width, 4 * lanes)


def woven(value, width):
    chans = value.shape[1] // 2
    split = [value[:, i * chans : (i + 1) * chans].reshape(-1, 1, width, chans) for i in range(2)]
    return jnp.concatenate(split, 1).reshape(-1, chans)


def placed(group):
    place, section = lax.axis_index("space"), lax.axis_index("section")
    band = (section * lax.axis_size("space") + place) // group
    return lax.axis_index("tm"), section, band, place % group


def window_kernel(halo, span, video_ref, *rest):
    targets, wide_ref = rest[:-1], rest[-1]
    unit = placed(len(targets))[3]
    frames, rows, columns, chans = video_ref.shape
    edge = jnp.zeros((frames, rows, halo, chans), F32)
    wide_ref[:, :, :halo] = edge
    wide_ref[:, :, halo + columns :] = edge
    wide_ref[:, :, halo : halo + columns] = video_ref[...].astype(F32)
    for step, target in enumerate(targets):
        at = jnp.bitwise_xor(unit, step) * (span - 2 * halo)
        target[...] = wide_ref[:, :, pl.ds(pl.multiple_of(at, 16), span)].astype(BF16)


def cotangent_kernel(reach, width, *rest):
    sources, targets, wide_ref = rest[:4], rest[4:-1], rest[-1]
    core, _, _, unit = placed(len(targets))
    frames_in, rows, columns, chans = sources[0].shape
    edge = jnp.zeros((2, 2 * frames_in, rows, reach, chans), F32)
    wide_ref[:, :, :, :reach] = edge
    wide_ref[:, :, :, reach + columns :] = edge
    for index, ref in enumerate(sources):
        whose = core if index % 2 == 0 else 1 - core
        wide_ref[index // 2, pl.ds(whose * frames_in, frames_in), :, reach : reach + columns] = ref[
            ...
        ].astype(F32)
    own = width - 2 * reach
    for step, target in enumerate(targets):
        at = (jnp.bitwise_xor(unit, step) * 2 + core) * own
        window = wide_ref[:, :, :, pl.ds(pl.multiple_of(at, 16), width)]
        target[...] = window.reshape(target.shape).astype(BF16)


def closing_kernel(group, mine_ref, other_ref, spatial_ref, temporal_ref, flat_ref):
    pieces, rows, chans = mine_ref.shape
    core, _, _, unit = placed(group)
    for whose, ref in ((core, mine_ref), (1 - core, other_ref)):
        for step in range(pieces):
            index = whose * pieces + jnp.bitwise_xor(jnp.bitwise_and(unit, pieces - 1), step)
            flat_ref[pl.ds(pl.multiple_of(index * rows, 16), rows)] = ref[step]
    count = spatial_ref.shape[1]
    for tap in range(count + temporal_ref.shape[1]):
        turned = flat_ref[tap * chans : (tap + 1) * chans].astype(F32).T
        if tap < count:
            spatial_ref[0, tap] = turned
        else:
            temporal_ref[0, tap - count] = turned


def place_kernels(core, section, w_ref, own_mine, own_other, mine_refs, other_refs):
    w_ref[core, section] = own_mine[...]
    w_ref[1 - core, section] = own_other[...]
    for step, (mine_ref, other_ref) in enumerate(zip(mine_refs, other_refs)):
        block = jnp.bitwise_xor(section, step + 1)
        w_ref[core, block] = mine_ref[...]
        w_ref[1 - core, block] = other_ref[...]


def forward_kernel(geometry, *rest):
    blocks, cores, group, frames_in, rows_in, halo, tile, width, height, columns = geometry
    core, section, band, unit = placed(group)
    odd = band % 2
    shared, rest = rest[: 2 * blocks], rest[2 * blocks :]
    arrived, rest = rest[:6], rest[6:]
    xo_ref, ho_ref = rest[:2]
    d_refs = rest[2 : 2 + blocks]
    x_ref, h_ref, mask_ref, w_ref, start_ref, pair_ref = rest[2 + blocks :]
    place_kernels(core, section, w_ref, *shared[:2], shared[2 : 1 + blocks], shared[1 + blocks :])
    frames = cores * frames_in
    high = tile + 2 * halo
    chans = w_ref.shape[-1]
    own_rows, own_cols = (halo, halo + tile), (halo, width - halo)
    row = band * tile - halo + lax.broadcasted_iota(jnp.int32, (high, width, chans), 0)
    left = (unit * cores + core) * (width - 2 * halo) - halo
    col = left + lax.broadcasted_iota(jnp.int32, (high, width, chans), 1)
    inside = (row >= 0) & (row < height) & (col >= 0) & (col < columns)
    mask_ref[...] = jnp.where(inside, 1.0, 0.0).astype(F32)

    def keep(block, frame, value, first):
        triple = [rolled(value, 1), value, rolled(value, -1)]
        count = value.shape[0] // width
        both = jnp.concatenate([part.astype(BF16) for part in triple], 1)
        x_ref[frame, first : first + count] = both.reshape(count, width, 3 * chans)
        start = own_rows[0] - 1 - first
        cut = [
            part.reshape(count, width, chans)[
                start : start + tile + 2, own_cols[0] : own_cols[1]
            ].astype(BF16)
            for part in triple
        ]
        xo_ref[block, frame] = jnp.concatenate(cut, 2)

    near = tile + halo - odd * (tile + halo)
    columns_at = pl.ds(pl.multiple_of(core * (width - 2 * halo), 16), width)
    for index, ref in enumerate(arrived):
        base = (halo, near, tile + halo - near)[index % 3]
        whose = core if index < 3 else 1 - core
        for step in range(group):
            row = base + jnp.bitwise_xor(unit, step) * rows_in
            start_ref[pl.ds(whose * frames_in, frames_in), pl.ds(row, rows_in)] = ref[
                step, :, :, columns_at, :
            ]
    for frame in range(frames):
        keep(0, frame, start_ref[frame].reshape(high * width, chans).astype(F32), 0)

    for block in range(blocks):
        first, last = block + 1, high - block - 1
        count = last - first
        pair_rows(w_ref, block, pair_ref)
        mask = mask_ref[first:last].reshape(count * width, chans)
        for frame in range(frames):
            taps = row_pairs(x_ref, frame, first - 1, count // 2)
            before = jnp.dot(taps, pair_ref[...], preferred_element_type=F32)
            before = woven(before, width)
            sigma = 0.5 + 0.5 * jnp.tanh(0.5 * before)
            masked = sigma * mask
            hidden = before * masked
            h_ref[frame, first:last] = hidden.astype(BF16).reshape(count, width, chans)
            hidden = hidden.reshape(count, width, chans)
            ho_ref[block, frame] = hidden[
                own_rows[0] - first : own_rows[1] - first, own_cols[0] : own_cols[1]
            ].astype(BF16)
            rim = block + 1
            kept = slice(own_rows[0] - rim - first, own_rows[1] + rim - first)
            sigma = sigma.reshape(count, width, chans)[kept]
            masked = masked.reshape(count, width, chans)[kept]
            d_refs[block][frame] = masked + hidden[kept] * (1.0 - sigma)
        if block + 1 == blocks:
            break
        for frame in range(0, frames, 2):
            start = max(frame - 2, 0)
            timeline = jnp.concatenate(
                [
                    h_ref[each, first:last].reshape(count * width, chans)
                    for each in range(start, frame + 2)
                ],
                1,
            )
            weights = pair_frames(w_ref, block, start, frame + 2 - start)
            both = jnp.dot(timeline, weights, preferred_element_type=F32)
            for inner in range(2):
                mixed = both[:, inner * chans : (inner + 1) * chans]
                old = x_ref[frame + inner, first:last, :, chans : 2 * chans].astype(F32)
                new = old.reshape(count * width, chans) + mixed
                keep(block + 1, frame + inner, new.astype(BF16).astype(F32), first)


def backward_kernel(geometry, factor, *rest):
    blocks, cores, group, frames_in, rows_in, halo, tile, width, height, columns = geometry
    core, section, band, unit = placed(group)
    rows_ref, four_ref, two_ref = rest[:3]
    rest = rest[3:]
    arrived, rest = rest[:group], rest[group:]
    xo_ref, ho_ref = rest[:2]
    d_refs = rest[2 : 2 + blocks]
    keep_ref, give_ref, mine_out, other_out = rest[2 + blocks : 6 + blocks]
    g_ref, da_ref, dao_ref, go_ref, grad_ref, out_ref = rest[6 + blocks :]
    frames = cores * frames_in
    chans = g_ref.shape[-1]
    rim = blocks
    own_cols = (halo, width - halo)
    per_core = keep_ref.shape[1]
    pixels = tile * (own_cols[1] - own_cols[0])

    half = group // 2
    side = halo - rim
    edge = jnp.zeros((frames, rows_in, side, chans), F32)

    def widened(value):
        value = value.astype(F32).reshape(frames, rows_in, width - 2 * side, chans)
        return jnp.concatenate([edge, value, edge], 2).astype(BF16)

    for step, ref in enumerate(arrived):
        at = jnp.bitwise_xor(unit, step)
        g_ref[:, pl.ds(rim + at * rows_in, rows_in)] = widened(ref[0])
        beyond = jnp.where(at < half, rim + tile + at * rows_in, (at - half) * rows_in)
        g_ref[:, pl.ds(beyond, rows_in)] = widened(ref[1])

    def put(block, tap, value):
        slot = jnp.where(core == tap // per_core, 0, 1)
        where = jnp.bitwise_xor(section, block)
        grad_ref[slot, where, tap % per_core] = (value * factor).astype(BF16)

    for block in reversed(range(blocks)):
        edge = block + 1
        first, last = rim - edge, rim + tile + edge
        count = last - first
        for frame in range(frames):
            go_ref[frame] = g_ref[frame, rim : rim + tile].astype(F32)[
                :, own_cols[0] : own_cols[1]
            ].astype(BF16)
        hiddens = []
        for frame in range(0, frames, 2):
            stop = min(frame + 4, frames)
            ahead = jnp.concatenate(
                [
                    g_ref[each, first:last].reshape(count * width, chans)
                    for each in range(frame, stop)
                ],
                1,
            )
            weights = four_ref[block] if stop - frame == 4 else two_ref[block]
            both = jnp.dot(ahead, weights, preferred_element_type=F32)
            hiddens += [both[:, :chans], both[:, chans:]]
        for frame in range(frames):
            hidden = hiddens[frame]
            slope = d_refs[block][frame].reshape(count * width, chans)
            value = (hidden * slope).astype(BF16).astype(F32)
            triple = [rolled(value, -1), value, rolled(value, 1)]
            both = jnp.concatenate([part.astype(BF16) for part in triple], 1)
            da_ref[frame, first:last] = both.reshape(count, width, 3 * chans)
            dao_ref[frame] = value.reshape(count, width, chans)[
                edge : edge + tile, own_cols[0] : own_cols[1]
            ].astype(BF16)
        for frame in range(frames):
            inner = count - 2
            taps = row_pairs(da_ref, frame, first, inner // 2)
            back = woven(jnp.dot(taps, rows_ref[block], preferred_element_type=F32), width)
            old = g_ref[frame, first + 1 : last - 1].astype(F32).reshape(inner * width, chans)
            new = (old + back).astype(BF16)
            if block:
                g_ref[frame, first + 1 : last - 1] = new.reshape(inner, width, chans)
            else:
                cut = new.astype(F32).reshape(inner, width, chans)[:, own_cols[0] : own_cols[1]]
                out_ref[frame] = cut.astype(BF16)
        slopes = dao_ref[...].reshape(frames * pixels, chans)
        taps = [
            xo_ref[block, :, ky : ky + tile].reshape(frames * pixels, 3 * chans) for ky in range(3)
        ]
        sums = dot_first(slopes, jnp.concatenate(taps, 1))
        for tap in range(9):
            put(block, tap, sums[:, tap * chans : (tap + 1) * chans])
        before = jnp.zeros((2 * pixels, chans), BF16)
        earlier = ho_ref[block].reshape(frames * pixels, chans)
        earlier = jnp.concatenate([before, earlier], 0)
        timeline = [earlier[kt * pixels : (kt + frames) * pixels] for kt in range(3)]
        sums = dot_first(
            go_ref[...].reshape(frames * pixels, chans), jnp.concatenate(timeline, 1)
        )
        for kt in range(3):
            put(block, 9 + kt, sums[:, kt * chans : (kt + 1) * chans])
    keep_ref[...] = grad_ref[0]
    give_ref[...] = grad_ref[1]
    for whose, target in ((core, mine_out), (1 - core, other_out)):
        for step in range(group):
            row = jnp.bitwise_xor(unit, step) * rows_in
            target[step] = out_ref[pl.ds(whose * frames_in, frames_in), pl.ds(row, rows_in)]


def swapped(value, axis="tm", step=1):
    count = lax.axis_size(axis)
    return lax.ppermute(value, axis, [(i, i ^ step) for i in range(count)])


def on_device(video, cotangent, spatial_weights, temporal_weights):
    blocks, cores, tiles = (lax.axis_size(name) for name in ("section", "tm", "space"))
    frames_in, rows_in, columns, chans = video.shape
    halo = 2 * blocks
    tile = halo
    group = tile // rows_in
    parties = cores * group
    own_width = columns // parties
    width = own_width + 2 * halo
    span = cores * own_width + 2 * halo
    vmem = pl.BlockSpec(memory_space=pltpu.VMEM)
    params = pltpu.CompilerParams(vmem_limit_bytes=32 * 2**20)

    bands = blocks * tiles // group
    core, section, band, unit = placed(group)

    def traded(value, shift):
        pairs = []
        for one in range(bands):
            other = ((one + shift) ^ 1) - shift
            if 0 <= other < bands:
                pairs += [(one * group + i, other * group + i) for i in range(group)]
        return lax.ppermute(value, ("section", "space"), pairs)

    total_rows = blocks * tiles * rows_in
    half = group // 2
    passed = []
    for one in range(bands - 1):
        for i in range(group):
            low, high = one * group + i, (one + 1) * group + i
            passed.append((high, low) if i < half else (low, high))
    cot_halo = lax.ppermute(cotangent, ("section", "space"), passed)

    padded = columns + 2 * halo
    cuts = pl.pallas_call(
        functools.partial(window_kernel, halo, span),
        name="windows",
        in_specs=[vmem],
        out_specs=[vmem] * group,
        out_shape=[jax.ShapeDtypeStruct((frames_in, rows_in, span, chans), BF16)] * group,
        scratch_shapes=[pltpu.VMEM((frames_in, rows_in, padded, chans), F32)],
        compiler_params=params,
    )(video)
    *cuts, spatial, temporal = lax.optimization_barrier(
        list(cuts) + [spatial_weights, temporal_weights]
    )
    def core_half(which):
        whole = jnp.concatenate([spatial[0], temporal[0]], 0)
        taps = whole.shape[0] // cores
        return lax.dynamic_slice_in_dim(whole, which * taps, taps, 0)

    half_kernels = core_half(core)

    def gathered(pieces):
        return jnp.stack([pieces[0]] + [swapped(pieces[i], "space", i) for i in range(1, group)])

    along_x = swapped(half_kernels, "section", 1)
    along_y = swapped(half_kernels, "section", 2)
    own_video, along_x, along_y, spatial, temporal = lax.optimization_barrier(
        [gathered(cuts), along_x, along_y, spatial, temporal]
    )
    near, far = traded(own_video, 0), traded(own_video, 1)
    mine = [along_x, along_y, swapped(along_x, "section", 2)]
    shared = mine + [swapped(each) for each in mine]
    rest_kernels = core_half(1 - core)

    narrow = own_width + 2 * blocks
    cuts = pl.pallas_call(
        functools.partial(cotangent_kernel, blocks, narrow),
        name="cotangent",
        in_specs=[vmem] * 4,
        out_specs=[vmem] * group,
        out_shape=[jax.ShapeDtypeStruct((2, cores * frames_in, rows_in * narrow, chans), BF16)] * group,
        scratch_shapes=[
            pltpu.VMEM((2, cores * frames_in, rows_in, columns + 2 * blocks, chans), F32)
        ],
        compiler_params=params,
    )(cotangent, swapped(cotangent), cot_halo, swapped(cot_halo))
    near, rest_kernels, *cuts = lax.optimization_barrier([near, rest_kernels] + list(cuts))
    shared = [half_kernels, rest_kernels] + shared
    videos = [own_video, near, far]
    videos += [swapped(each) for each in videos]
    cots = [cuts[0]] + [swapped(cuts[i], "space", i) for i in range(1, group)]

    geometry = (blocks, cores, group, frames_in, rows_in, halo, tile, width, total_rows, columns)
    frames = cores * frames_in
    high = tile + 2 * halo
    per_section = (blocks,) + half_kernels.shape
    taps = half_kernels.shape[0]
    all_kernels = (cores,) + per_section
    saved = [
        jax.ShapeDtypeStruct((frames, tile + 2 * block + 2, width, chans), F32)
        for block in range(blocks)
    ]
    cost = pl.CostEstimate(flops=6 * 10**9, bytes_accessed=8 * 10**6, transcendentals=10**6)
    features, hidden, *slopes = pl.pallas_call(
        functools.partial(forward_kernel, geometry),
        name="forward",
        in_specs=[vmem] * (2 * blocks + 6),
        out_specs=[vmem] * (2 + blocks),
        out_shape=[
            jax.ShapeDtypeStruct((blocks, frames, tile + 2, own_width, 3 * chans), BF16),
            jax.ShapeDtypeStruct((blocks, frames, tile, own_width, chans), BF16),
        ]
        + saved,
        scratch_shapes=[
            pltpu.VMEM((frames, high, width, 3 * chans), BF16),
            pltpu.VMEM((frames, high, width, chans), BF16),
            pltpu.VMEM((high, width, chans), F32),
            pltpu.VMEM(all_kernels, BF16),
            pltpu.VMEM((frames, high, width, chans), BF16),
            pltpu.VMEM((12 * chans, 2 * chans), BF16),
        ],
        compiler_params=params,
        cost_estimate=cost,
    )(*shared, *videos)

    back = jax.ShapeDtypeStruct((group, frames_in, rows_in, own_width, chans), BF16)
    features, *after = lax.optimization_barrier([features] + shared)
    arranged = [
        jax.ShapeDtypeStruct((blocks, rows * chans, 2 * chans), BF16) for rows in (12, 4, 2)
    ]
    arranged = pl.pallas_call(
        functools.partial(arrangement_kernel, group),
        name="arrangement",
        in_specs=[vmem] * len(after),
        out_specs=[vmem] * 3,
        out_shape=arranged,
        scratch_shapes=[pltpu.VMEM(all_kernels, BF16)],
        compiler_params=params,
        cost_estimate=pl.CostEstimate(flops=10**9, bytes_accessed=10**6, transcendentals=0),
    )(*after)
    pixel_count = frames * total_rows * columns
    factor = 1.0 / float(pixel_count) ** 0.5
    keep, give, mine_grad, other_grad = pl.pallas_call(
        functools.partial(backward_kernel, geometry, factor),
        name="backward",
        in_specs=[vmem] * (blocks + group + 5),
        out_specs=[vmem] * 4,
        out_shape=[
            jax.ShapeDtypeStruct(per_section, BF16),
            jax.ShapeDtypeStruct(per_section, BF16),
            back,
            back,
        ],
        scratch_shapes=[
            pltpu.VMEM((frames, tile + 2 * blocks, width, chans), BF16),
            pltpu.VMEM((frames, tile + 2 * blocks, width, 3 * chans), BF16),
            pltpu.VMEM((frames, tile, own_width, chans), BF16),
            pltpu.VMEM((frames, tile, own_width, chans), BF16),
            pltpu.VMEM(all_kernels, BF16),
            pltpu.VMEM((frames, tile, own_width, chans), BF16),
        ],
        compiler_params=params,
        cost_estimate=cost,
    )(*arranged, *cots, features, hidden, *slopes)

    got = swapped(give)
    parts = [(keep[i].astype(F32) + got[i].astype(F32)).astype(BF16) for i in range(blocks)]
    other_grad, *parts = lax.optimization_barrier([other_grad] + parts)
    parts = parts[:1] + [swapped(parts[i], "section", i) for i in range(1, blocks)]
    other_grad = swapped(other_grad)
    first = core == 0
    wide = jnp.concatenate(
        [jnp.where(first, mine_grad, other_grad), jnp.where(first, other_grad, mine_grad)], 3
    )
    strips = [wide[0]] + [swapped(wide[i], "space", i) for i in range(1, group)]
    received = lax.optimization_barrier(parts + strips)
    parts, strips = received[:blocks], received[blocks:]
    part = sum(each.astype(F32) for each in parts).astype(BF16)

    halves = part.reshape(2, -1, chans)
    low = unit % 2

    def picked(which):
        return lax.dynamic_index_in_dim(halves, which, 0, keepdims=False)

    part = (picked(low).astype(F32) + swapped(picked(1 - low), "space", 1).astype(F32)).astype(BF16)
    part = part.astype(F32) + swapped(part, "space", 2).astype(F32)
    if tiles != group:
        part = lax.psum(
            part, "space", axis_index_groups=[list(range(i, tiles, group)) for i in range(group)]
        )
    part = part.astype(BF16)
    pair = jnp.stack([part, swapped(part, "space", 1)])
    spatial_out, temporal_out = pl.pallas_call(
        functools.partial(closing_kernel, group),
        name="closing",
        in_specs=[vmem] * 2,
        out_specs=[vmem] * 2,
        out_shape=[
            jax.ShapeDtypeStruct(spatial_weights.shape, F32),
            jax.ShapeDtypeStruct(temporal_weights.shape, F32),
        ],
        scratch_shapes=[pltpu.VMEM((cores * taps * chans, chans), BF16)],
        compiler_params=params,
    )(pair, swapped(pair))

    grad_video = jnp.zeros(video.shape, BF16)
    for step, strip in enumerate(strips):
        grad_video = lax.dynamic_update_slice(
            grad_video, strip, (0, 0, (unit ^ step) * cores * own_width, 0)
        )
    return spatial_out, temporal_out, grad_video


def solution(mesh):
    return jax.shard_map(
        on_device,
        mesh=mesh,
        in_specs=(
            P("tm", ("section", "space"), None, None),
            P("tm", ("section", "space"), None, None),
            P("section", None, None, None),
            P("section", None, None, None),
        ),
        out_specs=(
            P("section", None, None, None),
            P("section", None, None, None),
            P("tm", ("section", "space"), None, None),
        ),
        check_vma=False,
    )
```

```python
import functools

import jax
import jax.numpy as jnp
from jax import lax
from jax.experimental import pallas as pl
from jax.experimental.pallas import tpu as pltpu
from jax.sharding import PartitionSpec as P

F32 = jnp.float32
BF16 = jnp.bfloat16


def rolled(value, steps):
    return pltpu.roll(value, steps % value.shape[0], 0)


def dot_first(left, right):
    return lax.dot_general(left, right, (((0,), (0,)), ((), ())), preferred_element_type=F32)


def kernel_of(w_ref, block, tap):
    taps = w_ref.shape[2]
    return w_ref[tap // taps, block, tap % taps]


def pair_rows(w_ref, block, pair_ref):
    chans = w_ref.shape[-1]
    for source in range(4):
        for target in range(2):
            ky = source - target
            for kx in range(3):
                at = (3 * source + kx) * chans
                tile = kernel_of(w_ref, block, 3 * ky + kx) if 0 <= ky < 3 else jnp.zeros((chans, chans), BF16)
                pair_ref[at : at + chans, target * chans : (target + 1) * chans] = tile


def turned(w_ref, block, tap):
    return kernel_of(w_ref, block, tap).astype(F32).T.astype(BF16)


def arrangement_kernel(group, *rest):
    shared, (rows_ref, four_ref, two_ref, w_ref) = rest[:-4], rest[-4:]
    core, section, _, _ = placed(group)
    blocks = rows_ref.shape[0]
    place_kernels(core, section, w_ref, *shared[:2], shared[2 : 1 + blocks], shared[1 + blocks :])
    for block in range(blocks):
        pair_rows_back(w_ref, block, rows_ref.at[block])
        four_ref[block] = pair_frames_back(w_ref, block, 4)
        two_ref[block] = pair_frames_back(w_ref, block, 2)


def pair_rows_back(w_ref, block, pair_ref):
    chans = w_ref.shape[-1]
    nothing = jnp.zeros((chans, chans), BF16)
    for kx in range(3):
        for ky in range(3):
            tile = turned(w_ref, block, 3 * ky + kx)
            for target in range(2):
                at = (3 * (2 + target - ky) + kx) * chans
                pair_ref[at : at + chans, target * chans : (target + 1) * chans] = tile
        for source, target in ((3, 0), (0, 1)):
            at = (3 * source + kx) * chans
            pair_ref[at : at + chans, target * chans : (target + 1) * chans] = nothing


def pair_frames(w_ref, block, first, count):
    chans = w_ref.shape[-1]
    columns = []
    for target in (count - 2, count - 1):
        tiles = []
        for source in range(count):
            kt = source - target + 2
            tiles.append(kernel_of(w_ref, block, 9 + kt) if 0 <= kt < 3 else jnp.zeros((chans, chans), BF16))
        columns.append(jnp.concatenate(tiles, 0))
    return jnp.concatenate(columns, 1)


def pair_frames_back(w_ref, block, count):
    chans = w_ref.shape[-1]
    tiles = [turned(w_ref, block, 9 + kt) for kt in range(3)]
    columns = []
    for target in range(2):
        column = []
        for source in range(count):
            kt = 2 - (source - target)
            column.append(tiles[kt] if 0 <= kt < 3 else jnp.zeros((chans, chans), BF16))
        columns.append(jnp.concatenate(column, 0))
    return jnp.concatenate(columns, 1)


def row_pairs(ref, frame, first, pairs):
    width, lanes = ref.shape[2:]
    rows = []
    for start in (first, first + 2):
        value = ref[frame, start : start + 2 * pairs].reshape(pairs, 2, width, lanes)
        rows += [value[:, 0], value[:, 1]]
    return jnp.concatenate(rows, 2).reshape(pairs * width, 4 * lanes)


def woven(value, width):
    chans = value.shape[1] // 2
    split = [value[:, i * chans : (i + 1) * chans].reshape(-1, 1, width, chans) for i in range(2)]
    return jnp.concatenate(split, 1).reshape(-1, chans)


def placed(group):
    place, section = lax.axis_index("space"), lax.axis_index("section")
    band = (section * lax.axis_size("space") + place) // group
    return lax.axis_index("tm"), section, band, place % group


def window_kernel(halo, span, video_ref, *rest):
    targets, wide_ref = rest[:-1], rest[-1]
    unit = placed(len(targets))[3]
    frames, rows, columns, chans = video_ref.shape
    edge = jnp.zeros((frames, rows, halo, chans), F32)
    wide_ref[:, :, :halo] = edge
    wide_ref[:, :, halo + columns :] = edge
    wide_ref[:, :, halo : halo + columns] = video_ref[...].astype(F32)
    for step, target in enumerate(targets):
        at = jnp.bitwise_xor(unit, step) * (span - 2 * halo)
        target[...] = wide_ref[:, :, pl.ds(pl.multiple_of(at, 16), span)].astype(BF16)


def cotangent_kernel(reach, width, *rest):
    sources, targets, wide_ref = rest[:4], rest[4:-1], rest[-1]
    core, _, _, unit = placed(len(targets))
    frames_in, rows, columns, chans = sources[0].shape
    edge = jnp.zeros((2, 2 * frames_in, rows, reach, chans), F32)
    wide_ref[:, :, :, :reach] = edge
    wide_ref[:, :, :, reach + columns :] = edge
    for index, ref in enumerate(sources):
        whose = core if index % 2 == 0 else 1 - core
        wide_ref[index // 2, pl.ds(whose * frames_in, frames_in), :, reach : reach + columns] = ref[
            ...
        ].astype(F32)
    own = width - 2 * reach
    for step, target in enumerate(targets):
        at = (jnp.bitwise_xor(unit, step) * 2 + core) * own
        window = wide_ref[:, :, :, pl.ds(pl.multiple_of(at, 16), width)]
        target[...] = window.reshape(target.shape).astype(BF16)


def closing_kernel(group, mine_ref, other_ref, spatial_ref, temporal_ref, flat_ref):
    pieces, rows, chans = mine_ref.shape
    core, _, _, unit = placed(group)
    for whose, ref in ((core, mine_ref), (1 - core, other_ref)):
        for step in range(pieces):
            index = whose * pieces + jnp.bitwise_xor(jnp.bitwise_and(unit, pieces - 1), step)
            flat_ref[pl.ds(pl.multiple_of(index * rows, 16), rows)] = ref[step]
    count = spatial_ref.shape[1]
    for tap in range(count + temporal_ref.shape[1]):
        turned = flat_ref[tap * chans : (tap + 1) * chans].astype(F32).T
        if tap < count:
            spatial_ref[0, tap] = turned
        else:
            temporal_ref[0, tap - count] = turned


def place_kernels(core, section, w_ref, own_mine, own_other, mine_refs, other_refs):
    w_ref[core, section] = own_mine[...]
    w_ref[1 - core, section] = own_other[...]
    for step, (mine_ref, other_ref) in enumerate(zip(mine_refs, other_refs)):
        block = jnp.bitwise_xor(section, step + 1)
        w_ref[core, block] = mine_ref[...]
        w_ref[1 - core, block] = other_ref[...]


def forward_kernel(geometry, *rest):
    blocks, cores, group, frames_in, rows_in, halo, tile, width, height, columns = geometry
    core, section, band, unit = placed(group)
    odd = band % 2
    shared, rest = rest[: 2 * blocks], rest[2 * blocks :]
    arrived, rest = rest[:6], rest[6:]
    xo_ref, ho_ref = rest[:2]
    d_refs = rest[2 : 2 + blocks]
    x_ref, h_ref, mask_ref, w_ref, start_ref, pair_ref = rest[2 + blocks :]
    place_kernels(core, section, w_ref, *shared[:2], shared[2 : 1 + blocks], shared[1 + blocks :])
    frames = cores * frames_in
    high = tile + 2 * halo
    chans = w_ref.shape[-1]
    own_rows, own_cols = (halo, halo + tile), (halo, width - halo)
    row = band * tile - halo + lax.broadcasted_iota(jnp.int32, (high, width, chans), 0)
    left = (unit * cores + core) * (width - 2 * halo) - halo
    col = left + lax.broadcasted_iota(jnp.int32, (high, width, chans), 1)
    inside = (row >= 0) & (row < height) & (col >= 0) & (col < columns)
    mask_ref[...] = jnp.where(inside, 1.0, 0.0).astype(F32)

    def keep(block, frame, value, first):
        triple = [rolled(value, 1), value, rolled(value, -1)]
        count = value.shape[0] // width
        both = jnp.concatenate([part.astype(BF16) for part in triple], 1)
        x_ref[frame, first : first + count] = both.reshape(count, width, 3 * chans)
        start = own_rows[0] - 1 - first
        cut = [
            part.reshape(count, width, chans)[
                start : start + tile + 2, own_cols[0] : own_cols[1]
            ].astype(BF16)
            for part in triple
        ]
        xo_ref[block, frame] = jnp.concatenate(cut, 2)

    near = tile + halo - odd * (tile + halo)
    columns_at = pl.ds(pl.multiple_of(core * (width - 2 * halo), 16), width)
    for index, ref in enumerate(arrived):
        base = (halo, near, tile + halo - near)[index % 3]
        whose = core if index < 3 else 1 - core
        for step in range(group):
            row = base + jnp.bitwise_xor(unit, step) * rows_in
            start_ref[pl.ds(whose * frames_in, frames_in), pl.ds(row, rows_in)] = ref[
                step, :, :, columns_at, :
            ]
    for frame in range(frames):
        keep(0, frame, start_ref[frame].reshape(high * width, chans).astype(F32), 0)

    for block in range(blocks):
        first, last = block + 1, high - block - 1
        count = last - first
        pair_rows(w_ref, block, pair_ref)
        mask = mask_ref[first:last].reshape(count * width, chans)
        for frame in range(frames):
            taps = row_pairs(x_ref, frame, first - 1, count // 2)
            before = jnp.dot(taps, pair_ref[...], preferred_element_type=F32)
            before = woven(before, width)
            sigma = 0.5 + 0.5 * jnp.tanh(0.5 * before)
            masked = sigma * mask
            hidden = before * masked
            h_ref[frame, first:last] = hidden.astype(BF16).reshape(count, width, chans)
            hidden = hidden.reshape(count, width, chans)
            ho_ref[block, frame] = hidden[
                own_rows[0] - first : own_rows[1] - first, own_cols[0] : own_cols[1]
            ].astype(BF16)
            rim = block + 1
            kept = slice(own_rows[0] - rim - first, own_rows[1] + rim - first)
            sigma = sigma.reshape(count, width, chans)[kept]
            masked = masked.reshape(count, width, chans)[kept]
            d_refs[block][frame] = masked + hidden[kept] * (1.0 - sigma)
        if block + 1 == blocks:
            break
        for frame in range(0, frames, 2):
            start = max(frame - 2, 0)
            timeline = jnp.concatenate(
                [
                    h_ref[each, first:last].reshape(count * width, chans)
                    for each in range(start, frame + 2)
                ],
                1,
            )
            weights = pair_frames(w_ref, block, start, frame + 2 - start)
            both = jnp.dot(timeline, weights, preferred_element_type=F32)
            for inner in range(2):
                mixed = both[:, inner * chans : (inner + 1) * chans]
                old = x_ref[frame + inner, first:last, :, chans : 2 * chans].astype(F32)
                new = old.reshape(count * width, chans) + mixed
                keep(block + 1, frame + inner, new.astype(BF16).astype(F32), first)


def backward_kernel(geometry, factor, *rest):
    blocks, cores, group, frames_in, rows_in, halo, tile, width, height, columns = geometry
    core, section, band, unit = placed(group)
    rows_ref, four_ref, two_ref = rest[:3]
    rest = rest[3:]
    arrived, rest = rest[:group], rest[group:]
    xo_ref, ho_ref = rest[:2]
    d_refs = rest[2 : 2 + blocks]
    keep_ref, give_ref, mine_out, other_out = rest[2 + blocks : 6 + blocks]
    g_ref, da_ref, dao_ref, go_ref, grad_ref, out_ref = rest[6 + blocks :]
    frames = cores * frames_in
    chans = g_ref.shape[-1]
    rim = blocks
    own_cols = (halo, width - halo)
    per_core = keep_ref.shape[1]
    pixels = tile * (own_cols[1] - own_cols[0])

    half = group // 2
    side = halo - rim
    edge = jnp.zeros((frames, rows_in, side, chans), F32)

    def widened(value):
        value = value.astype(F32).reshape(frames, rows_in, width - 2 * side, chans)
        return jnp.concatenate([edge, value, edge], 2).astype(BF16)

    for step, ref in enumerate(arrived):
        at = jnp.bitwise_xor(unit, step)
        g_ref[:, pl.ds(rim + at * rows_in, rows_in)] = widened(ref[0])
        beyond = jnp.where(at < half, rim + tile + at * rows_in, (at - half) * rows_in)
        g_ref[:, pl.ds(beyond, rows_in)] = widened(ref[1])

    def put(block, tap, value):
        slot = jnp.where(core == tap // per_core, 0, 1)
        where = jnp.bitwise_xor(section, block)
        grad_ref[slot, where, tap % per_core] = (value * factor).astype(BF16)

    for block in reversed(range(blocks)):
        edge = block + 1
        first, last = rim - edge, rim + tile + edge
        count = last - first
        for frame in range(frames):
            go_ref[frame] = g_ref[frame, rim : rim + tile].astype(F32)[
                :, own_cols[0] : own_cols[1]
            ].astype(BF16)
        hiddens = []
        for frame in range(0, frames, 2):
            stop = min(frame + 4, frames)
            ahead = jnp.concatenate(
                [
                    g_ref[each, first:last].reshape(count * width, chans)
                    for each in range(frame, stop)
                ],
                1,
            )
            weights = four_ref[block] if stop - frame == 4 else two_ref[block]
            both = jnp.dot(ahead, weights, preferred_element_type=F32)
            hiddens += [both[:, :chans], both[:, chans:]]
        for frame in range(frames):
            hidden = hiddens[frame]
            slope = d_refs[block][frame].reshape(count * width, chans)
            value = (hidden * slope).astype(BF16).astype(F32)
            triple = [rolled(value, -1), value, rolled(value, 1)]
            both = jnp.concatenate([part.astype(BF16) for part in triple], 1)
            da_ref[frame, first:last] = both.reshape(count, width, 3 * chans)
            dao_ref[frame] = value.reshape(count, width, chans)[
                edge : edge + tile, own_cols[0] : own_cols[1]
            ].astype(BF16)
        for frame in range(frames):
            inner = count - 2
            taps = row_pairs(da_ref, frame, first, inner // 2)
            back = woven(jnp.dot(taps, rows_ref[block], preferred_element_type=F32), width)
            old = g_ref[frame, first + 1 : last - 1].astype(F32).reshape(inner * width, chans)
            new = (old + back).astype(BF16)
            if block:
                g_ref[frame, first + 1 : last - 1] = new.reshape(inner, width, chans)
            else:
                cut = new.astype(F32).reshape(inner, width, chans)[:, own_cols[0] : own_cols[1]]
                out_ref[frame] = cut.astype(BF16)
        slopes = dao_ref[...].reshape(frames * pixels, chans)
        taps = [
            xo_ref[block, :, ky : ky + tile].reshape(frames * pixels, 3 * chans) for ky in range(3)
        ]
        sums = dot_first(slopes, jnp.concatenate(taps, 1))
        for tap in range(9):
            put(block, tap, sums[:, tap * chans : (tap + 1) * chans])
        before = jnp.zeros((2 * pixels, chans), BF16)
        earlier = ho_ref[block].reshape(frames * pixels, chans)
        earlier = jnp.concatenate([before, earlier], 0)
        timeline = [earlier[kt * pixels : (kt + frames) * pixels] for kt in range(3)]
        sums = dot_first(
            go_ref[...].reshape(frames * pixels, chans), jnp.concatenate(timeline, 1)
        )
        for kt in range(3):
            put(block, 9 + kt, sums[:, kt * chans : (kt + 1) * chans])
    keep_ref[...] = grad_ref[0]
    give_ref[...] = grad_ref[1]
    for whose, target in ((core, mine_out), (1 - core, other_out)):
        for step in range(group):
            row = jnp.bitwise_xor(unit, step) * rows_in
            target[step] = out_ref[pl.ds(whose * frames_in, frames_in), pl.ds(row, rows_in)]


def swapped(value, axis="tm", step=1):
    count = lax.axis_size(axis)
    return lax.ppermute(value, axis, [(i, i ^ step) for i in range(count)])


def on_device(video, cotangent, spatial_weights, temporal_weights):
    blocks, cores, tiles = (lax.axis_size(name) for name in ("section", "tm", "space"))
    frames_in, rows_in, columns, chans = video.shape
    halo = 2 * blocks
    tile = halo
    group = tile // rows_in
    parties = cores * group
    own_width = columns // parties
    width = own_width + 2 * halo
    span = cores * own_width + 2 * halo
    vmem = pl.BlockSpec(memory_space=pltpu.VMEM)
    params = pltpu.CompilerParams(vmem_limit_bytes=32 * 2**20)

    bands = blocks * tiles // group
    core, section, band, unit = placed(group)

    def traded(value, shift):
        pairs = []
        for one in range(bands):
            other = ((one + shift) ^ 1) - shift
            if 0 <= other < bands:
                pairs += [(one * group + i, other * group + i) for i in range(group)]
        return lax.ppermute(value, ("section", "space"), pairs)

    total_rows = blocks * tiles * rows_in
    half = group // 2
    passed = []
    for one in range(bands - 1):
        for i in range(group):
            low, high = one * group + i, (one + 1) * group + i
            passed.append((high, low) if i < half else (low, high))

    padded = columns + 2 * halo
    cuts = pl.pallas_call(
        functools.partial(window_kernel, halo, span),
        name="windows",
        in_specs=[vmem],
        out_specs=[vmem] * group,
        out_shape=[jax.ShapeDtypeStruct((frames_in, rows_in, span, chans), BF16)] * group,
        scratch_shapes=[pltpu.VMEM((frames_in, rows_in, padded, chans), F32)],
        compiler_params=params,
    )(video)
    *cuts, spatial, temporal = lax.optimization_barrier(
        list(cuts) + [spatial_weights, temporal_weights]
    )
    def core_half(which):
        whole = jnp.concatenate([spatial[0], temporal[0]], 0)
        taps = whole.shape[0] // cores
        return lax.dynamic_slice_in_dim(whole, which * taps, taps, 0)

    half_kernels = core_half(core)

    def gathered(pieces):
        return [pieces[0]] + [swapped(pieces[i], "space", i) for i in range(1, group)]

    along_x = swapped(half_kernels, "section", 1)
    along_y = swapped(half_kernels, "section", 2)
    pieces = gathered(cuts)
    pieces[1], cot_rows = lax.optimization_barrier([pieces[1], cotangent])
    cot_halo = lax.ppermute(cot_rows, ("section", "space"), passed)
    own_video = jnp.stack(pieces)
    _, along_x, along_y, spatial, temporal = lax.optimization_barrier(
        [own_video, along_x, along_y, spatial, temporal]
    )
    near, far = traded(own_video, 0), traded(own_video, 1)
    mine = [along_x, along_y, swapped(along_x, "section", 2)]
    shared = mine + [swapped(each) for each in mine]
    rest_kernels = core_half(1 - core)

    narrow = own_width + 2 * blocks
    cuts = pl.pallas_call(
        functools.partial(cotangent_kernel, blocks, narrow),
        name="cotangent",
        in_specs=[vmem] * 4,
        out_specs=[vmem] * group,
        out_shape=[jax.ShapeDtypeStruct((2, cores * frames_in, rows_in * narrow, chans), BF16)] * group,
        scratch_shapes=[
            pltpu.VMEM((2, cores * frames_in, rows_in, columns + 2 * blocks, chans), F32)
        ],
        compiler_params=params,
    )(cotangent, swapped(cotangent), cot_halo, swapped(cot_halo))
    near, rest_kernels, *cuts = lax.optimization_barrier([near, rest_kernels] + list(cuts))
    shared = [half_kernels, rest_kernels] + shared
    videos = [own_video, near, far]
    videos += [swapped(each) for each in videos]
    cots = [cuts[0]] + [swapped(cuts[i], "space", i) for i in range(1, group)]

    geometry = (blocks, cores, group, frames_in, rows_in, halo, tile, width, total_rows, columns)
    frames = cores * frames_in
    high = tile + 2 * halo
    per_section = (blocks,) + half_kernels.shape
    taps = half_kernels.shape[0]
    all_kernels = (cores,) + per_section
    saved = [
        jax.ShapeDtypeStruct((frames, tile + 2 * block + 2, width, chans), F32)
        for block in range(blocks)
    ]
    cost = pl.CostEstimate(flops=6 * 10**9, bytes_accessed=8 * 10**6, transcendentals=10**6)
    features, hidden, *slopes = pl.pallas_call(
        functools.partial(forward_kernel, geometry),
        name="forward",
        in_specs=[vmem] * (2 * blocks + 6),
        out_specs=[vmem] * (2 + blocks),
        out_shape=[
            jax.ShapeDtypeStruct((blocks, frames, tile + 2, own_width, 3 * chans), BF16),
            jax.ShapeDtypeStruct((blocks, frames, tile, own_width, chans), BF16),
        ]
        + saved,
        scratch_shapes=[
            pltpu.VMEM((frames, high, width, 3 * chans), BF16),
            pltpu.VMEM((frames, high, width, chans), BF16),
            pltpu.VMEM((high, width, chans), F32),
            pltpu.VMEM(all_kernels, BF16),
            pltpu.VMEM((frames, high, width, chans), BF16),
            pltpu.VMEM((12 * chans, 2 * chans), BF16),
        ],
        compiler_params=params,
        cost_estimate=cost,
    )(*shared, *videos)

    back = jax.ShapeDtypeStruct((group, frames_in, rows_in, own_width, chans), BF16)
    features, *after = lax.optimization_barrier([features] + shared)
    arranged = [
        jax.ShapeDtypeStruct((blocks, rows * chans, 2 * chans), BF16) for rows in (12, 4, 2)
    ]
    arranged = pl.pallas_call(
        functools.partial(arrangement_kernel, group),
        name="arrangement",
        in_specs=[vmem] * len(after),
        out_specs=[vmem] * 3,
        out_shape=arranged,
        scratch_shapes=[pltpu.VMEM(all_kernels, BF16)],
        compiler_params=params,
        cost_estimate=pl.CostEstimate(flops=10**9, bytes_accessed=10**6, transcendentals=0),
    )(*after)
    pixel_count = frames * total_rows * columns
    factor = 1.0 / float(pixel_count) ** 0.5
    keep, give, mine_grad, other_grad = pl.pallas_call(
        functools.partial(backward_kernel, geometry, factor),
        name="backward",
        in_specs=[vmem] * (blocks + group + 5),
        out_specs=[vmem] * 4,
        out_shape=[
            jax.ShapeDtypeStruct(per_section, BF16),
            jax.ShapeDtypeStruct(per_section, BF16),
            back,
            back,
        ],
        scratch_shapes=[
            pltpu.VMEM((frames, tile + 2 * blocks, width, chans), BF16),
            pltpu.VMEM((frames, tile + 2 * blocks, width, 3 * chans), BF16),
            pltpu.VMEM((frames, tile, own_width, chans), BF16),
            pltpu.VMEM((frames, tile, own_width, chans), BF16),
            pltpu.VMEM(all_kernels, BF16),
            pltpu.VMEM((frames, tile, own_width, chans), BF16),
        ],
        compiler_params=params,
        cost_estimate=cost,
    )(*arranged, *cots, features, hidden, *slopes)

    got = swapped(give)
    parts = [(keep[i].astype(F32) + got[i].astype(F32)).astype(BF16) for i in range(blocks)]
    other_grad, *parts = lax.optimization_barrier([other_grad] + parts)
    parts = parts[:1] + [swapped(parts[i], "section", i) for i in range(1, blocks)]
    other_grad = swapped(other_grad)
    first = core == 0
    wide = jnp.concatenate(
        [jnp.where(first, mine_grad, other_grad), jnp.where(first, other_grad, mine_grad)], 3
    )
    strips = [wide[0]] + [swapped(wide[i], "space", i) for i in range(1, group)]
    received = lax.optimization_barrier(parts + strips)
    parts, strips = received[:blocks], received[blocks:]
    part = sum(each.astype(F32) for each in parts).astype(BF16)

    halves = part.reshape(2, -1, chans)
    low = unit % 2

    def picked(which):
        return lax.dynamic_index_in_dim(halves, which, 0, keepdims=False)

    part = (picked(low).astype(F32) + swapped(picked(1 - low), "space", 1).astype(F32)).astype(BF16)
    part = part.astype(F32) + swapped(part, "space", 2).astype(F32)
    if tiles != group:
        part = lax.psum(
            part, "space", axis_index_groups=[list(range(i, tiles, group)) for i in range(group)]
        )
    part = part.astype(BF16)
    pair = jnp.stack([part, swapped(part, "space", 1)])
    spatial_out, temporal_out = pl.pallas_call(
        functools.partial(closing_kernel, group),
        name="closing",
        in_specs=[vmem] * 2,
        out_specs=[vmem] * 2,
        out_shape=[
            jax.ShapeDtypeStruct(spatial_weights.shape, F32),
            jax.ShapeDtypeStruct(temporal_weights.shape, F32),
        ],
        scratch_shapes=[pltpu.VMEM((cores * taps * chans, chans), BF16)],
        compiler_params=params,
    )(pair, swapped(pair))

    grad_video = jnp.zeros(video.shape, BF16)
    for step, strip in enumerate(strips):
        grad_video = lax.dynamic_update_slice(
            grad_video, strip, (0, 0, (unit ^ step) * cores * own_width, 0)
        )
    return spatial_out, temporal_out, grad_video


def solution(mesh):
    return jax.shard_map(
        on_device,
        mesh=mesh,
        in_specs=(
            P("tm", ("section", "space"), None, None),
            P("tm", ("section", "space"), None, None),
            P("section", None, None, None),
            P("section", None, None, None),
        ),
        out_specs=(
            P("section", None, None, None),
            P("section", None, None, None),
            P("tm", ("section", "space"), None, None),
        ),
        check_vma=False,
    )
```

```python
import functools

import jax
import jax.numpy as jnp
from jax import lax
from jax.experimental import pallas as pl
from jax.experimental.pallas import tpu as pltpu
from jax.sharding import PartitionSpec as P

F32 = jnp.float32
BF16 = jnp.bfloat16


def rolled(value, steps):
    return pltpu.roll(value, steps % value.shape[0], 0)


def dot_first(left, right):
    return lax.dot_general(left, right, (((0,), (0,)), ((), ())), preferred_element_type=F32)


def kernel_of(w_ref, block, tap):
    taps = w_ref.shape[2]
    return w_ref[tap // taps, block, tap % taps]


def pair_rows(w_ref, block, pair_ref):
    chans = w_ref.shape[-1]
    for source in range(4):
        for target in range(2):
            ky = source - target
            for kx in range(3):
                at = (3 * source + kx) * chans
                tile = kernel_of(w_ref, block, 3 * ky + kx) if 0 <= ky < 3 else jnp.zeros((chans, chans), BF16)
                pair_ref[at : at + chans, target * chans : (target + 1) * chans] = tile


def turned(w_ref, block, tap):
    return kernel_of(w_ref, block, tap).astype(F32).T.astype(BF16)


def pair_rows_back(w_ref, block, pair_ref):
    chans = w_ref.shape[-1]
    nothing = jnp.zeros((chans, chans), BF16)
    for kx in range(3):
        for ky in range(3):
            tile = turned(w_ref, block, 3 * ky + kx)
            for target in range(2):
                at = (3 * (2 + target - ky) + kx) * chans
                pair_ref[at : at + chans, target * chans : (target + 1) * chans] = tile
        for source, target in ((3, 0), (0, 1)):
            at = (3 * source + kx) * chans
            pair_ref[at : at + chans, target * chans : (target + 1) * chans] = nothing


def pair_frames(w_ref, block, first, count):
    chans = w_ref.shape[-1]
    columns = []
    for target in (count - 2, count - 1):
        tiles = []
        for source in range(count):
            kt = source - target + 2
            tiles.append(kernel_of(w_ref, block, 9 + kt) if 0 <= kt < 3 else jnp.zeros((chans, chans), BF16))
        columns.append(jnp.concatenate(tiles, 0))
    return jnp.concatenate(columns, 1)


def pair_frames_back(w_ref, block, count):
    chans = w_ref.shape[-1]
    tiles = [turned(w_ref, block, 9 + kt) for kt in range(3)]
    columns = []
    for target in range(2):
        column = []
        for source in range(count):
            kt = 2 - (source - target)
            column.append(tiles[kt] if 0 <= kt < 3 else jnp.zeros((chans, chans), BF16))
        columns.append(jnp.concatenate(column, 0))
    return jnp.concatenate(columns, 1)


def row_pairs(ref, frame, first, pairs):
    width, lanes = ref.shape[2:]
    rows = []
    for start in (first, first + 2):
        value = ref[frame, start : start + 2 * pairs].reshape(pairs, 2, width, lanes)
        rows += [value[:, 0], value[:, 1]]
    return jnp.concatenate(rows, 2).reshape(pairs * width, 4 * lanes)


def woven(value, width):
    chans = value.shape[1] // 2
    split = [value[:, i * chans : (i + 1) * chans].reshape(-1, 1, width, chans) for i in range(2)]
    return jnp.concatenate(split, 1).reshape(-1, chans)


def ordered(count):
    return [0] + list(range(count - 1, 0, -1))


def placed(group):
    place, section = lax.axis_index("space"), lax.axis_index("section")
    band = (section * lax.axis_size("space") + place) // group
    return lax.axis_index("tm"), section, band, place % group


def window_kernel(halo, span, video_ref, *rest):
    targets, wide_ref = rest[:-1], rest[-1]
    unit = placed(len(targets))[3]
    frames, rows, columns, chans = video_ref.shape
    edge = jnp.zeros((frames, rows, halo, chans), F32)
    wide_ref[:, :, :halo] = edge
    wide_ref[:, :, halo + columns :] = edge
    wide_ref[:, :, halo : halo + columns] = video_ref[...].astype(F32)
    for step, target in enumerate(targets):
        at = jnp.bitwise_xor(unit, step) * (span - 2 * halo)
        target[...] = wide_ref[:, :, pl.ds(pl.multiple_of(at, 16), span)].astype(BF16)


def cotangent_kernel(reach, width, *rest):
    sources, targets, wide_ref = rest[:4], rest[4:-1], rest[-1]
    core, _, _, unit = placed(len(targets))
    frames_in, rows, columns, chans = sources[0].shape
    edge = jnp.zeros((2, 2 * frames_in, rows, reach, chans), F32)
    wide_ref[:, :, :, :reach] = edge
    wide_ref[:, :, :, reach + columns :] = edge
    for index, ref in enumerate(sources):
        whose = core if index % 2 == 0 else 1 - core
        wide_ref[index // 2, pl.ds(whose * frames_in, frames_in), :, reach : reach + columns] = ref[
            ...
        ].astype(F32)
    own = width - 2 * reach
    for step, target in enumerate(targets):
        at = (jnp.bitwise_xor(unit, step) * 2 + core) * own
        window = wide_ref[:, :, :, pl.ds(pl.multiple_of(at, 16), width)]
        target[...] = window.reshape(target.shape).astype(BF16)


def closing_kernel(group, mine_ref, other_ref, spatial_ref, temporal_ref, flat_ref):
    pieces, rows, chans = mine_ref.shape
    core, _, _, unit = placed(group)
    for whose, ref in ((core, mine_ref), (1 - core, other_ref)):
        for step in range(pieces):
            index = whose * pieces + jnp.bitwise_xor(jnp.bitwise_and(unit, pieces - 1), step)
            flat_ref[pl.ds(pl.multiple_of(index * rows, 16), rows)] = ref[step]
    count = spatial_ref.shape[1]
    for tap in range(count + temporal_ref.shape[1]):
        turned = flat_ref[tap * chans : (tap + 1) * chans].astype(F32).T
        if tap < count:
            spatial_ref[0, tap] = turned
        else:
            temporal_ref[0, tap - count] = turned


def place_kernels(core, section, w_ref, own_mine, own_other, mine_refs, other_refs):
    w_ref[core, section] = own_mine[...]
    w_ref[1 - core, section] = own_other[...]
    for step, (mine_ref, other_ref) in enumerate(zip(mine_refs, other_refs)):
        block = jnp.bitwise_xor(section, step + 1)
        w_ref[core, block] = mine_ref[...]
        w_ref[1 - core, block] = other_ref[...]


def forward_kernel(geometry, *rest):
    blocks, cores, group, frames_in, rows_in, halo, tile, width, height, columns = geometry
    core, section, band, unit = placed(group)
    odd = band % 2
    shared, rest = rest[: 2 * blocks], rest[2 * blocks :]
    arrived, rest = rest[:6], rest[6:]
    xo_ref, ho_ref = rest[:2]
    d_refs = rest[2 : 2 + blocks]
    x_ref, h_ref, mask_ref, w_ref, start_ref, pair_ref = rest[2 + blocks :]
    place_kernels(core, section, w_ref, *shared[:2], shared[2 : 1 + blocks], shared[1 + blocks :])
    frames = cores * frames_in
    high = tile + 2 * halo
    chans = w_ref.shape[-1]
    own_rows, own_cols = (halo, halo + tile), (halo, width - halo)
    row = band * tile - halo + lax.broadcasted_iota(jnp.int32, (high, width, chans), 0)
    left = (unit * cores + core) * (width - 2 * halo) - halo
    col = left + lax.broadcasted_iota(jnp.int32, (high, width, chans), 1)
    inside = (row >= 0) & (row < height) & (col >= 0) & (col < columns)
    mask_ref[...] = jnp.where(inside, 1.0, 0.0).astype(F32)

    def keep(block, frame, value, first):
        triple = [rolled(value, 1), value, rolled(value, -1)]
        count = value.shape[0] // width
        both = jnp.concatenate([part.astype(BF16) for part in triple], 1)
        x_ref[frame, first : first + count] = both.reshape(count, width, 3 * chans)
        start = own_rows[0] - 1 - first
        cut = [
            part.reshape(count, width, chans)[
                start : start + tile + 2, own_cols[0] : own_cols[1]
            ].astype(BF16)
            for part in triple
        ]
        xo_ref[block, frame] = jnp.concatenate(cut, 2)

    near = tile + halo - odd * (tile + halo)
    columns_at = pl.ds(pl.multiple_of(core * (width - 2 * halo), 16), width)
    for index, ref in enumerate(arrived):
        base = (halo, near, tile + halo - near)[index % 3]
        whose = core if index < 3 else 1 - core
        for step in range(group):
            row = base + jnp.bitwise_xor(unit, step) * rows_in
            start_ref[pl.ds(whose * frames_in, frames_in), pl.ds(row, rows_in)] = ref[
                step, :, :, columns_at, :
            ]
    for frame in range(frames):
        keep(0, frame, start_ref[frame].reshape(high * width, chans).astype(F32), 0)

    for block in range(blocks):
        first, last = block + 1, high - block - 1
        count = last - first
        pair_rows(w_ref, block, pair_ref)
        mask = mask_ref[first:last].reshape(count * width, chans)
        for frame in range(frames):
            taps = row_pairs(x_ref, frame, first - 1, count // 2)
            before = jnp.dot(taps, pair_ref[...], preferred_element_type=F32)
            before = woven(before, width)
            sigma = 0.5 + 0.5 * jnp.tanh(0.5 * before)
            masked = sigma * mask
            hidden = before * masked
            h_ref[frame, first:last] = hidden.astype(BF16).reshape(count, width, chans)
            hidden = hidden.reshape(count, width, chans)
            ho_ref[block, frame] = hidden[
                own_rows[0] - first : own_rows[1] - first, own_cols[0] : own_cols[1]
            ].astype(BF16)
            rim = block + 1
            kept = slice(own_rows[0] - rim - first, own_rows[1] + rim - first)
            sigma = sigma.reshape(count, width, chans)[kept]
            masked = masked.reshape(count, width, chans)[kept]
            d_refs[block][frame] = masked + hidden[kept] * (1.0 - sigma)
        if block + 1 == blocks:
            break
        for frame in range(0, frames, 2):
            start = max(frame - 2, 0)
            timeline = jnp.concatenate(
                [
                    h_ref[each, first:last].reshape(count * width, chans)
                    for each in range(start, frame + 2)
                ],
                1,
            )
            weights = pair_frames(w_ref, block, start, frame + 2 - start)
            both = jnp.dot(timeline, weights, preferred_element_type=F32)
            for inner in range(2):
                mixed = both[:, inner * chans : (inner + 1) * chans]
                old = x_ref[frame + inner, first:last, :, chans : 2 * chans].astype(F32)
                new = old.reshape(count * width, chans) + mixed
                keep(block + 1, frame + inner, new.astype(BF16).astype(F32), first)


def backward_kernel(geometry, factor, *rest):
    blocks, cores, group, frames_in, rows_in, halo, tile, width, height, columns = geometry
    core, section, band, unit = placed(group)
    shared, rest = rest[: 2 * blocks], rest[2 * blocks :]
    arrived, rest = rest[:group], rest[group:]
    xo_ref, ho_ref = rest[:2]
    d_refs = rest[2 : 2 + blocks]
    keep_ref, give_ref, mine_out, other_out = rest[2 + blocks : 6 + blocks]
    g_ref, da_ref, dao_ref, go_ref, w_ref, grad_ref, out_ref, pair_ref = rest[6 + blocks :]
    place_kernels(core, section, w_ref, *shared[:2], shared[2 : 1 + blocks], shared[1 + blocks :])
    frames = cores * frames_in
    chans = w_ref.shape[-1]
    rim = blocks
    own_cols = (halo, width - halo)
    per_core = w_ref.shape[2]
    pixels = tile * (own_cols[1] - own_cols[0])

    half = group // 2
    side = halo - rim
    edge = jnp.zeros((frames, rows_in, side, chans), F32)

    def widened(value):
        value = value.astype(F32).reshape(frames, rows_in, width - 2 * side, chans)
        return jnp.concatenate([edge, value, edge], 2).astype(BF16)

    for step, ref in zip(ordered(group), arrived):
        at = jnp.bitwise_xor(unit, step)
        g_ref[:, pl.ds(rim + at * rows_in, rows_in)] = widened(ref[0])
        beyond = jnp.where(at < half, rim + tile + at * rows_in, (at - half) * rows_in)
        g_ref[:, pl.ds(beyond, rows_in)] = widened(ref[1])

    def put(block, tap, value):
        slot = jnp.where(core == tap // per_core, 0, 1)
        where = jnp.bitwise_xor(section, block)
        grad_ref[slot, where, tap % per_core] = (value * factor).astype(BF16)

    for block in reversed(range(blocks)):
        edge = block + 1
        first, last = rim - edge, rim + tile + edge
        count = last - first
        for frame in range(frames):
            go_ref[frame] = g_ref[frame, rim : rim + tile].astype(F32)[
                :, own_cols[0] : own_cols[1]
            ].astype(BF16)
        pair_rows_back(w_ref, block, pair_ref)
        hiddens = []
        for frame in range(0, frames, 2):
            stop = min(frame + 4, frames)
            ahead = jnp.concatenate(
                [
                    g_ref[each, first:last].reshape(count * width, chans)
                    for each in range(frame, stop)
                ],
                1,
            )
            weights = pair_frames_back(w_ref, block, stop - frame)
            both = jnp.dot(ahead, weights, preferred_element_type=F32)
            hiddens += [both[:, :chans], both[:, chans:]]
        for frame in range(frames):
            hidden = hiddens[frame]
            slope = d_refs[block][frame].reshape(count * width, chans)
            value = (hidden * slope).astype(BF16).astype(F32)
            triple = [rolled(value, -1), value, rolled(value, 1)]
            both = jnp.concatenate([part.astype(BF16) for part in triple], 1)
            da_ref[frame, first:last] = both.reshape(count, width, 3 * chans)
            dao_ref[frame] = value.reshape(count, width, chans)[
                edge : edge + tile, own_cols[0] : own_cols[1]
            ].astype(BF16)
        for frame in range(frames):
            inner = count - 2
            taps = row_pairs(da_ref, frame, first, inner // 2)
            back = woven(jnp.dot(taps, pair_ref[...], preferred_element_type=F32), width)
            old = g_ref[frame, first + 1 : last - 1].astype(F32).reshape(inner * width, chans)
            new = (old + back).astype(BF16)
            if block:
                g_ref[frame, first + 1 : last - 1] = new.reshape(inner, width, chans)
            else:
                cut = new.astype(F32).reshape(inner, width, chans)[:, own_cols[0] : own_cols[1]]
                out_ref[frame] = cut.astype(BF16)
        slopes = dao_ref[...].reshape(frames * pixels, chans)
        taps = [
            xo_ref[block, :, ky : ky + tile].reshape(frames * pixels, 3 * chans) for ky in range(3)
        ]
        sums = dot_first(slopes, jnp.concatenate(taps, 1))
        for tap in range(9):
            put(block, tap, sums[:, tap * chans : (tap + 1) * chans])
        before = jnp.zeros((2 * pixels, chans), BF16)
        earlier = ho_ref[block].reshape(frames * pixels, chans)
        earlier = jnp.concatenate([before, earlier], 0)
        timeline = [earlier[kt * pixels : (kt + frames) * pixels] for kt in range(3)]
        sums = dot_first(
            go_ref[...].reshape(frames * pixels, chans), jnp.concatenate(timeline, 1)
        )
        for kt in range(3):
            put(block, 9 + kt, sums[:, kt * chans : (kt + 1) * chans])
    keep_ref[...] = grad_ref[0]
    give_ref[...] = grad_ref[1]
    for whose, target in ((core, mine_out), (1 - core, other_out)):
        for step in range(group):
            row = jnp.bitwise_xor(unit, step) * rows_in
            target[step] = out_ref[pl.ds(whose * frames_in, frames_in), pl.ds(row, rows_in)]


def swapped(value, axis="tm", step=1):
    count = lax.axis_size(axis)
    return lax.ppermute(value, axis, [(i, i ^ step) for i in range(count)])


def on_device(video, cotangent, spatial_weights, temporal_weights):
    blocks, cores, tiles = (lax.axis_size(name) for name in ("section", "tm", "space"))
    frames_in, rows_in, columns, chans = video.shape
    halo = 2 * blocks
    tile = halo
    group = tile // rows_in
    parties = cores * group
    own_width = columns // parties
    width = own_width + 2 * halo
    span = cores * own_width + 2 * halo
    vmem = pl.BlockSpec(memory_space=pltpu.VMEM)
    params = pltpu.CompilerParams(vmem_limit_bytes=32 * 2**20)

    bands = blocks * tiles // group
    core, section, band, unit = placed(group)

    def traded(value, shift):
        pairs = []
        for one in range(bands):
            other = ((one + shift) ^ 1) - shift
            if 0 <= other < bands:
                pairs += [(one * group + i, other * group + i) for i in range(group)]
        return lax.ppermute(value, ("section", "space"), pairs)

    total_rows = blocks * tiles * rows_in
    half = group // 2
    passed = []
    for one in range(bands - 1):
        for i in range(group):
            low, high = one * group + i, (one + 1) * group + i
            passed.append((high, low) if i < half else (low, high))
    cot_halo = lax.ppermute(cotangent, ("section", "space"), passed)

    padded = columns + 2 * halo
    cuts = pl.pallas_call(
        functools.partial(window_kernel, halo, span),
        name="windows",
        in_specs=[vmem],
        out_specs=[vmem] * group,
        out_shape=[jax.ShapeDtypeStruct((frames_in, rows_in, span, chans), BF16)] * group,
        scratch_shapes=[pltpu.VMEM((frames_in, rows_in, padded, chans), F32)],
        compiler_params=params,
    )(video)
    *cuts, spatial, temporal = lax.optimization_barrier(
        list(cuts) + [spatial_weights, temporal_weights]
    )
    def core_half(which):
        whole = jnp.concatenate([spatial[0], temporal[0]], 0)
        taps = whole.shape[0] // cores
        return lax.dynamic_slice_in_dim(whole, which * taps, taps, 0)

    half_kernels = core_half(core)

    def gathered(pieces):
        return jnp.stack([pieces[0]] + [swapped(pieces[i], "space", i) for i in range(1, group)])

    along_x = swapped(half_kernels, "section", 1)
    along_y = swapped(half_kernels, "section", 2)
    own_video, along_x, along_y, spatial, temporal = lax.optimization_barrier(
        [gathered(cuts), along_x, along_y, spatial, temporal]
    )
    near, far = traded(own_video, 0), traded(own_video, 1)
    mine = [along_x, along_y, swapped(along_x, "section", 2)]
    shared = mine + [swapped(each) for each in mine]
    rest_kernels = core_half(1 - core)

    narrow = own_width + 2 * blocks
    cuts = pl.pallas_call(
        functools.partial(cotangent_kernel, blocks, narrow),
        name="cotangent",
        in_specs=[vmem] * 4,
        out_specs=[vmem] * group,
        out_shape=[jax.ShapeDtypeStruct((2, cores * frames_in, rows_in * narrow, chans), BF16)] * group,
        scratch_shapes=[
            pltpu.VMEM((2, cores * frames_in, rows_in, columns + 2 * blocks, chans), F32)
        ],
        compiler_params=params,
    )(cotangent, swapped(cotangent), cot_halo, swapped(cot_halo))
    near, rest_kernels, *cuts = lax.optimization_barrier([near, rest_kernels] + list(cuts))
    shared = [half_kernels, rest_kernels] + shared
    videos = [own_video, near, far]
    videos += [swapped(each) for each in videos]
    cots = [swapped(cuts[i], "space", i) if i else cuts[0] for i in ordered(group)]

    geometry = (blocks, cores, group, frames_in, rows_in, halo, tile, width, total_rows, columns)
    frames = cores * frames_in
    high = tile + 2 * halo
    per_section = (blocks,) + half_kernels.shape
    taps = half_kernels.shape[0]
    all_kernels = (cores,) + per_section
    saved = [
        jax.ShapeDtypeStruct((frames, tile + 2 * block + 2, width, chans), F32)
        for block in range(blocks)
    ]
    cost = pl.CostEstimate(flops=6 * 10**9, bytes_accessed=8 * 10**6, transcendentals=10**6)
    features, hidden, *slopes = pl.pallas_call(
        functools.partial(forward_kernel, geometry),
        name="forward",
        in_specs=[vmem] * (2 * blocks + 6),
        out_specs=[vmem] * (2 + blocks),
        out_shape=[
            jax.ShapeDtypeStruct((blocks, frames, tile + 2, own_width, 3 * chans), BF16),
            jax.ShapeDtypeStruct((blocks, frames, tile, own_width, chans), BF16),
        ]
        + saved,
        scratch_shapes=[
            pltpu.VMEM((frames, high, width, 3 * chans), BF16),
            pltpu.VMEM((frames, high, width, chans), BF16),
            pltpu.VMEM((high, width, chans), F32),
            pltpu.VMEM(all_kernels, BF16),
            pltpu.VMEM((frames, high, width, chans), BF16),
            pltpu.VMEM((12 * chans, 2 * chans), BF16),
        ],
        compiler_params=params,
        cost_estimate=cost,
    )(*shared, *videos)

    back = jax.ShapeDtypeStruct((group, frames_in, rows_in, own_width, chans), BF16)
    pixel_count = frames * total_rows * columns
    factor = 1.0 / float(pixel_count) ** 0.5
    keep, give, mine_grad, other_grad = pl.pallas_call(
        functools.partial(backward_kernel, geometry, factor),
        name="backward",
        in_specs=[vmem] * (3 * blocks + group + 2),
        out_specs=[vmem] * 4,
        out_shape=[
            jax.ShapeDtypeStruct(per_section, BF16),
            jax.ShapeDtypeStruct(per_section, BF16),
            back,
            back,
        ],
        scratch_shapes=[
            pltpu.VMEM((frames, tile + 2 * blocks, width, chans), BF16),
            pltpu.VMEM((frames, tile + 2 * blocks, width, 3 * chans), BF16),
            pltpu.VMEM((frames, tile, own_width, chans), BF16),
            pltpu.VMEM((frames, tile, own_width, chans), BF16),
            pltpu.VMEM(all_kernels, BF16),
            pltpu.VMEM(all_kernels, BF16),
            pltpu.VMEM((frames, tile, own_width, chans), BF16),
            pltpu.VMEM((12 * chans, 2 * chans), BF16),
        ],
        compiler_params=params,
        cost_estimate=cost,
    )(*shared, *cots, features, hidden, *slopes)

    got = swapped(give)
    parts = [(keep[i].astype(F32) + got[i].astype(F32)).astype(BF16) for i in range(blocks)]
    other_grad, *parts = lax.optimization_barrier([other_grad] + parts)
    parts = parts[:1] + [swapped(parts[i], "section", i) for i in range(1, blocks)]
    other_grad = swapped(other_grad)
    first = core == 0
    wide = jnp.concatenate(
        [jnp.where(first, mine_grad, other_grad), jnp.where(first, other_grad, mine_grad)], 3
    )
    strips = [wide[0]] + [swapped(wide[i], "space", i) for i in range(1, group)]
    received = lax.optimization_barrier(parts + strips)
    parts, strips = received[:blocks], received[blocks:]
    part = sum(each.astype(F32) for each in parts).astype(BF16)

    halves = part.reshape(2, -1, chans)
    low = unit % 2

    def picked(which):
        return lax.dynamic_index_in_dim(halves, which, 0, keepdims=False)

    part = (picked(low).astype(F32) + swapped(picked(1 - low), "space", 1).astype(F32)).astype(BF16)
    part = part.astype(F32) + swapped(part, "space", 2).astype(F32)
    if tiles != group:
        part = lax.psum(
            part, "space", axis_index_groups=[list(range(i, tiles, group)) for i in range(group)]
        )
    part = part.astype(BF16)
    pair = jnp.stack([part, swapped(part, "space", 1)])
    spatial_out, temporal_out = pl.pallas_call(
        functools.partial(closing_kernel, group),
        name="closing",
        in_specs=[vmem] * 2,
        out_specs=[vmem] * 2,
        out_shape=[
            jax.ShapeDtypeStruct(spatial_weights.shape, F32),
            jax.ShapeDtypeStruct(temporal_weights.shape, F32),
        ],
        scratch_shapes=[pltpu.VMEM((cores * taps * chans, chans), BF16)],
        compiler_params=params,
    )(pair, swapped(pair))

    grad_video = jnp.zeros(video.shape, BF16)
    for step, strip in enumerate(strips):
        grad_video = lax.dynamic_update_slice(
            grad_video, strip, (0, 0, (unit ^ step) * cores * own_width, 0)
        )
    return spatial_out, temporal_out, grad_video


def solution(mesh):
    return jax.shard_map(
        on_device,
        mesh=mesh,
        in_specs=(
            P("tm", ("section", "space"), None, None),
            P("tm", ("section", "space"), None, None),
            P("section", None, None, None),
            P("section", None, None, None),
        ),
        out_specs=(
            P("section", None, None, None),
            P("section", None, None, None),
            P("tm", ("section", "space"), None, None),
        ),
        check_vma=False,
    )
```
